32 devices in a mesh: groups: 2 (over y), attn: 4 (over z), expert: 4 (over x, core).
Axes of the slice: x: 2, y: 2, z: 4, core: 2. Of those that a mesh axis runs over, the one named last changes fastest.
Arguments:
- queries: bfloat16 [512, 3072], P(('groups', 'attn', 'expert')), parts along dimension 0, may hold values from -132 to 132
- cached_keys: bfloat16 [512, 96, 512], P(('groups', 'attn', 'expert')), parts along dimension 0, may hold values from -6 to 6
- cached_values: bfloat16 [512, 96, 512], P(('groups', 'attn', 'expert')), parts along dimension 0, may hold values from -6 to 6
- lengths: int32 [512], P(('groups', 'attn', 'expert')), parts along dimension 0, may hold values from 1 to 96, 12288 in all
- routes: int32 [512, 2], P(('groups', 'attn', 'expert')), parts along dimension 0, may hold values from 0 to 3, all different within a row; in each aligned block of 16 rows (0 to 15, 16 to 31, ...) at most 8 rows name the same one
- residual: bfloat16 [512, 3072], P(('groups', 'attn', 'expert')), parts along dimension 0, may hold values from -3 to 3
- norm_gain: float32 [3072], replicated, may hold values from 0.5 to 1.5
- router: bfloat16 [3072, 4], replicated, may hold values from -0.109375 to 0.109375
- gate_proj: bfloat16 [4, 3072, 8192], P('expert', None, 'attn'), may hold values from -0.109375 to 0.109375
- up_proj: bfloat16 [4, 3072, 8192], P('expert', None, 'attn'), may hold values from -0.109375 to 0.109375
- down_proj: bfloat16 [4, 8192, 3072], P('expert', 'attn'), may hold values from -0.0625 to 0.0625
Outputs:
- layer_out: bfloat16 [512, 3072], P(('groups', 'attn', 'expert')), parts along dimension 0
The draws below stay inside these ranges and needn't reach their ends.
There are 2 independent parts, one for each index of `groups`. The reference program is written for one: setup_inputs(seed, part) draws one part's arguments, and reference() takes and returns one part's arrays. A program takes and returns all parts, laid end to end along the dimension named above; an argument that names none is the same for every part. Nothing has to cross between parts.
Inputs may be any that keep to these rules, and one draw needn't show every extreme that they name: `routes`: each row names two different experts. Among the 16 rows of one device (aligned blocks of rows, in order) no expert is named by more than 8 rows, a bound that some block reaches. `lengths`: some request has all 96 slots live.
All inputs are finite; a program needn't handle non-finite values. No bound on the sum of `lengths` on one device may be relied on, other than what follows from the above.
Results may differ from the reference program's by a relative error of at most 0.0075.
Values may be sent and summed in bfloat16 or wider, within the bound.
No kernel may reach another device: no remote copies, remote signals or barrier semaphores. Data moves between devices by JAX's collectives and lax.ppermute only.
A program may use at most 128 MiB of HBM per device.

```python
import math
from functools import partial
import jax
import jax.numpy as jnp
import numpy as np
from jax import lax

D = 3072
HS = 128
QH = 24
KVH = 4
FF = 8192
REQ_DEV = 16
CACHE = 96
E = 4
GROUP = 6
CAP = 8
ROWS = 256
N_ATTN = 4
N_EXPERT = 4


def shared_keys(key):
    return jnp.clip(jax.random.normal(key, (ROWS, CACHE, KVH * HS), jnp.float32), -6.0, 6.0)


def draw_cached_keys(key, part):
    common = shared_keys(key)
    return common.astype(jnp.bfloat16)


def draw_queries(key, part):
    key = jax.random.fold_in(key, 12)
    drawn = jnp.clip(jax.random.normal(key, (ROWS, QH * HS), jnp.float32), -6.0, 6.0)
    return drawn.astype(jnp.bfloat16)


def steps_of(own_key, dims, shards, smallest, top_value):
    def one(dim, parts):
        heights = jax.random.uniform(jax.random.fold_in(jax.random.fold_in(own_key, 6), dim), (parts,), jnp.float32, smallest / len(shards), top_value / len(shards))
        return jnp.repeat(jnp.exp(heights), dims[dim] // parts).reshape((-1,) + (1,) * (len(dims) - dim - 1))

    gain = one(*shards[0])
    for cut in shards[1:]:
        gain = gain * one(*cut)
    return gain


def length_profile(count, total, limit, lean):
    loads = [(1 << 20) // math.isqrt(standing ** lean) + 1 for standing in range(2, count + 1)]
    surplus, holding = total - limit - (count - 1), [1] * (count - 1)
    while surplus > 0:
        movable = [i for i in range(count - 1) if holding[i] < limit]
        mass, left = sum([loads[i] for i in movable]), surplus
        for i in movable:
            addition = min(limit - holding[i], max(1, left * loads[i] // mass), surplus)
            holding[i] = holding[i] + addition
            surplus = surplus - addition
    return np.array([limit] + holding)


def uneven_parts(rng, amount, total, bound, skew):
    if amount == 2:
        one = jax.random.randint(rng, (), max(1, total - bound), min(bound, total - 1) + 1)
        return jnp.stack([one, total - one])
    sizes = jnp.asarray(length_profile(amount, total, bound, skew), jnp.int32)
    couples = (amount - 1) // 2
    giver, receiver = sizes[1:1 + 2 * couples:2], sizes[2:2 + 2 * couples:2]
    margin = jnp.minimum(giver - 1, bound - receiver)
    moved = jax.random.randint(jax.random.fold_in(rng, 1), (couples,), 0, 1 << 20) % (margin + 1)
    sizes = sizes.at[1:1 + 2 * couples:2].set(giver - moved).at[2:2 + 2 * couples:2].set(receiver + moved)
    return sizes[jax.random.permutation(jax.random.fold_in(rng, 2), amount)]


def assign_block(stream_key, own, number, rows, number_of, top, reach, skew):
    sequence = jax.random.permutation(stream_key, number_of)
    crowded, usual = portions_of(number_of, rows * top, reach, skew, True), portions_of(number_of, rows * top, reach, skew, False)
    places = jnp.arange(number_of)

    def named(tallies, rotation):
        used = int((tallies > 0).sum())
        fixed = max(1, used // 4)
        moved = fixed + (places - fixed + rotation * (used - fixed)) % max(1, number_of - fixed)
        return jnp.zeros((number_of,), jnp.int32).at[sequence[jnp.where(places < fixed, places, moved)]].set(jnp.asarray(tallies, jnp.int32))

    tallies = jnp.where(number % 4 == 0, named(crowded, number // 4), named(usual, number - number // 4 - 1))
    mixed = jax.random.permutation(jax.random.fold_in(own, 3), number_of)
    source_of, taker = mixed[0:number_of // 2 * 2:2], mixed[1:number_of // 2 * 2:2]
    slack = jnp.minimum(tallies[source_of] - 1, reach - tallies[taker]) // 2
    slack = jnp.where((source_of == sequence[0]) | (taker == sequence[0]) | (tallies[taker] == 0), 0, jnp.maximum(slack, 0))
    moved = jax.random.randint(jax.random.fold_in(own, 4), (number_of // 2,), 0, 1 << 20) % (slack + 1)
    tallies = tallies.at[source_of].add(-moved).at[taker].add(moved)
    labels = jnp.searchsorted(jnp.cumsum(tallies), jnp.arange(rows * top), side="right").astype(jnp.int32)
    table = labels.reshape(top, rows).T
    table = table[jax.random.permutation(jax.random.fold_in(own, 1), rows)]
    rotation = jax.random.randint(jax.random.fold_in(own, 2), (rows, 1), 0, top)
    return jnp.take_along_axis(table, (jnp.arange(top)[None, :] + rotation) % top, axis=1)


def portions_of(amount, total, bound, skew, full):
    weights = [(1 << 20) // math.isqrt(grade ** skew) + 1 for grade in range(1, amount + 1)]
    largest = bound if full else min(bound, max(-(-total // amount), total * weights[0] // sum(weights)))
    least = 1 if total - largest >= amount - 1 else 0
    holding, rest = [largest] + [least] * (amount - 1), total - largest - least * (amount - 1)
    while rest > 0:
        candidates = [i for i in range(1, amount) if holding[i] < largest] or [i for i in range(1, amount) if holding[i] < bound]
        mass, remaining = sum([weights[i] for i in candidates]), rest
        for i in candidates:
            addition = min(bound - holding[i], max(1, remaining * weights[i] // mass), rest)
            holding[i] = holding[i] + addition
            rest = rest - addition
    return np.array(holding)


def noise(rng, dims, spread, bound, split=(), held_as=jnp.bfloat16):
    values = jax.random.normal(rng, dims, jnp.float32) * spread
    if len(split) > 0:
        values = steps_of(rng, dims, split, -0.22, 0.18) * values
    return jnp.clip(values, min=-bound, max=bound).astype(held_as)


def setup_inputs(seed: int = 0, part: int = 0) -> dict:
    splits = jax.random.split(jax.random.key(seed), 12)
    part_splits = jax.random.split(jax.random.fold_in(splits[11], part), 12)
    queries = draw_queries(jax.random.fold_in(jax.random.fold_in(splits[11], part), 71), part)
    cached_keys = draw_cached_keys(jax.random.fold_in(jax.random.fold_in(splits[11], part), 71), part)
    cached_values = noise(part_splits[2], (ROWS, CACHE, KVH * HS), 1.0, 6.0, ((0, 16),))
    lengths = uneven_parts(part_splits[3], ROWS, ROWS * CACHE // 2, CACHE, 2).astype(jnp.int32)
    routes_keys = jax.random.split(jax.random.fold_in(part_splits[4], 1), ROWS // REQ_DEV)
    routes_turns = jax.random.permutation(jax.random.fold_in(part_splits[4], 3), ROWS // REQ_DEV)
    routes = jax.vmap(lambda own, number: assign_block(jax.random.fold_in(part_splits[4], 2), own, number, REQ_DEV, E, 2, CAP, 2))(routes_keys, routes_turns).reshape((ROWS, 2))
    residual = noise(part_splits[5], (ROWS, D), 0.5, 3.0, ((0, 16),))
    norm_gain = jnp.clip(1.0 + 0.1 * jax.random.normal(splits[6], (D,), jnp.float32), 0.5, 1.5)
    router = noise(splits[7], (D, E), D ** -0.5, 0.109375)
    gate_proj = noise(splits[8], (E, D, FF), D ** -0.5, 0.109375, ((0, 4), (2, 4)))
    up_proj = noise(splits[9], (E, D, FF), D ** -0.5, 0.109375, ((0, 4), (2, 4)))
    down_proj = noise(splits[10], (E, FF, D), FF ** -0.5, 0.0625, ((0, 4), (1, 4)))
    return {"queries": queries, "cached_keys": cached_keys, "cached_values": cached_values, "lengths": lengths, "routes": routes, "residual": residual, "norm_gain": norm_gain, "router": router, "gate_proj": gate_proj, "up_proj": up_proj, "down_proj": down_proj}


def attend(queries, cached_keys, cached_values, lengths):
    batch = queries.shape[0]
    window = cached_keys.shape[1]
    grouped = queries.astype(jnp.float32).reshape(batch, KVH, GROUP, HS)
    key_heads = cached_keys.astype(jnp.float32).reshape(batch, window, KVH, HS)
    value_heads = cached_values.astype(jnp.float32).reshape(batch, window, KVH, HS)
    scores = jnp.einsum('rkgd,rtkd->rkgt', grouped, key_heads) * HS ** (-0.5)
    visible = jnp.arange(window, dtype=jnp.int32)[None, :] < lengths[:, None]
    scores = jnp.where(visible[:, None, None, :], scores, -1e+30)
    highest = lax.optimization_barrier(jnp.max(scores, axis=-1, keepdims=True))
    powers = jnp.exp(scores - highest)
    weights = lax.optimization_barrier((powers / lax.optimization_barrier(jnp.sum(powers, axis=-1, keepdims=True))).astype(jnp.bfloat16))
    attended = jnp.einsum('rkgt,rtkd->rkgd', weights.astype(jnp.float32), value_heads)
    return attended.reshape(batch, KVH * GROUP * HS)

def gating(normed, router, routes):
    logits = jnp.dot(normed, router, preferred_element_type=jnp.float32)
    experts = router.shape[1]
    choose = routes[:, :, None] == jnp.arange(experts, dtype=jnp.int32)[None, None, :]
    picked = lax.optimization_barrier(jnp.sum(jnp.where(choose, logits[:, None, :], 0.0), axis=-1))
    first = 1.0 / (1.0 + jnp.exp(picked[:, 1] - picked[:, 0]))
    second = 1.0 / (1.0 + jnp.exp(picked[:, 0] - picked[:, 1]))
    return jnp.stack([first, second], axis=1)

def slot_table(routes, experts):
    listed = routes.reshape(-1)
    choose = (listed[:, None] == jnp.arange(experts, dtype=jnp.int32)[None, :]).astype(jnp.int32)
    earlier = jnp.cumsum(choose, axis=0) - choose
    position = lax.optimization_barrier(jnp.sum(earlier * choose, axis=1))
    target = listed * CAP + position
    return target[None, :] == jnp.arange(experts * CAP, dtype=jnp.int32)[:, None]

def expert_apply(inputs):
    slots, w_gate, w_up, w_down = inputs
    flattened = slots.reshape(-1, D)
    gate_part = jnp.dot(flattened, w_gate, preferred_element_type=jnp.float32)
    up_part = jnp.dot(flattened, w_up, preferred_element_type=jnp.float32)
    hidden = (jax.nn.silu(gate_part) * up_part).astype(jnp.bfloat16)
    pieces = FF // N_ATTN
    hidden_blocks = hidden.reshape(-1, N_ATTN, pieces).astype(jnp.float32)
    down_blocks = w_down.reshape(N_ATTN, pieces, D).astype(jnp.float32)
    partials = jnp.einsum('raf,afd->ard', hidden_blocks, down_blocks)
    partials = lax.optimization_barrier(partials.astype(jnp.bfloat16)).astype(jnp.float32)
    result = lax.optimization_barrier(jnp.sum(partials, axis=0)).astype(jnp.bfloat16)
    return result.reshape(slots.shape)

def reference(queries, cached_keys, cached_values, lengths, routes, residual, norm_gain, router, gate_proj, up_proj, down_proj):
    attended = attend(queries, cached_keys, cached_values, lengths)
    stream = residual.astype(jnp.float32) + attended
    scale = lax.rsqrt(lax.optimization_barrier(jnp.mean(stream * stream, axis=-1, keepdims=True)) + 1e-05)
    normed = (stream * scale * norm_gain).astype(jnp.bfloat16)
    gates = gating(normed, router, routes)
    devices = N_ATTN * N_EXPERT
    tables = jax.vmap(partial(slot_table, experts=E))(routes.reshape(devices, REQ_DEV, 2)).astype(jnp.float32)
    row_tables = tables.reshape(devices, E, CAP, REQ_DEV, 2).sum(axis=-1)
    buffers = jnp.einsum('vecr,vrd->evcd', row_tables, normed.reshape(devices, REQ_DEV, D).astype(jnp.float32)).astype(jnp.bfloat16)
    outputs = lax.map(expert_apply, (buffers, gate_proj, up_proj, down_proj))
    flat_outputs = jnp.transpose(outputs, (1, 0, 2, 3)).reshape(devices, E * CAP, D).astype(jnp.float32)
    picked = jnp.einsum('vsa,vsd->vad', tables, flat_outputs).reshape(ROWS, 2, D)
    return (stream + lax.optimization_barrier(jnp.sum(gates[:, :, None] * picked, axis=1))).astype(jnp.bfloat16)
```

```python
import jax
import jax.numpy as jnp
from jax import lax
from jax.sharding import PartitionSpec as P

HS = 128
KVH = 4
GROUP = 6
CAP = 8
LANES = 128


def attend(queries, cached_keys, cached_values, lengths):
    batch = queries.shape[0]
    window = cached_keys.shape[1]
    grouped = queries.reshape(batch, KVH, GROUP, HS)
    key_heads = cached_keys.reshape(batch, window, KVH, HS)
    value_heads = cached_values.reshape(batch, window, KVH, HS)
    scores = jnp.einsum(
        "rkgd,rtkd->rkgt", grouped, key_heads, preferred_element_type=jnp.float32
    ) * HS ** (-0.5)
    visible = jnp.arange(window, dtype=jnp.int32)[None, :] < lengths[:, None]
    scores = jnp.where(visible[:, None, None, :], scores, -1e30)
    highest = jnp.max(scores, axis=-1, keepdims=True)
    powers = jnp.exp(scores - highest)
    weights = (powers / jnp.sum(powers, axis=-1, keepdims=True)).astype(jnp.bfloat16)
    attended = jnp.einsum(
        "rkgt,rtkd->rkgd", weights, value_heads, preferred_element_type=jnp.float32
    )
    return attended.reshape(batch, KVH * GROUP * HS)


def gating(normed, router, routes):
    logits = jnp.dot(normed, router, preferred_element_type=jnp.float32)
    experts = router.shape[1]
    choose = routes[:, :, None] == jnp.arange(experts, dtype=jnp.int32)[None, None, :]
    picked = jnp.sum(jnp.where(choose, logits[:, None, :], 0.0), axis=-1)
    first = 1.0 / (1.0 + jnp.exp(picked[:, 1] - picked[:, 0]))
    second = 1.0 / (1.0 + jnp.exp(picked[:, 0] - picked[:, 1]))
    return jnp.stack([first, second], axis=1)


def slot_table(named, experts):
    listed = named.reshape(-1)
    choose = (listed[:, None] == jnp.arange(experts, dtype=jnp.int32)[None, :]).astype(jnp.int32)
    earlier = jnp.cumsum(choose, axis=0) - choose
    position = jnp.sum(earlier * choose, axis=1)
    target = listed * CAP + position
    return target[None, :] == jnp.arange(experts * CAP, dtype=jnp.int32)[:, None]


def swap(value, axis, step):
    if step == 0:
        return value
    count = lax.axis_size(axis)
    return lax.ppermute(value, axis, [(i, i ^ step) for i in range(count)])


def shards(
    queries,
    cached_keys,
    cached_values,
    lengths,
    routes,
    residual,
    norm_gain,
    router,
    gate_proj,
    up_proj,
    down_proj,
):
    batch, width = queries.shape
    experts = router.shape[1]
    layers = lax.axis_size("attn")
    columns = lax.axis_size("expert")
    me = lax.axis_index("expert")
    attended = attend(queries, cached_keys, cached_values, lengths)
    stream = residual.astype(jnp.float32) + attended
    scale = lax.rsqrt(jnp.mean(stream * stream, axis=-1, keepdims=True) + 1e-05)
    normed = (stream * scale * norm_gain).astype(jnp.bfloat16)
    named = jnp.pad(routes.astype(jnp.bfloat16), ((0, 0), (0, LANES - 2)))
    payload = jnp.concatenate([normed, named], axis=1)
    chunks = [swap(payload, "attn", step) for step in range(layers)]
    groups = [[0], list(range(1, layers))]

    tables, gates, inputs = [None] * layers, [None] * layers, {}
    for group in groups:
        slots = []
        for j in group:
            rows = chunks[j][:, :width]
            owners = chunks[j][:, width : width + 2].astype(jnp.int32)
            gates[j] = gating(rows, router, owners)
            tables[j] = slot_table(owners ^ me, experts)
            row_table = jnp.any(tables[j].reshape(experts * CAP, batch, 2), axis=-1)
            slots.append(
                jnp.dot(row_table.astype(jnp.bfloat16), rows, preferred_element_type=jnp.float32)
                .astype(jnp.bfloat16)
                .reshape(experts, CAP, width)
            )
        slots = jnp.concatenate(slots, axis=1)
        for step in range(columns):
            inputs[group[0], step] = swap(slots[step], "expert", step)

    order = [(group, step) for group in groups for step in range(columns)]
    gathered = jnp.concatenate([inputs[group[0], step] for group, step in order], axis=0)
    gate_part = jnp.dot(gathered, gate_proj[0], preferred_element_type=jnp.float32)
    up_part = jnp.dot(gathered, up_proj[0], preferred_element_type=jnp.float32)
    hidden = (jax.nn.silu(gate_part) * up_part).astype(jnp.bfloat16)
    partial = jnp.dot(hidden, down_proj[0], preferred_element_type=jnp.float32).astype(jnp.bfloat16)

    total = stream
    at, pieces = 0, {}
    for group, step in order:
        count = len(group) * CAP
        pieces[group[0], step] = partial[at : at + count]
        at += count
    for group in groups[::-1]:
        returned = [swap(pieces[group[0], step], "expert", step) for step in range(columns)]
        for place, j in list(enumerate(group))[::-1]:
            mine = jnp.concatenate(
                [block[place * CAP : (place + 1) * CAP] for block in returned], axis=0
            )
            picked = jnp.einsum(
                "sa,sd->ad", tables[j].astype(jnp.bfloat16), mine, preferred_element_type=jnp.float32
            ).reshape(batch, 2, width)
            mixed = jnp.sum(gates[j][:, :, None] * picked, axis=1)
            if j:
                mixed = swap(mixed.astype(jnp.bfloat16), "attn", j).astype(jnp.float32)
            total = total + mixed
    return total.astype(jnp.bfloat16)


def solution(mesh):
    in_specs = (
        P(("groups", "attn", "expert"), None),
        P(("groups", "attn", "expert"), None, None),
        P(("groups", "attn", "expert"), None, None),
        P(("groups", "attn", "expert")),
        P(("groups", "attn", "expert"), None),
        P(("groups", "attn", "expert"), None),
        P(),
        P(),
        P("expert", None, "attn"),
        P("expert", None, "attn"),
        P("expert", "attn", None),
    )
    out_specs = P(("groups", "attn", "expert"), None)
    return jax.shard_map(shards, mesh=mesh, in_specs=in_specs, out_specs=out_specs, check_vma=False)
```

```python
import functools

import jax
import jax.numpy as jnp
from jax import lax
from jax.experimental import pallas as pl
from jax.experimental.pallas import tpu as pltpu
from jax.sharding import PartitionSpec as P

HS = 128
KVH = 4
GROUP = 6
CAP = 8
LANES = 128
MIB = 1 << 20
F32 = jnp.float32
BF16 = jnp.bfloat16
ANY = pl.BlockSpec(memory_space=pl.ANY)
WHOLE = pl.BlockSpec(memory_space=pltpu.VMEM)
SCALAR = pl.BlockSpec(memory_space=pltpu.SMEM)


def dot(a, b, dims=((1,), (0,))):
    return lax.dot_general(a, b, (dims, ((), ())), preferred_element_type=F32)


def iota(shape, dim):
    return lax.broadcasted_iota(jnp.int32, shape, dim)


def slot_map(owners, chunks, batch, experts):
    rows, slots = chunks * batch, experts * chunks * CAP
    slot = iota((rows, slots), 1)
    row = iota((rows, slots), 0)
    expert = slot // (chunks * CAP)
    chunk = (slot // CAP) % chunks
    named = (owners[:, 0:1] == expert) | (owners[:, 1:2] == expert)
    named = named & (row // batch == chunk)
    named = jnp.where(named, 1.0, 0.0)
    left, right = iota((rows, rows), 0), iota((rows, rows), 1)
    before = jnp.where(right < left, 1.0, 0.0).astype(BF16)
    place = dot(before, named.astype(BF16))
    wanted = (slot % CAP).astype(F32)
    return jnp.where(place == wanted, named, 0.0)


def dispatch(me, rows, named, chunks, experts):
    owners = named[:, 0:2].astype(F32).astype(jnp.int32) ^ me
    table = slot_map(owners, chunks, rows.shape[0] // chunks, experts)
    return dot(table.astype(BF16), rows, ((0,), (0,)))


def combine(me, rows, named, router, returned, chunks, experts):
    routes = named[:, 0:2].astype(F32).astype(jnp.int32)
    logits = dot(rows, router, ((1,), (1,)))
    lane = iota(logits.shape, 1)
    first = jnp.sum(jnp.where(lane == routes[:, 0:1], logits, 0.0), axis=1, keepdims=True)
    second = jnp.sum(jnp.where(lane == routes[:, 1:2], logits, 0.0), axis=1, keepdims=True)
    gate0 = 1.0 / (1.0 + jnp.exp(second - first))
    gate1 = 1.0 / (1.0 + jnp.exp(first - second))
    owners = routes ^ me
    table = slot_map(owners, chunks, rows.shape[0] // chunks, experts)
    expert = iota(table.shape, 1) // (chunks * CAP)
    gates = table * jnp.where(owners[:, 0:1] == expert, gate0, gate1)
    high = gates.astype(BF16)
    low = (gates - high.astype(F32)).astype(BF16)
    return dot(high, returned) + dot(low, returned)


def attend_kernel(
    me_ref, lengths_ref, queries_ref, keys_ref, values_ref, routes_ref, residual_ref, gain_ref,
    stream_ref, payload_ref, *rest,
):
    slots, attended = rest[:-1], rest[-1]
    head = pl.program_id(0)
    batch, window, _ = keys_ref.shape
    keys = keys_ref[...].reshape(batch * window, HS)
    values = values_ref[...].reshape(batch * window, HS)
    block = queries_ref[...]
    stacked = jnp.concatenate([block[:, g * HS : (g + 1) * HS] for g in range(GROUP)], axis=0)
    scores = dot(stacked, keys, ((1,), (1,))) * HS ** (-0.5)
    column = iota((batch, batch * window), 1)
    row = iota((batch, batch * window), 0)
    length = jnp.zeros((batch, batch * window), jnp.int32)
    for r in range(batch):
        length = jnp.where(row == r, lengths_ref[r], length)
    begin = row * window
    bias = jnp.where((column >= begin) & (column < begin + length), 0.0, -1e30)
    scores = scores + jnp.concatenate([bias] * GROUP, axis=0)
    highest = jnp.max(scores, axis=1, keepdims=True)
    powers = jnp.exp(scores - highest)
    weights = (powers / jnp.sum(powers, axis=1, keepdims=True)).astype(BF16)
    mixed = dot(weights, values)
    attended[head] = jnp.concatenate(
        [mixed[g * batch : (g + 1) * batch] for g in range(GROUP)], axis=1
    )

    @pl.when(head == KVH - 1)
    def finish():
        stream = residual_ref[...].astype(F32) + jnp.concatenate(
            [attended[k] for k in range(KVH)], axis=1
        )
        width = stream.shape[1]
        scale = lax.rsqrt(jnp.mean(stream * stream, axis=1, keepdims=True) + 1e-05)
        normed = (stream * scale * gain_ref[...]).astype(BF16)
        lane = iota((batch, LANES), 1)
        same = iota((batch, batch), 0) == iota((batch, batch), 1)
        routes = [
            jnp.sum(jnp.where(same, routes_ref[k : k + 1, :], 0), axis=1, keepdims=True).astype(F32)
            for k in range(2)
        ]
        named = jnp.where(lane == 0, routes[0], jnp.where(lane == 1, routes[1], 0.0))
        named = named.astype(BF16)
        stream_ref[...] = stream
        payload_ref[:, :width] = normed
        payload_ref[:, width:] = named
        out = dispatch(me_ref[0], normed, named, 1, len(slots))
        for e, ref in enumerate(slots):
            ref[...] = out[e * CAP : (e + 1) * CAP].astype(BF16)


def split_kernel(me_ref, *refs, chunks, after):
    refs = refs[after:]
    payload = jnp.concatenate([ref[...] for ref in refs[:chunks]], axis=0)
    slots = refs[chunks:]
    width = slots[0].shape[1]
    rows, named = payload[:, :width], payload[:, width:]
    out = dispatch(me_ref[0], rows, named, chunks, len(slots))
    span = chunks * CAP
    for e, ref in enumerate(slots):
        ref[...] = out[e * span : (e + 1) * span].astype(BF16)


def expert_kernel(*refs, pieces):
    xs, (gate_ref, up_ref, down_ref) = refs[:pieces], refs[pieces : pieces + 3]
    outs = refs[pieces + 3 : 2 * pieces + 3]
    rows_ref, hidden_ref = refs[2 * pieces + 3 :]
    rows_ref[...] = jnp.concatenate([ref[...].astype(F32) for ref in xs], axis=0).astype(BF16)
    width, units = gate_ref.shape
    tile = min(256, units)

    @pl.loop(0, units // tile)
    def _(i):
        at = pl.ds(pl.multiple_of(i * tile, tile), tile)
        gate = dot(rows_ref[...], gate_ref[:, at])
        up = dot(rows_ref[...], up_ref[:, at])
        hidden_ref[:, at] = (jax.nn.silu(gate) * up).astype(BF16)

    @pl.loop(0, width // tile)
    def _(i):
        at = pl.ds(pl.multiple_of(i * tile, tile), tile)
        out = dot(hidden_ref[...], down_ref[:, at])
        begin = 0
        for ref in outs:
            count = ref.shape[0]
            ref[:, at] = out[begin : begin + count].astype(BF16)
            begin += count


def load_kernel(after_ref, *refs, count):
    del after_ref
    token_ref, sems = refs[-2:]
    copies = [
        pltpu.make_async_copy(source, target, sems.at[i])
        for i, (source, target) in enumerate(zip(refs[:count], refs[count : 2 * count]))
    ]
    for copy in copies:
        copy.start()
    for copy in copies:
        copy.wait()
    token_ref[...] = jnp.zeros_like(token_ref)


def load(after, *weights):
    size = sum(w.size * w.dtype.itemsize for w in weights)
    return pl.pallas_call(
        functools.partial(load_kernel, count=len(weights)),
        in_specs=[ANY] * (1 + len(weights)),
        out_specs=[WHOLE] * (len(weights) + 1),
        out_shape=[pltpu.VMEM(w.shape, w.dtype) for w in weights]
        + [jax.ShapeDtypeStruct((8, LANES), F32)],
        scratch_shapes=[pltpu.SemaphoreType.DMA((len(weights),))],
        compiler_params=params(0),
        cost_estimate=pl.CostEstimate(flops=0, bytes_accessed=2 * size, transcendentals=0),
    )(after, *[in_hbm(w) for w in weights])


def in_hbm(value):
    return pltpu.with_memory_space_constraint(value, pltpu.HBM)


def in_vmem(value):
    return pltpu.with_memory_space_constraint(value, pltpu.VMEM)


def mix_kernel(me_ref, router_ref, *refs, chunks, experts):
    payload = jnp.concatenate([ref[...] for ref in refs[:chunks]], axis=0)
    returned = jnp.concatenate(
        [ref[...].astype(F32) for ref in refs[chunks : chunks + experts]], axis=0
    ).astype(BF16)
    outs = refs[chunks + experts :]
    batch, width = outs[0].shape
    rows, named = payload[:, :width], payload[:, width:]
    mixed = combine(me_ref[0], rows, named, router_ref[...], returned, chunks, experts)
    for j, ref in enumerate(outs):
        ref[...] = mixed[j * batch : (j + 1) * batch].astype(BF16)


def finish_kernel(me_ref, router_ref, payload_ref, stream_ref, *refs, experts):
    returned = jnp.concatenate([ref[...].astype(F32) for ref in refs[:experts]], axis=0)
    out_ref = refs[-1]
    width = out_ref.shape[1]
    rows, named = payload_ref[:, :width], payload_ref[:, width:]
    total = stream_ref[...] + combine(
        me_ref[0], rows, named, router_ref[...], returned.astype(BF16), 1, experts
    )
    for ref in refs[experts:-1]:
        total = total + ref[...].astype(F32)
    out_ref[...] = total.astype(BF16)


def swap(value, axis, step):
    if step == 0:
        return value
    count = lax.axis_size(axis)
    return lax.ppermute(value, axis, [(i, i ^ step) for i in range(count)])


def params(elements):
    return pltpu.CompilerParams(vmem_limit_bytes=min(48 * MIB, 2 * MIB + 10 * elements))


def shards(
    queries,
    cached_keys,
    cached_values,
    lengths,
    routes,
    residual,
    norm_gain,
    router,
    gate_proj,
    up_proj,
    down_proj,
):
    batch, width = queries.shape
    window = cached_keys.shape[1]
    experts = router.shape[1]
    layers = lax.axis_size("attn")
    remote = layers - 1
    me = lax.axis_index("expert").astype(jnp.int32).reshape(1)
    full = lambda shape: pl.BlockSpec(shape, lambda k: (0,) * len(shape))
    shape = jax.ShapeDtypeStruct
    wide = width + LANES
    span = width // KVH

    stream, payload, *slots = pl.pallas_call(
        attend_kernel,
        grid=(KVH,),
        in_specs=[
            SCALAR,
            SCALAR,
            pl.BlockSpec((batch, span), lambda k: (0, k)),
            pl.BlockSpec((batch, window, HS), lambda k: (0, 0, k)),
            pl.BlockSpec((batch, window, HS), lambda k: (0, 0, k)),
            full((2, batch)),
            full((batch, width)),
            full((1, width)),
        ],
        out_specs=[full((batch, width)), full((batch, wide))] + [full((CAP, width))] * experts,
        out_shape=[shape((batch, width), F32), shape((batch, wide), BF16)]
        + [shape((CAP, width), BF16)] * experts,
        scratch_shapes=[pltpu.VMEM((KVH, batch, span), F32)],
        compiler_params=params(28 * batch * width),
    )(
        me,
        lengths,
        *[in_hbm(a) for a in (queries, cached_keys, cached_values, routes.T, residual, norm_gain[None])],
    )
    router = router.T

    payloads = [swap(payload, "attn", j) for j in range(1, layers)]
    near = [swap(slots[e], "expert", e) for e in range(experts)]
    *first, token = load(payload, gate_proj[0], up_proj[0])
    ahead = [*near[1:], token]
    slots = pl.pallas_call(
        functools.partial(split_kernel, chunks=remote, after=len(ahead)),
        in_specs=[SCALAR] + [WHOLE] * (len(ahead) + remote),
        out_specs=[WHOLE] * experts,
        out_shape=[shape((remote * CAP, width), BF16)] * experts,
        compiler_params=params(experts * remote * CAP * width),
    )(me, *ahead, *payloads)
    far = [swap(slots[e], "expert", e) for e in range(experts)]
    *second, _ = load(slots[0], down_proj[0])

    inputs = near + far
    total_rows = sum(block.shape[0] for block in inputs)
    units = gate_proj.shape[2]
    weights = [in_vmem(w) for w in (*first, *second)]
    results = pl.pallas_call(
        functools.partial(expert_kernel, pieces=len(inputs)),
        in_specs=[WHOLE] * (len(inputs) + 3),
        out_specs=[WHOLE] * len(inputs),
        out_shape=[shape(block.shape, BF16) for block in inputs],
        scratch_shapes=[pltpu.VMEM((total_rows, width), BF16), pltpu.VMEM((total_rows, units), BF16)],
        compiler_params=params(total_rows * width),
    )(*inputs, *weights)

    far = [swap(results[experts + e], "expert", e) for e in range(experts)]
    near = [swap(results[e], "expert", e) for e in range(experts)]
    mixed = pl.pallas_call(
        functools.partial(mix_kernel, chunks=remote, experts=experts),
        in_specs=[SCALAR] + [WHOLE] * (1 + remote + experts),
        out_specs=[WHOLE] * remote,
        out_shape=[shape((batch, width), BF16)] * remote,
        compiler_params=params(experts * remote * CAP * width),
    )(me, router, *payloads, *far)
    mixed = [swap(block, "attn", j + 1) for j, block in enumerate(mixed)]
    return pl.pallas_call(
        functools.partial(finish_kernel, experts=experts),
        in_specs=[SCALAR] + [WHOLE] * (3 + experts + remote),
        out_specs=WHOLE,
        out_shape=shape((batch, width), BF16),
        compiler_params=params(total_rows * width),
    )(me, router, payload, stream, *near, *mixed)


def solution(mesh):
    in_specs = (
        P(("groups", "attn", "expert"), None),
        P(("groups", "attn", "expert"), None, None),
        P(("groups", "attn", "expert"), None, None),
        P(("groups", "attn", "expert")),
        P(("groups", "attn", "expert"), None),
        P(("groups", "attn", "expert"), None),
        P(),
        P(),
        P("expert", None, "attn"),
        P("expert", None, "attn"),
        P("expert", "attn", None),
    )
    out_specs = P(("groups", "attn", "expert"), None)
    return jax.shard_map(shards, mesh=mesh, in_specs=in_specs, out_specs=out_specs, check_vma=False)
```

```python
import functools

import jax
import jax.numpy as jnp
from jax import lax
from jax.experimental import pallas as pl
from jax.experimental.pallas import tpu as pltpu
from jax.sharding import PartitionSpec as P

HS = 128
KVH = 4
GROUP = 6
CAP = 8
LANES = 128
MIB = 1 << 20
F32 = jnp.float32
BF16 = jnp.bfloat16
BUSY = pl.CostEstimate(flops=12_000_000_000, bytes_accessed=4_000_000, transcendentals=0)
ANY = pl.BlockSpec(memory_space=pl.ANY)
WHOLE = pl.BlockSpec(memory_space=pltpu.VMEM)
SCALAR = pl.BlockSpec(memory_space=pltpu.SMEM)


def dot(a, b, dims=((1,), (0,))):
    return lax.dot_general(a, b, (dims, ((), ())), preferred_element_type=F32)


def iota(shape, dim):
    return lax.broadcasted_iota(jnp.int32, shape, dim)


def slot_map(owners, chunks, batch, experts):
    rows, slots = chunks * batch, experts * chunks * CAP
    slot = iota((rows, slots), 1)
    row = iota((rows, slots), 0)
    expert = slot // (chunks * CAP)
    chunk = (slot // CAP) % chunks
    named = (owners[:, 0:1] == expert) | (owners[:, 1:2] == expert)
    named = named & (row // batch == chunk)
    named = jnp.where(named, 1.0, 0.0)
    left, right = iota((rows, rows), 0), iota((rows, rows), 1)
    before = jnp.where(right < left, 1.0, 0.0).astype(BF16)
    place = dot(before, named.astype(BF16))
    wanted = (slot % CAP).astype(F32)
    return jnp.where(place == wanted, named, 0.0)


def dispatch(me, rows, named, chunks, experts):
    owners = named[:, 0:2].astype(F32).astype(jnp.int32) ^ me
    table = slot_map(owners, chunks, rows.shape[0] // chunks, experts)
    return dot(table.astype(BF16), rows, ((0,), (0,)))


def combine(me, rows, named, router, returned, chunks, experts):
    routes = named[:, 0:2].astype(F32).astype(jnp.int32)
    logits = dot(rows, router, ((1,), (1,)))
    lane = iota(logits.shape, 1)
    first = jnp.sum(jnp.where(lane == routes[:, 0:1], logits, 0.0), axis=1, keepdims=True)
    second = jnp.sum(jnp.where(lane == routes[:, 1:2], logits, 0.0), axis=1, keepdims=True)
    gate0 = 1.0 / (1.0 + jnp.exp(second - first))
    gate1 = 1.0 / (1.0 + jnp.exp(first - second))
    owners = routes ^ me
    table = slot_map(owners, chunks, rows.shape[0] // chunks, experts)
    expert = iota(table.shape, 1) // (chunks * CAP)
    gates = table * jnp.where(owners[:, 0:1] == expert, gate0, gate1)
    high = gates.astype(BF16)
    low = (gates - high.astype(F32)).astype(BF16)
    return dot(high, returned) + dot(low, returned)


def attend_kernel(
    me_ref, lengths_ref, queries_ref, keys_ref, values_ref, routes_ref, residual_ref, gain_ref,
    stream_ref, payload_ref, *rest,
):
    slots, attended = rest[:-1], rest[-1]
    head = pl.program_id(0)
    batch, window, _ = keys_ref.shape
    keys = keys_ref[...].reshape(batch * window, HS)
    values = values_ref[...].reshape(batch * window, HS)
    block = queries_ref[...]
    stacked = jnp.concatenate([block[:, g * HS : (g + 1) * HS] for g in range(GROUP)], axis=0)
    scores = dot(stacked, keys, ((1,), (1,))) * HS ** (-0.5)
    column = iota((batch, batch * window), 1)
    row = iota((batch, batch * window), 0)
    length = jnp.zeros((batch, batch * window), jnp.int32)
    for r in range(batch):
        length = jnp.where(row == r, lengths_ref[r], length)
    begin = row * window
    bias = jnp.where((column >= begin) & (column < begin + length), 0.0, -1e30)
    scores = scores + jnp.concatenate([bias] * GROUP, axis=0)
    highest = jnp.max(scores, axis=1, keepdims=True)
    powers = jnp.exp(scores - highest)
    weights = (powers / jnp.sum(powers, axis=1, keepdims=True)).astype(BF16)
    mixed = dot(weights, values)
    attended[head] = jnp.concatenate(
        [mixed[g * batch : (g + 1) * batch] for g in range(GROUP)], axis=1
    )

    @pl.when(head == KVH - 1)
    def finish():
        stream = residual_ref[...].astype(F32) + jnp.concatenate(
            [attended[k] for k in range(KVH)], axis=1
        )
        width = stream.shape[1]
        scale = lax.rsqrt(jnp.mean(stream * stream, axis=1, keepdims=True) + 1e-05)
        normed = (stream * scale * gain_ref[...]).astype(BF16)
        lane = iota((batch, LANES), 1)
        same = iota((batch, batch), 0) == iota((batch, batch), 1)
        routes = [
            jnp.sum(jnp.where(same, routes_ref[k : k + 1, :], 0), axis=1, keepdims=True).astype(F32)
            for k in range(2)
        ]
        named = jnp.where(lane == 0, routes[0], jnp.where(lane == 1, routes[1], 0.0))
        named = named.astype(BF16)
        stream_ref[...] = stream
        payload_ref[:, :width] = normed
        payload_ref[:, width:] = named
        out = dispatch(me_ref[0], normed, named, 1, len(slots))
        for e, ref in enumerate(slots):
            ref[...] = out[e * CAP : (e + 1) * CAP].astype(BF16)


def split_kernel(me_ref, *refs, chunks, after):
    refs = refs[after:]
    payload = jnp.concatenate([ref[...] for ref in refs[:chunks]], axis=0)
    slots = refs[chunks:]
    width = slots[0].shape[1]
    rows, named = payload[:, :width], payload[:, width:]
    out = dispatch(me_ref[0], rows, named, chunks, len(slots))
    span = chunks * CAP
    for e, ref in enumerate(slots):
        ref[...] = out[e * span : (e + 1) * span].astype(BF16)


def expert_kernel(*refs, pieces):
    xs, (gate_ref, up_ref, down_ref) = refs[:pieces], refs[pieces : pieces + 3]
    outs = refs[pieces + 3 : 2 * pieces + 3]
    rows_ref, hidden_ref = refs[2 * pieces + 3 :]
    rows_ref[...] = jnp.concatenate([ref[...].astype(F32) for ref in xs], axis=0).astype(BF16)
    width, units = gate_ref.shape
    tile = min(256, units)

    @pl.loop(0, units // tile)
    def _(i):
        at = pl.ds(pl.multiple_of(i * tile, tile), tile)
        gate = dot(rows_ref[...], gate_ref[:, at])
        up = dot(rows_ref[...], up_ref[:, at])
        hidden_ref[:, at] = (jax.nn.silu(gate) * up).astype(BF16)

    @pl.loop(0, width // tile)
    def _(i):
        at = pl.ds(pl.multiple_of(i * tile, tile), tile)
        out = dot(hidden_ref[...], down_ref[:, at])
        begin = 0
        for ref in outs:
            count = ref.shape[0]
            ref[:, at] = out[begin : begin + count].astype(BF16)
            begin += count


def in_hbm(value):
    return pltpu.with_memory_space_constraint(value, pltpu.HBM)


def mix_kernel(me_ref, router_ref, *refs, chunks, experts):
    payload = jnp.concatenate([ref[...] for ref in refs[:chunks]], axis=0)
    returned = jnp.concatenate(
        [ref[...].astype(F32) for ref in refs[chunks : chunks + experts]], axis=0
    ).astype(BF16)
    outs = refs[chunks + experts :]
    batch, width = outs[0].shape
    rows, named = payload[:, :width], payload[:, width:]
    mixed = combine(me_ref[0], rows, named, router_ref[...], returned, chunks, experts)
    for j, ref in enumerate(outs):
        ref[...] = mixed[j * batch : (j + 1) * batch].astype(BF16)


def finish_kernel(me_ref, router_ref, payload_ref, stream_ref, *refs, experts):
    returned = jnp.concatenate([ref[...].astype(F32) for ref in refs[:experts]], axis=0)
    out_ref = refs[-1]
    width = out_ref.shape[1]
    rows, named = payload_ref[:, :width], payload_ref[:, width:]
    total = stream_ref[...] + combine(
        me_ref[0], rows, named, router_ref[...], returned.astype(BF16), 1, experts
    )
    for ref in refs[experts:-1]:
        total = total + ref[...].astype(F32)
    out_ref[...] = total.astype(BF16)


def swap(value, axis, step):
    if step == 0:
        return value
    count = lax.axis_size(axis)
    return lax.ppermute(value, axis, [(i, i ^ step) for i in range(count)])


def params(elements):
    return pltpu.CompilerParams(vmem_limit_bytes=min(48 * MIB, 2 * MIB + 10 * elements))


def shards(
    queries,
    cached_keys,
    cached_values,
    lengths,
    routes,
    residual,
    norm_gain,
    router,
    gate_proj,
    up_proj,
    down_proj,
):
    batch, width = queries.shape
    window = cached_keys.shape[1]
    experts = router.shape[1]
    layers = lax.axis_size("attn")
    remote = layers - 1
    me = lax.axis_index("expert").astype(jnp.int32).reshape(1)
    full = lambda shape: pl.BlockSpec(shape, lambda k: (0,) * len(shape))
    shape = jax.ShapeDtypeStruct
    wide = width + LANES
    span = width // KVH

    stream, payload, *slots = pl.pallas_call(
        attend_kernel,
        grid=(KVH,),
        in_specs=[
            SCALAR,
            SCALAR,
            pl.BlockSpec((batch, span), lambda k: (0, k)),
            pl.BlockSpec((batch, window, HS), lambda k: (0, 0, k)),
            pl.BlockSpec((batch, window, HS), lambda k: (0, 0, k)),
            full((2, batch)),
            full((batch, width)),
            full((1, width)),
        ],
        out_specs=[full((batch, width)), full((batch, wide))] + [full((CAP, width))] * experts,
        out_shape=[shape((batch, width), F32), shape((batch, wide), BF16)]
        + [shape((CAP, width), BF16)] * experts,
        scratch_shapes=[pltpu.VMEM((KVH, batch, span), F32)],
        compiler_params=params(28 * batch * width),
        cost_estimate=BUSY,
    )(
        me,
        lengths,
        *[in_hbm(a) for a in (queries, cached_keys, cached_values, routes.T, residual, norm_gain[None])],
    )
    router = router.T

    payloads = [swap(payload, "attn", j) for j in range(1, layers)]
    near = [swap(slots[e], "expert", e) for e in range(experts)]
    ahead = [*near[1:]]
    slots = pl.pallas_call(
        functools.partial(split_kernel, chunks=remote, after=len(ahead)),
        in_specs=[SCALAR] + [WHOLE] * (len(ahead) + remote),
        out_specs=[WHOLE] * experts,
        out_shape=[shape((remote * CAP, width), BF16)] * experts,
        cost_estimate=BUSY,
        compiler_params=params(experts * remote * CAP * width),
    )(me, *ahead, *payloads)
    far = [swap(slots[e], "expert", e) for e in range(experts)]
    inputs = near + far
    total_rows = sum(block.shape[0] for block in inputs)
    units = gate_proj.shape[2]
    weights = [gate_proj[0], up_proj[0], down_proj[0]]
    results = pl.pallas_call(
        functools.partial(expert_kernel, pieces=len(inputs)),
        in_specs=[WHOLE] * (len(inputs) + 3),
        out_specs=[WHOLE] * len(inputs),
        out_shape=[shape(block.shape, BF16) for block in inputs],
        scratch_shapes=[pltpu.VMEM((total_rows, width), BF16), pltpu.VMEM((total_rows, units), BF16)],
        compiler_params=params(total_rows * width),
    )(*inputs, *weights)

    far = [swap(results[experts + e], "expert", e) for e in range(experts)]
    near = [swap(results[e], "expert", e) for e in range(experts)]
    mixed = pl.pallas_call(
        functools.partial(mix_kernel, chunks=remote, experts=experts),
        in_specs=[SCALAR] + [WHOLE] * (1 + remote + experts),
        out_specs=[WHOLE] * remote,
        out_shape=[shape((batch, width), BF16)] * remote,
        compiler_params=params(experts * remote * CAP * width),
    )(me, router, *payloads, *far)
    mixed = [swap(block, "attn", j + 1) for j, block in enumerate(mixed)]
    return pl.pallas_call(
        functools.partial(finish_kernel, experts=experts),
        in_specs=[SCALAR] + [WHOLE] * (3 + experts + remote),
        out_specs=WHOLE,
        out_shape=shape((batch, width), BF16),
        compiler_params=params(total_rows * width),
    )(me, router, payload, stream, *near, *mixed)


def solution(mesh):
    in_specs = (
        P(("groups", "attn", "expert"), None),
        P(("groups", "attn", "expert"), None, None),
        P(("groups", "attn", "expert"), None, None),
        P(("groups", "attn", "expert")),
        P(("groups", "attn", "expert"), None),
        P(("groups", "attn", "expert"), None),
        P(),
        P(),
        P("expert", None, "attn"),
        P("expert", None, "attn"),
        P("expert", "attn", None),
    )
    out_specs = P(("groups", "attn", "expert"), None)
    return jax.shard_map(shards, mesh=mesh, in_specs=in_specs, out_specs=out_specs, check_vma=False)
```

```python
import functools

import jax
import jax.numpy as jnp
from jax import lax
from jax.experimental import pallas as pl
from jax.experimental.pallas import tpu as pltpu
from jax.sharding import PartitionSpec as P

HS = 128
KVH = 4
GROUP = 6
CAP = 8
LANES = 128
BLOCK = 8
MIB = 1 << 20
F32 = jnp.float32
BF16 = jnp.bfloat16
BUSY = pl.CostEstimate(flops=12_000_000_000, bytes_accessed=4_000_000, transcendentals=0)
ANY = pl.BlockSpec(memory_space=pl.ANY)
WHOLE = pl.BlockSpec(memory_space=pltpu.VMEM)
SCALAR = pl.BlockSpec(memory_space=pltpu.SMEM)


def dot(a, b, dims=((1,), (0,))):
    return lax.dot_general(a, b, (dims, ((), ())), preferred_element_type=F32)


def iota(shape, dim):
    return lax.broadcasted_iota(jnp.int32, shape, dim)


def slot_map(owners, chunks, batch, experts):
    rows, slots = chunks * batch, experts * chunks * CAP
    slot = iota((rows, slots), 1)
    row = iota((rows, slots), 0)
    expert = slot // (chunks * CAP)
    chunk = (slot // CAP) % chunks
    named = (owners[:, 0:1] == expert) | (owners[:, 1:2] == expert)
    named = named & (row // batch == chunk)
    named = jnp.where(named, 1.0, 0.0)
    left, right = iota((rows, rows), 0), iota((rows, rows), 1)
    before = jnp.where(right < left, 1.0, 0.0).astype(BF16)
    place = dot(before, named.astype(BF16))
    wanted = (slot % CAP).astype(F32)
    return jnp.where(place == wanted, named, 0.0)


def dispatch(me, rows, named, chunks, experts):
    owners = named[:, 0:2].astype(F32).astype(jnp.int32) ^ me
    table = slot_map(owners, chunks, rows.shape[0] // chunks, experts)
    return dot(table.astype(BF16), rows, ((0,), (0,)))


def combine(me, rows, named, router, returned, chunks, experts):
    routes = named[:, 0:2].astype(F32).astype(jnp.int32)
    logits = dot(rows, router, ((1,), (1,)))
    lane = iota(logits.shape, 1)
    first = jnp.sum(jnp.where(lane == routes[:, 0:1], logits, 0.0), axis=1, keepdims=True)
    second = jnp.sum(jnp.where(lane == routes[:, 1:2], logits, 0.0), axis=1, keepdims=True)
    gate0 = 1.0 / (1.0 + jnp.exp(second - first))
    gate1 = 1.0 / (1.0 + jnp.exp(first - second))
    owners = routes ^ me
    table = slot_map(owners, chunks, rows.shape[0] // chunks, experts)
    expert = iota(table.shape, 1) // (chunks * CAP)
    gates = table * jnp.where(owners[:, 0:1] == expert, gate0, gate1)
    high = gates.astype(BF16)
    low = (gates - high.astype(F32)).astype(BF16)
    return dot(high, returned) + dot(low, returned)


def attend_kernel(
    lengths_hbm, queries_hbm, keys_hbm, values_hbm, routes_hbm, residual_hbm, gain_hbm,
    stream_ref, payload_ref,
    lengths_ref, queries_ref, keys_ref, values_ref, routes_ref, residual_ref, gain_ref, sems,
):
    batch, window, _ = keys_ref.shape
    width = queries_ref.shape[1]
    span = width // KVH
    blocks = [pl.ds(begin, BLOCK) for begin in range(0, batch, BLOCK)]
    small = [
        (lengths_hbm, lengths_ref), (queries_hbm, queries_ref), (routes_hbm, routes_ref),
        (residual_hbm, residual_ref), (gain_hbm, gain_ref),
    ]
    caches = [
        (source.at[block], target.at[block])
        for block in blocks
        for source, target in ((keys_hbm, keys_ref), (values_hbm, values_ref))
    ]
    copies = [
        pltpu.make_async_copy(source, target, sems.at[i])
        for i, (source, target) in enumerate(small[:2] + caches + small[2:])
    ]
    for copy in copies:
        copy.start()
    copies[0].wait()
    copies[1].wait()
    same = iota((batch, batch), 0) == iota((batch, batch), 1)

    def upright(row):
        return jnp.sum(jnp.where(same, row, 0), axis=1, keepdims=True)

    lengths = upright(lengths_ref[...])
    queries = queries_ref[...].astype(F32)
    row = iota((BLOCK, BLOCK * window), 0)
    column = iota((BLOCK, BLOCK * window), 1) - row * window
    attended = []
    for i, block in enumerate(blocks):
        begin = i * BLOCK
        bias = jnp.where((column >= 0) & (column < lengths[begin : begin + BLOCK]), 0.0, -1e30)
        bias = jnp.concatenate([bias] * GROUP, axis=0)
        copies[2 + 2 * i].wait()
        copies[3 + 2 * i].wait()
        heads = []
        for k in range(KVH):
            keys = keys_ref[block, :, k * HS : (k + 1) * HS].reshape(BLOCK * window, HS)
            values = values_ref[block, :, k * HS : (k + 1) * HS].reshape(BLOCK * window, HS)
            stacked = jnp.concatenate(
                [
                    queries[begin : begin + BLOCK, k * span + g * HS : k * span + (g + 1) * HS]
                    for g in range(GROUP)
                ],
                axis=0,
            ).astype(BF16)
            scores = dot(stacked, keys, ((1,), (1,))) * HS ** (-0.5) + bias
            highest = jnp.max(scores, axis=1, keepdims=True)
            powers = jnp.exp(scores - highest)
            weights = (powers / jnp.sum(powers, axis=1, keepdims=True)).astype(BF16)
            mixed = dot(weights, values)
            heads += [mixed[g * BLOCK : (g + 1) * BLOCK] for g in range(GROUP)]
        attended.append(jnp.concatenate(heads, axis=1))
    for copy in copies[2 + 2 * len(blocks) :]:
        copy.wait()
    stream = residual_ref[...].astype(F32) + jnp.concatenate(attended, axis=0)
    scale = lax.rsqrt(jnp.mean(stream * stream, axis=1, keepdims=True) + 1e-05)
    lane = iota((batch, LANES), 1)
    routes = [upright(routes_ref[k : k + 1, :]).astype(F32) for k in range(2)]
    named = jnp.where(lane == 0, routes[0], jnp.where(lane == 1, routes[1], 0.0))
    stream_ref[...] = stream
    payload_ref[:, :width] = (stream * scale * gain_ref[...]).astype(BF16)
    payload_ref[:, width:] = named.astype(BF16)


def split_kernel(me_ref, *refs, chunks, after):
    refs = refs[after:]
    payload = jnp.concatenate([ref[...] for ref in refs[:chunks]], axis=0)
    slots = refs[chunks:]
    width = slots[0].shape[1]
    rows, named = payload[:, :width], payload[:, width:]
    out = dispatch(me_ref[0], rows, named, chunks, len(slots))
    span = chunks * CAP
    for e, ref in enumerate(slots):
        ref[...] = out[e * span : (e + 1) * span].astype(BF16)


def expert_kernel(*refs, pieces):
    xs, (gate_ref, up_ref, down_ref) = refs[:pieces], refs[pieces : pieces + 3]
    outs = refs[pieces + 3 : 2 * pieces + 3]
    rows_ref, hidden_ref = refs[2 * pieces + 3 :]
    begin = 0
    for ref in xs:
        rows_ref[begin : begin + ref.shape[0], :] = ref[...]
        begin += ref.shape[0]
    width, units = gate_ref.shape
    tile = min(256, units)

    @pl.loop(0, units // tile)
    def _(i):
        at = pl.ds(pl.multiple_of(i * tile, tile), tile)
        gate = dot(rows_ref[...], gate_ref[:, at])
        up = dot(rows_ref[...], up_ref[:, at])
        hidden_ref[:, at] = (jax.nn.silu(gate) * up).astype(BF16)

    @pl.loop(0, width // tile)
    def _(i):
        at = pl.ds(pl.multiple_of(i * tile, tile), tile)
        out = dot(hidden_ref[...], down_ref[:, at])
        begin = 0
        for ref in outs:
            count = ref.shape[0]
            ref[:, at] = out[begin : begin + count].astype(BF16)
            begin += count


def mix_kernel(me_ref, router_ref, *refs, chunks, experts, own, after):
    refs = refs[after:]
    payload = jnp.concatenate([ref[...] for ref in refs[:chunks]], axis=0)
    returned = jnp.concatenate([ref[...] for ref in refs[chunks : chunks + experts]], axis=0)
    outs = refs[chunks + experts + own :]
    batch, width = outs[0].shape
    rows, named = payload[:, :width], payload[:, width:]
    mixed = combine(me_ref[0], rows, named, router_ref[...], returned, chunks, experts)
    for j, ref in enumerate(outs):
        part = mixed[j * batch : (j + 1) * batch]
        if own and j == 0:
            ref[...] = refs[chunks + experts][...] + part
        else:
            ref[...] = part.astype(BF16)


def finish_kernel(stream_ref, *refs):
    total = stream_ref[...]
    for ref in refs[:-1]:
        total = total + ref[...].astype(F32)
    refs[-1][...] = total.astype(BF16)


def in_hbm(value):
    return pltpu.with_memory_space_constraint(value, pltpu.HBM)


def swap(value, axis, step):
    if step == 0:
        return value
    count = lax.axis_size(axis)
    return lax.ppermute(value, axis, [(i, i ^ step) for i in range(count)])


def params(elements):
    return pltpu.CompilerParams(vmem_limit_bytes=min(48 * MIB, 2 * MIB + 10 * elements))


def shards(
    queries,
    cached_keys,
    cached_values,
    lengths,
    routes,
    residual,
    norm_gain,
    router,
    gate_proj,
    up_proj,
    down_proj,
):
    batch, width = queries.shape
    experts = router.shape[1]
    layers = lax.axis_size("attn")
    me = lax.axis_index("expert").astype(jnp.int32).reshape(1)
    router = router.T
    shape = jax.ShapeDtypeStruct
    operands = [
        in_hbm(a)
        for a in (
            lengths[None], queries, cached_keys, cached_values, routes.T, residual, norm_gain[None]
        )
    ]
    stream, payload = pl.pallas_call(
        attend_kernel,
        in_specs=[ANY] * len(operands),
        out_specs=[WHOLE, WHOLE],
        out_shape=[shape((batch, width), F32), shape((batch, width + LANES), BF16)],
        scratch_shapes=[pltpu.VMEM(a.shape, a.dtype) for a in operands]
        + [pltpu.SemaphoreType.DMA((5 + 2 * (batch // BLOCK),))],
        compiler_params=params(28 * batch * width),
        cost_estimate=pl.CostEstimate(flops=10**9, bytes_accessed=4 * 10**6, transcendentals=10**6),
    )(*operands)

    chunks = [swap(payload, "attn", j) for j in range(layers)]
    groups = [list(range(2)), list(range(2, layers))]
    inputs, ahead = [], []
    for group in groups:
        count = len(group)
        slots = pl.pallas_call(
            functools.partial(split_kernel, chunks=count, after=len(ahead)),
            in_specs=[SCALAR] + [ANY] * len(ahead) + [WHOLE] * count,
            out_specs=[WHOLE] * experts,
            out_shape=[shape((count * CAP, width), BF16)] * experts,
            cost_estimate=BUSY,
            compiler_params=params(experts * count * CAP * width),
        )(me, *ahead, *[chunks[j] for j in group])
        arrived = [swap(slots[e], "expert", e) for e in range(experts)]
        ahead = arrived[1:2]
        inputs += arrived

    total_rows = sum(block.shape[0] for block in inputs)
    units = gate_proj.shape[2]
    results = pl.pallas_call(
        functools.partial(expert_kernel, pieces=len(inputs)),
        in_specs=[WHOLE] * (len(inputs) + 3),
        out_specs=[WHOLE] * len(inputs),
        out_shape=[shape(block.shape, BF16) for block in inputs],
        scratch_shapes=[pltpu.VMEM((total_rows, width), BF16), pltpu.VMEM((total_rows, units), BF16)],
        compiler_params=params(total_rows * width),
    )(*inputs, gate_proj[0], up_proj[0], down_proj[0])

    received, before = [], []
    for i, group in list(enumerate(groups))[::-1]:
        count, own = len(group), int(group[0] == 0)
        returned = [swap(results[i * experts + e], "expert", e) for e in range(experts)]
        mixed = pl.pallas_call(
            functools.partial(
                mix_kernel, chunks=count, experts=experts, own=own, after=len(before)
            ),
            in_specs=[SCALAR, WHOLE]
            + [ANY] * len(before)
            + [WHOLE] * (count + experts + own),
            out_specs=[WHOLE] * count,
            out_shape=[shape((batch, width), F32 if j == 0 else BF16) for j in group],
            compiler_params=params(experts * count * CAP * width),
        )(me, router, *before, *[chunks[j] for j in group], *returned, *[stream] * own)
        before = mixed[:1]
        received = [swap(block, "attn", j) for j, block in zip(group, mixed)] + received
    return pl.pallas_call(
        finish_kernel,
        in_specs=[WHOLE] * len(received),
        out_specs=WHOLE,
        out_shape=shape((batch, width), BF16),
        compiler_params=params(2 * layers * batch * width),
    )(*received)


def solution(mesh):
    in_specs = (
        P(("groups", "attn", "expert"), None),
        P(("groups", "attn", "expert"), None, None),
        P(("groups", "attn", "expert"), None, None),
        P(("groups", "attn", "expert")),
        P(("groups", "attn", "expert"), None),
        P(("groups", "attn", "expert"), None),
        P(),
        P(),
        P("expert", None, "attn"),
        P("expert", None, "attn"),
        P("expert", "attn", None),
    )
    out_specs = P(("groups", "attn", "expert"), None)
    return jax.shard_map(shards, mesh=mesh, in_specs=in_specs, out_specs=out_specs, check_vma=False)
```

```python
import functools

import jax
import jax.numpy as jnp
from jax import lax
from jax.experimental import pallas as pl
from jax.experimental.pallas import tpu as pltpu
from jax.sharding import PartitionSpec as P

HS = 128
KVH = 4
GROUP = 6
CAP = 8
LANES = 128
PAIR = 2
EARLY = 1
MIB = 1 << 20
F32 = jnp.float32
BF16 = jnp.bfloat16
LIGHT = pl.CostEstimate(flops=0, bytes_accessed=0, transcendentals=0)
BUSY = pl.CostEstimate(flops=24 * 10**9, bytes_accessed=0, transcendentals=0)
ANY = pl.BlockSpec(memory_space=pl.ANY)
WHOLE = pl.BlockSpec(memory_space=pltpu.VMEM)
SCALAR = pl.BlockSpec(memory_space=pltpu.SMEM)


def dot(a, b, dims=((1,), (0,))):
    return lax.dot_general(a, b, (dims, ((), ())), preferred_element_type=F32)


def iota(shape, dim):
    return lax.broadcasted_iota(jnp.int32, shape, dim)


def slot_map(owners, chunks, batch, experts):
    rows, slots = chunks * batch, experts * chunks * CAP
    slot = iota((rows, slots), 1)
    row = iota((rows, slots), 0)
    expert = slot // (chunks * CAP)
    chunk = (slot // CAP) % chunks
    named = (owners[:, 0:1] == expert) | (owners[:, 1:2] == expert)
    named = named & (row // batch == chunk)
    named = jnp.where(named, 1.0, 0.0)
    left, right = iota((rows, rows), 0), iota((rows, rows), 1)
    before = jnp.where(right < left, 1.0, 0.0).astype(BF16)
    place = dot(before, named.astype(BF16))
    wanted = (slot % CAP).astype(F32)
    return jnp.where(place == wanted, named, 0.0)


def dispatch(me, rows, named, chunks, experts):
    owners = named[:, 0:2].astype(F32).astype(jnp.int32) ^ me
    table = slot_map(owners, chunks, rows.shape[0] // chunks, experts)
    return dot(table.astype(BF16), rows, ((0,), (0,)))


def combine(me, rows, named, router, returned, chunks, experts):
    routes = named[:, 0:2].astype(F32).astype(jnp.int32)
    logits = dot(rows, router, ((1,), (1,)))
    lane = iota(logits.shape, 1)
    first = jnp.sum(jnp.where(lane == routes[:, 0:1], logits, 0.0), axis=1, keepdims=True)
    second = jnp.sum(jnp.where(lane == routes[:, 1:2], logits, 0.0), axis=1, keepdims=True)
    gate0 = 1.0 / (1.0 + jnp.exp(second - first))
    gate1 = 1.0 / (1.0 + jnp.exp(first - second))
    owners = routes ^ me
    table = slot_map(owners, chunks, rows.shape[0] // chunks, experts)
    expert = iota(table.shape, 1) // (chunks * CAP)
    gates = table * jnp.where(owners[:, 0:1] == expert, gate0, gate1)
    high = gates.astype(BF16)
    low = (gates - high.astype(F32)).astype(BF16)
    return dot(high, returned) + dot(low, returned)


def attend_kernel(
    lengths_hbm, queries_hbm, keys_hbm, values_hbm, routes_hbm, residual_hbm, gain_hbm,
    stream_ref, payload_ref,
    lengths_ref, queries_ref, keys_ref, values_ref, routes_ref, residual_ref, gain_ref, sems,
):
    batch, window, _ = keys_ref.shape
    width = queries_ref.shape[1]
    span = width // KVH
    parts = [pl.ds(begin, PAIR * HS) for begin in range(0, KVH * HS, PAIR * HS)]
    small = [
        (lengths_hbm, lengths_ref), (queries_hbm, queries_ref), (routes_hbm, routes_ref),
        (residual_hbm, residual_ref), (gain_hbm, gain_ref),
    ]
    caches = [
        pair
        for part in parts
        for pair in (
            (keys_hbm.at[:, :, part], keys_ref.at[:, :, part]),
            (values_hbm.at[:, :, part], values_ref.at[:, 0:window, part]),
        )
    ]
    copies = [
        pltpu.make_async_copy(source, target, sems.at[i])
        for i, (source, target) in enumerate(small[:2] + caches + small[2:])
    ]
    for copy in copies:
        copy.start()
    padded = values_ref.shape[1]
    if padded > window:
        pad = (batch, padded - window, values_ref.shape[2])
        values_ref[:, window:, :] = jnp.zeros(pad, BF16)
    copies[0].wait()
    copies[1].wait()
    same = iota((batch, batch), 0) == iota((batch, batch), 1)

    def upright(row):
        return jnp.sum(jnp.where(same, row, 0), axis=1, keepdims=True)

    queries = queries_ref[...]
    lanes = PAIR * GROUP * batch
    full = -(-lanes // LANES) * LANES
    request = iota((window, full), 1) % batch
    length = jnp.zeros((1, full), jnp.int32)
    for r in range(batch):
        length = jnp.where(request[0:1] == r, lengths_ref[0:1, r : r + 1], length)
    visible = iota((window, full), 0) < length
    owner = iota((lanes, padded), 0) % batch
    attended = []
    for i, part in enumerate(parts):
        spread = []
        for k in range(PAIR):
            at = [(i * PAIR + k) * span + g * HS for g in range(GROUP)]
            stacked = jnp.concatenate([queries[:, c : c + HS] for c in at], axis=0)
            blank = jnp.zeros_like(stacked)
            spread.append(
                jnp.concatenate([stacked if j == k else blank for j in range(PAIR)], axis=1)
            )
        if full > lanes:
            spread.append(jnp.zeros((full - lanes, PAIR * HS), BF16))
        spread = jnp.concatenate(spread, axis=0)
        copies[2 + 2 * i].wait()
        keys = keys_ref[:, :, part].reshape(batch * window, PAIR * HS)
        products = dot(keys, spread, ((1,), (1,)))
        scores = products[:window]
        for r in range(1, batch):
            scores = jnp.where(request == r, products[r * window : (r + 1) * window], scores)
        scores = jnp.where(visible, scores * HS ** (-0.5), -1e30)
        powers = jnp.exp(scores - jnp.max(scores, axis=0, keepdims=True))
        weights = powers / jnp.sum(powers, axis=0, keepdims=True)
        if padded > window:
            weights = jnp.concatenate([weights, jnp.zeros((padded - window, full), F32)], axis=0)
        weights = weights.T[:lanes]
        weights = jnp.concatenate(
            [jnp.where(owner == r, weights, 0.0).astype(BF16) for r in range(batch)], axis=1
        )
        copies[3 + 2 * i].wait()
        values = values_ref[:, :, part].reshape(batch * padded, PAIR * HS)
        mixed = dot(weights, values)
        attended += [
            mixed[h * batch : (h + 1) * batch, h // GROUP * HS : (h // GROUP + 1) * HS]
            for h in range(PAIR * GROUP)
        ]
    for copy in copies[2 + 2 * len(parts) :]:
        copy.wait()
    stream = residual_ref[...].astype(F32) + jnp.concatenate(attended, axis=1)
    scale = lax.rsqrt(jnp.mean(stream * stream, axis=1, keepdims=True) + 1e-05)
    lane = iota((batch, LANES), 1)
    routes = [upright(routes_ref[k : k + 1, :]).astype(F32) for k in range(2)]
    named = jnp.where(lane == 0, routes[0], jnp.where(lane == 1, routes[1], 0.0))
    stream_ref[...] = stream
    payload_ref[:, :width] = (stream * scale * gain_ref[...]).astype(BF16)
    payload_ref[:, width:] = named.astype(BF16)


def split_kernel(me_ref, *refs, chunks, after):
    refs = refs[after:]
    payload = jnp.concatenate([ref[...] for ref in refs[:chunks]], axis=0)
    slots = refs[chunks:]
    width = slots[0].shape[1]
    rows, named = payload[:, :width], payload[:, width:]
    out = dispatch(me_ref[0], rows, named, chunks, len(slots))
    span = chunks * CAP
    for e, ref in enumerate(slots):
        ref[...] = out[e * span : (e + 1) * span].astype(BF16)


def expert_kernel(*refs, pieces):
    xs, (gate_ref, up_ref, down_ref) = refs[:pieces], refs[pieces : pieces + 3]
    outs = refs[pieces + 3 : 2 * pieces + 3]
    rows_ref, hidden_ref = refs[2 * pieces + 3 :]
    rows_ref[...] = jnp.concatenate([ref[...].astype(F32) for ref in xs], axis=0).astype(BF16)
    width, units = gate_ref.shape
    tile = min(256, units)

    @pl.loop(0, units // tile)
    def _(i):
        at = pl.ds(pl.multiple_of(i * tile, tile), tile)
        gate = dot(rows_ref[...], gate_ref[:, at])
        up = dot(rows_ref[...], up_ref[:, at])
        hidden_ref[:, at] = (jax.nn.silu(gate) * up).astype(BF16)

    @pl.loop(0, width // tile)
    def _(i):
        at = pl.ds(pl.multiple_of(i * tile, tile), tile)
        out = dot(hidden_ref[...], down_ref[:, at])
        begin = 0
        for ref in outs:
            count = ref.shape[0]
            ref[:, at] = out[begin : begin + count].astype(BF16)
            begin += count


def mix_kernel(me_ref, router_ref, *refs, chunks, experts, later):
    payload = jnp.concatenate([ref[...] for ref in refs[:chunks]], axis=0)
    returned = jnp.concatenate(
        [ref[...].astype(F32) for ref in refs[chunks : chunks + experts]], axis=0
    ).astype(BF16)
    outs = refs[len(refs) - chunks - later : len(refs) - later]
    batch, width = outs[0].shape
    rows, named = payload[:, :width], payload[:, width:]
    mixed = combine(me_ref[0], rows, named, router_ref[...], returned, chunks, experts)
    for j, ref in enumerate(outs):
        part = mixed[j * batch : (j + 1) * batch]
        if ref.dtype == F32:
            for other in refs[chunks + experts : len(refs) - chunks - later]:
                part = part + other[...].astype(F32)
            ref[...] = part
        else:
            ref[...] = part.astype(BF16)


def finish_kernel(stream_ref, *refs):
    total = stream_ref[...]
    for ref in refs[:-1]:
        total = total + ref[...].astype(F32)
    refs[-1][...] = total.astype(BF16)


def in_hbm(value):
    return pltpu.with_memory_space_constraint(value, pltpu.HBM)


def swap(value, axis, step):
    if step == 0:
        return value
    count = lax.axis_size(axis)
    return lax.ppermute(value, axis, [(i, i ^ step) for i in range(count)])


def params(elements):
    return pltpu.CompilerParams(vmem_limit_bytes=min(48 * MIB, 2 * MIB + 10 * elements))


def shards(
    queries,
    cached_keys,
    cached_values,
    lengths,
    routes,
    residual,
    norm_gain,
    router,
    gate_proj,
    up_proj,
    down_proj,
):
    batch, width = queries.shape
    experts = router.shape[1]
    layers = lax.axis_size("attn")
    me = lax.axis_index("expert").astype(jnp.int32).reshape(1)
    router = router.T
    shape = jax.ShapeDtypeStruct
    operands = [
        in_hbm(a)
        for a in (
            lengths[None], queries, cached_keys, cached_values, routes.T, residual, norm_gain[None]
        )
    ]
    window, depth = cached_values.shape[1:]
    held = [a.shape for a in operands]
    held[3] = (batch, -(-window // LANES) * LANES, depth)
    stream, payload = pl.pallas_call(
        attend_kernel,
        in_specs=[ANY] * len(operands),
        out_specs=[WHOLE, WHOLE],
        out_shape=[shape((batch, width), F32), shape((batch, width + LANES), BF16)],
        scratch_shapes=[pltpu.VMEM(size, a.dtype) for size, a in zip(held, operands)]
        + [pltpu.SemaphoreType.DMA((5 + 2 * (KVH // PAIR),))],
        compiler_params=params(28 * batch * width),
        cost_estimate=pl.CostEstimate(flops=10**9, bytes_accessed=4 * 10**6, transcendentals=0),
    )(*operands)

    chunks = [swap(payload, "attn", j) for j in range(layers)]
    groups = [[0, 1], [2], list(range(3, layers))]
    inputs, ahead = [], []
    for group in groups:
        count = len(group)
        slots = pl.pallas_call(
            functools.partial(split_kernel, chunks=count, after=len(ahead)),
            in_specs=[SCALAR] + [ANY] * len(ahead) + [WHOLE] * count,
            out_specs=[WHOLE] * experts,
            out_shape=[shape((count * CAP, width), BF16)] * experts,
            cost_estimate=BUSY if group == [2] else LIGHT,
            compiler_params=params(experts * count * CAP * width),
        )(me, *ahead, *[chunks[j] for j in group])
        arrived = [swap(slots[e], "expert", e) for e in range(experts)]
        ahead = arrived[1:2]
        inputs += arrived

    total_rows = sum(block.shape[0] for block in inputs)
    units = gate_proj.shape[2]
    results = pl.pallas_call(
        functools.partial(expert_kernel, pieces=len(inputs)),
        in_specs=[WHOLE] * (len(inputs) + 3),
        out_specs=[WHOLE] * len(inputs),
        out_shape=[shape(block.shape, BF16) for block in inputs],
        scratch_shapes=[pltpu.VMEM((total_rows, width), BF16), pltpu.VMEM((total_rows, units), BF16)],
        compiler_params=params(total_rows * width),
    )(*inputs, gate_proj[0], up_proj[0], down_proj[0])

    results = [results[i : i + experts] for i in range(0, len(results), experts)]
    received = []
    for i, group in list(enumerate(groups))[::-1]:
        count, own = len(group), int(group[0] == 0)
        returned = [swap(results[i][e], "expert", e) for e in range(experts)]
        later = results[0][1:] if i == 1 else []
        added = [stream, *received[EARLY:]] if own else []
        operands = [me, router, *[chunks[j] for j in group], *returned, *added]
        mixed = pl.pallas_call(
            functools.partial(mix_kernel, chunks=count, experts=experts, later=len(later)),
            in_specs=[SCALAR] + [WHOLE] * (len(operands) - 1) + [ANY] * len(later),
            out_specs=[WHOLE] * count + [ANY] * len(later),
            out_shape=[shape((batch, width), F32 if j == 0 else BF16) for j in group]
            + [shape(block.shape, BF16) for block in later],
            cost_estimate=LIGHT,
            input_output_aliases={len(operands) + k: count + k for k in range(len(later))},
            compiler_params=params(experts * count * CAP * width),
        )(*operands, *later)
        if later:
            results[0] = [results[0][0], *mixed[count:]]
        received = received[:EARLY] if own else received
        received = [swap(block, "attn", j) for j, block in zip(group, mixed)] + received
    return pl.pallas_call(
        finish_kernel,
        in_specs=[WHOLE] * len(received),
        out_specs=WHOLE,
        out_shape=shape((batch, width), BF16),
        compiler_params=params(2 * layers * batch * width),
    )(*received)


def solution(mesh):
    in_specs = (
        P(("groups", "attn", "expert"), None),
        P(("groups", "attn", "expert"), None, None),
        P(("groups", "attn", "expert"), None, None),
        P(("groups", "attn", "expert")),
        P(("groups", "attn", "expert"), None),
        P(("groups", "attn", "expert"), None),
        P(),
        P(),
        P("expert", None, "attn"),
        P("expert", None, "attn"),
        P("expert", "attn", None),
    )
    out_specs = P(("groups", "attn", "expert"), None)
    return jax.shard_map(shards, mesh=mesh, in_specs=in_specs, out_specs=out_specs, check_vma=False)
```

```python
import functools

import jax
import jax.numpy as jnp
from jax import lax
from jax.experimental import pallas as pl
from jax.experimental.pallas import tpu as pltpu
from jax.sharding import PartitionSpec as P

HS = 128
KVH = 4
GROUP = 6
CAP = 8
LANES = 128
PAIR = 2
MIB = 1 << 20
F32 = jnp.float32
BF16 = jnp.bfloat16
LIGHT = pl.CostEstimate(flops=0, bytes_accessed=0, transcendentals=0)
BUSY = pl.CostEstimate(flops=24 * 10**9, bytes_accessed=0, transcendentals=0)
ANY = pl.BlockSpec(memory_space=pl.ANY)
WHOLE = pl.BlockSpec(memory_space=pltpu.VMEM)
SCALAR = pl.BlockSpec(memory_space=pltpu.SMEM)


def dot(a, b, dims=((1,), (0,))):
    return lax.dot_general(a, b, (dims, ((), ())), preferred_element_type=F32)


def iota(shape, dim):
    return lax.broadcasted_iota(jnp.int32, shape, dim)


def slot_map(owners, chunks, batch, experts):
    rows, slots = chunks * batch, experts * chunks * CAP
    slot = iota((rows, slots), 1)
    row = iota((rows, slots), 0)
    expert = slot // (chunks * CAP)
    chunk = (slot // CAP) % chunks
    named = (owners[:, 0:1] == expert) | (owners[:, 1:2] == expert)
    named = named & (row // batch == chunk)
    named = jnp.where(named, 1.0, 0.0)
    left, right = iota((rows, rows), 0), iota((rows, rows), 1)
    before = jnp.where(right < left, 1.0, 0.0).astype(BF16)
    place = dot(before, named.astype(BF16))
    wanted = (slot % CAP).astype(F32)
    return jnp.where(place == wanted, named, 0.0)


def dispatch(me, rows, named, chunks, experts):
    owners = named[:, 0:2].astype(F32).astype(jnp.int32) ^ me
    table = slot_map(owners, chunks, rows.shape[0] // chunks, experts)
    return dot(table.astype(BF16), rows, ((0,), (0,)))


def combine(me, rows, named, router, returned, chunks, experts):
    routes = named[:, 0:2].astype(F32).astype(jnp.int32)
    logits = dot(rows, router, ((1,), (1,)))
    lane = iota(logits.shape, 1)
    first = jnp.sum(jnp.where(lane == routes[:, 0:1], logits, 0.0), axis=1, keepdims=True)
    second = jnp.sum(jnp.where(lane == routes[:, 1:2], logits, 0.0), axis=1, keepdims=True)
    gate0 = 1.0 / (1.0 + jnp.exp(second - first))
    gate1 = 1.0 / (1.0 + jnp.exp(first - second))
    owners = routes ^ me
    table = slot_map(owners, chunks, rows.shape[0] // chunks, experts)
    expert = iota(table.shape, 1) // (chunks * CAP)
    gates = table * jnp.where(owners[:, 0:1] == expert, gate0, gate1)
    high = gates.astype(BF16)
    low = (gates - high.astype(F32)).astype(BF16)
    return dot(high, returned) + dot(low, returned)


def attend_kernel(
    lengths_hbm, queries_hbm, keys_hbm, values_hbm, routes_hbm, residual_hbm, gain_hbm,
    stream_ref, payload_ref,
    lengths_ref, queries_ref, keys_ref, values_ref, routes_ref, residual_ref, gain_ref, sems,
):
    batch, window, _ = keys_ref.shape
    width = queries_ref.shape[1]
    span = width // KVH
    parts = [pl.ds(begin, PAIR * HS) for begin in range(0, KVH * HS, PAIR * HS)]
    small = [
        (lengths_hbm, lengths_ref), (queries_hbm, queries_ref), (routes_hbm, routes_ref),
        (residual_hbm, residual_ref), (gain_hbm, gain_ref),
    ]
    caches = [
        pair
        for part in parts
        for pair in (
            (keys_hbm.at[:, :, part], keys_ref.at[:, :, part]),
            (values_hbm.at[:, :, part], values_ref.at[:, 0:window, part]),
        )
    ]
    copies = [
        pltpu.make_async_copy(source, target, sems.at[i])
        for i, (source, target) in enumerate(small[:2] + caches + small[2:])
    ]
    for copy in copies:
        copy.start()
    padded = values_ref.shape[1]
    if padded > window:
        pad = (batch, padded - window, values_ref.shape[2])
        values_ref[:, window:, :] = jnp.zeros(pad, BF16)
    copies[0].wait()
    copies[1].wait()
    same = iota((batch, batch), 0) == iota((batch, batch), 1)

    def upright(row):
        return jnp.sum(jnp.where(same, row, 0), axis=1, keepdims=True)

    queries = queries_ref[...]
    lanes = PAIR * GROUP * batch
    full = -(-lanes // LANES) * LANES
    request = iota((window, full), 1) % batch
    length = jnp.zeros((1, full), jnp.int32)
    for r in range(batch):
        length = jnp.where(request[0:1] == r, lengths_ref[0:1, r : r + 1], length)
    visible = iota((window, full), 0) < length
    owner = iota((lanes, padded), 0) % batch
    attended = []
    for i, part in enumerate(parts):
        spread = []
        for k in range(PAIR):
            at = [(i * PAIR + k) * span + g * HS for g in range(GROUP)]
            stacked = jnp.concatenate([queries[:, c : c + HS] for c in at], axis=0)
            blank = jnp.zeros_like(stacked)
            spread.append(
                jnp.concatenate([stacked if j == k else blank for j in range(PAIR)], axis=1)
            )
        if full > lanes:
            spread.append(jnp.zeros((full - lanes, PAIR * HS), BF16))
        spread = jnp.concatenate(spread, axis=0)
        copies[2 + 2 * i].wait()
        keys = keys_ref[:, :, part].reshape(batch * window, PAIR * HS)
        products = dot(keys, spread, ((1,), (1,)))
        scores = products[:window]
        for r in range(1, batch):
            scores = jnp.where(request == r, products[r * window : (r + 1) * window], scores)
        scores = jnp.where(visible, scores * HS ** (-0.5), -1e30)
        powers = jnp.exp(scores - jnp.max(scores, axis=0, keepdims=True))
        weights = powers / jnp.sum(powers, axis=0, keepdims=True)
        if padded > window:
            weights = jnp.concatenate([weights, jnp.zeros((padded - window, full), F32)], axis=0)
        weights = weights.T[:lanes]
        weights = jnp.concatenate(
            [jnp.where(owner == r, weights, 0.0).astype(BF16) for r in range(batch)], axis=1
        )
        copies[3 + 2 * i].wait()
        values = values_ref[:, :, part].reshape(batch * padded, PAIR * HS)
        mixed = dot(weights, values)
        attended += [
            mixed[h * batch : (h + 1) * batch, h // GROUP * HS : (h // GROUP + 1) * HS]
            for h in range(PAIR * GROUP)
        ]
    for copy in copies[2 + 2 * len(parts) :]:
        copy.wait()
    stream = residual_ref[...].astype(F32) + jnp.concatenate(attended, axis=1)
    scale = lax.rsqrt(jnp.mean(stream * stream, axis=1, keepdims=True) + 1e-05)
    lane = iota((batch, LANES), 1)
    routes = [upright(routes_ref[k : k + 1, :]).astype(F32) for k in range(2)]
    named = jnp.where(lane == 0, routes[0], jnp.where(lane == 1, routes[1], 0.0))
    stream_ref[...] = stream
    payload_ref[:, :width] = (stream * scale * gain_ref[...]).astype(BF16)
    payload_ref[:, width:] = named.astype(BF16)


def split_kernel(me_ref, *refs, chunks, after):
    refs = refs[after:]
    payload = jnp.concatenate([ref[...] for ref in refs[:chunks]], axis=0)
    slots = refs[chunks:]
    width = slots[0].shape[1]
    rows, named = payload[:, :width], payload[:, width:]
    out = dispatch(me_ref[0], rows, named, chunks, len(slots))
    span = chunks * CAP
    for e, ref in enumerate(slots):
        ref[...] = out[e * span : (e + 1) * span].astype(BF16)


def expert_kernel(*refs, pieces):
    xs, (gate_ref, up_ref, down_ref) = refs[:pieces], refs[pieces : pieces + 3]
    outs = refs[pieces + 3 : 2 * pieces + 3]
    rows_ref, hidden_ref = refs[2 * pieces + 3 :]
    rows_ref[...] = jnp.concatenate([ref[...].astype(F32) for ref in xs], axis=0).astype(BF16)
    width, units = gate_ref.shape
    tile = min(256, units)

    @pl.loop(0, units // tile)
    def _(i):
        at = pl.ds(pl.multiple_of(i * tile, tile), tile)
        gate = dot(rows_ref[...], gate_ref[:, at])
        up = dot(rows_ref[...], up_ref[:, at])
        hidden_ref[:, at] = (jax.nn.silu(gate) * up).astype(BF16)

    @pl.loop(0, width // tile)
    def _(i):
        at = pl.ds(pl.multiple_of(i * tile, tile), tile)
        out = dot(hidden_ref[...], down_ref[:, at])
        begin = 0
        for ref in outs:
            count = ref.shape[0]
            ref[:, at] = out[begin : begin + count].astype(BF16)
            begin += count


def mix_kernel(me_ref, router_ref, *refs, chunks, experts):
    payload = jnp.concatenate([ref[...] for ref in refs[:chunks]], axis=0)
    returned = jnp.concatenate(
        [ref[...].astype(F32) for ref in refs[chunks : chunks + experts]], axis=0
    ).astype(BF16)
    added, outs = refs[chunks + experts : len(refs) - chunks], refs[len(refs) - chunks :]
    batch, width = outs[0].shape
    rows, named = payload[:, :width], payload[:, width:]
    mixed = combine(me_ref[0], rows, named, router_ref[...], returned, chunks, experts)
    for j, ref in enumerate(outs):
        part = mixed[j * batch : (j + 1) * batch]
        for other in added if j == 0 else []:
            part = part + other[...]
        ref[...] = part.astype(ref.dtype)


def mix(me, router, payloads, returned, added):
    chunks, experts = len(payloads), len(returned)
    width = returned[0].shape[1]
    batch = payloads[0].shape[0]
    returned = [swap(block, "expert", e) for e, block in enumerate(returned)]
    operands = [me, router, *payloads, *returned, *added]
    return pl.pallas_call(
        functools.partial(mix_kernel, chunks=chunks, experts=experts),
        in_specs=[SCALAR] + [WHOLE] * (len(operands) - 1),
        out_specs=[WHOLE] * chunks,
        out_shape=[
            jax.ShapeDtypeStruct((batch, width), BF16 if j % 2 else F32) for j in range(chunks)
        ],
        cost_estimate=LIGHT,
        compiler_params=params(experts * chunks * CAP * width),
    )(*operands)


def add_kernel(*refs):
    total = refs[0][...]
    for ref in refs[1:-1]:
        total = total + ref[...].astype(F32)
    refs[-1][...] = total.astype(BF16)


def in_hbm(value):
    return pltpu.with_memory_space_constraint(value, pltpu.HBM)


def swap(value, axis, step):
    if step == 0:
        return value
    count = lax.axis_size(axis)
    return lax.ppermute(value, axis, [(i, i ^ step) for i in range(count)])


def params(elements):
    return pltpu.CompilerParams(vmem_limit_bytes=min(48 * MIB, 2 * MIB + 10 * elements))


def shards(
    queries,
    cached_keys,
    cached_values,
    lengths,
    routes,
    residual,
    norm_gain,
    router,
    gate_proj,
    up_proj,
    down_proj,
):
    batch, width = queries.shape
    experts = router.shape[1]
    layers = lax.axis_size("attn")
    me = lax.axis_index("expert").astype(jnp.int32).reshape(1)
    router = router.T
    shape = jax.ShapeDtypeStruct
    operands = [
        in_hbm(a)
        for a in (
            lengths[None], queries, cached_keys, cached_values, routes.T, residual, norm_gain[None]
        )
    ]
    window, depth = cached_values.shape[1:]
    held = [a.shape for a in operands]
    held[3] = (batch, -(-window // LANES) * LANES, depth)
    stream, payload = pl.pallas_call(
        attend_kernel,
        in_specs=[ANY] * len(operands),
        out_specs=[WHOLE, WHOLE],
        out_shape=[shape((batch, width), F32), shape((batch, width + LANES), BF16)],
        scratch_shapes=[pltpu.VMEM(size, a.dtype) for size, a in zip(held, operands)]
        + [pltpu.SemaphoreType.DMA((5 + 2 * (KVH // PAIR),))],
        compiler_params=params(28 * batch * width),
        cost_estimate=pl.CostEstimate(flops=10**9, bytes_accessed=4 * 10**6, transcendentals=0),
    )(*operands)

    chunks = []
    for j in range(layers):
        passed = j > 1 and j % 2
        chunks.append(swap(chunks[j - 1], "attn", 1) if passed else swap(payload, "attn", j))
    groups = [[0, 1], list(range(2, layers))]
    inputs, ahead = [], []
    for group in groups:
        count = len(group)
        slots = pl.pallas_call(
            functools.partial(split_kernel, chunks=count, after=len(ahead)),
            in_specs=[SCALAR] + [ANY] * len(ahead) + [WHOLE] * count,
            out_specs=[WHOLE] * experts,
            out_shape=[shape((count * CAP, width), BF16)] * experts,
            cost_estimate=BUSY,
            compiler_params=params(experts * count * CAP * width),
        )(me, *ahead, *[chunks[j] for j in group])
        arrived = [swap(slots[e], "expert", e) for e in range(experts)]
        ahead = arrived[1:2]
        inputs += arrived

    total_rows = sum(block.shape[0] for block in inputs)
    units = gate_proj.shape[2]
    results = pl.pallas_call(
        functools.partial(expert_kernel, pieces=len(inputs)),
        in_specs=[WHOLE] * (len(inputs) + 3),
        out_specs=[WHOLE] * len(inputs),
        out_shape=[shape(block.shape, BF16) for block in inputs],
        scratch_shapes=[pltpu.VMEM((total_rows, width), BF16), pltpu.VMEM((total_rows, units), BF16)],
        compiler_params=params(total_rows * width),
    )(*inputs, gate_proj[0], up_proj[0], down_proj[0])

    near, far = results[:experts], results[experts:]
    far = mix(me, router, [chunks[j] for j in groups[1]], far, [])
    kept, sent = far[::2], far[1::2]
    passed = [swap(block, "attn", 1) for block in sent]
    received = []
    for j, own, other in zip(groups[1][::2], kept, passed):
        total = pl.pallas_call(
            add_kernel,
            in_specs=[WHOLE, WHOLE],
            out_specs=WHOLE,
            out_shape=shape((batch, width), BF16),
            cost_estimate=LIGHT,
            compiler_params=params(2 * batch * width),
        )(own, other)
        received.append(swap(total, "attn", j))
    base, first = mix(me, router, chunks[:2], near, [stream])
    received = [swap(first, "attn", 1), *received]
    return pl.pallas_call(
        add_kernel,
        in_specs=[WHOLE] * (1 + len(received)),
        out_specs=WHOLE,
        out_shape=shape((batch, width), BF16),
        cost_estimate=LIGHT,
        compiler_params=params(2 * layers * batch * width),
    )(base, *received)


def solution(mesh):
    in_specs = (
        P(("groups", "attn", "expert"), None),
        P(("groups", "attn", "expert"), None, None),
        P(("groups", "attn", "expert"), None, None),
        P(("groups", "attn", "expert")),
        P(("groups", "attn", "expert"), None),
        P(("groups", "attn", "expert"), None),
        P(),
        P(),
        P("expert", None, "attn"),
        P("expert", None, "attn"),
        P("expert", "attn", None),
    )
    out_specs = P(("groups", "attn", "expert"), None)
    return jax.shard_map(shards, mesh=mesh, in_specs=in_specs, out_specs=out_specs, check_vma=False)
```

```python
import functools

import jax
import jax.numpy as jnp
from jax import lax
from jax.experimental import pallas as pl
from jax.experimental.pallas import tpu as pltpu
from jax.sharding import PartitionSpec as P

HS = 128
KVH = 4
GROUP = 6
CAP = 8
LANES = 128
PAIR = 2
MIB = 1 << 20
F32 = jnp.float32
BF16 = jnp.bfloat16
LIGHT = pl.CostEstimate(flops=0, bytes_accessed=0, transcendentals=0)
BUSY = pl.CostEstimate(flops=24 * 10**9, bytes_accessed=0, transcendentals=0)
ANY = pl.BlockSpec(memory_space=pl.ANY)
WHOLE = pl.BlockSpec(memory_space=pltpu.VMEM)
SCALAR = pl.BlockSpec(memory_space=pltpu.SMEM)


def dot(a, b, dims=((1,), (0,))):
    return lax.dot_general(a, b, (dims, ((), ())), preferred_element_type=F32)


def iota(shape, dim):
    return lax.broadcasted_iota(jnp.int32, shape, dim)


def slot_map(owners, chunks, batch, experts):
    rows, slots = chunks * batch, experts * chunks * CAP
    slot = iota((rows, slots), 1)
    row = iota((rows, slots), 0)
    expert = slot // (chunks * CAP)
    chunk = (slot // CAP) % chunks
    named = (owners[:, 0:1] == expert) | (owners[:, 1:2] == expert)
    named = named & (row // batch == chunk)
    named = jnp.where(named, 1.0, 0.0)
    left, right = iota((rows, rows), 0), iota((rows, rows), 1)
    before = jnp.where(right < left, 1.0, 0.0).astype(BF16)
    place = dot(before, named.astype(BF16))
    wanted = (slot % CAP).astype(F32)
    return jnp.where(place == wanted, named, 0.0)


def dispatch(me, rows, named, chunks, experts):
    owners = named[:, 0:2].astype(F32).astype(jnp.int32) ^ me
    table = slot_map(owners, chunks, rows.shape[0] // chunks, experts)
    return dot(table.astype(BF16), rows, ((0,), (0,)))


def combine(me, rows, named, router, returned, chunks, experts):
    routes = named[:, 0:2].astype(F32).astype(jnp.int32)
    logits = dot(rows, router, ((1,), (1,)))
    lane = iota(logits.shape, 1)
    first = jnp.sum(jnp.where(lane == routes[:, 0:1], logits, 0.0), axis=1, keepdims=True)
    second = jnp.sum(jnp.where(lane == routes[:, 1:2], logits, 0.0), axis=1, keepdims=True)
    gate0 = 1.0 / (1.0 + jnp.exp(second - first))
    gate1 = 1.0 / (1.0 + jnp.exp(first - second))
    owners = routes ^ me
    table = slot_map(owners, chunks, rows.shape[0] // chunks, experts)
    expert = iota(table.shape, 1) // (chunks * CAP)
    gates = table * jnp.where(owners[:, 0:1] == expert, gate0, gate1)
    high = gates.astype(BF16)
    low = (gates - high.astype(F32)).astype(BF16)
    return dot(high, returned) + dot(low, returned)


def attend_kernel(
    _, lengths_hbm, queries_hbm, keys_hbm, values_hbm, routes_hbm, residual_hbm, gain_hbm,
    stream_ref, payload_ref,
    lengths_ref, queries_ref, keys_ref, values_ref, routes_ref, residual_ref, gain_ref, sems,
):
    batch, window, _ = keys_ref.shape
    width = queries_ref.shape[1]
    span = width // KVH
    parts = [pl.ds(begin, PAIR * HS) for begin in range(0, KVH * HS, PAIR * HS)]
    small = [
        (lengths_hbm, lengths_ref), (queries_hbm, queries_ref), (routes_hbm, routes_ref),
        (residual_hbm, residual_ref), (gain_hbm, gain_ref),
    ]
    caches = [
        pair
        for part in parts
        for pair in (
            (keys_hbm.at[:, :, part], keys_ref.at[:, :, part]),
            (values_hbm.at[:, :, part], values_ref.at[:, 0:window, part]),
        )
    ]
    copies = [
        pltpu.make_async_copy(source, target, sems.at[i])
        for i, (source, target) in enumerate(small[:2] + caches + small[2:])
    ]
    for copy in copies:
        copy.start()
    padded = values_ref.shape[1]
    if padded > window:
        pad = (batch, padded - window, values_ref.shape[2])
        values_ref[:, window:, :] = jnp.zeros(pad, BF16)
    copies[0].wait()
    copies[1].wait()
    same = iota((batch, batch), 0) == iota((batch, batch), 1)

    def upright(row):
        return jnp.sum(jnp.where(same, row, 0), axis=1, keepdims=True)

    queries = queries_ref[...]
    lanes = PAIR * GROUP * batch
    full = -(-lanes // LANES) * LANES
    request = iota((window, full), 1) % batch
    length = jnp.zeros((1, full), jnp.int32)
    for r in range(batch):
        length = jnp.where(request[0:1] == r, lengths_ref[0:1, r : r + 1], length)
    visible = iota((window, full), 0) < length
    owner = iota((lanes, padded), 0) % batch
    attended = []
    for i, part in enumerate(parts):
        spread = []
        for k in range(PAIR):
            at = [(i * PAIR + k) * span + g * HS for g in range(GROUP)]
            stacked = jnp.concatenate([queries[:, c : c + HS] for c in at], axis=0)
            blank = jnp.zeros_like(stacked)
            spread.append(
                jnp.concatenate([stacked if j == k else blank for j in range(PAIR)], axis=1)
            )
        if full > lanes:
            spread.append(jnp.zeros((full - lanes, PAIR * HS), BF16))
        spread = jnp.concatenate(spread, axis=0)
        copies[2 + 2 * i].wait()
        keys = keys_ref[:, :, part].reshape(batch * window, PAIR * HS)
        products = dot(keys, spread, ((1,), (1,)))
        scores = products[:window]
        for r in range(1, batch):
            scores = jnp.where(request == r, products[r * window : (r + 1) * window], scores)
        scores = jnp.where(visible, scores * HS ** (-0.5), -1e30)
        powers = jnp.exp(scores - jnp.max(scores, axis=0, keepdims=True))
        weights = powers / jnp.sum(powers, axis=0, keepdims=True)
        if padded > window:
            weights = jnp.concatenate([weights, jnp.zeros((padded - window, full), F32)], axis=0)
        weights = weights.T[:lanes]
        weights = jnp.concatenate(
            [jnp.where(owner == r, weights, 0.0).astype(BF16) for r in range(batch)], axis=1
        )
        copies[3 + 2 * i].wait()
        values = values_ref[:, :, part].reshape(batch * padded, PAIR * HS)
        mixed = dot(weights, values)
        attended += [
            mixed[h * batch : (h + 1) * batch, h // GROUP * HS : (h // GROUP + 1) * HS]
            for h in range(PAIR * GROUP)
        ]
    for copy in copies[2 + 2 * len(parts) :]:
        copy.wait()
    stream = residual_ref[...].astype(F32) + jnp.concatenate(attended, axis=1)
    scale = lax.rsqrt(jnp.mean(stream * stream, axis=1, keepdims=True) + 1e-05)
    lane = iota((batch, LANES), 1)
    routes = [upright(routes_ref[k : k + 1, :]).astype(F32) for k in range(2)]
    named = jnp.where(lane == 0, routes[0], jnp.where(lane == 1, routes[1], 0.0))
    stream_ref[...] = stream
    payload_ref[:, :width] = (stream * scale * gain_ref[...]).astype(BF16)
    payload_ref[:, width:] = named.astype(BF16)


def split_kernel(me_ref, *refs, chunks, after):
    refs = refs[after:]
    payload = jnp.concatenate([ref[...] for ref in refs[:chunks]], axis=0)
    slots = refs[chunks:]
    width = slots[0].shape[1]
    rows, named = payload[:, :width], payload[:, width:]
    out = dispatch(me_ref[0], rows, named, chunks, len(slots))
    span = chunks * CAP
    for e, ref in enumerate(slots):
        ref[...] = out[e * span : (e + 1) * span].astype(BF16)


def expert_kernel(*refs, pieces):
    xs, (gate_ref, up_ref, down_ref) = refs[:pieces], refs[pieces : pieces + 3]
    outs = refs[pieces + 3 : 2 * pieces + 3]
    rows_ref, hidden_ref = refs[2 * pieces + 3 :]
    rows_ref[...] = jnp.concatenate([ref[...].astype(F32) for ref in xs], axis=0).astype(BF16)
    width, units = gate_ref.shape
    tile = min(256, units)

    @pl.loop(0, units // tile)
    def _(i):
        at = pl.ds(pl.multiple_of(i * tile, tile), tile)
        gate = dot(rows_ref[...], gate_ref[:, at])
        up = dot(rows_ref[...], up_ref[:, at])
        hidden_ref[:, at] = (jax.nn.silu(gate) * up).astype(BF16)

    @pl.loop(0, width // tile)
    def _(i):
        at = pl.ds(pl.multiple_of(i * tile, tile), tile)
        out = dot(hidden_ref[...], down_ref[:, at])
        begin = 0
        for ref in outs:
            count = ref.shape[0]
            ref[:, at] = out[begin : begin + count].astype(BF16)
            begin += count


def mix_kernel(me_ref, router_ref, *refs, chunks, experts, after):
    refs = refs[after:]
    payload = jnp.concatenate([ref[...] for ref in refs[:chunks]], axis=0)
    order = farthest_first(experts)
    returned = jnp.concatenate(
        [refs[chunks + order.index(e)][...].astype(F32) for e in range(experts)], axis=0
    ).astype(BF16)
    added, outs = refs[chunks + experts : len(refs) - chunks], refs[len(refs) - chunks :]
    batch, width = outs[0].shape
    rows, named = payload[:, :width], payload[:, width:]
    mixed = combine(me_ref[0], rows, named, router_ref[...], returned, chunks, experts)
    for j, ref in enumerate(outs):
        part = mixed[j * batch : (j + 1) * batch]
        for other in added if j == 0 else []:
            part = part + other[...]
        ref[...] = part.astype(ref.dtype)


def mix(me, router, payloads, returned, added, after):
    chunks, experts = len(payloads), len(returned)
    width = returned[0].shape[1]
    batch = payloads[0].shape[0]
    returned = [swap(block, "expert", e) for e, block in zip(farthest_first(experts), returned)]
    operands = [me, router, *after, *payloads, *returned, *added]
    return pl.pallas_call(
        functools.partial(mix_kernel, chunks=chunks, experts=experts, after=len(after)),
        in_specs=[SCALAR, WHOLE] + [ANY] * len(after) + [WHOLE] * (len(operands) - 2 - len(after)),
        out_specs=[WHOLE] * chunks,
        out_shape=[
            jax.ShapeDtypeStruct((batch, width), F32 if added and j == 0 else BF16)
            for j in range(chunks)
        ],
        cost_estimate=LIGHT,
        compiler_params=params(experts * chunks * CAP * width),
    )(*operands)


def add_kernel(*refs):
    total = refs[0][...]
    for ref in refs[1:-1]:
        total = total + ref[...].astype(F32)
    refs[-1][...] = total.astype(BF16)


def in_hbm(value):
    return pltpu.with_memory_space_constraint(value, pltpu.HBM)


def swap(value, axis, step):
    if step == 0:
        return value
    count = lax.axis_size(axis)
    return lax.ppermute(value, axis, [(i, i ^ step) for i in range(count)])


def farthest_first(count):
    return [0, *range(count - 1, 0, -1)]


def params(elements):
    return pltpu.CompilerParams(vmem_limit_bytes=min(48 * MIB, 2 * MIB + 10 * elements))


def shards(
    queries,
    cached_keys,
    cached_values,
    lengths,
    routes,
    residual,
    norm_gain,
    router,
    gate_proj,
    up_proj,
    down_proj,
):
    batch, width = queries.shape
    experts = router.shape[1]
    layers = lax.axis_size("attn")
    me = lax.axis_index("expert").astype(jnp.int32).reshape(1)
    router = router.T
    shape = jax.ShapeDtypeStruct
    operands = [
        in_hbm(a)
        for a in (
            lengths[None], queries, cached_keys, cached_values, routes.T, residual, norm_gain[None]
        )
    ]
    window, depth = cached_values.shape[1:]
    held = [a.shape for a in operands]
    held[3] = (batch, -(-window // LANES) * LANES, depth)
    stream, payload = pl.pallas_call(
        attend_kernel,
        in_specs=[SCALAR] + [ANY] * len(operands),
        out_specs=[WHOLE, WHOLE],
        out_shape=[shape((batch, width), F32), shape((batch, width + LANES), BF16)],
        scratch_shapes=[pltpu.VMEM(size, a.dtype) for size, a in zip(held, operands)]
        + [pltpu.SemaphoreType.DMA((5 + 2 * (KVH // PAIR),))],
        compiler_params=params(28 * batch * width),
        cost_estimate=LIGHT,
    )(me, *operands)

    chunks = [swap(payload, "attn", j) for j in range(layers)]
    groups = [[0, 1], list(range(2, layers))]
    inputs, ahead = [], []
    for group in groups:
        count = len(group)
        slots = pl.pallas_call(
            functools.partial(split_kernel, chunks=count, after=len(ahead)),
            in_specs=[SCALAR] + [ANY] * len(ahead) + [WHOLE] * count,
            out_specs=[WHOLE] * experts,
            out_shape=[shape((count * CAP, width), BF16)] * experts,
            cost_estimate=BUSY if group == groups[0] else LIGHT,
            compiler_params=params(experts * count * CAP * width),
        )(me, *ahead, *[chunks[j] for j in group])
        arrived = [swap(slots[e], "expert", e) for e in farthest_first(experts)]
        ahead = arrived[1:2]
        inputs += arrived

    total_rows = sum(block.shape[0] for block in inputs)
    units = gate_proj.shape[2]
    results = pl.pallas_call(
        functools.partial(expert_kernel, pieces=len(inputs)),
        in_specs=[WHOLE] * (len(inputs) + 3),
        out_specs=[WHOLE] * len(inputs),
        out_shape=[shape(block.shape, BF16) for block in inputs],
        scratch_shapes=[pltpu.VMEM((total_rows, width), BF16), pltpu.VMEM((total_rows, units), BF16)],
        compiler_params=params(total_rows * width),
    )(*inputs, gate_proj[0], up_proj[0], down_proj[0])

    near, far = results[:experts], results[experts:]
    far = mix(me, router, [chunks[j] for j in groups[1]], far, [], [])
    base, first = mix(me, router, chunks[:2], near, [stream], far[:1])
    received = [swap(block, "attn", j + 1) for j, block in enumerate([first, *far])]
    return pl.pallas_call(
        add_kernel,
        in_specs=[WHOLE] * layers,
        out_specs=WHOLE,
        out_shape=shape((batch, width), BF16),
        cost_estimate=LIGHT,
        compiler_params=params(2 * layers * batch * width),
    )(base, *received)


def solution(mesh):
    in_specs = (
        P(("groups", "attn", "expert"), None),
        P(("groups", "attn", "expert"), None, None),
        P(("groups", "attn", "expert"), None, None),
        P(("groups", "attn", "expert")),
        P(("groups", "attn", "expert"), None),
        P(("groups", "attn", "expert"), None),
        P(),
        P(),
        P("expert", None, "attn"),
        P("expert", None, "attn"),
        P("expert", "attn", None),
    )
    out_specs = P(("groups", "attn", "expert"), None)
    return jax.shard_map(shards, mesh=mesh, in_specs=in_specs, out_specs=out_specs, check_vma=False)
```

```python
import functools

import jax
import jax.numpy as jnp
from jax import lax
from jax.experimental import pallas as pl
from jax.experimental.pallas import tpu as pltpu
from jax.sharding import PartitionSpec as P

HS = 128
KVH = 4
GROUP = 6
CAP = 8
LANES = 128
PAIR = 2
STRIPS = 6
MIB = 1 << 20
F32 = jnp.float32
BF16 = jnp.bfloat16
LIGHT = pl.CostEstimate(flops=0, bytes_accessed=0, transcendentals=0)
BUSY = pl.CostEstimate(flops=24 * 10**9, bytes_accessed=0, transcendentals=0)
ANY = pl.BlockSpec(memory_space=pl.ANY)
WHOLE = pl.BlockSpec(memory_space=pltpu.VMEM)
SCALAR = pl.BlockSpec(memory_space=pltpu.SMEM)


def dot(a, b, dims=((1,), (0,))):
    return lax.dot_general(a, b, (dims, ((), ())), preferred_element_type=F32)


def iota(shape, dim):
    return lax.broadcasted_iota(jnp.int32, shape, dim)


def slot_map(owners, chunks, batch, experts):
    rows, slots = chunks * batch, experts * chunks * CAP
    slot = iota((rows, slots), 1)
    row = iota((rows, slots), 0)
    expert = slot // (chunks * CAP)
    chunk = (slot // CAP) % chunks
    named = (owners[:, 0:1] == expert) | (owners[:, 1:2] == expert)
    named = named & (row // batch == chunk)
    named = jnp.where(named, 1.0, 0.0)
    left, right = iota((rows, rows), 0), iota((rows, rows), 1)
    before = jnp.where(right < left, 1.0, 0.0).astype(BF16)
    place = dot(before, named.astype(BF16))
    wanted = (slot % CAP).astype(F32)
    return jnp.where(place == wanted, named, 0.0)


def dispatch(me, rows, named, chunks, experts):
    owners = named[:, 0:2].astype(F32).astype(jnp.int32) ^ me
    table = slot_map(owners, chunks, rows.shape[0] // chunks, experts)
    return dot(table.astype(BF16), rows, ((0,), (0,)))


def combine(me, rows, named, router, returned, chunks, experts):
    routes = named[:, 0:2].astype(F32).astype(jnp.int32)
    logits = dot(rows, router, ((1,), (1,)))
    lane = iota(logits.shape, 1)
    first = jnp.sum(jnp.where(lane == routes[:, 0:1], logits, 0.0), axis=1, keepdims=True)
    second = jnp.sum(jnp.where(lane == routes[:, 1:2], logits, 0.0), axis=1, keepdims=True)
    gate0 = 1.0 / (1.0 + jnp.exp(second - first))
    gate1 = 1.0 / (1.0 + jnp.exp(first - second))
    owners = routes ^ me
    table = slot_map(owners, chunks, rows.shape[0] // chunks, experts)
    expert = iota(table.shape, 1) // (chunks * CAP)
    gates = table * jnp.where(owners[:, 0:1] == expert, gate0, gate1)
    high = gates.astype(BF16)
    low = (gates - high.astype(F32)).astype(BF16)
    return dot(high, returned) + dot(low, returned)


def attend_kernel(
    _, lengths_hbm, queries_hbm, keys_hbm, values_hbm, routes_hbm, residual_hbm, gain_hbm,
    stream_ref, payload_ref,
    lengths_ref, queries_ref, keys_ref, values_ref, routes_ref, residual_ref, gain_ref, sems,
):
    batch, window, _ = keys_ref.shape
    width = queries_ref.shape[1]
    span = width // KVH
    parts = [pl.ds(begin, PAIR * HS) for begin in range(0, KVH * HS, PAIR * HS)]
    small = [
        (lengths_hbm, lengths_ref), (queries_hbm, queries_ref), (routes_hbm, routes_ref),
        (residual_hbm, residual_ref), (gain_hbm, gain_ref),
    ]
    caches = [
        pair
        for part in parts
        for pair in (
            (keys_hbm.at[:, :, part], keys_ref.at[:, :, part]),
            (values_hbm.at[:, :, part], values_ref.at[:, 0:window, part]),
        )
    ]
    copies = [
        pltpu.make_async_copy(source, target, sems.at[i])
        for i, (source, target) in enumerate(small[:2] + caches + small[2:])
    ]
    for copy in copies:
        copy.start()
    padded = values_ref.shape[1]
    if padded > window:
        pad = (batch, padded - window, values_ref.shape[2])
        values_ref[:, window:, :] = jnp.zeros(pad, BF16)
    copies[0].wait()
    copies[1].wait()
    same = iota((batch, batch), 0) == iota((batch, batch), 1)

    def upright(row):
        return jnp.sum(jnp.where(same, row, 0), axis=1, keepdims=True)

    queries = queries_ref[...]
    lanes = PAIR * GROUP * batch
    full = -(-lanes // LANES) * LANES
    request = iota((window, full), 1) % batch
    length = jnp.zeros((1, full), jnp.int32)
    for r in range(batch):
        length = jnp.where(request[0:1] == r, lengths_ref[0:1, r : r + 1], length)
    visible = iota((window, full), 0) < length
    owner = iota((lanes, padded), 0) % batch
    attended = []
    for i, part in enumerate(parts):
        spread = []
        for k in range(PAIR):
            at = [(i * PAIR + k) * span + g * HS for g in range(GROUP)]
            stacked = jnp.concatenate([queries[:, c : c + HS] for c in at], axis=0)
            blank = jnp.zeros_like(stacked)
            spread.append(
                jnp.concatenate([stacked if j == k else blank for j in range(PAIR)], axis=1)
            )
        if full > lanes:
            spread.append(jnp.zeros((full - lanes, PAIR * HS), BF16))
        spread = jnp.concatenate(spread, axis=0)
        copies[2 + 2 * i].wait()
        keys = keys_ref[:, :, part].reshape(batch * window, PAIR * HS)
        products = dot(keys, spread, ((1,), (1,)))
        scores = products[:window]
        for r in range(1, batch):
            scores = jnp.where(request == r, products[r * window : (r + 1) * window], scores)
        scores = jnp.where(visible, scores * HS ** (-0.5), -1e30)
        powers = jnp.exp(scores - jnp.max(scores, axis=0, keepdims=True))
        weights = powers / jnp.sum(powers, axis=0, keepdims=True)
        if padded > window:
            weights = jnp.concatenate([weights, jnp.zeros((padded - window, full), F32)], axis=0)
        weights = weights.T[:lanes]
        weights = jnp.concatenate(
            [jnp.where(owner == r, weights, 0.0).astype(BF16) for r in range(batch)], axis=1
        )
        copies[3 + 2 * i].wait()
        values = values_ref[:, :, part].reshape(batch * padded, PAIR * HS)
        mixed = dot(weights, values)
        attended += [
            mixed[h * batch : (h + 1) * batch, h // GROUP * HS : (h // GROUP + 1) * HS]
            for h in range(PAIR * GROUP)
        ]
    for copy in copies[2 + 2 * len(parts) :]:
        copy.wait()
    stream = residual_ref[...].astype(F32) + jnp.concatenate(attended, axis=1)
    scale = lax.rsqrt(jnp.mean(stream * stream, axis=1, keepdims=True) + 1e-05)
    lane = iota((batch, LANES), 1)
    routes = [upright(routes_ref[k : k + 1, :]).astype(F32) for k in range(2)]
    named = jnp.where(lane == 0, routes[0], jnp.where(lane == 1, routes[1], 0.0))
    stream_ref[...] = stream
    payload_ref[:, :width] = (stream * scale * gain_ref[...]).astype(BF16)
    payload_ref[:, width:] = named.astype(BF16)


def split_kernel(me_ref, *refs, chunks, experts, after):
    refs = refs[after:]
    payload = jnp.concatenate([ref[...] for ref in refs[:chunks]], axis=0)
    outs = refs[chunks:]
    width = payload.shape[1] - LANES
    rows, named = payload[:, :width], payload[:, width:]
    slots = dispatch(me_ref[0], rows, named, chunks, experts)
    span, part = chunks * CAP, outs[0].shape[1]
    for i, ref in enumerate(outs):
        p, e = i // experts, i % experts
        ref[...] = slots[e * span : (e + 1) * span, p * part : (p + 1) * part].astype(BF16)


def begin_kernel(*refs, near, far):
    gate_ref, up_ref, gate_out, up_out, rows_ref = refs[near + far :]
    half = rows_ref.shape[1]
    blocks = [ref[:, :half] for ref in refs[:near]] + [ref[...] for ref in refs[near : near + far]]
    rows_ref[...] = jnp.concatenate([block.astype(F32) for block in blocks], axis=0).astype(BF16)
    units = gate_ref.shape[1]
    tile = min(256, units)

    @pl.loop(0, units // tile)
    def _(i):
        at = pl.ds(pl.multiple_of(i * tile, tile), tile)
        gate_out[:, at] = dot(rows_ref[...], gate_ref[:half, at])
        up_out[:, at] = dot(rows_ref[...], up_ref[:half, at])


def end_kernel(*refs, near, far):
    gate_in, up_in, gate_ref, up_ref, down_hbm = refs[near + far : near + far + 5]
    outs = refs[near + far + 5 : -4]
    rows_ref, hidden_ref, down_ref, sems = refs[-4:]
    half = rows_ref.shape[1]
    width, units = gate_ref.shape
    strip = width // sems.shape[0]
    copies = []
    for c in range(sems.shape[0]):
        at = pl.ds(c * strip, strip)
        copies.append(pltpu.make_async_copy(down_hbm.at[:, at], down_ref.at[:, at], sems.at[c]))
        copies[-1].start()
    blocks = [ref[:, half:] for ref in refs[:near]] + [ref[...] for ref in refs[near : near + far]]
    rows_ref[...] = jnp.concatenate([block.astype(F32) for block in blocks], axis=0).astype(BF16)
    tile = min(256, units)

    @pl.loop(0, units // tile)
    def _(i):
        at = pl.ds(pl.multiple_of(i * tile, tile), tile)
        gate = gate_in[:, at] + dot(rows_ref[...], gate_ref[half:, at])
        up = up_in[:, at] + dot(rows_ref[...], up_ref[half:, at])
        hidden_ref[:, at] = (jax.nn.silu(gate) * up).astype(BF16)

    for c, copy in enumerate(copies):
        copy.wait()

        @pl.loop(0, strip // tile)
        def _(i):
            at = pl.ds(pl.multiple_of(c * strip + i * tile, tile), tile)
            out = dot(hidden_ref[...], down_ref[:, at])
            begin = 0
            for ref in outs:
                count = ref.shape[0]
                ref[:, at] = out[begin : begin + count].astype(BF16)
                begin += count


def mix_kernel(me_ref, router_ref, *refs, chunks, experts, after):
    refs = refs[after:]
    payload = jnp.concatenate([ref[...] for ref in refs[:chunks]], axis=0)
    order = farthest_first(experts)
    returned = jnp.concatenate(
        [refs[chunks + order.index(e)][...].astype(F32) for e in range(experts)], axis=0
    ).astype(BF16)
    added, outs = refs[chunks + experts : len(refs) - chunks], refs[len(refs) - chunks :]
    batch, width = outs[0].shape
    rows, named = payload[:, :width], payload[:, width:]
    mixed = combine(me_ref[0], rows, named, router_ref[...], returned, chunks, experts)
    for j, ref in enumerate(outs):
        part = mixed[j * batch : (j + 1) * batch]
        for other in added if j == 0 else []:
            part = part + other[...]
        ref[...] = part.astype(ref.dtype)


def mix(me, router, payloads, returned, added, after):
    chunks, experts = len(payloads), len(returned)
    width = returned[0].shape[1]
    batch = payloads[0].shape[0]
    returned = [swap(block, "expert", e) for e, block in zip(farthest_first(experts), returned)]
    operands = [me, router, *after, *payloads, *returned, *added]
    return pl.pallas_call(
        functools.partial(mix_kernel, chunks=chunks, experts=experts, after=len(after)),
        in_specs=[SCALAR, WHOLE] + [ANY] * len(after) + [WHOLE] * (len(operands) - 2 - len(after)),
        out_specs=[WHOLE] * chunks,
        out_shape=[
            jax.ShapeDtypeStruct((batch, width), F32 if added and j == 0 else BF16)
            for j in range(chunks)
        ],
        cost_estimate=LIGHT,
        compiler_params=params(experts * chunks * CAP * width),
    )(*operands)


def add_kernel(*refs):
    total = refs[0][...]
    for ref in refs[1:-1]:
        total = total + ref[...].astype(F32)
    refs[-1][...] = total.astype(BF16)


def in_hbm(value):
    return pltpu.with_memory_space_constraint(value, pltpu.HBM)


def swap(value, axis, step):
    if step == 0:
        return value
    count = lax.axis_size(axis)
    return lax.ppermute(value, axis, [(i, i ^ step) for i in range(count)])


def farthest_first(count):
    return [0, *range(count - 1, 0, -1)]


def params(elements):
    return pltpu.CompilerParams(vmem_limit_bytes=min(48 * MIB, 2 * MIB + 10 * elements))


def shards(
    queries,
    cached_keys,
    cached_values,
    lengths,
    routes,
    residual,
    norm_gain,
    router,
    gate_proj,
    up_proj,
    down_proj,
):
    batch, width = queries.shape
    experts = router.shape[1]
    layers = lax.axis_size("attn")
    me = lax.axis_index("expert").astype(jnp.int32).reshape(1)
    router = router.T
    shape = jax.ShapeDtypeStruct
    operands = [
        in_hbm(a)
        for a in (
            lengths[None], queries, cached_keys, cached_values, routes.T, residual, norm_gain[None]
        )
    ]
    window, depth = cached_values.shape[1:]
    held = [a.shape for a in operands]
    held[3] = (batch, -(-window // LANES) * LANES, depth)
    stream, payload = pl.pallas_call(
        attend_kernel,
        in_specs=[SCALAR] + [ANY] * len(operands),
        out_specs=[WHOLE, WHOLE],
        out_shape=[shape((batch, width), F32), shape((batch, width + LANES), BF16)],
        scratch_shapes=[pltpu.VMEM(size, a.dtype) for size, a in zip(held, operands)]
        + [pltpu.SemaphoreType.DMA((5 + 2 * (KVH // PAIR),))],
        compiler_params=params(28 * batch * width),
        cost_estimate=LIGHT,
    )(me, *operands)

    chunks = [swap(payload, "attn", j) for j in range(layers)]
    groups = [[0, 1], list(range(2, layers))]
    half = width // 2
    order = farthest_first(experts)

    def send(group, columns, after):
        count, parts = len(group), width // columns
        slots = pl.pallas_call(
            functools.partial(split_kernel, chunks=count, experts=experts, after=len(after)),
            in_specs=[SCALAR] + [ANY] * len(after) + [WHOLE] * count,
            out_specs=[WHOLE] * (parts * experts),
            out_shape=[shape((count * CAP, columns), BF16)] * (parts * experts),
            cost_estimate=LIGHT if after else BUSY,
            compiler_params=params(experts * count * CAP * width),
        )(me, *after, *[chunks[j] for j in group])
        return [
            swap(slots[p * experts + e], "expert", e) for p in range(parts) for e in order
        ]

    near = send(groups[0], width, [])
    far = send(groups[1], half, near[1:2])
    total_rows = sum(block.shape[0] for block in near + far[:experts])
    units = gate_proj.shape[2]
    counts = {"near": experts, "far": experts}
    sums = pl.pallas_call(
        functools.partial(begin_kernel, **counts),
        in_specs=[WHOLE] * (2 * experts + 2),
        out_specs=[WHOLE] * 2,
        out_shape=[shape((total_rows, units), F32)] * 2,
        scratch_shapes=[pltpu.VMEM((total_rows, half), BF16)],
        cost_estimate=pl.CostEstimate(
            flops=4 * total_rows * half * units, bytes_accessed=0, transcendentals=0
        ),
        compiler_params=params(total_rows * width),
    )(*near, *far[:experts], gate_proj[0], up_proj[0])
    results = pl.pallas_call(
        functools.partial(end_kernel, **counts),
        in_specs=[WHOLE] * (2 * experts + 4) + [ANY],
        out_specs=[WHOLE] * (2 * experts),
        out_shape=[shape((block.shape[0], width), BF16) for block in near + far[:experts]],
        scratch_shapes=[
            pltpu.VMEM((total_rows, half), BF16),
            pltpu.VMEM((total_rows, units), BF16),
            pltpu.VMEM((units, width), BF16),
            pltpu.SemaphoreType.DMA((STRIPS,)),
        ],
        compiler_params=params(total_rows * width + units * width // 5),
    )(*near, *far[experts:], *sums, gate_proj[0], up_proj[0], in_hbm(down_proj[0]))

    near, far = results[:experts], results[experts:]
    far = mix(me, router, [chunks[j] for j in groups[1]], far, [], [])
    base, first = mix(me, router, chunks[:2], near, [stream], far[:1])
    received = [swap(block, "attn", j + 1) for j, block in enumerate([first, *far])]
    return pl.pallas_call(
        add_kernel,
        in_specs=[WHOLE] * layers,
        out_specs=WHOLE,
        out_shape=shape((batch, width), BF16),
        cost_estimate=LIGHT,
        compiler_params=params(2 * layers * batch * width),
    )(base, *received)


def solution(mesh):
    in_specs = (
        P(("groups", "attn", "expert"), None),
        P(("groups", "attn", "expert"), None, None),
        P(("groups", "attn", "expert"), None, None),
        P(("groups", "attn", "expert")),
        P(("groups", "attn", "expert"), None),
        P(("groups", "attn", "expert"), None),
        P(),
        P(),
        P("expert", None, "attn"),
        P("expert", None, "attn"),
        P("expert", "attn", None),
    )
    out_specs = P(("groups", "attn", "expert"), None)
    return jax.shard_map(shards, mesh=mesh, in_specs=in_specs, out_specs=out_specs, check_vma=False)
```

```python
import functools

import jax
import jax.numpy as jnp
from jax import lax
from jax.experimental import pallas as pl
from jax.experimental.pallas import tpu as pltpu
from jax.sharding import PartitionSpec as P

HS = 128
KVH = 4
GROUP = 6
CAP = 8
LANES = 128
PAIR = 2
STRIPS = 3
MIB = 1 << 20
F32 = jnp.float32
BF16 = jnp.bfloat16
LIGHT = pl.CostEstimate(flops=0, bytes_accessed=0, transcendentals=0)
BUSY = pl.CostEstimate(flops=24 * 10**9, bytes_accessed=0, transcendentals=0)
ANY = pl.BlockSpec(memory_space=pl.ANY)
WHOLE = pl.BlockSpec(memory_space=pltpu.VMEM)
SCALAR = pl.BlockSpec(memory_space=pltpu.SMEM)


def dot(a, b, dims=((1,), (0,))):
    return lax.dot_general(a, b, (dims, ((), ())), preferred_element_type=F32)


def iota(shape, dim):
    return lax.broadcasted_iota(jnp.int32, shape, dim)


def slot_map(owners, chunks, batch, experts):
    rows, slots = chunks * batch, experts * chunks * CAP
    slot = iota((rows, slots), 1)
    row = iota((rows, slots), 0)
    expert = slot // (chunks * CAP)
    chunk = (slot // CAP) % chunks
    named = (owners[:, 0:1] == expert) | (owners[:, 1:2] == expert)
    named = named & (row // batch == chunk)
    named = jnp.where(named, 1.0, 0.0)
    left, right = iota((rows, rows), 0), iota((rows, rows), 1)
    before = jnp.where(right < left, 1.0, 0.0).astype(BF16)
    place = dot(before, named.astype(BF16))
    wanted = (slot % CAP).astype(F32)
    return jnp.where(place == wanted, named, 0.0)


def dispatch(me, rows, named, chunks, experts):
    owners = named[:, 0:2].astype(F32).astype(jnp.int32) ^ me
    table = slot_map(owners, chunks, rows.shape[0] // chunks, experts)
    return dot(table.astype(BF16), rows, ((0,), (0,)))


def combine(me, rows, named, router, returned, chunks, experts):
    routes = named[:, 0:2].astype(F32).astype(jnp.int32)
    logits = dot(rows, router, ((1,), (1,)))
    lane = iota(logits.shape, 1)
    first = jnp.sum(jnp.where(lane == routes[:, 0:1], logits, 0.0), axis=1, keepdims=True)
    second = jnp.sum(jnp.where(lane == routes[:, 1:2], logits, 0.0), axis=1, keepdims=True)
    gate0 = 1.0 / (1.0 + jnp.exp(second - first))
    gate1 = 1.0 / (1.0 + jnp.exp(first - second))
    owners = routes ^ me
    table = slot_map(owners, chunks, rows.shape[0] // chunks, experts)
    expert = iota(table.shape, 1) // (chunks * CAP)
    gates = table * jnp.where(owners[:, 0:1] == expert, gate0, gate1)
    high = gates.astype(BF16)
    low = (gates - high.astype(F32)).astype(BF16)
    return dot(high, returned) + dot(low, returned)


def attend_kernel(
    _, lengths_hbm, queries_hbm, keys_hbm, values_hbm, routes_hbm, residual_hbm, gain_hbm,
    stream_ref, payload_ref,
    lengths_ref, queries_ref, keys_ref, values_ref, routes_ref, residual_ref, gain_ref, sems,
):
    batch, window, _ = keys_ref.shape
    width = queries_ref.shape[1]
    span = width // KVH
    parts = [pl.ds(begin, PAIR * HS) for begin in range(0, KVH * HS, PAIR * HS)]
    small = [
        (lengths_hbm, lengths_ref), (queries_hbm, queries_ref), (routes_hbm, routes_ref),
        (residual_hbm, residual_ref), (gain_hbm, gain_ref),
    ]
    caches = [
        pair
        for part in parts
        for pair in (
            (keys_hbm.at[:, :, part], keys_ref.at[:, :, part]),
            (values_hbm.at[:, :, part], values_ref.at[:, 0:window, part]),
        )
    ]
    copies = [
        pltpu.make_async_copy(source, target, sems.at[i])
        for i, (source, target) in enumerate(small[:2] + caches + small[2:])
    ]
    for copy in copies:
        copy.start()
    padded = values_ref.shape[1]
    if padded > window:
        pad = (batch, padded - window, values_ref.shape[2])
        values_ref[:, window:, :] = jnp.zeros(pad, BF16)
    copies[0].wait()
    copies[1].wait()
    same = iota((batch, batch), 0) == iota((batch, batch), 1)

    def upright(row):
        return jnp.sum(jnp.where(same, row, 0), axis=1, keepdims=True)

    queries = queries_ref[...]
    lanes = PAIR * GROUP * batch
    full = -(-lanes // LANES) * LANES
    request = iota((window, full), 1) % batch
    length = jnp.zeros((1, full), jnp.int32)
    for r in range(batch):
        length = jnp.where(request[0:1] == r, lengths_ref[0:1, r : r + 1], length)
    visible = iota((window, full), 0) < length
    owner = iota((lanes, padded), 0) % batch
    attended = []
    for i, part in enumerate(parts):
        spread = []
        for k in range(PAIR):
            at = [(i * PAIR + k) * span + g * HS for g in range(GROUP)]
            stacked = jnp.concatenate([queries[:, c : c + HS] for c in at], axis=0)
            blank = jnp.zeros_like(stacked)
            spread.append(
                jnp.concatenate([stacked if j == k else blank for j in range(PAIR)], axis=1)
            )
        if full > lanes:
            spread.append(jnp.zeros((full - lanes, PAIR * HS), BF16))
        spread = jnp.concatenate(spread, axis=0)
        copies[2 + 2 * i].wait()
        keys = keys_ref[:, :, part].reshape(batch * window, PAIR * HS)
        products = dot(keys, spread, ((1,), (1,)))
        scores = products[:window]
        for r in range(1, batch):
            scores = jnp.where(request == r, products[r * window : (r + 1) * window], scores)
        scores = jnp.where(visible, scores * HS ** (-0.5), -1e30)
        powers = jnp.exp(scores - jnp.max(scores, axis=0, keepdims=True))
        weights = powers / jnp.sum(powers, axis=0, keepdims=True)
        if padded > window:
            weights = jnp.concatenate([weights, jnp.zeros((padded - window, full), F32)], axis=0)
        weights = weights.T[:lanes]
        weights = jnp.concatenate(
            [jnp.where(owner == r, weights, 0.0).astype(BF16) for r in range(batch)], axis=1
        )
        copies[3 + 2 * i].wait()
        values = values_ref[:, :, part].reshape(batch * padded, PAIR * HS)
        mixed = dot(weights, values)
        attended += [
            mixed[h * batch : (h + 1) * batch, h // GROUP * HS : (h // GROUP + 1) * HS]
            for h in range(PAIR * GROUP)
        ]
    for copy in copies[2 + 2 * len(parts) :]:
        copy.wait()
    stream = residual_ref[...].astype(F32) + jnp.concatenate(attended, axis=1)
    scale = lax.rsqrt(jnp.mean(stream * stream, axis=1, keepdims=True) + 1e-05)
    lane = iota((batch, LANES), 1)
    routes = [upright(routes_ref[k : k + 1, :]).astype(F32) for k in range(2)]
    named = jnp.where(lane == 0, routes[0], jnp.where(lane == 1, routes[1], 0.0))
    stream_ref[...] = stream
    payload_ref[:, :width] = (stream * scale * gain_ref[...]).astype(BF16)
    payload_ref[:, width:] = named.astype(BF16)


def pass_kernel(after_ref, value_ref, out_ref):
    pass


def pass_on(after, value):
    return pl.pallas_call(
        pass_kernel,
        in_specs=[ANY, ANY],
        out_specs=ANY,
        out_shape=jax.ShapeDtypeStruct(value.shape, value.dtype),
        input_output_aliases={1: 0},
        cost_estimate=LIGHT,
        compiler_params=params(0),
    )(after, value)


def split_kernel(me_ref, *refs, chunks, experts, after):
    refs = refs[after:]
    payload = jnp.concatenate([ref[...] for ref in refs[:chunks]], axis=0)
    outs = refs[chunks:]
    width = payload.shape[1] - LANES
    rows, named = payload[:, :width], payload[:, width:]
    slots = dispatch(me_ref[0], rows, named, chunks, experts)
    span, part = chunks * CAP, outs[0].shape[1]
    for i, ref in enumerate(outs):
        p, e = i // experts, i % experts
        ref[...] = slots[e * span : (e + 1) * span, p * part : (p + 1) * part].astype(BF16)


def strip_copies(source, begin, target, sems):
    strip = target.shape[1] // sems.shape[0]
    copies = [
        pltpu.make_async_copy(
            source.at[:, pl.ds(begin + c * strip, strip)],
            target.at[:, pl.ds(c * strip, strip)],
            sems.at[c],
        )
        for c in range(sems.shape[0])
    ]
    for copy in copies:
        copy.start()
    return copies


def begin_kernel(*refs, near, far):
    gate_ref, up_ref, down_hbm, gate_out, up_out, down_out, rows_ref, sems = refs[near + far :]
    half = rows_ref.shape[1]
    copies = strip_copies(down_hbm, 0, down_out, sems)
    blocks = [ref[:, :half] for ref in refs[:near]] + [ref[...] for ref in refs[near : near + far]]
    rows_ref[...] = jnp.concatenate([block.astype(F32) for block in blocks], axis=0).astype(BF16)
    units = gate_ref.shape[1]
    tile = min(256, units)

    @pl.loop(0, units // tile)
    def _(i):
        at = pl.ds(pl.multiple_of(i * tile, tile), tile)
        gate_out[:, at] = dot(rows_ref[...], gate_ref[:half, at])
        up_out[:, at] = dot(rows_ref[...], up_ref[:half, at])

    for copy in copies:
        copy.wait()


def end_kernel(*refs, near, far):
    gate_in, up_in, down_in, gate_ref, up_ref, down_hbm = refs[near + far : near + far + 6]
    outs = refs[near + far + 6 : -4]
    rows_ref, hidden_ref, down_ref, sems = refs[-4:]
    half = rows_ref.shape[1]
    width, units = gate_ref.shape
    copies = strip_copies(down_hbm, half, down_ref, sems)
    blocks = [ref[:, half:] for ref in refs[:near]] + [ref[...] for ref in refs[near : near + far]]
    rows_ref[...] = jnp.concatenate([block.astype(F32) for block in blocks], axis=0).astype(BF16)
    tile = min(256, units)

    @pl.loop(0, units // tile)
    def _(i):
        at = pl.ds(pl.multiple_of(i * tile, tile), tile)
        gate = gate_in[:, at] + dot(rows_ref[...], gate_ref[half:, at])
        up = up_in[:, at] + dot(rows_ref[...], up_ref[half:, at])
        hidden_ref[:, at] = (jax.nn.silu(gate) * up).astype(BF16)

    def down(source, begin, first, columns):
        @pl.loop(0, columns // tile)
        def _(i):
            at = pl.multiple_of(i * tile, tile)
            out = dot(hidden_ref[...], source[:, pl.ds(first + at, tile)])
            row = 0
            for ref in outs:
                count = ref.shape[0]
                ref[:, pl.ds(begin + first + at, tile)] = out[row : row + count].astype(BF16)
                row += count

    strip = half // len(copies)
    down(down_in, 0, 0, half)
    for c, copy in enumerate(copies):
        copy.wait()
        down(down_ref, half, c * strip, strip)


def mix_kernel(me_ref, router_ref, *refs, chunks, experts, after):
    refs = refs[after:]
    payload = jnp.concatenate([ref[...] for ref in refs[:chunks]], axis=0)
    order = farthest_first(experts)
    returned = jnp.concatenate(
        [refs[chunks + order.index(e)][...].astype(F32) for e in range(experts)], axis=0
    ).astype(BF16)
    added, outs = refs[chunks + experts : len(refs) - chunks], refs[len(refs) - chunks :]
    batch, width = outs[0].shape
    rows, named = payload[:, :width], payload[:, width:]
    mixed = combine(me_ref[0], rows, named, router_ref[...], returned, chunks, experts)
    for j, ref in enumerate(outs):
        part = mixed[j * batch : (j + 1) * batch]
        for other in added if j == 0 else []:
            part = part + other[...]
        ref[...] = part.astype(ref.dtype)


def mix(me, router, payloads, returned, added, after):
    chunks, experts = len(payloads), len(returned)
    width = returned[0].shape[1]
    batch = payloads[0].shape[0]
    returned = [swap(block, "expert", e) for e, block in zip(farthest_first(experts), returned)]
    operands = [me, router, *after, *payloads, *returned, *added]
    return pl.pallas_call(
        functools.partial(mix_kernel, chunks=chunks, experts=experts, after=len(after)),
        in_specs=[SCALAR, WHOLE] + [ANY] * len(after) + [WHOLE] * (len(operands) - 2 - len(after)),
        out_specs=[WHOLE] * chunks,
        out_shape=[
            jax.ShapeDtypeStruct((batch, width), F32 if added and j == 0 else BF16)
            for j in range(chunks)
        ],
        cost_estimate=LIGHT,
        compiler_params=params(experts * chunks * CAP * width),
    )(*operands)


def add_kernel(*refs):
    total = refs[0][...]
    for ref in refs[1:-1]:
        total = total + ref[...].astype(F32)
    refs[-1][...] = total.astype(BF16)


def in_hbm(value):
    return pltpu.with_memory_space_constraint(value, pltpu.HBM)


def swap(value, axis, step):
    if step == 0:
        return value
    count = lax.axis_size(axis)
    return lax.ppermute(value, axis, [(i, i ^ step) for i in range(count)])


def farthest_first(count):
    return [0, *range(count - 1, 0, -1)]


def params(elements):
    return pltpu.CompilerParams(vmem_limit_bytes=min(48 * MIB, 2 * MIB + 10 * elements))


def shards(
    queries,
    cached_keys,
    cached_values,
    lengths,
    routes,
    residual,
    norm_gain,
    router,
    gate_proj,
    up_proj,
    down_proj,
):
    batch, width = queries.shape
    experts = router.shape[1]
    layers = lax.axis_size("attn")
    me = lax.axis_index("expert").astype(jnp.int32).reshape(1)
    router = router.T
    shape = jax.ShapeDtypeStruct
    operands = [
        in_hbm(a)
        for a in (
            lengths[None], queries, cached_keys, cached_values, routes.T, residual, norm_gain[None]
        )
    ]
    window, depth = cached_values.shape[1:]
    held = [a.shape for a in operands]
    held[3] = (batch, -(-window // LANES) * LANES, depth)
    stream, payload = pl.pallas_call(
        attend_kernel,
        in_specs=[SCALAR] + [ANY] * len(operands),
        out_specs=[WHOLE, WHOLE],
        out_shape=[shape((batch, width), F32), shape((batch, width + LANES), BF16)],
        scratch_shapes=[pltpu.VMEM(size, a.dtype) for size, a in zip(held, operands)]
        + [pltpu.SemaphoreType.DMA((5 + 2 * (KVH // PAIR),))],
        compiler_params=params(28 * batch * width),
        cost_estimate=LIGHT,
    )(me, *operands)

    chunks = [swap(payload, "attn", j) if j < 2 or j % 2 == 0 else None for j in range(layers)]
    groups = [[0, 1], list(range(2, layers))]
    half = width // 2
    order = farthest_first(experts)

    def send(group, columns, after):
        count, parts = len(group), width // columns
        slots = pl.pallas_call(
            functools.partial(split_kernel, chunks=count, experts=experts, after=len(after)),
            in_specs=[SCALAR] + [ANY] * len(after) + [WHOLE] * count,
            out_specs=[WHOLE] * (parts * experts),
            out_shape=[shape((count * CAP, columns), BF16)] * (parts * experts),
            cost_estimate=LIGHT if after else BUSY,
            compiler_params=params(experts * count * CAP * width),
        )(me, *after, *[chunks[j] for j in group])
        return [
            swap(slots[p * experts + e], "expert", e) for p in range(parts) for e in order
        ]

    near = send(groups[0], width, [])
    for j in range(3, layers, 2):
        chunks[j] = swap(pass_on(near[1], chunks[j - 1]), "attn", 1)
    far = send(groups[1], half, near[1:2])
    total_rows = sum(block.shape[0] for block in near + far[:experts])
    units = gate_proj.shape[2]
    counts = {"near": experts, "far": experts}
    sums = pl.pallas_call(
        functools.partial(begin_kernel, **counts),
        in_specs=[WHOLE] * (2 * experts + 2) + [ANY],
        out_specs=[WHOLE] * 3,
        out_shape=[shape((total_rows, units), F32)] * 2 + [pltpu.VMEM((units, half), BF16)],
        scratch_shapes=[pltpu.VMEM((total_rows, half), BF16), pltpu.SemaphoreType.DMA((STRIPS,))],
        cost_estimate=pl.CostEstimate(
            flops=4 * total_rows * half * units, bytes_accessed=0, transcendentals=0
        ),
        compiler_params=params(total_rows * width),
    )(*near, *far[:experts], gate_proj[0], up_proj[0], in_hbm(down_proj[0]))
    results = pl.pallas_call(
        functools.partial(end_kernel, **counts),
        in_specs=[WHOLE] * (2 * experts + 5) + [ANY],
        out_specs=[WHOLE] * (2 * experts),
        out_shape=[shape((block.shape[0], width), BF16) for block in near + far[:experts]],
        scratch_shapes=[
            pltpu.VMEM((total_rows, half), BF16),
            pltpu.VMEM((total_rows, units), BF16),
            pltpu.VMEM((units, half), BF16),
            pltpu.SemaphoreType.DMA((STRIPS,)),
        ],
        compiler_params=params(total_rows * width + units * half // 5),
    )(*near, *far[experts:], *sums, gate_proj[0], up_proj[0], in_hbm(down_proj[0]))

    near, far = results[:experts], results[experts:]
    far = mix(me, router, [chunks[j] for j in groups[1]], far, [], [])
    base, first = mix(me, router, chunks[:2], near, [stream], far[:1])
    received = [swap(block, "attn", j + 1) for j, block in enumerate([first, *far])]
    return pl.pallas_call(
        add_kernel,
        in_specs=[WHOLE] * layers,
        out_specs=WHOLE,
        out_shape=shape((batch, width), BF16),
        cost_estimate=LIGHT,
        compiler_params=params(2 * layers * batch * width),
    )(base, *received)


def solution(mesh):
    in_specs = (
        P(("groups", "attn", "expert"), None),
        P(("groups", "attn", "expert"), None, None),
        P(("groups", "attn", "expert"), None, None),
        P(("groups", "attn", "expert")),
        P(("groups", "attn", "expert"), None),
        P(("groups", "attn", "expert"), None),
        P(),
        P(),
        P("expert", None, "attn"),
        P("expert", None, "attn"),
        P("expert", "attn", None),
    )
    out_specs = P(("groups", "attn", "expert"), None)
    return jax.shard_map(shards, mesh=mesh, in_specs=in_specs, out_specs=out_specs, check_vma=False)
```

```python
import functools

import jax
import jax.numpy as jnp
from jax import lax
from jax.experimental import pallas as pl
from jax.experimental.pallas import tpu as pltpu
from jax.sharding import PartitionSpec as P

HS = 128
KVH = 4
GROUP = 6
CAP = 8
LANES = 128
PAIR = 2
STRIPS = 3
TILE = 256
UNROLL = 2
MIB = 1 << 20
F32 = jnp.float32
BF16 = jnp.bfloat16
LIGHT = pl.CostEstimate(flops=0, bytes_accessed=0, transcendentals=0)
BUSY = pl.CostEstimate(flops=24 * 10**9, bytes_accessed=0, transcendentals=0)
ANY = pl.BlockSpec(memory_space=pl.ANY)
WHOLE = pl.BlockSpec(memory_space=pltpu.VMEM)
SCALAR = pl.BlockSpec(memory_space=pltpu.SMEM)


def dot(a, b, dims=((1,), (0,))):
    return lax.dot_general(a, b, (dims, ((), ())), preferred_element_type=F32)


def iota(shape, dim):
    return lax.broadcasted_iota(jnp.int32, shape, dim)


def slot_map(owners, chunks, batch, experts):
    rows, slots = chunks * batch, experts * chunks * CAP
    slot = iota((rows, slots), 1)
    row = iota((rows, slots), 0)
    expert = slot // (chunks * CAP)
    chunk = (slot // CAP) % chunks
    named = (owners[:, 0:1] == expert) | (owners[:, 1:2] == expert)
    named = named & (row // batch == chunk)
    named = jnp.where(named, 1.0, 0.0)
    left, right = iota((rows, rows), 0), iota((rows, rows), 1)
    before = jnp.where(right < left, 1.0, 0.0).astype(BF16)
    place = dot(before, named.astype(BF16))
    wanted = (slot % CAP).astype(F32)
    return jnp.where(place == wanted, named, 0.0)


def dispatch(me, rows, named, chunks, experts):
    owners = named[:, 0:2].astype(F32).astype(jnp.int32) ^ me
    table = slot_map(owners, chunks, rows.shape[0] // chunks, experts)
    return dot(table.astype(BF16), rows, ((0,), (0,)))


def combine(me, rows, named, router, returned, chunks, experts):
    routes = named[:, 0:2].astype(F32).astype(jnp.int32)
    logits = dot(rows, router, ((1,), (1,)))
    lane = iota(logits.shape, 1)
    first = jnp.sum(jnp.where(lane == routes[:, 0:1], logits, 0.0), axis=1, keepdims=True)
    second = jnp.sum(jnp.where(lane == routes[:, 1:2], logits, 0.0), axis=1, keepdims=True)
    gate0 = 1.0 / (1.0 + jnp.exp(second - first))
    gate1 = 1.0 / (1.0 + jnp.exp(first - second))
    owners = routes ^ me
    table = slot_map(owners, chunks, rows.shape[0] // chunks, experts)
    expert = iota(table.shape, 1) // (chunks * CAP)
    gates = table * jnp.where(owners[:, 0:1] == expert, gate0, gate1)
    high = gates.astype(BF16)
    low = (gates - high.astype(F32)).astype(BF16)
    return dot(high, returned) + dot(low, returned)


def attend_kernel(
    _, lengths_hbm, queries_hbm, keys_hbm, values_hbm, routes_hbm, residual_hbm, gain_hbm,
    stream_ref, payload_ref,
    lengths_ref, queries_ref, keys_ref, values_ref, routes_ref, residual_ref, gain_ref, sems,
):
    batch, window, _ = keys_ref.shape
    width = queries_ref.shape[1]
    span = width // KVH
    parts = [pl.ds(begin, PAIR * HS) for begin in range(0, KVH * HS, PAIR * HS)]
    small = [
        (lengths_hbm, lengths_ref), (queries_hbm, queries_ref), (routes_hbm, routes_ref),
        (residual_hbm, residual_ref), (gain_hbm, gain_ref),
    ]
    caches = [
        pair
        for part in parts
        for pair in (
            (keys_hbm.at[:, :, part], keys_ref.at[:, :, part]),
            (values_hbm.at[:, :, part], values_ref.at[:, 0:window, part]),
        )
    ]
    copies = [
        pltpu.make_async_copy(source, target, sems.at[i])
        for i, (source, target) in enumerate(small[:2] + caches + small[2:])
    ]
    for copy in copies:
        copy.start()
    padded = values_ref.shape[1]
    if padded > window:
        pad = (batch, padded - window, values_ref.shape[2])
        values_ref[:, window:, :] = jnp.zeros(pad, BF16)
    copies[0].wait()
    copies[1].wait()
    same = iota((batch, batch), 0) == iota((batch, batch), 1)

    def upright(row):
        return jnp.sum(jnp.where(same, row, 0), axis=1, keepdims=True)

    queries = queries_ref[...]
    lanes = PAIR * GROUP * batch
    full = -(-lanes // LANES) * LANES
    request = iota((window, full), 1) % batch
    length = jnp.zeros((1, full), jnp.int32)
    for r in range(batch):
        length = jnp.where(request[0:1] == r, lengths_ref[0:1, r : r + 1], length)
    visible = iota((window, full), 0) < length
    owner = iota((lanes, padded), 0) % batch
    attended = []
    for i, part in enumerate(parts):
        spread = []
        for k in range(PAIR):
            at = [(i * PAIR + k) * span + g * HS for g in range(GROUP)]
            stacked = jnp.concatenate([queries[:, c : c + HS] for c in at], axis=0)
            blank = jnp.zeros_like(stacked)
            spread.append(
                jnp.concatenate([stacked if j == k else blank for j in range(PAIR)], axis=1)
            )
        if full > lanes:
            spread.append(jnp.zeros((full - lanes, PAIR * HS), BF16))
        spread = jnp.concatenate(spread, axis=0)
        copies[2 + 2 * i].wait()
        keys = keys_ref[:, :, part].reshape(batch * window, PAIR * HS)
        products = dot(keys, spread, ((1,), (1,)))
        scores = products[:window]
        for r in range(1, batch):
            scores = jnp.where(request == r, products[r * window : (r + 1) * window], scores)
        scores = jnp.where(visible, scores * HS ** (-0.5), -1e30)
        powers = jnp.exp(scores - jnp.max(scores, axis=0, keepdims=True))
        weights = powers / jnp.sum(powers, axis=0, keepdims=True)
        if padded > window:
            weights = jnp.concatenate([weights, jnp.zeros((padded - window, full), F32)], axis=0)
        weights = weights.T[:lanes]
        weights = jnp.concatenate(
            [jnp.where(owner == r, weights, 0.0).astype(BF16) for r in range(batch)], axis=1
        )
        copies[3 + 2 * i].wait()
        values = values_ref[:, :, part].reshape(batch * padded, PAIR * HS)
        mixed = dot(weights, values)
        attended += [
            mixed[h * batch : (h + 1) * batch, h // GROUP * HS : (h // GROUP + 1) * HS]
            for h in range(PAIR * GROUP)
        ]
    for copy in copies[2 + 2 * len(parts) :]:
        copy.wait()
    stream = residual_ref[...].astype(F32) + jnp.concatenate(attended, axis=1)
    scale = lax.rsqrt(jnp.mean(stream * stream, axis=1, keepdims=True) + 1e-05)
    lane = iota((batch, LANES), 1)
    routes = [upright(routes_ref[k : k + 1, :]).astype(F32) for k in range(2)]
    named = jnp.where(lane == 0, routes[0], jnp.where(lane == 1, routes[1], 0.0))
    stream_ref[...] = stream
    payload_ref[:, :width] = (stream * scale * gain_ref[...]).astype(BF16)
    payload_ref[:, width:] = named.astype(BF16)


def split_kernel(me_ref, *refs, chunks, experts, after):
    refs = refs[after:]
    payload = jnp.concatenate([ref[...] for ref in refs[:chunks]], axis=0)
    outs = refs[chunks:]
    width = payload.shape[1] - LANES
    rows, named = payload[:, :width], payload[:, width:]
    slots = dispatch(me_ref[0], rows, named, chunks, experts)
    span, part = chunks * CAP, outs[0].shape[1]
    for i, ref in enumerate(outs):
        p, e = i // experts, i % experts
        ref[...] = slots[e * span : (e + 1) * span, p * part : (p + 1) * part].astype(BF16)


def strip_copies(source, begin, target, sems):
    strip = target.shape[1] // sems.shape[0]
    copies = [
        pltpu.make_async_copy(
            source.at[:, pl.ds(begin + c * strip, strip)],
            target.at[:, pl.ds(c * strip, strip)],
            sems.at[c],
        )
        for c in range(sems.shape[0])
    ]
    for copy in copies:
        copy.start()
    return copies


def load_rows(rows_ref, full, halves, begin):
    width = rows_ref.shape[1]
    blocks = [ref[:, begin : begin + width] for ref in full] + [ref[...] for ref in halves]
    rows_ref[...] = jnp.concatenate([block.astype(F32) for block in blocks], axis=0).astype(BF16)


def tiles(count, tile):
    def run(body):
        @pl.loop(0, count // tile, unroll=UNROLL)
        def _(i):
            body(pl.ds(pl.multiple_of(i * tile, tile), tile))

    return run


def store_rows(outs, at, value, near):
    count = outs[0].shape[0] - near
    for e, ref in enumerate(outs):
        first, second = e * near, len(outs) * near + e * count
        rows = [value[first : first + near], value[second : second + count]]
        ref[:, at] = jnp.concatenate(rows, axis=0).astype(BF16)


def begin_kernel(*refs, near, far):
    gate_ref, up_ref, down_hbm, gate_out, up_out, down_out, rows_ref, sems = refs[near + far :]
    half = rows_ref.shape[1]
    copies = strip_copies(down_hbm, 0, down_out, sems)
    load_rows(rows_ref, refs[:near], refs[near : near + far], 0)
    units = gate_ref.shape[1]

    @tiles(units, min(TILE, units))
    def _(at):
        gate_out[:, at] = dot(rows_ref[...], gate_ref[:half, at])
        up_out[:, at] = dot(rows_ref[...], up_ref[:half, at])

    for copy in copies:
        copy.wait()


def middle_kernel(*refs, near, far):
    gate_in, up_in, down_in, gate_ref, up_ref, down_hbm = refs[near + far : near + far + 6]
    outs = refs[near + far + 6 : -4]
    hidden_ref, down_out, rows_ref, sems = refs[-4:]
    half = rows_ref.shape[1]
    copies = strip_copies(down_hbm, half, down_out, sems)
    load_rows(rows_ref, refs[:near], refs[near : near + far], half)
    units = gate_ref.shape[1]

    @tiles(units, min(TILE, units))
    def _(at):
        gate = gate_in[:, at] + dot(rows_ref[...], gate_ref[half:, at])
        up = up_in[:, at] + dot(rows_ref[...], up_ref[half:, at])
        hidden_ref[:, at] = (jax.nn.silu(gate) * up).astype(BF16)

    @tiles(half, min(TILE, half))
    def _(at):
        store_rows(outs, at, dot(hidden_ref[...], down_in[:, at]), refs[0].shape[0])

    for copy in copies:
        copy.wait()


def end_kernel(hidden_ref, down_ref, *outs, near):
    half = down_ref.shape[1]

    @tiles(half, min(TILE, half))
    def _(at):
        store_rows(outs, at, dot(hidden_ref[...], down_ref[:, at]), near)


def mix_kernel(me_ref, router_ref, *refs, layers, columns):
    outs, stream_ref = refs[-layers:], refs[-layers - 1]
    blocks = refs[layers : -layers - 1]
    experts = len(blocks)
    order = farthest_first(experts)
    batch, width = stream_ref.shape
    payload = jnp.concatenate([ref[...] for ref in refs[:layers]], axis=0)
    returned = jnp.concatenate([blocks[order.index(e)][...] for e in range(experts)], axis=0)
    rows, named = payload[:, :width], payload[:, width:]
    mixed = combine(me_ref[0], rows, named, router_ref[...], returned, layers, experts)
    for j, ref in enumerate(outs):
        part = mixed[j * batch : (j + 1) * batch]
        if j == 0:
            part = part + stream_ref[:, columns]
        ref[...] = part.astype(ref.dtype)


def finish_kernel(*refs, parts):
    out_ref = refs[-1]
    span, count = out_ref.shape[1] // parts, len(refs[:-1]) // parts
    for p in range(parts):
        total = refs[p * count][...]
        for ref in refs[p * count + 1 : (p + 1) * count]:
            total = total + ref[...].astype(F32)
        out_ref[:, p * span : (p + 1) * span] = total.astype(BF16)


def in_hbm(value):
    return pltpu.with_memory_space_constraint(value, pltpu.HBM)


def swap(value, axis, step):
    if step == 0:
        return value
    count = lax.axis_size(axis)
    return lax.ppermute(value, axis, [(i, i ^ step) for i in range(count)])


def farthest_first(count):
    return [0, *range(count - 1, 0, -1)]


def params(elements):
    return pltpu.CompilerParams(vmem_limit_bytes=min(48 * MIB, 2 * MIB + 10 * elements))


def shards(
    queries,
    cached_keys,
    cached_values,
    lengths,
    routes,
    residual,
    norm_gain,
    router,
    gate_proj,
    up_proj,
    down_proj,
):
    batch, width = queries.shape
    experts = router.shape[1]
    layers = lax.axis_size("attn")
    me = lax.axis_index("expert").astype(jnp.int32).reshape(1)
    router = router.T
    shape = jax.ShapeDtypeStruct
    operands = [
        in_hbm(a)
        for a in (
            lengths[None], queries, cached_keys, cached_values, routes.T, residual, norm_gain[None]
        )
    ]
    window, depth = cached_values.shape[1:]
    held = [a.shape for a in operands]
    held[3] = (batch, -(-window // LANES) * LANES, depth)
    stream, payload = pl.pallas_call(
        attend_kernel,
        in_specs=[SCALAR] + [ANY] * len(operands),
        out_specs=[WHOLE, WHOLE],
        out_shape=[shape((batch, width), F32), shape((batch, width + LANES), BF16)],
        scratch_shapes=[pltpu.VMEM(size, a.dtype) for size, a in zip(held, operands)]
        + [pltpu.SemaphoreType.DMA((5 + 2 * (KVH // PAIR),))],
        compiler_params=params(28 * batch * width),
        cost_estimate=LIGHT,
    )(me, *operands)

    chunks = [swap(payload, "attn", j) for j in range(layers)]
    groups = [[0, 1], list(range(2, layers))]
    half = width // 2
    order = farthest_first(experts)

    def send(group, columns, after):
        count, parts = len(group), width // columns
        slots = pl.pallas_call(
            functools.partial(split_kernel, chunks=count, experts=experts, after=len(after)),
            in_specs=[SCALAR] + [ANY] * len(after) + [WHOLE] * count,
            out_specs=[WHOLE] * (parts * experts),
            out_shape=[shape((count * CAP, columns), BF16)] * (parts * experts),
            cost_estimate=LIGHT if after else BUSY,
            compiler_params=params(experts * count * CAP * width),
        )(me, *after, *[chunks[j] for j in group])
        return [
            swap(slots[p * experts + e], "expert", e) for p in range(parts) for e in order
        ]

    near = send(groups[0], width, [])
    far = send(groups[1], half, near[1:2])
    total_rows = sum(block.shape[0] for block in near + far[:experts])
    units = gate_proj.shape[2]
    counts = {"near": experts, "far": experts}
    sums = pl.pallas_call(
        functools.partial(begin_kernel, **counts),
        in_specs=[WHOLE] * (2 * experts + 2) + [ANY],
        out_specs=[WHOLE] * 3,
        out_shape=[shape((total_rows, units), F32)] * 2 + [pltpu.VMEM((units, half), BF16)],
        scratch_shapes=[pltpu.VMEM((total_rows, half), BF16), pltpu.SemaphoreType.DMA((STRIPS,))],
        cost_estimate=pl.CostEstimate(
            flops=4 * total_rows * half * units, bytes_accessed=0, transcendentals=0
        ),
        compiler_params=params(total_rows * width),
    )(*near, *far[:experts], gate_proj[0], up_proj[0], in_hbm(down_proj[0]))
    halves = [shape((layers * CAP, half), BF16)] * experts
    *first, hidden, down = pl.pallas_call(
        functools.partial(middle_kernel, **counts),
        in_specs=[WHOLE] * (2 * experts + 5) + [ANY],
        out_specs=[WHOLE] * (experts + 2),
        out_shape=halves + [shape((total_rows, units), BF16), pltpu.VMEM((units, half), BF16)],
        scratch_shapes=[pltpu.VMEM((total_rows, half), BF16), pltpu.SemaphoreType.DMA((STRIPS,))],
        compiler_params=params(total_rows * width),
    )(*near, *far[experts:], *sums, gate_proj[0], up_proj[0], in_hbm(down_proj[0]))
    second = pl.pallas_call(
        functools.partial(end_kernel, near=near[0].shape[0]),
        in_specs=[WHOLE] * 2,
        out_specs=[WHOLE] * experts,
        out_shape=halves,
        cost_estimate=pl.CostEstimate(
            flops=2 * total_rows * half * units, bytes_accessed=0, transcendentals=0
        ),
        compiler_params=params(total_rows * width),
    )(hidden, down)

    sums = []
    for p, blocks in enumerate((first, second)):
        returned = [swap(block, "expert", e) for e, block in zip(order, blocks)]
        operands = [me, router, *chunks, *returned, stream]
        mixed = pl.pallas_call(
            functools.partial(
                mix_kernel,
                layers=layers,
                columns=slice(p * half, (p + 1) * half),
            ),
            in_specs=[SCALAR] + [WHOLE] * (len(operands) - 1),
            out_specs=[WHOLE] * layers,
            out_shape=[shape((batch, half), BF16 if j else F32) for j in range(layers)],
            cost_estimate=LIGHT,
            compiler_params=params(experts * layers * CAP * half),
        )(*operands)
        sums += [swap(mixed[j], "attn", j) for j in farthest_first(layers)]
    return pl.pallas_call(
        functools.partial(finish_kernel, parts=2),
        in_specs=[WHOLE] * len(sums),
        out_specs=WHOLE,
        out_shape=shape((batch, width), BF16),
        cost_estimate=LIGHT,
        compiler_params=params(2 * layers * batch * width),
    )(*sums)


def solution(mesh):
    in_specs = (
        P(("groups", "attn", "expert"), None),
        P(("groups", "attn", "expert"), None, None),
        P(("groups", "attn", "expert"), None, None),
        P(("groups", "attn", "expert")),
        P(("groups", "attn", "expert"), None),
        P(("groups", "attn", "expert"), None),
        P(),
        P(),
        P("expert", None, "attn"),
        P("expert", None, "attn"),
        P("expert", "attn", None),
    )
    out_specs = P(("groups", "attn", "expert"), None)
    return jax.shard_map(shards, mesh=mesh, in_specs=in_specs, out_specs=out_specs, check_vma=False)
```

```python
import functools

import jax
import jax.numpy as jnp
from jax import lax
from jax.experimental import pallas as pl
from jax.experimental.pallas import tpu as pltpu
from jax.sharding import PartitionSpec as P

HS = 128
KVH = 4
GROUP = 6
CAP = 8
LANES = 128
PAIR = 2
STRIPS = 3
TILE = 256
UNROLL = 2
MIB = 1 << 20
F32 = jnp.float32
BF16 = jnp.bfloat16
LIGHT = pl.CostEstimate(flops=0, bytes_accessed=0, transcendentals=0)
BUSY = pl.CostEstimate(flops=24 * 10**9, bytes_accessed=0, transcendentals=0)
MID = pl.CostEstimate(flops=2 * 10**9, bytes_accessed=0, transcendentals=0)
ANY = pl.BlockSpec(memory_space=pl.ANY)
WHOLE = pl.BlockSpec(memory_space=pltpu.VMEM)
SCALAR = pl.BlockSpec(memory_space=pltpu.SMEM)


def dot(a, b, dims=((1,), (0,))):
    return lax.dot_general(a, b, (dims, ((), ())), preferred_element_type=F32)


def iota(shape, dim):
    return lax.broadcasted_iota(jnp.int32, shape, dim)


def slot_map(owners, chunks, batch, experts):
    rows, slots = chunks * batch, experts * chunks * CAP
    slot = iota((rows, slots), 1)
    row = iota((rows, slots), 0)
    expert = slot // (chunks * CAP)
    chunk = (slot // CAP) % chunks
    named = (owners[:, 0:1] == expert) | (owners[:, 1:2] == expert)
    named = named & (row // batch == chunk)
    named = jnp.where(named, 1.0, 0.0)
    left, right = iota((rows, rows), 0), iota((rows, rows), 1)
    before = jnp.where(right < left, 1.0, 0.0).astype(BF16)
    place = dot(before, named.astype(BF16))
    wanted = (slot % CAP).astype(F32)
    return jnp.where(place == wanted, named, 0.0)


def dispatch(me, rows, named, chunks, experts):
    owners = named[:, 0:2].astype(F32).astype(jnp.int32) ^ me
    table = slot_map(owners, chunks, rows.shape[0] // chunks, experts)
    return dot(table.astype(BF16), rows, ((0,), (0,)))


def combine(me, rows, named, router, returned, chunks, experts):
    routes = named[:, 0:2].astype(F32).astype(jnp.int32)
    logits = dot(rows, router, ((1,), (1,)))
    lane = iota(logits.shape, 1)
    first = jnp.sum(jnp.where(lane == routes[:, 0:1], logits, 0.0), axis=1, keepdims=True)
    second = jnp.sum(jnp.where(lane == routes[:, 1:2], logits, 0.0), axis=1, keepdims=True)
    gate0 = 1.0 / (1.0 + jnp.exp(second - first))
    gate1 = 1.0 / (1.0 + jnp.exp(first - second))
    owners = routes ^ me
    table = slot_map(owners, chunks, rows.shape[0] // chunks, experts)
    expert = iota(table.shape, 1) // (chunks * CAP)
    gates = table * jnp.where(owners[:, 0:1] == expert, gate0, gate1)
    high = gates.astype(BF16)
    low = (gates - high.astype(F32)).astype(BF16)
    return dot(high, returned) + dot(low, returned)


def attend_kernel(
    _, lengths_hbm, queries_hbm, keys_hbm, values_hbm, routes_hbm, residual_hbm, gain_hbm,
    stream_ref, first_ref, second_ref,
    lengths_ref, queries_ref, keys_ref, values_ref, routes_ref, residual_ref, gain_ref, sems,
):
    batch, window, _ = keys_ref.shape
    width = queries_ref.shape[1]
    span = width // KVH
    parts = [pl.ds(begin, PAIR * HS) for begin in range(0, KVH * HS, PAIR * HS)]
    small = [
        (lengths_hbm, lengths_ref), (queries_hbm, queries_ref), (routes_hbm, routes_ref),
        (residual_hbm, residual_ref), (gain_hbm, gain_ref),
    ]
    caches = [
        pair
        for part in parts
        for pair in (
            (keys_hbm.at[:, :, part], keys_ref.at[:, :, part]),
            (values_hbm.at[:, :, part], values_ref.at[:, 0:window, part]),
        )
    ]
    copies = [
        pltpu.make_async_copy(source, target, sems.at[i])
        for i, (source, target) in enumerate(small[:2] + caches + small[2:])
    ]
    for copy in copies:
        copy.start()
    padded = values_ref.shape[1]
    if padded > window:
        pad = (batch, padded - window, values_ref.shape[2])
        values_ref[:, window:, :] = jnp.zeros(pad, BF16)
    copies[0].wait()
    copies[1].wait()
    same = iota((batch, batch), 0) == iota((batch, batch), 1)

    def upright(row):
        return jnp.sum(jnp.where(same, row, 0), axis=1, keepdims=True)

    queries = queries_ref[...]
    lanes = PAIR * GROUP * batch
    full = -(-lanes // LANES) * LANES
    request = iota((window, full), 1) % batch
    length = jnp.zeros((1, full), jnp.int32)
    for r in range(batch):
        length = jnp.where(request[0:1] == r, lengths_ref[0:1, r : r + 1], length)
    visible = iota((window, full), 0) < length
    owner = iota((lanes, padded), 0) % batch
    attended = []
    for i, part in enumerate(parts):
        spread = []
        for k in range(PAIR):
            at = [(i * PAIR + k) * span + g * HS for g in range(GROUP)]
            stacked = jnp.concatenate([queries[:, c : c + HS] for c in at], axis=0)
            blank = jnp.zeros_like(stacked)
            spread.append(
                jnp.concatenate([stacked if j == k else blank for j in range(PAIR)], axis=1)
            )
        if full > lanes:
            spread.append(jnp.zeros((full - lanes, PAIR * HS), BF16))
        spread = jnp.concatenate(spread, axis=0)
        copies[2 + 2 * i].wait()
        keys = keys_ref[:, :, part].reshape(batch * window, PAIR * HS)
        products = dot(keys, spread, ((1,), (1,)))
        scores = products[:window]
        for r in range(1, batch):
            scores = jnp.where(request == r, products[r * window : (r + 1) * window], scores)
        scores = jnp.where(visible, scores * HS ** (-0.5), -1e30)
        powers = jnp.exp(scores - jnp.max(scores, axis=0, keepdims=True))
        weights = powers / jnp.sum(powers, axis=0, keepdims=True)
        if padded > window:
            weights = jnp.concatenate([weights, jnp.zeros((padded - window, full), F32)], axis=0)
        weights = weights.T[:lanes]
        weights = jnp.concatenate(
            [jnp.where(owner == r, weights, 0.0).astype(BF16) for r in range(batch)], axis=1
        )
        copies[3 + 2 * i].wait()
        values = values_ref[:, :, part].reshape(batch * padded, PAIR * HS)
        mixed = dot(weights, values)
        attended += [
            mixed[h * batch : (h + 1) * batch, h // GROUP * HS : (h // GROUP + 1) * HS]
            for h in range(PAIR * GROUP)
        ]
    for copy in copies[2 + 2 * len(parts) :]:
        copy.wait()
    stream = residual_ref[...].astype(F32) + jnp.concatenate(attended, axis=1)
    scale = lax.rsqrt(jnp.mean(stream * stream, axis=1, keepdims=True) + 1e-05)
    lane = iota((batch, LANES), 1)
    routes = [upright(routes_ref[k : k + 1, :]).astype(F32) for k in range(2)]
    named = jnp.where(lane == 0, routes[0], jnp.where(lane == 1, routes[1], 0.0))
    stream_ref[...] = stream
    half = width // 2
    normed = (stream * scale * gain_ref[...]).astype(BF16)
    first_ref[:, :half] = normed[:, :half]
    first_ref[:, half:] = named.astype(BF16)
    second_ref[...] = normed[:, half:]


def pass_kernel(*_):
    pass


def stack(refs):
    return jnp.concatenate([ref[...] for ref in refs], axis=0)


def split_kernel(me_ref, *refs, layers, part):
    payload = stack(refs[:layers])
    half = payload.shape[1] - LANES
    named = payload[:, half:]
    rows = stack(refs[layers : 2 * layers]) if part else payload[:, :half]
    outs = refs[(1 + part) * layers :]
    slots = dispatch(me_ref[0], rows, named, layers, len(outs))
    span = layers * CAP
    for e, ref in enumerate(outs):
        ref[...] = slots[e * span : (e + 1) * span].astype(BF16)


def strip_copies(source, begin, target, sems):
    strip = target.shape[1] // sems.shape[0]
    copies = [
        pltpu.make_async_copy(
            source.at[:, pl.ds(begin + c * strip, strip)],
            target.at[:, pl.ds(c * strip, strip)],
            sems.at[c],
        )
        for c in range(sems.shape[0])
    ]
    for copy in copies:
        copy.start()
    return copies


def tiles(count, tile):
    def run(body):
        @pl.loop(0, count // tile, unroll=UNROLL)
        def _(i):
            body(pl.ds(pl.multiple_of(i * tile, tile), tile))

    return run


def store_rows(outs, at, value):
    span = outs[0].shape[0]
    for e, ref in enumerate(outs):
        ref[:, at] = value[e * span : (e + 1) * span].astype(BF16)


def begin_kernel(*refs, experts):
    gate_ref, up_ref, down_hbm, gate_out, up_out, down_out, rows_ref, sems = refs[experts:]
    half = rows_ref.shape[1]
    copies = strip_copies(down_hbm, 0, down_out, sems)
    rows_ref[...] = stack(refs[:experts])
    units = gate_ref.shape[1]

    @tiles(units, min(TILE, units))
    def _(at):
        gate_out[:, at] = dot(rows_ref[...], gate_ref[:half, at])
        up_out[:, at] = dot(rows_ref[...], up_ref[:half, at])

    for copy in copies:
        copy.wait()


def middle_kernel(*refs, experts):
    gate_in, up_in, down_in, gate_ref, up_ref, down_hbm = refs[experts : experts + 6]
    outs = refs[experts + 6 : -4]
    hidden_ref, down_out, rows_ref, sems = refs[-4:]
    half = rows_ref.shape[1]
    copies = strip_copies(down_hbm, half, down_out, sems)
    rows_ref[...] = stack(refs[:experts])
    units = gate_ref.shape[1]

    @tiles(units, min(TILE, units))
    def _(at):
        gate = gate_in[:, at] + dot(rows_ref[...], gate_ref[half:, at])
        up = up_in[:, at] + dot(rows_ref[...], up_ref[half:, at])
        hidden_ref[:, at] = (jax.nn.silu(gate) * up).astype(BF16)

    @tiles(half, min(TILE, half))
    def _(at):
        store_rows(outs, at, dot(hidden_ref[...], down_in[:, at]))

    for copy in copies:
        copy.wait()


def end_kernel(hidden_ref, down_ref, *outs):
    half = down_ref.shape[1]

    @tiles(half, min(TILE, half))
    def _(at):
        store_rows(outs, at, dot(hidden_ref[...], down_ref[:, at]))


def mix_kernel(me_ref, router_ref, *refs, layers, part):
    outs, stream_ref = refs[-layers:], refs[-layers - 1]
    blocks = refs[2 * layers : -layers - 1]
    experts = len(blocks)
    order = farthest_first(experts)
    batch, half = outs[0].shape
    payload = stack(refs[:layers])
    named = payload[:, half:]
    rows = jnp.concatenate([payload[:, :half], stack(refs[layers : 2 * layers])], axis=1)
    returned = stack([blocks[order.index(e)] for e in range(experts)])
    mixed = combine(me_ref[0], rows, named, router_ref[...], returned, layers, experts)
    for j, ref in enumerate(outs):
        value = mixed[j * batch : (j + 1) * batch]
        if j == 0:
            value = value + stream_ref[:, part * half : (part + 1) * half]
        ref[...] = value.astype(ref.dtype)


def finish_kernel(*refs, parts):
    out_ref = refs[-1]
    span, count = out_ref.shape[1] // parts, len(refs[:-1]) // parts
    for p in range(parts):
        total = refs[p * count][...]
        for ref in refs[p * count + 1 : (p + 1) * count]:
            total = total + ref[...].astype(F32)
        out_ref[:, p * span : (p + 1) * span] = total.astype(BF16)


def in_hbm(value):
    return pltpu.with_memory_space_constraint(value, pltpu.HBM)


def swap(value, axis, step):
    if step == 0:
        return value
    count = lax.axis_size(axis)
    return lax.ppermute(value, axis, [(i, i ^ step) for i in range(count)])


def farthest_first(count):
    return [0, *range(count - 1, 0, -1)]


def params(elements):
    return pltpu.CompilerParams(vmem_limit_bytes=min(48 * MIB, 2 * MIB + 10 * elements))


def shards(
    queries,
    cached_keys,
    cached_values,
    lengths,
    routes,
    residual,
    norm_gain,
    router,
    gate_proj,
    up_proj,
    down_proj,
):
    batch, width = queries.shape
    experts = router.shape[1]
    layers = lax.axis_size("attn")
    me = lax.axis_index("expert").astype(jnp.int32).reshape(1)
    router = router.T
    shape = jax.ShapeDtypeStruct
    operands = [
        in_hbm(a)
        for a in (
            lengths[None], queries, cached_keys, cached_values, routes.T, residual, norm_gain[None]
        )
    ]
    window, depth = cached_values.shape[1:]
    held = [a.shape for a in operands]
    held[3] = (batch, -(-window // LANES) * LANES, depth)
    half = width // 2
    stream, *payload = pl.pallas_call(
        attend_kernel,
        in_specs=[SCALAR] + [ANY] * len(operands),
        out_specs=[WHOLE] * 3,
        out_shape=[
            shape((batch, width), F32), shape((batch, half + LANES), BF16), shape((batch, half), BF16)
        ],
        scratch_shapes=[pltpu.VMEM(size, a.dtype) for size, a in zip(held, operands)]
        + [pltpu.SemaphoreType.DMA((5 + 2 * (KVH // PAIR),))],
        compiler_params=params(28 * batch * width),
        cost_estimate=LIGHT,
    )(me, *operands)

    payload = pl.pallas_call(
        pass_kernel,
        in_specs=[ANY] * 2,
        out_specs=[ANY] * 2,
        out_shape=[shape(block.shape, BF16) for block in payload],
        input_output_aliases={0: 0, 1: 1},
        cost_estimate=BUSY,
        compiler_params=params(0),
    )(*payload)

    order = farthest_first(experts)
    chunks, arrived = [], []
    for part in range(2):
        came = {j: swap(payload[part], "attn", j) for j in farthest_first(layers)}
        chunks += [came[j] for j in range(layers)]
        slots = pl.pallas_call(
            functools.partial(split_kernel, layers=layers, part=part),
            in_specs=[SCALAR] + [WHOLE] * len(chunks),
            out_specs=[WHOLE] * experts,
            out_shape=[shape((layers * CAP, half), BF16)] * experts,
            cost_estimate=MID if part else LIGHT,
            compiler_params=params(experts * layers * CAP * half),
        )(me, *chunks)
        arrived.append([swap(slots[e], "expert", e) for e in order])

    total_rows = experts * layers * CAP
    units = gate_proj.shape[2]
    gate, up, down = gate_proj[0], up_proj[0], in_hbm(down_proj[0])
    rows = pltpu.VMEM((total_rows, half), BF16)
    strips = pltpu.SemaphoreType.DMA((STRIPS,))
    halves = [shape((layers * CAP, half), BF16)] * experts
    *sums, down_first = pl.pallas_call(
        functools.partial(begin_kernel, experts=experts),
        in_specs=[WHOLE] * (experts + 2) + [ANY],
        out_specs=[WHOLE] * 3,
        out_shape=[shape((total_rows, units), F32)] * 2 + [pltpu.VMEM((units, half), BF16)],
        scratch_shapes=[rows, strips],
        cost_estimate=pl.CostEstimate(
            flops=4 * total_rows * half * units, bytes_accessed=0, transcendentals=0
        ),
        compiler_params=params(total_rows * width),
    )(*arrived[0], gate, up, down)
    *first, hidden, down_second = pl.pallas_call(
        functools.partial(middle_kernel, experts=experts),
        in_specs=[WHOLE] * (experts + 5) + [ANY],
        out_specs=[WHOLE] * (experts + 2),
        out_shape=halves + [shape((total_rows, units), BF16), pltpu.VMEM((units, half), BF16)],
        scratch_shapes=[rows, strips],
        compiler_params=params(total_rows * width),
    )(*arrived[1], *sums, down_first, gate, up, down)
    second = pl.pallas_call(
        end_kernel,
        in_specs=[WHOLE] * 2,
        out_specs=[WHOLE] * experts,
        out_shape=halves,
        cost_estimate=pl.CostEstimate(
            flops=2 * total_rows * half * units, bytes_accessed=0, transcendentals=0
        ),
        compiler_params=params(total_rows * width),
    )(hidden, down_second)

    sums = []
    for part, blocks in enumerate((first, second)):
        returned = [swap(block, "expert", e) for e, block in zip(order, blocks)]
        mixed = pl.pallas_call(
            functools.partial(mix_kernel, layers=layers, part=part),
            in_specs=[SCALAR] + [WHOLE] * (2 + 2 * layers + experts),
            out_specs=[WHOLE] * layers,
            out_shape=[shape((batch, half), BF16 if j else F32) for j in range(layers)],
            cost_estimate=LIGHT,
            compiler_params=params(experts * layers * CAP * half),
        )(me, router, *chunks, *returned, stream)
        sums += [swap(mixed[j], "attn", j) for j in farthest_first(layers)]
    return pl.pallas_call(
        functools.partial(finish_kernel, parts=2),
        in_specs=[WHOLE] * len(sums),
        out_specs=WHOLE,
        out_shape=shape((batch, width), BF16),
        cost_estimate=LIGHT,
        compiler_params=params(2 * layers * batch * width),
    )(*sums)


def solution(mesh):
    in_specs = (
        P(("groups", "attn", "expert"), None),
        P(("groups", "attn", "expert"), None, None),
        P(("groups", "attn", "expert"), None, None),
        P(("groups", "attn", "expert")),
        P(("groups", "attn", "expert"), None),
        P(("groups", "attn", "expert"), None),
        P(),
        P(),
        P("expert", None, "attn"),
        P("expert", None, "attn"),
        P("expert", "attn", None),
    )
    out_specs = P(("groups", "attn", "expert"), None)
    return jax.shard_map(shards, mesh=mesh, in_specs=in_specs, out_specs=out_specs, check_vma=False)
```

```python
import functools

import jax
import jax.numpy as jnp
from jax import lax
from jax.experimental import pallas as pl
from jax.experimental.pallas import tpu as pltpu
from jax.sharding import PartitionSpec as P

HS = 128
KVH = 4
GROUP = 6
CAP = 8
LANES = 128
PAIR = 2
BLOCK = 4
STRIPS = 3
TILE = 256
UNROLL = 2
MIB = 1 << 20
F32 = jnp.float32
BF16 = jnp.bfloat16
LIGHT = pl.CostEstimate(flops=0, bytes_accessed=0, transcendentals=0)
BUSY = pl.CostEstimate(flops=24 * 10**9, bytes_accessed=0, transcendentals=0)
MID = pl.CostEstimate(flops=2 * 10**9, bytes_accessed=0, transcendentals=0)
ANY = pl.BlockSpec(memory_space=pl.ANY)
WHOLE = pl.BlockSpec(memory_space=pltpu.VMEM)
SCALAR = pl.BlockSpec(memory_space=pltpu.SMEM)


def dot(a, b, dims=((1,), (0,))):
    return lax.dot_general(a, b, (dims, ((), ())), preferred_element_type=F32)


def iota(shape, dim):
    return lax.broadcasted_iota(jnp.int32, shape, dim)


def slot_map(owners, chunks, batch, experts):
    rows, slots = chunks * batch, experts * chunks * CAP
    slot = iota((rows, slots), 1)
    row = iota((rows, slots), 0)
    expert = slot // (chunks * CAP)
    chunk = (slot // CAP) % chunks
    named = (owners[:, 0:1] == expert) | (owners[:, 1:2] == expert)
    named = named & (row // batch == chunk)
    named = jnp.where(named, 1.0, 0.0)
    left, right = iota((rows, rows), 0), iota((rows, rows), 1)
    before = jnp.where(right < left, 1.0, 0.0).astype(BF16)
    place = dot(before, named.astype(BF16))
    wanted = (slot % CAP).astype(F32)
    return jnp.where(place == wanted, named, 0.0)


def dispatch(me, rows, named, chunks, experts):
    owners = named[:, 0:2].astype(F32).astype(jnp.int32) ^ me
    table = slot_map(owners, chunks, rows.shape[0] // chunks, experts)
    return dot(table.astype(BF16), rows, ((0,), (0,)))


def weigh_kernel(me_ref, router_ref, *refs, layers):
    high_ref, low_ref = refs[-2:]
    rows, named = gather(refs[:-2], layers)
    routes = named[:, 0:2].astype(F32).astype(jnp.int32)
    logits = dot(rows, router_ref[...], ((1,), (1,)))
    experts = logits.shape[1]
    lane = iota(logits.shape, 1)
    first = jnp.sum(jnp.where(lane == routes[:, 0:1], logits, 0.0), axis=1, keepdims=True)
    second = jnp.sum(jnp.where(lane == routes[:, 1:2], logits, 0.0), axis=1, keepdims=True)
    gate0 = 1.0 / (1.0 + jnp.exp(second - first))
    gate1 = 1.0 / (1.0 + jnp.exp(first - second))
    owners = routes ^ me_ref[0]
    table = slot_map(owners, layers, rows.shape[0] // layers, experts)
    expert = iota(table.shape, 1) // (layers * CAP)
    gates = table * jnp.where(owners[:, 0:1] == expert, gate0, gate1)
    high = gates.astype(BF16)
    high_ref[...] = high
    low_ref[...] = (gates - high.astype(F32)).astype(BF16)


def attend_kernel(
    _, lengths_hbm, queries_hbm, keys_hbm, values_hbm, routes_hbm, residual_hbm, gain_hbm,
    stream_ref, first_ref, second_ref, whole_ref,
    lengths_ref, queries_ref, keys_ref, values_ref, routes_ref, residual_ref, gain_ref, sems,
):
    batch, window, _ = keys_ref.shape
    width = queries_ref.shape[1]
    span = width // KVH
    parts = [pl.ds(begin, PAIR * HS) for begin in range(0, KVH * HS, PAIR * HS)]
    small = [
        (lengths_hbm, lengths_ref), (queries_hbm, queries_ref), (routes_hbm, routes_ref),
        (residual_hbm, residual_ref), (gain_hbm, gain_ref),
    ]
    blocks = [pl.ds(begin, BLOCK) for begin in range(0, batch, BLOCK)]
    groups = [
        small[:2],
        [(keys_hbm.at[block], keys_ref.at[block]) for block in blocks],
        [(values_hbm.at[block], values_ref.at[block, 0:window]) for block in blocks],
        small[2:],
    ]
    at, copies = 0, []
    for group in groups:
        copies.append([])
        for source, target in group:
            copies[-1].append(pltpu.make_async_copy(source, target, sems.at[at]))
            copies[-1][-1].start()
            at += 1

    def wait(group):
        for copy in copies[group]:
            copy.wait()

    padded = values_ref.shape[1]
    if padded > window:
        pad = (batch, padded - window, values_ref.shape[2])
        values_ref[:, window:, :] = jnp.zeros(pad, BF16)
    wait(0)
    same = iota((batch, batch), 0) == iota((batch, batch), 1)

    def upright(row):
        return jnp.sum(jnp.where(same, row, 0), axis=1, keepdims=True)

    queries = queries_ref[...]
    lanes = PAIR * GROUP * batch
    full = -(-lanes // LANES) * LANES
    request = iota((window, full), 1) % batch
    length = jnp.zeros((1, full), jnp.int32)
    for r in range(batch):
        length = jnp.where(request[0:1] == r, lengths_ref[0:1, r : r + 1], length)
    visible = iota((window, full), 0) < length
    owner = iota((lanes, padded), 0) % batch
    attended = []
    for i, part in enumerate(parts):
        spread = []
        for k in range(PAIR):
            at = [(i * PAIR + k) * span + g * HS for g in range(GROUP)]
            stacked = jnp.concatenate([queries[:, c : c + HS] for c in at], axis=0)
            blank = jnp.zeros_like(stacked)
            spread.append(
                jnp.concatenate([stacked if j == k else blank for j in range(PAIR)], axis=1)
            )
        if full > lanes:
            spread.append(jnp.zeros((full - lanes, PAIR * HS), BF16))
        spread = jnp.concatenate(spread, axis=0)
        if i == 0:
            wait(1)
        keys = keys_ref[:, :, part].reshape(batch * window, PAIR * HS)
        products = dot(keys, spread, ((1,), (1,)))
        scores = products[:window]
        for r in range(1, batch):
            scores = jnp.where(request == r, products[r * window : (r + 1) * window], scores)
        scores = jnp.where(visible, scores * HS ** (-0.5), -1e30)
        powers = jnp.exp(scores - jnp.max(scores, axis=0, keepdims=True))
        weights = powers / jnp.sum(powers, axis=0, keepdims=True)
        if padded > window:
            weights = jnp.concatenate([weights, jnp.zeros((padded - window, full), F32)], axis=0)
        weights = weights.T[:lanes]
        weights = jnp.concatenate(
            [jnp.where(owner == r, weights, 0.0).astype(BF16) for r in range(batch)], axis=1
        )
        if i == 0:
            wait(2)
        values = values_ref[:, :, part].reshape(batch * padded, PAIR * HS)
        mixed = dot(weights, values)
        attended += [
            mixed[h * batch : (h + 1) * batch, h // GROUP * HS : (h // GROUP + 1) * HS]
            for h in range(PAIR * GROUP)
        ]
    wait(3)
    stream = residual_ref[...].astype(F32) + jnp.concatenate(attended, axis=1)
    scale = lax.rsqrt(jnp.mean(stream * stream, axis=1, keepdims=True) + 1e-05)
    lane = iota((batch, LANES), 1)
    routes = [upright(routes_ref[k : k + 1, :]).astype(F32) for k in range(2)]
    named = jnp.where(lane == 0, routes[0], jnp.where(lane == 1, routes[1], 0.0))
    stream_ref[...] = stream
    half = width // 2
    normed = (stream * scale * gain_ref[...]).astype(BF16)
    first_ref[:, :half] = normed[:, :half]
    first_ref[:, half:] = named.astype(BF16)
    second_ref[...] = normed[:, half:]
    whole_ref[:, :width] = normed
    whole_ref[:, width:] = named.astype(BF16)


def pass_kernel(*_):
    pass


def stack(refs):
    return jnp.concatenate([ref[...] for ref in refs], axis=0)


def first_half(refs):
    half = refs[0].shape[1] - LANES
    blocks = [ref[...] for ref in refs]
    rows = [block[:, :half] for block in blocks]
    named = [block[:, block.shape[1] - LANES :] for block in blocks]
    return jnp.concatenate(rows, axis=0), jnp.concatenate(named, axis=0)


def second_half(refs, neighbour):
    half = refs[0].shape[1]
    blocks = [refs[0][...], neighbour[:, half : 2 * half], *[ref[...] for ref in refs[1:]]]
    return jnp.concatenate(blocks, axis=0)


def gather(refs, layers):
    rows, named = first_half(refs[:layers])
    return jnp.concatenate([rows, second_half(refs[layers:], refs[1])], axis=1), named


def split_kernel(me_ref, *refs, layers, part):
    rows, named = first_half(refs[:layers])
    outs = refs[layers:]
    if part:
        rows, outs = second_half(refs[layers : 2 * layers - 1], refs[1]), refs[2 * layers - 1 :]
    slots = dispatch(me_ref[0], rows, named, layers, len(outs))
    span = layers * CAP
    for e, ref in enumerate(outs):
        ref[...] = slots[e * span : (e + 1) * span].astype(BF16)


def strip_copies(source, begin, target, sems):
    strip = target.shape[1] // sems.shape[0]
    copies = [
        pltpu.make_async_copy(
            source.at[:, pl.ds(begin + c * strip, strip)],
            target.at[:, pl.ds(c * strip, strip)],
            sems.at[c],
        )
        for c in range(sems.shape[0])
    ]
    for copy in copies:
        copy.start()
    return copies


def tiles(count, tile):
    def run(body):
        @pl.loop(0, count // tile, unroll=UNROLL)
        def _(i):
            body(pl.ds(pl.multiple_of(i * tile, tile), tile))

    return run


def store_rows(outs, at, value):
    span = outs[0].shape[0]
    for e, ref in enumerate(outs):
        ref[:, at] = value[e * span : (e + 1) * span].astype(BF16)


def begin_kernel(*refs, experts):
    _, gate_ref, up_ref, down_hbm, gate_out, up_out, down_out, rows_ref, sems = refs[experts:]
    half = rows_ref.shape[1]
    copies = strip_copies(down_hbm, 0, down_out, sems)
    rows_ref[...] = stack(refs[:experts])
    units = gate_ref.shape[1]

    @tiles(units, min(TILE, units))
    def _(at):
        gate_out[:, at] = dot(rows_ref[...], gate_ref[:half, at])
        up_out[:, at] = dot(rows_ref[...], up_ref[:half, at])

    for copy in copies:
        copy.wait()


def middle_kernel(*refs, experts):
    gate_in, up_in, down_in, gate_ref, up_ref, down_hbm = refs[experts : experts + 6]
    outs = refs[experts + 6 : -4]
    hidden_ref, down_out, rows_ref, sems = refs[-4:]
    half = rows_ref.shape[1]
    copies = strip_copies(down_hbm, half, down_out, sems)
    rows_ref[...] = stack(refs[:experts])
    units = gate_ref.shape[1]

    @tiles(units, min(TILE, units))
    def _(at):
        gate = gate_in[:, at] + dot(rows_ref[...], gate_ref[half:, at])
        up = up_in[:, at] + dot(rows_ref[...], up_ref[half:, at])
        hidden_ref[:, at] = (jax.nn.silu(gate) * up).astype(BF16)

    @tiles(half, min(TILE, half))
    def _(at):
        store_rows(outs, at, dot(hidden_ref[...], down_in[:, at]))

    for copy in copies:
        copy.wait()


def end_kernel(hidden_ref, down_ref, *outs):
    half = down_ref.shape[1]

    @tiles(half, min(TILE, half))
    def _(at):
        store_rows(outs, at, dot(hidden_ref[...], down_ref[:, at]))


def mix_kernel(high_ref, low_ref, *refs, layers, part):
    outs, stream_ref = refs[-layers:], refs[-layers - 1]
    blocks = refs[: -layers - 1]
    order = farthest_first(len(blocks))
    returned = stack([blocks[order.index(e)] for e in range(len(blocks))])
    mixed = dot(high_ref[...], returned) + dot(low_ref[...], returned)
    batch, half = outs[0].shape
    for j, ref in enumerate(outs):
        value = mixed[j * batch : (j + 1) * batch]
        if j == 0:
            value = value + stream_ref[:, part * half : (part + 1) * half]
        ref[...] = value.astype(ref.dtype)


def add_kernel(*refs):
    out_ref = refs[-1]
    span = refs[-2].shape[1]
    if out_ref.shape[1] > span:
        out_ref[:, :span] = refs[0][...]
        refs = refs[1:]
    total = refs[0][...]
    for ref in refs[1:-1]:
        total = total + ref[...].astype(F32)
    out_ref[:, out_ref.shape[1] - span :] = total.astype(BF16)


def in_hbm(value):
    return pltpu.with_memory_space_constraint(value, pltpu.HBM)


def swap(value, axis, step):
    if step == 0:
        return value
    count = lax.axis_size(axis)
    return lax.ppermute(value, axis, [(i, i ^ step) for i in range(count)])


def farthest_first(count):
    return [0, *range(count - 1, 0, -1)]


def params(elements):
    return pltpu.CompilerParams(vmem_limit_bytes=min(48 * MIB, 2 * MIB + 10 * elements))


def shards(
    queries,
    cached_keys,
    cached_values,
    lengths,
    routes,
    residual,
    norm_gain,
    router,
    gate_proj,
    up_proj,
    down_proj,
):
    batch, width = queries.shape
    experts = router.shape[1]
    layers = lax.axis_size("attn")
    me = lax.axis_index("expert").astype(jnp.int32).reshape(1)
    router = router.T
    shape = jax.ShapeDtypeStruct
    operands = [
        in_hbm(a)
        for a in (
            lengths[None], queries, cached_keys, cached_values, routes.T, residual, norm_gain[None]
        )
    ]
    window, depth = cached_values.shape[1:]
    held = [a.shape for a in operands]
    held[3] = (batch, -(-window // LANES) * LANES, depth)
    half = width // 2
    stream, *payload = pl.pallas_call(
        attend_kernel,
        in_specs=[SCALAR] + [ANY] * len(operands),
        out_specs=[WHOLE] * 4,
        out_shape=[shape((batch, width), F32)]
        + [shape((batch, size), BF16) for size in (half + LANES, half, width + LANES)],
        scratch_shapes=[pltpu.VMEM(size, a.dtype) for size, a in zip(held, operands)]
        + [pltpu.SemaphoreType.DMA((5 + 2 * (batch // BLOCK),))],
        compiler_params=params(28 * batch * width),
        cost_estimate=LIGHT,
    )(me, *operands)

    payload = pl.pallas_call(
        pass_kernel,
        in_specs=[ANY] * 3,
        out_specs=[ANY] * 3,
        out_shape=[shape(block.shape, BF16) for block in payload],
        input_output_aliases={i: i for i in range(3)},
        cost_estimate=BUSY,
        compiler_params=params(0),
    )(*payload)

    order = farthest_first(experts)
    chunks, arrived = [], []
    for part in range(2):
        came = {0: payload[part]}
        for j in farthest_first(layers)[1:]:
            if j != 1 or part == 0:
                came[j] = swap(payload[2 if j == 1 else part], "attn", j)
        chunks += [came[j] for j in sorted(came)]
        slots = pl.pallas_call(
            functools.partial(split_kernel, layers=layers, part=part),
            in_specs=[SCALAR] + [WHOLE] * len(chunks),
            out_specs=[WHOLE] * experts,
            out_shape=[shape((layers * CAP, half), BF16)] * experts,
            cost_estimate=MID if part else LIGHT,
            compiler_params=params(experts * layers * CAP * half),
        )(me, *chunks)
        arrived.append([swap(slots[e], "expert", e) for e in order])
    gates = pl.pallas_call(
        functools.partial(weigh_kernel, layers=layers),
        in_specs=[SCALAR] + [WHOLE] * (1 + len(chunks)),
        out_specs=[WHOLE] * 2,
        out_shape=[shape((layers * batch, experts * layers * CAP), BF16)] * 2,
        cost_estimate=LIGHT,
        compiler_params=params(layers * batch * width),
    )(me, router, *chunks)

    total_rows = experts * layers * CAP
    units = gate_proj.shape[2]
    gate, up, down = gate_proj[0], up_proj[0], in_hbm(down_proj[0])
    rows = pltpu.VMEM((total_rows, half), BF16)
    strips = pltpu.SemaphoreType.DMA((STRIPS,))
    halves = [shape((layers * CAP, half), BF16)] * experts
    *sums, down_first = pl.pallas_call(
        functools.partial(begin_kernel, experts=experts),
        in_specs=[WHOLE] * experts + [ANY] + [WHOLE] * 2 + [ANY],
        out_specs=[WHOLE] * 3,
        out_shape=[shape((total_rows, units), F32)] * 2 + [pltpu.VMEM((units, half), BF16)],
        scratch_shapes=[rows, strips],
        cost_estimate=pl.CostEstimate(
            flops=4 * total_rows * half * units, bytes_accessed=0, transcendentals=0
        ),
        compiler_params=params(total_rows * width),
    )(*arrived[0], gates[0], gate, up, down)
    *first, hidden, down_second = pl.pallas_call(
        functools.partial(middle_kernel, experts=experts),
        in_specs=[WHOLE] * (experts + 5) + [ANY],
        out_specs=[WHOLE] * (experts + 2),
        out_shape=halves + [shape((total_rows, units), BF16), pltpu.VMEM((units, half), BF16)],
        scratch_shapes=[rows, strips],
        compiler_params=params(total_rows * width),
    )(*arrived[1], *sums, down_first, gate, up, down)
    second = pl.pallas_call(
        end_kernel,
        in_specs=[WHOLE] * 2,
        out_specs=[WHOLE] * experts,
        out_shape=halves,
        cost_estimate=pl.CostEstimate(
            flops=2 * total_rows * half * units, bytes_accessed=0, transcendentals=0
        ),
        compiler_params=params(total_rows * width),
    )(hidden, down_second)

    done = []
    for part, blocks in enumerate((first, second)):
        returned = [swap(block, "expert", e) for e, block in zip(order, blocks)]
        mixed = pl.pallas_call(
            functools.partial(mix_kernel, layers=layers, part=part),
            in_specs=[WHOLE] * (3 + experts),
            out_specs=[WHOLE] * layers,
            out_shape=[shape((batch, half), BF16 if j else F32) for j in range(layers)],
            cost_estimate=LIGHT,
            compiler_params=params(experts * layers * CAP * half),
        )(*gates, *returned, stream)
        sums = [swap(mixed[j], "attn", j) for j in farthest_first(layers)]
        done = [
            pl.pallas_call(
                add_kernel,
                in_specs=[WHOLE] * (layers + len(done)),
                out_specs=WHOLE,
                out_shape=shape((batch, width if part else half), BF16),
                cost_estimate=LIGHT,
                compiler_params=params(layers * batch * width),
            )(*done, *sums)
        ]
    return done[0]


def solution(mesh):
    in_specs = (
        P(("groups", "attn", "expert"), None),
        P(("groups", "attn", "expert"), None, None),
        P(("groups", "attn", "expert"), None, None),
        P(("groups", "attn", "expert")),
        P(("groups", "attn", "expert"), None),
        P(("groups", "attn", "expert"), None),
        P(),
        P(),
        P("expert", None, "attn"),
        P("expert", None, "attn"),
        P("expert", "attn", None),
    )
    out_specs = P(("groups", "attn", "expert"), None)
    return jax.shard_map(shards, mesh=mesh, in_specs=in_specs, out_specs=out_specs, check_vma=False)
```

```python
import functools

import jax
import jax.numpy as jnp
from jax import lax
from jax.experimental import pallas as pl
from jax.experimental.pallas import tpu as pltpu
from jax.sharding import PartitionSpec as P

HS = 128
KVH = 4
GROUP = 6
CAP = 8
LANES = 128
PAIR = 2
BLOCK = 4
STRIPS = 3
TILE = 256
UNROLL = 2
MIB = 1 << 20
F32 = jnp.float32
BF16 = jnp.bfloat16
LIGHT = pl.CostEstimate(flops=0, bytes_accessed=0, transcendentals=0)
BUSY = pl.CostEstimate(flops=24 * 10**9, bytes_accessed=0, transcendentals=0)
MID = pl.CostEstimate(flops=2 * 10**9, bytes_accessed=0, transcendentals=0)
ANY = pl.BlockSpec(memory_space=pl.ANY)
WHOLE = pl.BlockSpec(memory_space=pltpu.VMEM)
SCALAR = pl.BlockSpec(memory_space=pltpu.SMEM)


def dot(a, b, dims=((1,), (0,))):
    return lax.dot_general(a, b, (dims, ((), ())), preferred_element_type=F32)


def iota(shape, dim):
    return lax.broadcasted_iota(jnp.int32, shape, dim)


def slot_map(owners, chunks, batch, experts):
    rows, slots = chunks * batch, experts * chunks * CAP
    slot = iota((rows, slots), 1)
    row = iota((rows, slots), 0)
    expert = slot // (chunks * CAP)
    chunk = (slot // CAP) % chunks
    named = (owners[:, 0:1] == expert) | (owners[:, 1:2] == expert)
    named = named & (row // batch == chunk)
    named = jnp.where(named, 1.0, 0.0)
    left, right = iota((rows, rows), 0), iota((rows, rows), 1)
    before = jnp.where(right < left, 1.0, 0.0).astype(BF16)
    place = dot(before, named.astype(BF16))
    wanted = (slot % CAP).astype(F32)
    return jnp.where(place == wanted, named, 0.0)


def dispatch(me, rows, named, chunks, experts):
    owners = named[:, 0:2].astype(F32).astype(jnp.int32) ^ me
    table = slot_map(owners, chunks, rows.shape[0] // chunks, experts)
    return dot(table.astype(BF16), rows, ((0,), (0,)))


def weigh_kernel(me_ref, router_ref, *refs, layers):
    high_ref, low_ref = refs[-2:]
    parts, named = gather(refs[:-2], layers)
    rows = jnp.concatenate(parts, axis=1)
    routes = named[:, 0:2].astype(F32).astype(jnp.int32)
    logits = dot(rows, router_ref[...], ((1,), (1,)))
    experts = logits.shape[1]
    lane = iota(logits.shape, 1)
    first = jnp.sum(jnp.where(lane == routes[:, 0:1], logits, 0.0), axis=1, keepdims=True)
    second = jnp.sum(jnp.where(lane == routes[:, 1:2], logits, 0.0), axis=1, keepdims=True)
    gate0 = 1.0 / (1.0 + jnp.exp(second - first))
    gate1 = 1.0 / (1.0 + jnp.exp(first - second))
    owners = routes ^ me_ref[0]
    table = slot_map(owners, layers, rows.shape[0] // layers, experts)
    expert = iota(table.shape, 1) // (layers * CAP)
    gates = table * jnp.where(owners[:, 0:1] == expert, gate0, gate1)
    high = gates.astype(BF16)
    high_ref[...] = high
    low_ref[...] = (gates - high.astype(F32)).astype(BF16)


def attend_kernel(
    _, lengths_hbm, queries_hbm, keys_hbm, values_hbm, routes_hbm, residual_hbm, gain_hbm,
    stream_ref, first_ref, second_ref,
    lengths_ref, queries_ref, keys_ref, values_ref, routes_ref, residual_ref, gain_ref, sems,
):
    batch, window, _ = keys_ref.shape
    width = queries_ref.shape[1]
    span = width // KVH
    parts = [pl.ds(begin, PAIR * HS) for begin in range(0, KVH * HS, PAIR * HS)]
    small = [
        (lengths_hbm, lengths_ref), (queries_hbm, queries_ref), (routes_hbm, routes_ref),
        (residual_hbm, residual_ref), (gain_hbm, gain_ref),
    ]
    blocks = [pl.ds(begin, BLOCK) for begin in range(0, batch, BLOCK)]
    groups = [
        small[:2],
        [(keys_hbm.at[block], keys_ref.at[block]) for block in blocks],
        [(values_hbm.at[block], values_ref.at[block, 0:window]) for block in blocks],
        small[2:],
    ]
    at, copies = 0, []
    for group in groups:
        copies.append([])
        for source, target in group:
            copies[-1].append(pltpu.make_async_copy(source, target, sems.at[at]))
            copies[-1][-1].start()
            at += 1

    def wait(group):
        for copy in copies[group]:
            copy.wait()

    padded = values_ref.shape[1]
    if padded > window:
        pad = (batch, padded - window, values_ref.shape[2])
        values_ref[:, window:, :] = jnp.zeros(pad, BF16)
    wait(0)
    same = iota((batch, batch), 0) == iota((batch, batch), 1)

    def upright(row):
        return jnp.sum(jnp.where(same, row, 0), axis=1, keepdims=True)

    queries = queries_ref[...]
    lanes = PAIR * GROUP * batch
    full = -(-lanes // LANES) * LANES
    request = iota((window, full), 1) % batch
    length = jnp.zeros((1, full), jnp.int32)
    for r in range(batch):
        length = jnp.where(request[0:1] == r, lengths_ref[0:1, r : r + 1], length)
    visible = iota((window, full), 0) < length
    owner = iota((lanes, padded), 0) % batch
    attended = []
    for i, part in enumerate(parts):
        spread = []
        for k in range(PAIR):
            at = [(i * PAIR + k) * span + g * HS for g in range(GROUP)]
            stacked = jnp.concatenate([queries[:, c : c + HS] for c in at], axis=0)
            blank = jnp.zeros_like(stacked)
            spread.append(
                jnp.concatenate([stacked if j == k else blank for j in range(PAIR)], axis=1)
            )
        if full > lanes:
            spread.append(jnp.zeros((full - lanes, PAIR * HS), BF16))
        spread = jnp.concatenate(spread, axis=0)
        if i == 0:
            wait(1)
        keys = keys_ref[:, :, part].reshape(batch * window, PAIR * HS)
        products = dot(keys, spread, ((1,), (1,)))
        scores = products[:window]
        for r in range(1, batch):
            scores = jnp.where(request == r, products[r * window : (r + 1) * window], scores)
        scores = jnp.where(visible, scores * HS ** (-0.5), -1e30)
        powers = jnp.exp(scores - jnp.max(scores, axis=0, keepdims=True))
        weights = powers / jnp.sum(powers, axis=0, keepdims=True)
        if padded > window:
            weights = jnp.concatenate([weights, jnp.zeros((padded - window, full), F32)], axis=0)
        weights = weights.T[:lanes]
        weights = jnp.concatenate(
            [jnp.where(owner == r, weights, 0.0).astype(BF16) for r in range(batch)], axis=1
        )
        if i == 0:
            wait(2)
        values = values_ref[:, :, part].reshape(batch * padded, PAIR * HS)
        mixed = dot(weights, values)
        attended += [
            mixed[h * batch : (h + 1) * batch, h // GROUP * HS : (h // GROUP + 1) * HS]
            for h in range(PAIR * GROUP)
        ]
    wait(3)
    stream = residual_ref[...].astype(F32) + jnp.concatenate(attended, axis=1)
    scale = lax.rsqrt(jnp.mean(stream * stream, axis=1, keepdims=True) + 1e-05)
    lane = iota((batch, LANES), 1)
    routes = [upright(routes_ref[k : k + 1, :]).astype(F32) for k in range(2)]
    named = jnp.where(lane == 0, routes[0], jnp.where(lane == 1, routes[1], 0.0))
    stream_ref[...] = stream
    half = width // 2
    normed = (stream * scale * gain_ref[...]).astype(BF16)
    first_ref[:, :half] = normed[:, :half]
    first_ref[:, half:] = named.astype(BF16)
    second_ref[...] = normed[:, half:]


def pass_kernel(*_):
    pass


def stack(refs):
    return jnp.concatenate([ref[...] for ref in refs], axis=0)


def gather(refs, layers):
    first = stack(refs[:layers])
    half = first.shape[1] - LANES
    parts = [first[:, :half]] + [stack(refs[at : at + layers]) for at in range(layers, len(refs), layers)]
    return parts, first[:, half:]


def split_kernel(me_ref, *refs, layers, part):
    parts, named = gather(refs[: (1 + part) * layers], layers)
    outs = refs[(1 + part) * layers :]
    slots = dispatch(me_ref[0], parts[part], named, layers, len(outs))
    span = layers * CAP
    for e, ref in enumerate(outs):
        ref[...] = slots[e * span : (e + 1) * span].astype(BF16)


def strip_copies(source, begin, target, sems):
    strip = target.shape[1] // sems.shape[0]
    copies = [
        pltpu.make_async_copy(
            source.at[:, pl.ds(begin + c * strip, strip)],
            target.at[:, pl.ds(c * strip, strip)],
            sems.at[c],
        )
        for c in range(sems.shape[0])
    ]
    for copy in copies:
        copy.start()
    return copies


def tiles(count, tile):
    def run(body):
        @pl.loop(0, count // tile, unroll=UNROLL)
        def _(i):
            body(pl.ds(pl.multiple_of(i * tile, tile), tile))

    return run


def store_rows(outs, at, value):
    span = outs[0].shape[0]
    for e, ref in enumerate(outs):
        ref[:, at] = value[e * span : (e + 1) * span].astype(BF16)


def begin_kernel(*refs, experts):
    _, gate_ref, up_ref, down_hbm, gate_out, up_out, down_out, rows_ref, sems = refs[experts:]
    half = rows_ref.shape[1]
    copies = strip_copies(down_hbm, 0, down_out, sems)
    rows_ref[...] = stack(refs[:experts])
    units = gate_ref.shape[1]

    @tiles(units, min(TILE, units))
    def _(at):
        gate_out[:, at] = dot(rows_ref[...], gate_ref[:half, at])
        up_out[:, at] = dot(rows_ref[...], up_ref[:half, at])

    for copy in copies:
        copy.wait()


def middle_kernel(*refs, experts):
    gate_in, up_in, down_in, gate_ref, up_ref, down_hbm = refs[experts : experts + 6]
    outs = refs[experts + 6 : -4]
    hidden_ref, down_out, rows_ref, sems = refs[-4:]
    half = rows_ref.shape[1]
    copies = strip_copies(down_hbm, half, down_out, sems)
    rows_ref[...] = stack(refs[:experts])
    units = gate_ref.shape[1]

    @tiles(units, min(TILE, units))
    def _(at):
        gate = gate_in[:, at] + dot(rows_ref[...], gate_ref[half:, at])
        up = up_in[:, at] + dot(rows_ref[...], up_ref[half:, at])
        hidden_ref[:, at] = (jax.nn.silu(gate) * up).astype(BF16)

    @tiles(half, min(TILE, half))
    def _(at):
        store_rows(outs, at, dot(hidden_ref[...], down_in[:, at]))

    for copy in copies:
        copy.wait()


def end_kernel(hidden_ref, down_ref, *outs):
    half = down_ref.shape[1]

    @tiles(half, min(TILE, half))
    def _(at):
        store_rows(outs, at, dot(hidden_ref[...], down_ref[:, at]))


def mix_kernel(high_ref, low_ref, *refs, layers, part):
    outs, stream_ref = refs[-layers:], refs[-layers - 1]
    blocks = refs[: -layers - 1]
    order = farthest_first(len(blocks))
    returned = stack([blocks[order.index(e)] for e in range(len(blocks))])
    mixed = dot(high_ref[...], returned) + dot(low_ref[...], returned)
    batch, half = outs[0].shape
    for j, ref in enumerate(outs):
        value = mixed[j * batch : (j + 1) * batch]
        if j == 0:
            value = value + stream_ref[:, part * half : (part + 1) * half]
        ref[...] = value.astype(ref.dtype)


def add_kernel(*refs):
    out_ref = refs[-1]
    span = refs[-2].shape[1]
    if out_ref.shape[1] > span:
        out_ref[:, :span] = refs[0][...]
        refs = refs[1:]
    total = refs[0][...]
    for ref in refs[1:-1]:
        total = total + ref[...].astype(F32)
    out_ref[:, out_ref.shape[1] - span :] = total.astype(BF16)


def in_hbm(value):
    return pltpu.with_memory_space_constraint(value, pltpu.HBM)


def swap(value, axis, step):
    if step == 0:
        return value
    count = lax.axis_size(axis)
    return lax.ppermute(value, axis, [(i, i ^ step) for i in range(count)])


def farthest_first(count):
    return [0, *range(count - 1, 0, -1)]


def params(elements):
    return pltpu.CompilerParams(vmem_limit_bytes=min(48 * MIB, 2 * MIB + 10 * elements))


def shards(
    queries,
    cached_keys,
    cached_values,
    lengths,
    routes,
    residual,
    norm_gain,
    router,
    gate_proj,
    up_proj,
    down_proj,
):
    batch, width = queries.shape
    experts = router.shape[1]
    layers = lax.axis_size("attn")
    me = lax.axis_index("expert").astype(jnp.int32).reshape(1)
    router = router.T
    shape = jax.ShapeDtypeStruct
    operands = [
        in_hbm(a)
        for a in (
            lengths[None], queries, cached_keys, cached_values, routes.T, residual, norm_gain[None]
        )
    ]
    window, depth = cached_values.shape[1:]
    held = [a.shape for a in operands]
    held[3] = (batch, -(-window // LANES) * LANES, depth)
    half = width // 2
    stream, *payload = pl.pallas_call(
        attend_kernel,
        in_specs=[SCALAR] + [ANY] * len(operands),
        out_specs=[WHOLE] * 3,
        out_shape=[shape((batch, width), F32)]
        + [shape((batch, size), BF16) for size in (half + LANES, half)],
        scratch_shapes=[pltpu.VMEM(size, a.dtype) for size, a in zip(held, operands)]
        + [pltpu.SemaphoreType.DMA((5 + 2 * (batch // BLOCK),))],
        compiler_params=params(28 * batch * width),
        cost_estimate=LIGHT,
    )(me, *operands)

    payload = pl.pallas_call(
        pass_kernel,
        in_specs=[ANY] * 2,
        out_specs=[ANY] * 2,
        out_shape=[shape(block.shape, BF16) for block in payload],
        input_output_aliases={0: 0, 1: 1},
        cost_estimate=BUSY,
        compiler_params=params(0),
    )(*payload)

    order = farthest_first(experts)
    chunks, arrived = [], []
    for part in range(2):
        came = {j: swap(payload[part], "attn", j) for j in farthest_first(layers)}
        chunks += [came[j] for j in range(layers)]
        slots = pl.pallas_call(
            functools.partial(split_kernel, layers=layers, part=part),
            in_specs=[SCALAR] + [WHOLE] * len(chunks),
            out_specs=[WHOLE] * experts,
            out_shape=[shape((layers * CAP, half), BF16)] * experts,
            cost_estimate=MID if part else LIGHT,
            compiler_params=params(experts * layers * CAP * half),
        )(me, *chunks)
        arrived.append([swap(slots[e], "expert", e) for e in order])
    gates = pl.pallas_call(
        functools.partial(weigh_kernel, layers=layers),
        in_specs=[SCALAR] + [WHOLE] * (1 + len(chunks)),
        out_specs=[WHOLE] * 2,
        out_shape=[shape((layers * batch, experts * layers * CAP), BF16)] * 2,
        cost_estimate=LIGHT,
        compiler_params=params(layers * batch * width),
    )(me, router, *chunks)

    total_rows = experts * layers * CAP
    units = gate_proj.shape[2]
    gate, up, down = gate_proj[0], up_proj[0], in_hbm(down_proj[0])
    rows = pltpu.VMEM((total_rows, half), BF16)
    strips = pltpu.SemaphoreType.DMA((STRIPS,))
    halves = [shape((layers * CAP, half), BF16)] * experts
    *sums, down_first = pl.pallas_call(
        functools.partial(begin_kernel, experts=experts),
        in_specs=[WHOLE] * experts + [ANY] + [WHOLE] * 2 + [ANY],
        out_specs=[WHOLE] * 3,
        out_shape=[shape((total_rows, units), F32)] * 2 + [pltpu.VMEM((units, half), BF16)],
        scratch_shapes=[rows, strips],
        cost_estimate=pl.CostEstimate(
            flops=4 * total_rows * half * units, bytes_accessed=0, transcendentals=0
        ),
        compiler_params=params(total_rows * width),
    )(*arrived[0], gates[0], gate, up, down)
    *first, hidden, down_second = pl.pallas_call(
        functools.partial(middle_kernel, experts=experts),
        in_specs=[WHOLE] * (experts + 5) + [ANY],
        out_specs=[WHOLE] * (experts + 2),
        out_shape=halves + [shape((total_rows, units), BF16), pltpu.VMEM((units, half), BF16)],
        scratch_shapes=[rows, strips],
        compiler_params=params(total_rows * width),
    )(*arrived[1], *sums, down_first, gate, up, down)
    second = pl.pallas_call(
        end_kernel,
        in_specs=[WHOLE] * 2,
        out_specs=[WHOLE] * experts,
        out_shape=halves,
        cost_estimate=pl.CostEstimate(
            flops=2 * total_rows * half * units, bytes_accessed=0, transcendentals=0
        ),
        compiler_params=params(total_rows * width),
    )(hidden, down_second)

    done = []
    for part, blocks in enumerate((first, second)):
        returned = [swap(block, "expert", e) for e, block in zip(order, blocks)]
        mixed = pl.pallas_call(
            functools.partial(mix_kernel, layers=layers, part=part),
            in_specs=[WHOLE] * (3 + experts),
            out_specs=[WHOLE] * layers,
            out_shape=[shape((batch, half), BF16 if j else F32) for j in range(layers)],
            cost_estimate=LIGHT,
            compiler_params=params(experts * layers * CAP * half),
        )(*gates, *returned, stream)
        sums = [swap(mixed[j], "attn", j) for j in farthest_first(layers)]
        done = [
            pl.pallas_call(
                add_kernel,
                in_specs=[WHOLE] * (layers + len(done)),
                out_specs=WHOLE,
                out_shape=shape((batch, width if part else half), BF16),
                cost_estimate=LIGHT,
                compiler_params=params(layers * batch * width),
            )(*done, *sums)
        ]
    return done[0]


def solution(mesh):
    in_specs = (
        P(("groups", "attn", "expert"), None),
        P(("groups", "attn", "expert"), None, None),
        P(("groups", "attn", "expert"), None, None),
        P(("groups", "attn", "expert")),
        P(("groups", "attn", "expert"), None),
        P(("groups", "attn", "expert"), None),
        P(),
        P(),
        P("expert", None, "attn"),
        P("expert", None, "attn"),
        P("expert", "attn", None),
    )
    out_specs = P(("groups", "attn", "expert"), None)
    return jax.shard_map(shards, mesh=mesh, in_specs=in_specs, out_specs=out_specs, check_vma=False)
```

```python
import functools

import jax
import jax.numpy as jnp
from jax import lax
from jax.experimental import pallas as pl
from jax.experimental.pallas import tpu as pltpu
from jax.sharding import PartitionSpec as P

HS = 128
KVH = 4
GROUP = 6
CAP = 8
LANES = 128
PAIR = 2
BLOCK = 4
STRIPS = 3
TILE = 256
UNROLL = 2
MIB = 1 << 20
F32 = jnp.float32
BF16 = jnp.bfloat16
LIGHT = pl.CostEstimate(flops=0, bytes_accessed=0, transcendentals=0)
BUSY = pl.CostEstimate(flops=24 * 10**9, bytes_accessed=0, transcendentals=0)
MID = pl.CostEstimate(flops=2 * 10**9, bytes_accessed=0, transcendentals=0)
ANY = pl.BlockSpec(memory_space=pl.ANY)
WHOLE = pl.BlockSpec(memory_space=pltpu.VMEM)
SCALAR = pl.BlockSpec(memory_space=pltpu.SMEM)


def dot(a, b, dims=((1,), (0,))):
    return lax.dot_general(a, b, (dims, ((), ())), preferred_element_type=F32)


def iota(shape, dim):
    return lax.broadcasted_iota(jnp.int32, shape, dim)


def split(index, size):
    if size & (size - 1):
        return lax.div(index, size), lax.rem(index, size)
    return index >> (size.bit_length() - 1), index & (size - 1)


def slot_map(owners, chunks, batch, experts):
    rows, slots = chunks * batch, experts * chunks * CAP
    slot = iota((rows, slots), 1)
    row = iota((rows, slots), 0)
    group, wanted = split(slot, CAP)
    expert, chunk = split(group, chunks)
    named = (owners[:, 0:1] == expert) | (owners[:, 1:2] == expert)
    named = named & (split(row, batch)[0] == chunk)
    named = jnp.where(named, 1.0, 0.0)
    left, right = iota((rows, rows), 0), iota((rows, rows), 1)
    before = jnp.where(right < left, 1.0, 0.0).astype(BF16)
    place = dot(before, named.astype(BF16))
    return jnp.where(place == wanted.astype(F32), named, 0.0)


def dispatch(me, rows, named, chunks, experts):
    owners = named[:, 0:2].astype(F32).astype(jnp.int32) ^ me
    table = slot_map(owners, chunks, rows.shape[0] // chunks, experts)
    return dot(table.astype(BF16), rows, ((0,), (0,)))


def weigh_kernel(me_ref, router_ref, *refs, layers):
    high_ref, low_ref = refs[-2:]
    parts, named = gather(refs[:-2], layers)
    rows = jnp.concatenate(parts, axis=1)
    routes = named[:, 0:2].astype(F32).astype(jnp.int32)
    logits = dot(rows, router_ref[...], ((1,), (1,)))
    experts = logits.shape[1]
    lane = iota(logits.shape, 1)
    first = jnp.sum(jnp.where(lane == routes[:, 0:1], logits, 0.0), axis=1, keepdims=True)
    second = jnp.sum(jnp.where(lane == routes[:, 1:2], logits, 0.0), axis=1, keepdims=True)
    gate0 = 1.0 / (1.0 + jnp.exp(second - first))
    gate1 = 1.0 / (1.0 + jnp.exp(first - second))
    owners = routes ^ me_ref[0]
    table = slot_map(owners, layers, rows.shape[0] // layers, experts)
    expert, _ = split(iota(table.shape, 1), layers * CAP)
    gates = table * jnp.where(owners[:, 0:1] == expert, gate0, gate1)
    high = gates.astype(BF16)
    high_ref[...] = high
    low_ref[...] = (gates - high.astype(F32)).astype(BF16)


def attend_kernel(
    _, lengths_hbm, queries_hbm, keys_hbm, values_hbm, routes_hbm, residual_hbm, gain_hbm,
    stream_ref, first_ref, second_ref,
    lengths_ref, queries_ref, keys_ref, values_ref, routes_ref, residual_ref, gain_ref, sems,
):
    batch, window, _ = keys_ref.shape
    width = queries_ref.shape[1]
    span = width // KVH
    parts = [pl.ds(begin, PAIR * HS) for begin in range(0, KVH * HS, PAIR * HS)]
    small = [
        (lengths_hbm, lengths_ref), (queries_hbm, queries_ref), (routes_hbm, routes_ref),
        (residual_hbm, residual_ref), (gain_hbm, gain_ref),
    ]
    blocks = [pl.ds(begin, BLOCK) for begin in range(0, batch, BLOCK)]
    groups = [
        small[:2],
        [(keys_hbm.at[block], keys_ref.at[block]) for block in blocks],
        [(values_hbm.at[block], values_ref.at[block, 0:window]) for block in blocks],
        small[2:],
    ]
    at, copies = 0, []
    for group in groups:
        copies.append([])
        for source, target in group:
            copies[-1].append(pltpu.make_async_copy(source, target, sems.at[at]))
            copies[-1][-1].start()
            at += 1

    def wait(group):
        for copy in copies[group]:
            copy.wait()

    padded = values_ref.shape[1]
    if padded > window:
        pad = (batch, padded - window, values_ref.shape[2])
        values_ref[:, window:, :] = jnp.zeros(pad, BF16)
    wait(0)
    same = iota((batch, batch), 0) == iota((batch, batch), 1)

    def upright(row):
        return jnp.sum(jnp.where(same, row, 0), axis=1, keepdims=True)

    queries = queries_ref[...]
    lanes = PAIR * GROUP * batch
    full = -(-lanes // LANES) * LANES
    _, request = split(iota((window, full), 1), batch)
    length = jnp.zeros((1, full), jnp.int32)
    for r in range(batch):
        length = jnp.where(request[0:1] == r, lengths_ref[0:1, r : r + 1], length)
    visible = iota((window, full), 0) < length
    _, owner = split(iota((lanes, padded), 0), batch)
    attended = []
    for i, part in enumerate(parts):
        spread = []
        for k in range(PAIR):
            at = [(i * PAIR + k) * span + g * HS for g in range(GROUP)]
            stacked = jnp.concatenate([queries[:, c : c + HS] for c in at], axis=0)
            blank = jnp.zeros_like(stacked)
            spread.append(
                jnp.concatenate([stacked if j == k else blank for j in range(PAIR)], axis=1)
            )
        if full > lanes:
            spread.append(jnp.zeros((full - lanes, PAIR * HS), BF16))
        spread = jnp.concatenate(spread, axis=0)
        if i == 0:
            wait(1)
        keys = keys_ref[:, :, part].reshape(batch * window, PAIR * HS)
        products = dot(keys, spread, ((1,), (1,)))
        scores = products[:window]
        for r in range(1, batch):
            scores = jnp.where(request == r, products[r * window : (r + 1) * window], scores)
        scores = jnp.where(visible, scores * HS ** (-0.5), -1e30)
        powers = jnp.exp(scores - jnp.max(scores, axis=0, keepdims=True))
        weights = powers / jnp.sum(powers, axis=0, keepdims=True)
        if padded > window:
            weights = jnp.concatenate([weights, jnp.zeros((padded - window, full), F32)], axis=0)
        weights = weights.T[:lanes]
        weights = jnp.concatenate(
            [jnp.where(owner == r, weights, 0.0).astype(BF16) for r in range(batch)], axis=1
        )
        if i == 0:
            wait(2)
        values = values_ref[:, :, part].reshape(batch * padded, PAIR * HS)
        mixed = dot(weights, values)
        attended += [
            mixed[h * batch : (h + 1) * batch, h // GROUP * HS : (h // GROUP + 1) * HS]
            for h in range(PAIR * GROUP)
        ]
    wait(3)
    stream = residual_ref[...].astype(F32) + jnp.concatenate(attended, axis=1)
    scale = lax.rsqrt(jnp.mean(stream * stream, axis=1, keepdims=True) + 1e-05)
    lane = iota((batch, LANES), 1)
    routes = [upright(routes_ref[k : k + 1, :]).astype(F32) for k in range(2)]
    named = jnp.where(lane == 0, routes[0], jnp.where(lane == 1, routes[1], 0.0))
    stream_ref[...] = stream
    half = width // 2
    normed = (stream * scale * gain_ref[...]).astype(BF16)
    first_ref[:, :half] = normed[:, :half]
    first_ref[:, half:] = named.astype(BF16)
    second_ref[...] = normed[:, half:]


def pass_kernel(*_):
    pass


def pass_on(values, cost, after):
    first = len(after)
    return pl.pallas_call(
        pass_kernel,
        in_specs=[ANY] * (first + len(values)),
        out_specs=[ANY] * len(values),
        out_shape=[jax.ShapeDtypeStruct(value.shape, value.dtype) for value in values],
        input_output_aliases={first + i: i for i in range(len(values))},
        cost_estimate=cost,
        compiler_params=params(0),
    )(*after, *values)


def stack(refs):
    return jnp.concatenate([ref[...] for ref in refs], axis=0)


def gather(refs, layers):
    first = stack(refs[:layers])
    half = first.shape[1] - LANES
    parts = [first[:, :half]] + [stack(refs[at : at + layers]) for at in range(layers, len(refs), layers)]
    return parts, first[:, half:]


def split_kernel(me_ref, *refs, layers, part):
    parts, named = gather(refs[: (1 + part) * layers], layers)
    outs = refs[(1 + part) * layers :]
    slots = dispatch(me_ref[0], parts[part], named, layers, len(outs))
    span = layers * CAP
    for e, ref in enumerate(outs):
        ref[...] = slots[e * span : (e + 1) * span].astype(BF16)


def strip_copies(source, begin, target, sems):
    strip = target.shape[1] // sems.shape[0]
    copies = [
        pltpu.make_async_copy(
            source.at[:, pl.ds(begin + c * strip, strip)],
            target.at[:, pl.ds(c * strip, strip)],
            sems.at[c],
        )
        for c in range(sems.shape[0])
    ]
    for copy in copies:
        copy.start()
    return copies


def tiles(count, tile):
    def run(body):
        @pl.loop(0, count // tile, unroll=UNROLL)
        def _(i):
            body(pl.ds(pl.multiple_of(i * tile, tile), tile))

    return run


def store_rows(outs, at, value):
    span = outs[0].shape[0]
    for e, ref in enumerate(outs):
        ref[:, at] = value[e * span : (e + 1) * span].astype(BF16)


def begin_kernel(*refs, experts):
    _, gate_ref, up_ref, down_hbm, gate_out, up_out, down_out, rows_ref, sems = refs[experts:]
    half = rows_ref.shape[1]
    copies = strip_copies(down_hbm, 0, down_out, sems)
    rows_ref[...] = stack(refs[:experts])
    units = gate_ref.shape[1]

    @tiles(units, min(TILE, units))
    def _(at):
        gate_out[:, at] = dot(rows_ref[...], gate_ref[:half, at])
        up_out[:, at] = dot(rows_ref[...], up_ref[:half, at])

    for copy in copies:
        copy.wait()


def middle_kernel(*refs, experts):
    gate_in, up_in, down_in, gate_ref, up_ref, down_hbm = refs[experts : experts + 6]
    outs = refs[experts + 6 : -4]
    hidden_ref, down_out, rows_ref, sems = refs[-4:]
    half = rows_ref.shape[1]
    copies = strip_copies(down_hbm, half, down_out, sems)
    rows_ref[...] = stack(refs[:experts])
    units = gate_ref.shape[1]

    @tiles(units, min(TILE, units))
    def _(at):
        gate = gate_in[:, at] + dot(rows_ref[...], gate_ref[half:, at])
        up = up_in[:, at] + dot(rows_ref[...], up_ref[half:, at])
        hidden_ref[:, at] = (jax.nn.silu(gate) * up).astype(BF16)

    @tiles(half, min(TILE, half))
    def _(at):
        store_rows(outs, at, dot(hidden_ref[...], down_in[:, at]))

    for copy in copies:
        copy.wait()


def end_kernel(hidden_ref, down_ref, *outs):
    half = down_ref.shape[1]

    @tiles(half, min(TILE, half))
    def _(at):
        store_rows(outs, at, dot(hidden_ref[...], down_ref[:, at]))


def mix_kernel(high_ref, low_ref, *refs, layers, part):
    outs, stream_ref = refs[-layers:], refs[-layers - 1]
    blocks = refs[: -layers - 1]
    order = farthest_first(len(blocks))
    returned = stack([blocks[order.index(e)] for e in range(len(blocks))])
    mixed = dot(high_ref[...], returned) + dot(low_ref[...], returned)
    batch, half = outs[0].shape
    for j, ref in enumerate(outs):
        value = mixed[j * batch : (j + 1) * batch]
        if j == 0:
            value = value + stream_ref[:, part * half : (part + 1) * half]
        ref[...] = value.astype(ref.dtype)


def add_kernel(*refs):
    out_ref = refs[-1]
    span = refs[-2].shape[1]
    if out_ref.shape[1] > span:
        out_ref[:, :span] = refs[0][...]
        refs = refs[1:]
    total = refs[0][...]
    for ref in refs[1:-1]:
        total = total + ref[...].astype(F32)
    out_ref[:, out_ref.shape[1] - span :] = total.astype(BF16)


def in_hbm(value):
    return pltpu.with_memory_space_constraint(value, pltpu.HBM)


def swap(value, axis, step):
    if step == 0:
        return value
    count = lax.axis_size(axis)
    return lax.ppermute(value, axis, [(i, i ^ step) for i in range(count)])


def farthest_first(count):
    return [0, *range(count - 1, 0, -1)]


def params(elements):
    return pltpu.CompilerParams(vmem_limit_bytes=min(48 * MIB, 2 * MIB + 10 * elements))


def shards(
    queries,
    cached_keys,
    cached_values,
    lengths,
    routes,
    residual,
    norm_gain,
    router,
    gate_proj,
    up_proj,
    down_proj,
):
    batch, width = queries.shape
    experts = router.shape[1]
    layers = lax.axis_size("attn")
    me = lax.axis_index("expert").astype(jnp.int32).reshape(1)
    router = router.T
    shape = jax.ShapeDtypeStruct
    operands = [
        in_hbm(a)
        for a in (
            lengths[None], queries, cached_keys, cached_values, routes.T, residual, norm_gain[None]
        )
    ]
    window, depth = cached_values.shape[1:]
    held = [a.shape for a in operands]
    held[3] = (batch, -(-window // LANES) * LANES, depth)
    half = width // 2
    stream, *payload = pl.pallas_call(
        attend_kernel,
        in_specs=[SCALAR] + [ANY] * len(operands),
        out_specs=[WHOLE] * 3,
        out_shape=[shape((batch, width), F32)]
        + [shape((batch, size), BF16) for size in (half + LANES, half)],
        scratch_shapes=[pltpu.VMEM(size, a.dtype) for size, a in zip(held, operands)]
        + [pltpu.SemaphoreType.DMA((5 + 2 * (batch // BLOCK),))],
        compiler_params=params(28 * batch * width),
        cost_estimate=LIGHT,
    )(me, *operands)

    payload = pass_on(payload, BUSY, [])

    order = farthest_first(experts)
    chunks, arrived = [], []
    for part in range(2):
        came = {j: swap(payload[part], "attn", j) for j in farthest_first(layers)}
        chunks += [came[j] for j in range(layers)]
        slots = pl.pallas_call(
            functools.partial(split_kernel, layers=layers, part=part),
            in_specs=[SCALAR] + [WHOLE] * len(chunks),
            out_specs=[WHOLE] * experts,
            out_shape=[shape((layers * CAP, half), BF16)] * experts,
            cost_estimate=MID if part else LIGHT,
            compiler_params=params(experts * layers * CAP * half),
        )(me, *chunks)
        arrived.append([swap(slots[e], "expert", e) for e in order])
    gates = pl.pallas_call(
        functools.partial(weigh_kernel, layers=layers),
        in_specs=[SCALAR] + [WHOLE] * (1 + len(chunks)),
        out_specs=[WHOLE] * 2,
        out_shape=[shape((layers * batch, experts * layers * CAP), BF16)] * 2,
        cost_estimate=LIGHT,
        compiler_params=params(layers * batch * width),
    )(me, router, *chunks)

    total_rows = experts * layers * CAP
    units = gate_proj.shape[2]
    gate, up, down = gate_proj[0], up_proj[0], in_hbm(down_proj[0])
    rows = pltpu.VMEM((total_rows, half), BF16)
    strips = pltpu.SemaphoreType.DMA((STRIPS,))
    halves = [shape((layers * CAP, half), BF16)] * experts
    *sums, down_first = pl.pallas_call(
        functools.partial(begin_kernel, experts=experts),
        in_specs=[WHOLE] * experts + [ANY] + [WHOLE] * 2 + [ANY],
        out_specs=[WHOLE] * 3,
        out_shape=[shape((total_rows, units), F32)] * 2 + [pltpu.VMEM((units, half), BF16)],
        scratch_shapes=[rows, strips],
        cost_estimate=pl.CostEstimate(
            flops=4 * total_rows * half * units, bytes_accessed=0, transcendentals=0
        ),
        compiler_params=params(total_rows * width),
    )(*arrived[0], gates[0], gate, up, down)
    *first, hidden, down_second = pl.pallas_call(
        functools.partial(middle_kernel, experts=experts),
        in_specs=[WHOLE] * (experts + 5) + [ANY],
        out_specs=[WHOLE] * (experts + 2),
        out_shape=halves + [shape((total_rows, units), BF16), pltpu.VMEM((units, half), BF16)],
        scratch_shapes=[rows, strips],
        compiler_params=params(total_rows * width),
    )(*arrived[1], *sums, down_first, gate, up, down)
    second = pl.pallas_call(
        end_kernel,
        in_specs=[WHOLE] * 2,
        out_specs=[WHOLE] * experts,
        out_shape=halves,
        cost_estimate=pl.CostEstimate(
            flops=2 * total_rows * half * units, bytes_accessed=0, transcendentals=0
        ),
        compiler_params=params(total_rows * width),
    )(hidden, down_second)

    done = []
    for part, blocks in enumerate((first, second)):
        if part:
            blocks = pass_on(blocks, LIGHT, returned[1:2])
        returned = [swap(block, "expert", e) for e, block in zip(order, blocks)]
        mixed = pl.pallas_call(
            functools.partial(mix_kernel, layers=layers, part=part),
            in_specs=[WHOLE] * (3 + experts),
            out_specs=[WHOLE] * layers,
            out_shape=[shape((batch, half), BF16 if j else F32) for j in range(layers)],
            cost_estimate=LIGHT,
            compiler_params=params(experts * layers * CAP * half),
        )(*gates, *returned, stream)
        distances = [0, 1, *range(layers - 1, 1, -1)] if part else farthest_first(layers)
        sums = [swap(mixed[j], "attn", j) for j in distances]
        done = [
            pl.pallas_call(
                add_kernel,
                in_specs=[WHOLE] * (layers + len(done)),
                out_specs=WHOLE,
                out_shape=shape((batch, width if part else half), BF16),
                cost_estimate=LIGHT,
                compiler_params=params(layers * batch * width),
            )(*done, *sums)
        ]
    return done[0]


def solution(mesh):
    in_specs = (
        P(("groups", "attn", "expert"), None),
        P(("groups", "attn", "expert"), None, None),
        P(("groups", "attn", "expert"), None, None),
        P(("groups", "attn", "expert")),
        P(("groups", "attn", "expert"), None),
        P(("groups", "attn", "expert"), None),
        P(),
        P(),
        P("expert", None, "attn"),
        P("expert", None, "attn"),
        P("expert", "attn", None),
    )
    out_specs = P(("groups", "attn", "expert"), None)
    return jax.shard_map(shards, mesh=mesh, in_specs=in_specs, out_specs=out_specs, check_vma=False)
```

```python
import functools

import jax
import jax.numpy as jnp
from jax import lax
from jax.experimental import pallas as pl
from jax.experimental.pallas import tpu as pltpu
from jax.sharding import PartitionSpec as P

HS = 128
KVH = 4
GROUP = 6
CAP = 8
LANES = 128
PAIR = 2
BLOCK = 4
STRIPS = 3
TILE = 256
UNROLL = 2
MIB = 1 << 20
F32 = jnp.float32
BF16 = jnp.bfloat16
LIGHT = pl.CostEstimate(flops=0, bytes_accessed=0, transcendentals=0)
BUSY = pl.CostEstimate(flops=24 * 10**9, bytes_accessed=0, transcendentals=0)
MID = pl.CostEstimate(flops=2 * 10**9, bytes_accessed=0, transcendentals=0)
ANY = pl.BlockSpec(memory_space=pl.ANY)
WHOLE = pl.BlockSpec(memory_space=pltpu.VMEM)
SCALAR = pl.BlockSpec(memory_space=pltpu.SMEM)


def dot(a, b, dims=((1,), (0,))):
    return lax.dot_general(a, b, (dims, ((), ())), preferred_element_type=F32)


def iota(shape, dim):
    return lax.broadcasted_iota(jnp.int32, shape, dim)


def split(index, size):
    if size & (size - 1):
        return lax.div(index, size), lax.rem(index, size)
    return index >> (size.bit_length() - 1), index & (size - 1)


def slot_map(owners, chunks, batch, experts):
    rows, slots = chunks * batch, experts * chunks * CAP
    slot = iota((rows, slots), 1)
    row = iota((rows, slots), 0)
    group, wanted = split(slot, CAP)
    expert, chunk = split(group, chunks)
    named = (owners[:, 0:1] == expert) | (owners[:, 1:2] == expert)
    named = named & (split(row, batch)[0] == chunk)
    named = jnp.where(named, 1.0, 0.0)
    left, right = iota((rows, rows), 0), iota((rows, rows), 1)
    before = jnp.where(right < left, 1.0, 0.0).astype(BF16)
    place = dot(before, named.astype(BF16))
    return jnp.where(place == wanted.astype(F32), named, 0.0)


def dispatch(me, rows, named, chunks, experts):
    owners = named[:, 0:2].astype(F32).astype(jnp.int32) ^ me
    table = slot_map(owners, chunks, rows.shape[0] // chunks, experts)
    return dot(table.astype(BF16), rows, ((0,), (0,)))


def weigh_kernel(me_ref, router_ref, *refs, layers):
    high_ref, low_ref = refs[-2:]
    parts, named = gather(refs[:-2], layers)
    rows = jnp.concatenate(parts, axis=1)
    routes = named[:, 0:2].astype(F32).astype(jnp.int32)
    logits = dot(rows, router_ref[...], ((1,), (1,)))
    experts = logits.shape[1]
    lane = iota(logits.shape, 1)
    first = jnp.sum(jnp.where(lane == routes[:, 0:1], logits, 0.0), axis=1, keepdims=True)
    second = jnp.sum(jnp.where(lane == routes[:, 1:2], logits, 0.0), axis=1, keepdims=True)
    gate0 = 1.0 / (1.0 + jnp.exp(second - first))
    gate1 = 1.0 / (1.0 + jnp.exp(first - second))
    owners = routes ^ me_ref[0]
    table = slot_map(owners, layers, rows.shape[0] // layers, experts)
    expert, _ = split(iota(table.shape, 1), layers * CAP)
    gates = table * jnp.where(owners[:, 0:1] == expert, gate0, gate1)
    high = gates.astype(BF16)
    high_ref[...] = high
    low_ref[...] = (gates - high.astype(F32)).astype(BF16)


def attend_kernel(
    _, lengths_hbm, queries_hbm, keys_hbm, values_hbm, routes_hbm, residual_hbm, gain_hbm,
    stream_ref, first_ref, second_ref,
    lengths_ref, queries_ref, keys_ref, values_ref, routes_ref, residual_ref, gain_ref, sems,
):
    batch, window, _ = keys_ref.shape
    width = queries_ref.shape[1]
    span = width // KVH
    parts = [pl.ds(begin, PAIR * HS) for begin in range(0, KVH * HS, PAIR * HS)]
    small = [
        (lengths_hbm, lengths_ref), (queries_hbm, queries_ref), (routes_hbm, routes_ref),
        (residual_hbm, residual_ref), (gain_hbm, gain_ref),
    ]
    blocks = [pl.ds(begin, BLOCK) for begin in range(0, batch, BLOCK)]
    groups = [
        small[:2],
        [(keys_hbm.at[block], keys_ref.at[block]) for block in blocks],
        [(values_hbm.at[block], values_ref.at[block, 0:window]) for block in blocks],
        small[2:],
    ]
    at, copies = 0, []
    for group in groups:
        copies.append([])
        for source, target in group:
            copies[-1].append(pltpu.make_async_copy(source, target, sems.at[at]))
            copies[-1][-1].start()
            at += 1

    def wait(group):
        for copy in copies[group]:
            copy.wait()

    padded = values_ref.shape[1]
    if padded > window:
        pad = (batch, padded - window, values_ref.shape[2])
        values_ref[:, window:, :] = jnp.zeros(pad, BF16)
    wait(0)
    same = iota((batch, batch), 0) == iota((batch, batch), 1)

    def upright(row):
        return jnp.sum(jnp.where(same, row, 0), axis=1, keepdims=True)

    queries = queries_ref[...]
    lanes = PAIR * GROUP * batch
    full = -(-lanes // LANES) * LANES
    _, request = split(iota((window, full), 1), batch)
    length = jnp.zeros((1, full), jnp.int32)
    for r in range(batch):
        length = jnp.where(request[0:1] == r, lengths_ref[0:1, r : r + 1], length)
    visible = iota((window, full), 0) < length
    _, owner = split(iota((lanes, padded), 0), batch)
    spreads = []
    for i in range(len(parts)):
        spread = []
        for k in range(PAIR):
            at = [(i * PAIR + k) * span + g * HS for g in range(GROUP)]
            stacked = jnp.concatenate([queries[:, c : c + HS] for c in at], axis=0)
            blank = jnp.zeros_like(stacked)
            spread.append(
                jnp.concatenate([stacked if j == k else blank for j in range(PAIR)], axis=1)
            )
        if full > lanes:
            spread.append(jnp.zeros((full - lanes, PAIR * HS), BF16))
        spreads.append(jnp.concatenate(spread, axis=0))
    wait(1)
    weighted = []
    for spread, part in zip(spreads, parts):
        keys = keys_ref[:, :, part].reshape(batch * window, PAIR * HS)
        products = dot(keys, spread, ((1,), (1,)))
        scores = products[:window]
        for r in range(1, batch):
            scores = jnp.where(request == r, products[r * window : (r + 1) * window], scores)
        scores = jnp.where(visible, scores * HS ** (-0.5), -1e30)
        powers = jnp.exp(scores - jnp.max(scores, axis=0, keepdims=True))
        weights = powers / jnp.sum(powers, axis=0, keepdims=True)
        if padded > window:
            weights = jnp.concatenate([weights, jnp.zeros((padded - window, full), F32)], axis=0)
        weights = weights.T[:lanes]
        weighted.append(
            jnp.concatenate(
                [jnp.where(owner == r, weights, 0.0).astype(BF16) for r in range(batch)], axis=1
            )
        )
    wait(2)
    attended = []
    for weights, part in zip(weighted, parts):
        values = values_ref[:, :, part].reshape(batch * padded, PAIR * HS)
        mixed = dot(weights, values)
        attended += [
            mixed[h * batch : (h + 1) * batch, h // GROUP * HS : (h // GROUP + 1) * HS]
            for h in range(PAIR * GROUP)
        ]
    wait(3)
    stream = residual_ref[...].astype(F32) + jnp.concatenate(attended, axis=1)
    scale = lax.rsqrt(jnp.mean(stream * stream, axis=1, keepdims=True) + 1e-05)
    lane = iota((batch, LANES), 1)
    routes = [upright(routes_ref[k : k + 1, :]).astype(F32) for k in range(2)]
    named = jnp.where(lane == 0, routes[0], jnp.where(lane == 1, routes[1], 0.0))
    stream_ref[...] = stream
    half = width // 2
    normed = (stream * scale * gain_ref[...]).astype(BF16)
    first_ref[:, :half] = normed[:, :half]
    first_ref[:, half:] = named.astype(BF16)
    second_ref[...] = normed[:, half:]


def pass_kernel(*_):
    pass


def pass_on(values, cost):
    return pl.pallas_call(
        pass_kernel,
        in_specs=[ANY] * len(values),
        out_specs=[ANY] * len(values),
        out_shape=[jax.ShapeDtypeStruct(value.shape, value.dtype) for value in values],
        input_output_aliases={i: i for i in range(len(values))},
        cost_estimate=cost,
        compiler_params=params(0),
    )(*values)


def stack(refs):
    return jnp.concatenate([ref[...] for ref in refs], axis=0)


def gather(refs, layers):
    first = stack(refs[:layers])
    half = first.shape[1] - LANES
    parts = [first[:, :half]] + [stack(refs[at : at + layers]) for at in range(layers, len(refs), layers)]
    return parts, first[:, half:]


def split_kernel(me_ref, *refs, layers, part):
    parts, named = gather(refs[: (1 + part) * layers], layers)
    outs = refs[(1 + part) * layers :]
    slots = dispatch(me_ref[0], parts[part], named, layers, len(outs))
    span = layers * CAP
    for e, ref in enumerate(outs):
        ref[...] = slots[e * span : (e + 1) * span].astype(BF16)


def strip_copies(source, begin, target, sems):
    strip = target.shape[1] // sems.shape[0]
    copies = [
        pltpu.make_async_copy(
            source.at[:, pl.ds(begin + c * strip, strip)],
            target.at[:, pl.ds(c * strip, strip)],
            sems.at[c],
        )
        for c in range(sems.shape[0])
    ]
    for copy in copies:
        copy.start()
    return copies


def tiles(count, tile):
    def run(body):
        @pl.loop(0, count // tile, unroll=UNROLL)
        def _(i):
            body(pl.ds(pl.multiple_of(i * tile, tile), tile))

    return run


def store_rows(outs, at, value):
    span = outs[0].shape[0]
    for e, ref in enumerate(outs):
        ref[:, at] = value[e * span : (e + 1) * span].astype(BF16)


def begin_kernel(*refs, experts):
    _, gate_ref, up_ref, down_hbm, gate_out, up_out, down_out, rows_ref, sems = refs[experts:]
    half = rows_ref.shape[1]
    copies = strip_copies(down_hbm, 0, down_out, sems)
    rows_ref[...] = stack(refs[:experts])
    units = gate_ref.shape[1]

    @tiles(units, min(TILE, units))
    def _(at):
        gate_out[:, at] = dot(rows_ref[...], gate_ref[:half, at])
        up_out[:, at] = dot(rows_ref[...], up_ref[:half, at])

    for copy in copies:
        copy.wait()


def middle_kernel(*refs, experts):
    gate_in, up_in, down_in, gate_ref, up_ref, down_hbm = refs[experts : experts + 6]
    outs = refs[experts + 6 : -4]
    hidden_ref, down_out, rows_ref, sems = refs[-4:]
    half = rows_ref.shape[1]
    copies = strip_copies(down_hbm, half, down_out, sems)
    rows_ref[...] = stack(refs[:experts])
    units = gate_ref.shape[1]

    @tiles(units, min(TILE, units))
    def _(at):
        gate = gate_in[:, at] + dot(rows_ref[...], gate_ref[half:, at])
        up = up_in[:, at] + dot(rows_ref[...], up_ref[half:, at])
        hidden_ref[:, at] = (jax.nn.silu(gate) * up).astype(BF16)

    @tiles(half, min(TILE, half))
    def _(at):
        store_rows(outs, at, dot(hidden_ref[...], down_in[:, at]))

    for copy in copies:
        copy.wait()


def end_kernel(hidden_ref, down_ref, *outs):
    half = down_ref.shape[1]

    @tiles(half, min(TILE, half))
    def _(at):
        store_rows(outs, at, dot(hidden_ref[...], down_ref[:, at]))


def mix_kernel(high_ref, low_ref, *refs, layers, part):
    outs, stream_ref = refs[-layers:], refs[-layers - 1]
    blocks = refs[: -layers - 1]
    order = farthest_first(len(blocks))
    returned = stack([blocks[order.index(e)] for e in range(len(blocks))])
    mixed = dot(high_ref[...], returned) + dot(low_ref[...], returned)
    batch, half = outs[0].shape
    for j, ref in enumerate(outs):
        value = mixed[j * batch : (j + 1) * batch]
        if j == 0:
            value = value + stream_ref[:, part * half : (part + 1) * half]
        ref[...] = value.astype(ref.dtype)


def add_kernel(*refs):
    out_ref = refs[-1]
    span = refs[-2].shape[1]
    if out_ref.shape[1] > span:
        out_ref[:, :span] = refs[0][...]
        refs = refs[1:]
    total = refs[0][...]
    for ref in refs[1:-1]:
        total = total + ref[...].astype(F32)
    out_ref[:, out_ref.shape[1] - span :] = total.astype(BF16)


def in_hbm(value):
    return pltpu.with_memory_space_constraint(value, pltpu.HBM)


def swap(value, axis, step):
    if step == 0:
        return value
    count = lax.axis_size(axis)
    return lax.ppermute(value, axis, [(i, i ^ step) for i in range(count)])


def farthest_first(count):
    return [0, *range(count - 1, 0, -1)]


def params(elements):
    return pltpu.CompilerParams(vmem_limit_bytes=min(48 * MIB, 2 * MIB + 10 * elements))


def shards(
    queries,
    cached_keys,
    cached_values,
    lengths,
    routes,
    residual,
    norm_gain,
    router,
    gate_proj,
    up_proj,
    down_proj,
):
    batch, width = queries.shape
    experts = router.shape[1]
    layers = lax.axis_size("attn")
    me = lax.axis_index("expert").astype(jnp.int32).reshape(1)
    router = router.T
    shape = jax.ShapeDtypeStruct
    operands = [
        in_hbm(a)
        for a in (
            lengths[None], queries, cached_keys, cached_values, routes.T, residual, norm_gain[None]
        )
    ]
    window, depth = cached_values.shape[1:]
    held = [a.shape for a in operands]
    held[3] = (batch, -(-window // LANES) * LANES, depth)
    half = width // 2
    stream, *payload = pl.pallas_call(
        attend_kernel,
        in_specs=[SCALAR] + [ANY] * len(operands),
        out_specs=[WHOLE] * 3,
        out_shape=[shape((batch, width), F32)]
        + [shape((batch, size), BF16) for size in (half + LANES, half)],
        scratch_shapes=[pltpu.VMEM(size, a.dtype) for size, a in zip(held, operands)]
        + [pltpu.SemaphoreType.DMA((5 + 2 * (batch // BLOCK),))],
        compiler_params=params(28 * batch * width),
        cost_estimate=LIGHT,
    )(me, *operands)

    payload = pass_on(payload, BUSY)

    order = farthest_first(experts)
    chunks, arrived = [], []
    for part in range(2):
        came = {j: swap(payload[part], "attn", j) for j in farthest_first(layers)}
        chunks += [came[j] for j in range(layers)]
        slots = pl.pallas_call(
            functools.partial(split_kernel, layers=layers, part=part),
            in_specs=[SCALAR] + [WHOLE] * len(chunks),
            out_specs=[WHOLE] * experts,
            out_shape=[shape((layers * CAP, half), BF16)] * experts,
            cost_estimate=MID if part else LIGHT,
            compiler_params=params(experts * layers * CAP * half),
        )(me, *chunks)
        arrived.append([swap(slots[e], "expert", e) for e in order])
    gates = pl.pallas_call(
        functools.partial(weigh_kernel, layers=layers),
        in_specs=[SCALAR] + [WHOLE] * (1 + len(chunks)),
        out_specs=[WHOLE] * 2,
        out_shape=[shape((layers * batch, experts * layers * CAP), BF16)] * 2,
        cost_estimate=LIGHT,
        compiler_params=params(layers * batch * width),
    )(me, router, *chunks)

    total_rows = experts * layers * CAP
    units = gate_proj.shape[2]
    gate, up, down = gate_proj[0], up_proj[0], in_hbm(down_proj[0])
    rows = pltpu.VMEM((total_rows, half), BF16)
    strips = pltpu.SemaphoreType.DMA((STRIPS,))
    halves = [shape((layers * CAP, half), BF16)] * experts
    *sums, down_first = pl.pallas_call(
        functools.partial(begin_kernel, experts=experts),
        in_specs=[WHOLE] * experts + [ANY] + [WHOLE] * 2 + [ANY],
        out_specs=[WHOLE] * 3,
        out_shape=[shape((total_rows, units), F32)] * 2 + [pltpu.VMEM((units, half), BF16)],
        scratch_shapes=[rows, strips],
        cost_estimate=pl.CostEstimate(
            flops=4 * total_rows * half * units, bytes_accessed=0, transcendentals=0
        ),
        compiler_params=params(total_rows * width),
    )(*arrived[0], gates[0], gate, up, down)
    *first, hidden, down_second = pl.pallas_call(
        functools.partial(middle_kernel, experts=experts),
        in_specs=[WHOLE] * (experts + 5) + [ANY],
        out_specs=[WHOLE] * (experts + 2),
        out_shape=halves + [shape((total_rows, units), BF16), pltpu.VMEM((units, half), BF16)],
        scratch_shapes=[rows, strips],
        compiler_params=params(total_rows * width),
    )(*arrived[1], *sums, down_first, gate, up, down)
    second = pl.pallas_call(
        end_kernel,
        in_specs=[WHOLE] * 2,
        out_specs=[WHOLE] * experts,
        out_shape=halves,
        cost_estimate=pl.CostEstimate(
            flops=2 * total_rows * half * units, bytes_accessed=0, transcendentals=0
        ),
        compiler_params=params(total_rows * width),
    )(hidden, down_second)

    done = []
    for part, blocks in enumerate((first, second)):
        returned = [swap(block, "expert", e) for e, block in zip(order, blocks)]
        mixed = pl.pallas_call(
            functools.partial(mix_kernel, layers=layers, part=part),
            in_specs=[WHOLE] * (3 + experts),
            out_specs=[WHOLE] * layers,
            out_shape=[shape((batch, half), BF16 if j else F32) for j in range(layers)],
            cost_estimate=LIGHT,
            compiler_params=params(experts * layers * CAP * half),
        )(*gates, *returned, stream)
        sums = [swap(mixed[j], "attn", j) for j in farthest_first(layers)]
        done = [
            pl.pallas_call(
                add_kernel,
                in_specs=[WHOLE] * (layers + len(done)),
                out_specs=WHOLE,
                out_shape=shape((batch, width if part else half), BF16),
                cost_estimate=LIGHT,
                compiler_params=params(layers * batch * width),
            )(*done, *sums)
        ]
    return done[0]


def solution(mesh):
    in_specs = (
        P(("groups", "attn", "expert"), None),
        P(("groups", "attn", "expert"), None, None),
        P(("groups", "attn", "expert"), None, None),
        P(("groups", "attn", "expert")),
        P(("groups", "attn", "expert"), None),
        P(("groups", "attn", "expert"), None),
        P(),
        P(),
        P("expert", None, "attn"),
        P("expert", None, "attn"),
        P("expert", "attn", None),
    )
    out_specs = P(("groups", "attn", "expert"), None)
    return jax.shard_map(shards, mesh=mesh, in_specs=in_specs, out_specs=out_specs, check_vma=False)
```

```python
import functools

import jax
import jax.numpy as jnp
from jax import lax
from jax.experimental import pallas as pl
from jax.experimental.pallas import tpu as pltpu
from jax.sharding import PartitionSpec as P

HS = 128
KVH = 4
GROUP = 6
CAP = 8
LANES = 128
PAIR = 2
BLOCK = 8
STRIPS = 3
TILE = 256
UNROLL = 2
MIB = 1 << 20
F32 = jnp.float32
BF16 = jnp.bfloat16
LIGHT = pl.CostEstimate(flops=0, bytes_accessed=0, transcendentals=0)
BUSY = pl.CostEstimate(flops=24 * 10**9, bytes_accessed=0, transcendentals=0)
MID = pl.CostEstimate(flops=2 * 10**9, bytes_accessed=0, transcendentals=0)
ANY = pl.BlockSpec(memory_space=pl.ANY)
WHOLE = pl.BlockSpec(memory_space=pltpu.VMEM)
SCALAR = pl.BlockSpec(memory_space=pltpu.SMEM)


def dot(a, b, dims=((1,), (0,))):
    return lax.dot_general(a, b, (dims, ((), ())), preferred_element_type=F32)


def iota(shape, dim):
    return lax.broadcasted_iota(jnp.int32, shape, dim)


def split(index, size):
    if size & (size - 1):
        return lax.div(index, size), lax.rem(index, size)
    return index >> (size.bit_length() - 1), index & (size - 1)


def slot_map(me, named, chunks, experts):
    named = named[:, 0:4].astype(F32).astype(jnp.int32)
    owners, places = named[:, 0:2] ^ me, named[:, 2:4]
    rows, slots = named.shape[0], experts * chunks * CAP
    group, place = split(iota((rows, slots), 1), CAP)
    expert, chunk = split(group, chunks)
    taken = [(owners[:, k : k + 1] == expert) & (places[:, k : k + 1] == place) for k in range(2)]
    here = split(iota((rows, slots), 0), rows // chunks)[0] == chunk
    return taken[0] & here, taken[1] & here


def dispatch(me, rows, named, chunks, experts):
    first, second = slot_map(me, named, chunks, experts)
    table = jnp.where(first | second, 1.0, 0.0).astype(BF16)
    return dot(table, rows, ((0,), (0,)))


def weigh_kernel(me_ref, router_ref, *refs, layers):
    high_ref, low_ref = refs[-2:]
    parts, named = gather(refs[:-2], layers)
    rows = jnp.concatenate(parts, axis=1)
    routes = named[:, 0:2].astype(F32).astype(jnp.int32)
    logits = dot(rows, router_ref[...], ((1,), (1,)))
    experts = logits.shape[1]
    lane = iota(logits.shape, 1)
    first = jnp.sum(jnp.where(lane == routes[:, 0:1], logits, 0.0), axis=1, keepdims=True)
    second = jnp.sum(jnp.where(lane == routes[:, 1:2], logits, 0.0), axis=1, keepdims=True)
    gate0 = 1.0 / (1.0 + jnp.exp(second - first))
    gate1 = 1.0 / (1.0 + jnp.exp(first - second))
    taken = slot_map(me_ref[0], named, layers, experts)
    gates = jnp.where(taken[0], gate0, jnp.where(taken[1], gate1, 0.0))
    high = gates.astype(BF16)
    high_ref[...] = high
    low_ref[...] = (gates - high.astype(F32)).astype(BF16)


def attend_kernel(
    _, lengths_hbm, queries_hbm, keys_hbm, values_hbm, routes_hbm, residual_hbm, gain_hbm,
    stream_ref, first_ref, second_ref,
    lengths_ref, queries_ref, keys_ref, values_ref, routes_ref, residual_ref, gain_ref, sems,
):
    batch, window, _ = keys_ref.shape
    width = queries_ref.shape[1]
    span = width // KVH
    parts = [pl.ds(begin, PAIR * HS) for begin in range(0, KVH * HS, PAIR * HS)]
    small = [
        (lengths_hbm, lengths_ref), (queries_hbm, queries_ref), (routes_hbm, routes_ref),
        (residual_hbm, residual_ref), (gain_hbm, gain_ref),
    ]
    blocks = [pl.ds(begin, BLOCK) for begin in range(0, batch, BLOCK)]
    groups = [
        small[:3],
        *[[(keys_hbm.at[block], keys_ref.at[block])] for block in blocks],
        [(values_hbm.at[block], values_ref.at[block, 0:window]) for block in blocks],
        small[3:],
    ]
    at, copies = 0, []
    for group in groups:
        copies.append([])
        for source, target in group:
            copies[-1].append(pltpu.make_async_copy(source, target, sems.at[at]))
            copies[-1][-1].start()
            at += 1

    def wait(group):
        for copy in copies[group]:
            copy.wait()

    padded = values_ref.shape[1]
    if padded > window:
        pad = (batch, padded - window, values_ref.shape[2])
        values_ref[:, window:, :] = jnp.zeros(pad, BF16)
    wait(0)
    same = iota((batch, batch), 0) == iota((batch, batch), 1)

    def upright(row):
        return jnp.sum(jnp.where(same, row, 0), axis=1, keepdims=True)

    named, lane = jnp.zeros((batch, LANES), jnp.int32), iota((batch, LANES), 1)
    before = iota((batch, batch), 1) < iota((batch, batch), 0)
    listed = [routes_ref[k : k + 1, :] for k in range(2)]
    for k in range(2):
        route = upright(listed[k])
        earlier = before & ((listed[0] == route) | (listed[1] == route))
        place = jnp.sum(jnp.where(earlier, 1, 0), axis=1, keepdims=True)
        named = jnp.where(lane == k, route, jnp.where(lane == 2 + k, place, named))
    named = named.astype(F32).astype(BF16)
    queries = queries_ref[...]
    lanes = PAIR * GROUP * batch
    full = -(-lanes // LANES) * LANES
    _, request = split(iota((window, full), 1), batch)
    length = jnp.zeros((1, full), jnp.int32)
    for r in range(batch):
        length = jnp.where(request[0:1] == r, lengths_ref[0:1, r : r + 1], length)
    visible = iota((window, full), 0) < length
    _, owner = split(iota((lanes, padded), 0), batch)
    spreads = []
    for i in range(len(parts)):
        spread = []
        for k in range(PAIR):
            at = [(i * PAIR + k) * span + g * HS for g in range(GROUP)]
            stacked = jnp.concatenate([queries[:, c : c + HS] for c in at], axis=0)
            blank = jnp.zeros_like(stacked)
            spread.append(
                jnp.concatenate([stacked if j == k else blank for j in range(PAIR)], axis=1)
            )
        if full > lanes:
            spread.append(jnp.zeros((full - lanes, PAIR * HS), BF16))
        spreads.append(jnp.concatenate(spread, axis=0))
    total = [jnp.zeros((window, full), F32) for _ in parts]
    for b, block in enumerate(blocks):
        wait(1 + b)
        for i, part in enumerate(parts):
            keys = keys_ref[block, :, part].reshape(BLOCK * window, PAIR * HS)
            products = dot(keys, spreads[i], ((1,), (1,)))
            for r in range(BLOCK):
                mine = request == b * BLOCK + r
                total[i] = jnp.where(mine, products[r * window : (r + 1) * window], total[i])
    weighted = []
    for scores in total:
        scores = jnp.where(visible, scores * HS ** (-0.5), -1e30)
        powers = jnp.exp(scores - jnp.max(scores, axis=0, keepdims=True))
        weights = powers / jnp.sum(powers, axis=0, keepdims=True)
        if padded > window:
            weights = jnp.concatenate([weights, jnp.zeros((padded - window, full), F32)], axis=0)
        weights = weights.T[:lanes]
        weighted.append(
            jnp.concatenate(
                [jnp.where(owner == r, weights, 0.0).astype(BF16) for r in range(batch)], axis=1
            )
        )
    wait(-2)
    attended = []
    for weights, part in zip(weighted, parts):
        values = values_ref[:, :, part].reshape(batch * padded, PAIR * HS)
        mixed = dot(weights, values)
        attended += [
            mixed[h * batch : (h + 1) * batch, h // GROUP * HS : (h // GROUP + 1) * HS]
            for h in range(PAIR * GROUP)
        ]
    wait(-1)
    stream = residual_ref[...].astype(F32) + jnp.concatenate(attended, axis=1)
    scale = lax.rsqrt(jnp.mean(stream * stream, axis=1, keepdims=True) + 1e-05)
    stream_ref[...] = stream
    half = width // 2
    normed = (stream * scale * gain_ref[...]).astype(BF16)
    first_ref[:, :half] = normed[:, :half]
    first_ref[:, half:] = named
    second_ref[...] = normed[:, half:]


def pass_kernel(*_):
    pass


def pass_on(values, cost):
    return pl.pallas_call(
        pass_kernel,
        in_specs=[ANY] * len(values),
        out_specs=[ANY] * len(values),
        out_shape=[jax.ShapeDtypeStruct(value.shape, value.dtype) for value in values],
        input_output_aliases={i: i for i in range(len(values))},
        cost_estimate=cost,
        compiler_params=params(0),
    )(*values)


def stack(refs):
    return jnp.concatenate([ref[...] for ref in refs], axis=0)


def gather(refs, layers):
    first = stack(refs[:layers])
    half = first.shape[1] - LANES
    parts = [first[:, :half]] + [stack(refs[at : at + layers]) for at in range(layers, len(refs), layers)]
    return parts, first[:, half:]


def split_kernel(me_ref, *refs, layers, part):
    parts, named = gather(refs[: (1 + part) * layers], layers)
    outs = refs[(1 + part) * layers :]
    slots = dispatch(me_ref[0], parts[part], named, layers, len(outs))
    span = layers * CAP
    for e, ref in enumerate(outs):
        ref[...] = slots[e * span : (e + 1) * span].astype(BF16)


def strip_copies(source, begin, target, sems):
    strip = target.shape[1] // sems.shape[0]
    copies = [
        pltpu.make_async_copy(
            source.at[:, pl.ds(begin + c * strip, strip)],
            target.at[:, pl.ds(c * strip, strip)],
            sems.at[c],
        )
        for c in range(sems.shape[0])
    ]
    for copy in copies:
        copy.start()
    return copies


def tiles(count, tile):
    def run(body):
        @pl.loop(0, count // tile, unroll=UNROLL)
        def _(i):
            body(pl.ds(pl.multiple_of(i * tile, tile), tile))

    return run


def store_rows(outs, at, value):
    span = outs[0].shape[0]
    for e, ref in enumerate(outs):
        ref[:, at] = value[e * span : (e + 1) * span].astype(BF16)


def begin_kernel(*refs, experts):
    _, gate_ref, up_ref, down_hbm, gate_out, up_out, down_out, rows_ref, sems = refs[experts:]
    half = rows_ref.shape[1]
    copies = strip_copies(down_hbm, 0, down_out, sems)
    rows_ref[...] = stack(refs[:experts])
    units = gate_ref.shape[1]

    @tiles(units, min(TILE, units))
    def _(at):
        gate_out[:, at] = dot(rows_ref[...], gate_ref[:half, at])
        up_out[:, at] = dot(rows_ref[...], up_ref[:half, at])

    for copy in copies:
        copy.wait()


def middle_kernel(*refs, experts):
    gate_in, up_in, down_in, gate_ref, up_ref, down_hbm = refs[experts : experts + 6]
    outs = refs[experts + 6 : -4]
    hidden_ref, down_out, rows_ref, sems = refs[-4:]
    half = rows_ref.shape[1]
    copies = strip_copies(down_hbm, half, down_out, sems)
    rows_ref[...] = stack(refs[:experts])
    units = gate_ref.shape[1]

    @tiles(units, min(TILE, units))
    def _(at):
        gate = gate_in[:, at] + dot(rows_ref[...], gate_ref[half:, at])
        up = up_in[:, at] + dot(rows_ref[...], up_ref[half:, at])
        hidden_ref[:, at] = (jax.nn.silu(gate) * up).astype(BF16)

    @tiles(half, min(TILE, half))
    def _(at):
        store_rows(outs, at, dot(hidden_ref[...], down_in[:, at]))

    for copy in copies:
        copy.wait()


def end_kernel(hidden_ref, down_ref, *outs):
    half = down_ref.shape[1]

    @tiles(half, min(TILE, half))
    def _(at):
        store_rows(outs, at, dot(hidden_ref[...], down_ref[:, at]))


def mix_kernel(high_ref, low_ref, *refs, layers, part):
    outs, stream_ref = refs[-layers:], refs[-layers - 1]
    blocks = refs[: -layers - 1]
    order = farthest_first(len(blocks))
    returned = stack([blocks[order.index(e)] for e in range(len(blocks))])
    mixed = dot(high_ref[...], returned) + dot(low_ref[...], returned)
    batch, half = outs[0].shape
    for j, ref in enumerate(outs):
        value = mixed[j * batch : (j + 1) * batch]
        if j == 0:
            value = value + stream_ref[:, part * half : (part + 1) * half]
        ref[...] = value.astype(ref.dtype)


def add_kernel(*refs):
    out_ref = refs[-1]
    span = refs[-2].shape[1]
    if out_ref.shape[1] > span:
        out_ref[:, :span] = refs[0][...]
        refs = refs[1:]
    total = refs[0][...]
    for ref in refs[1:-1]:
        total = total + ref[...].astype(F32)
    out_ref[:, out_ref.shape[1] - span :] = total.astype(BF16)


def in_hbm(value):
    return pltpu.with_memory_space_constraint(value, pltpu.HBM)


def swap(value, axis, step):
    if step == 0:
        return value
    count = lax.axis_size(axis)
    return lax.ppermute(value, axis, [(i, i ^ step) for i in range(count)])


def farthest_first(count):
    return [0, *range(count - 1, 0, -1)]


def params(elements):
    return pltpu.CompilerParams(vmem_limit_bytes=min(48 * MIB, 2 * MIB + 10 * elements))


def shards(
    queries,
    cached_keys,
    cached_values,
    lengths,
    routes,
    residual,
    norm_gain,
    router,
    gate_proj,
    up_proj,
    down_proj,
):
    batch, width = queries.shape
    experts = router.shape[1]
    layers = lax.axis_size("attn")
    me = lax.axis_index("expert").astype(jnp.int32).reshape(1)
    router = router.T
    shape = jax.ShapeDtypeStruct
    operands = [
        in_hbm(a)
        for a in (
            lengths[None], queries, cached_keys, cached_values, routes.T, residual, norm_gain[None]
        )
    ]
    window, depth = cached_values.shape[1:]
    held = [a.shape for a in operands]
    held[3] = (batch, -(-window // LANES) * LANES, depth)
    half = width // 2
    stream, *payload = pl.pallas_call(
        attend_kernel,
        in_specs=[SCALAR] + [ANY] * len(operands),
        out_specs=[WHOLE] * 3,
        out_shape=[shape((batch, width), F32)]
        + [shape((batch, size), BF16) for size in (half + LANES, half)],
        scratch_shapes=[pltpu.VMEM(size, a.dtype) for size, a in zip(held, operands)]
        + [pltpu.SemaphoreType.DMA((5 + 2 * (batch // BLOCK),))],
        compiler_params=params(28 * batch * width),
        cost_estimate=LIGHT,
    )(me, *operands)

    payload = pass_on(payload, BUSY)

    order = farthest_first(experts)
    chunks, arrived = [], []
    for part in range(2):
        came = {j: swap(payload[part], "attn", j) for j in farthest_first(layers)}
        chunks += [came[j] for j in range(layers)]
        slots = pl.pallas_call(
            functools.partial(split_kernel, layers=layers, part=part),
            in_specs=[SCALAR] + [WHOLE] * len(chunks),
            out_specs=[WHOLE] * experts,
            out_shape=[shape((layers * CAP, half), BF16)] * experts,
            cost_estimate=MID if part else LIGHT,
            compiler_params=params(experts * layers * CAP * half),
        )(me, *chunks)
        arrived.append([swap(slots[e], "expert", e) for e in order])
    gates = pl.pallas_call(
        functools.partial(weigh_kernel, layers=layers),
        in_specs=[SCALAR] + [WHOLE] * (1 + len(chunks)),
        out_specs=[WHOLE] * 2,
        out_shape=[shape((layers * batch, experts * layers * CAP), BF16)] * 2,
        cost_estimate=LIGHT,
        compiler_params=params(layers * batch * width),
    )(me, router, *chunks)

    total_rows = experts * layers * CAP
    units = gate_proj.shape[2]
    gate, up, down = gate_proj[0], up_proj[0], in_hbm(down_proj[0])
    rows = pltpu.VMEM((total_rows, half), BF16)
    strips = pltpu.SemaphoreType.DMA((STRIPS,))
    halves = [shape((layers * CAP, half), BF16)] * experts
    *sums, down_first = pl.pallas_call(
        functools.partial(begin_kernel, experts=experts),
        in_specs=[WHOLE] * experts + [ANY] + [WHOLE] * 2 + [ANY],
        out_specs=[WHOLE] * 3,
        out_shape=[shape((total_rows, units), F32)] * 2 + [pltpu.VMEM((units, half), BF16)],
        scratch_shapes=[rows, strips],
        cost_estimate=pl.CostEstimate(
            flops=4 * total_rows * half * units, bytes_accessed=0, transcendentals=0
        ),
        compiler_params=params(total_rows * width),
    )(*arrived[0], gates[0], gate, up, down)
    *first, hidden, down_second = pl.pallas_call(
        functools.partial(middle_kernel, experts=experts),
        in_specs=[WHOLE] * (experts + 5) + [ANY],
        out_specs=[WHOLE] * (experts + 2),
        out_shape=halves + [shape((total_rows, units), BF16), pltpu.VMEM((units, half), BF16)],
        scratch_shapes=[rows, strips],
        compiler_params=params(total_rows * width),
    )(*arrived[1], *sums, down_first, gate, up, down)
    second = pl.pallas_call(
        end_kernel,
        in_specs=[WHOLE] * 2,
        out_specs=[WHOLE] * experts,
        out_shape=halves,
        cost_estimate=pl.CostEstimate(
            flops=2 * total_rows * half * units, bytes_accessed=0, transcendentals=0
        ),
        compiler_params=params(total_rows * width),
    )(hidden, down_second)

    done = []
    for part, blocks in enumerate((first, second)):
        returned = [swap(block, "expert", e) for e, block in zip(order, blocks)]
        mixed = pl.pallas_call(
            functools.partial(mix_kernel, layers=layers, part=part),
            in_specs=[WHOLE] * (3 + experts),
            out_specs=[WHOLE] * layers,
            out_shape=[shape((batch, half), BF16 if j else F32) for j in range(layers)],
            cost_estimate=LIGHT,
            compiler_params=params(experts * layers * CAP * half),
        )(*gates, *returned, stream)
        sums = [swap(mixed[j], "attn", j) for j in farthest_first(layers)]
        done = [
            pl.pallas_call(
                add_kernel,
                in_specs=[WHOLE] * (layers + len(done)),
                out_specs=WHOLE,
                out_shape=shape((batch, width if part else half), BF16),
                cost_estimate=LIGHT,
                compiler_params=params(layers * batch * width),
            )(*done, *sums)
        ]
    return done[0]


def solution(mesh):
    in_specs = (
        P(("groups", "attn", "expert"), None),
        P(("groups", "attn", "expert"), None, None),
        P(("groups", "attn", "expert"), None, None),
        P(("groups", "attn", "expert")),
        P(("groups", "attn", "expert"), None),
        P(("groups", "attn", "expert"), None),
        P(),
        P(),
        P("expert", None, "attn"),
        P("expert", None, "attn"),
        P("expert", "attn", None),
    )
    out_specs = P(("groups", "attn", "expert"), None)
    return jax.shard_map(shards, mesh=mesh, in_specs=in_specs, out_specs=out_specs, check_vma=False)
```

```python
import functools

import jax
import jax.numpy as jnp
from jax import lax
from jax.experimental import pallas as pl
from jax.experimental.pallas import tpu as pltpu
from jax.sharding import PartitionSpec as P

HS = 128
KVH = 4
GROUP = 6
CAP = 8
LANES = 128
PAIR = 2
BLOCK = 8
STRIPS = 3
TILE = 256
UNROLL = 2
MIB = 1 << 20
F32 = jnp.float32
BF16 = jnp.bfloat16
LIGHT = pl.CostEstimate(flops=0, bytes_accessed=0, transcendentals=0)
BUSY = pl.CostEstimate(flops=24 * 10**9, bytes_accessed=0, transcendentals=0)
MID = pl.CostEstimate(flops=2 * 10**9, bytes_accessed=0, transcendentals=0)
ANY = pl.BlockSpec(memory_space=pl.ANY)
WHOLE = pl.BlockSpec(memory_space=pltpu.VMEM)
SCALAR = pl.BlockSpec(memory_space=pltpu.SMEM)


def dot(a, b, dims=((1,), (0,))):
    return lax.dot_general(a, b, (dims, ((), ())), preferred_element_type=F32)


def iota(shape, dim):
    return lax.broadcasted_iota(jnp.int32, shape, dim)


def split(index, size):
    if size & (size - 1):
        return lax.div(index, size), lax.rem(index, size)
    return index >> (size.bit_length() - 1), index & (size - 1)


def slot_map(me, named, chunks, experts):
    named = named[:, 0:4].astype(F32).astype(jnp.int32)
    owners, places = named[:, 0:2] ^ me, named[:, 2:4]
    rows, slots = named.shape[0], experts * chunks * CAP
    group, place = split(iota((rows, slots), 1), CAP)
    expert, chunk = split(group, chunks)
    taken = [(owners[:, k : k + 1] == expert) & (places[:, k : k + 1] == place) for k in range(2)]
    here = split(iota((rows, slots), 0), rows // chunks)[0] == chunk
    return taken[0] & here, taken[1] & here


def dispatch(me, rows, named, chunks, experts):
    first, second = slot_map(me, named, chunks, experts)
    table = jnp.where(first | second, 1.0, 0.0).astype(BF16)
    return dot(table, rows, ((0,), (0,)))


def weigh_kernel(me_ref, router_ref, *refs, layers):
    high_ref, low_ref = refs[-2:]
    parts, named = gather(refs[:-2], layers)
    rows = jnp.concatenate(parts, axis=1)
    routes = named[:, 0:2].astype(F32).astype(jnp.int32)
    logits = dot(rows, router_ref[...], ((1,), (1,)))
    experts = logits.shape[1]
    lane = iota(logits.shape, 1)
    first = jnp.sum(jnp.where(lane == routes[:, 0:1], logits, 0.0), axis=1, keepdims=True)
    second = jnp.sum(jnp.where(lane == routes[:, 1:2], logits, 0.0), axis=1, keepdims=True)
    gate0 = 1.0 / (1.0 + jnp.exp(second - first))
    gate1 = 1.0 / (1.0 + jnp.exp(first - second))
    taken = slot_map(me_ref[0], named, layers, experts)
    gates = jnp.where(taken[0], gate0, jnp.where(taken[1], gate1, 0.0))
    high = gates.astype(BF16)
    high_ref[...] = high
    low_ref[...] = (gates - high.astype(F32)).astype(BF16)


def attend_kernel(
    _, lengths_hbm, queries_hbm, keys_hbm, values_hbm, routes_hbm, residual_hbm, gain_hbm,
    stream_ref, first_ref, second_ref,
    lengths_ref, queries_ref, keys_ref, values_ref, routes_ref, residual_ref, gain_ref, sems,
):
    batch, window, _ = keys_ref.shape
    width = queries_ref.shape[1]
    span = width // KVH
    parts = [pl.ds(begin, PAIR * HS) for begin in range(0, KVH * HS, PAIR * HS)]
    small = [
        (lengths_hbm, lengths_ref), (queries_hbm, queries_ref), (routes_hbm, routes_ref),
        (residual_hbm, residual_ref), (gain_hbm, gain_ref),
    ]
    blocks = [pl.ds(begin, BLOCK) for begin in range(0, batch, BLOCK)]
    groups = [
        small[:3],
        *[[(keys_hbm.at[block], keys_ref.at[block])] for block in blocks],
        [(values_hbm.at[block], values_ref.at[block, 0:window]) for block in blocks],
        small[3:],
    ]
    at, copies = 0, []
    for group in groups:
        copies.append([])
        for source, target in group:
            copies[-1].append(pltpu.make_async_copy(source, target, sems.at[at]))
            copies[-1][-1].start()
            at += 1

    def wait(group):
        for copy in copies[group]:
            copy.wait()

    padded = values_ref.shape[1]
    if padded > window:
        pad = (batch, padded - window, values_ref.shape[2])
        values_ref[:, window:, :] = jnp.zeros(pad, BF16)
    wait(0)
    same = iota((batch, batch), 0) == iota((batch, batch), 1)

    def upright(row):
        return jnp.sum(jnp.where(same, row, 0), axis=1, keepdims=True)

    named, lane = jnp.zeros((batch, LANES), jnp.int32), iota((batch, LANES), 1)
    before = iota((batch, batch), 1) < iota((batch, batch), 0)
    listed = [routes_ref[k : k + 1, :] for k in range(2)]
    for k in range(2):
        route = upright(listed[k])
        earlier = before & ((listed[0] == route) | (listed[1] == route))
        place = jnp.sum(jnp.where(earlier, 1, 0), axis=1, keepdims=True)
        named = jnp.where(lane == k, route, jnp.where(lane == 2 + k, place, named))
    named = named.astype(F32).astype(BF16)
    queries = queries_ref[...]
    lanes = PAIR * GROUP * batch
    full = -(-lanes // LANES) * LANES
    _, request = split(iota((window, full), 1), batch)
    length = jnp.zeros((1, full), jnp.int32)
    for r in range(batch):
        length = jnp.where(request[0:1] == r, lengths_ref[0:1, r : r + 1], length)
    visible = iota((window, full), 0) < length
    _, owner = split(iota((lanes, padded), 0), batch)
    spreads = []
    for i in range(len(parts)):
        spread = []
        for k in range(PAIR):
            at = [(i * PAIR + k) * span + g * HS for g in range(GROUP)]
            stacked = jnp.concatenate([queries[:, c : c + HS] for c in at], axis=0)
            blank = jnp.zeros_like(stacked)
            spread.append(
                jnp.concatenate([stacked if j == k else blank for j in range(PAIR)], axis=1)
            )
        if full > lanes:
            spread.append(jnp.zeros((full - lanes, PAIR * HS), BF16))
        spreads.append(jnp.concatenate(spread, axis=0))
    total = [jnp.zeros((window, full), F32) for _ in parts]
    for b, block in enumerate(blocks):
        wait(1 + b)
        for i, part in enumerate(parts):
            keys = keys_ref[block, :, part].reshape(BLOCK * window, PAIR * HS)
            products = dot(keys, spreads[i], ((1,), (1,)))
            for r in range(BLOCK):
                mine = request == b * BLOCK + r
                total[i] = jnp.where(mine, products[r * window : (r + 1) * window], total[i])
    weighted = []
    for scores in total:
        scores = jnp.where(visible, scores * HS ** (-0.5), -1e30)
        powers = jnp.exp(scores - jnp.max(scores, axis=0, keepdims=True))
        weights = powers / jnp.sum(powers, axis=0, keepdims=True)
        if padded > window:
            weights = jnp.concatenate([weights, jnp.zeros((padded - window, full), F32)], axis=0)
        weights = weights.T[:lanes]
        weighted.append(
            jnp.concatenate(
                [jnp.where(owner == r, weights, 0.0).astype(BF16) for r in range(batch)], axis=1
            )
        )
    wait(-2)
    attended = []
    for weights, part in zip(weighted, parts):
        values = values_ref[:, :, part].reshape(batch * padded, PAIR * HS)
        mixed = dot(weights, values)
        attended += [
            mixed[h * batch : (h + 1) * batch, h // GROUP * HS : (h // GROUP + 1) * HS]
            for h in range(PAIR * GROUP)
        ]
    wait(-1)
    stream = residual_ref[...].astype(F32) + jnp.concatenate(attended, axis=1)
    scale = lax.rsqrt(jnp.mean(stream * stream, axis=1, keepdims=True) + 1e-05)
    stream_ref[...] = stream
    half = width // 2
    normed = (stream * scale * gain_ref[...]).astype(BF16)
    first_ref[:, :half] = normed[:, :half]
    first_ref[:, half:] = named
    second_ref[...] = normed[:, half:]


def pass_kernel(*_):
    pass


def pass_on(values, cost):
    return pl.pallas_call(
        pass_kernel,
        in_specs=[ANY] * len(values),
        out_specs=[ANY] * len(values),
        out_shape=[jax.ShapeDtypeStruct(value.shape, value.dtype) for value in values],
        input_output_aliases={i: i for i in range(len(values))},
        cost_estimate=cost,
        compiler_params=params(0),
    )(*values)


def stack(refs):
    return jnp.concatenate([ref[...] for ref in refs], axis=0)


def gather(refs, layers):
    first = stack(refs[:layers])
    half = first.shape[1] - LANES
    parts = [first[:, :half]] + [stack(refs[at : at + layers]) for at in range(layers, len(refs), layers)]
    return parts, first[:, half:]


def split_kernel(me_ref, *refs, layers, part):
    parts, named = gather(refs[: (1 + part) * layers], layers)
    outs = refs[(1 + part) * layers :]
    slots = dispatch(me_ref[0], parts[part], named, layers, len(outs))
    span = layers * CAP
    for e, ref in enumerate(outs):
        ref[...] = slots[e * span : (e + 1) * span].astype(BF16)


def strip_copies(source, begin, target, sems):
    strip = target.shape[1] // sems.shape[0]
    copies = [
        pltpu.make_async_copy(
            source.at[:, pl.ds(begin + c * strip, strip)],
            target.at[:, pl.ds(c * strip, strip)],
            sems.at[c],
        )
        for c in range(sems.shape[0])
    ]
    for copy in copies:
        copy.start()
    return copies


def tiles(count, tile):
    def run(body):
        @pl.loop(0, count // tile, unroll=UNROLL)
        def _(i):
            body(pl.ds(pl.multiple_of(i * tile, tile), tile))

    return run


def store_rows(outs, at, value):
    span = outs[0].shape[0]
    for e, ref in enumerate(outs):
        ref[:, at] = value[e * span : (e + 1) * span].astype(BF16)


def begin_kernel(*refs, experts):
    _, gate_ref, up_ref, down_hbm, gate_out, up_out, down_out, rows_ref, sems = refs[experts:]
    half = rows_ref.shape[1]
    copies = strip_copies(down_hbm, 0, down_out, sems)
    rows_ref[...] = stack(refs[:experts])
    units = gate_ref.shape[1]

    @tiles(units, min(TILE, units))
    def _(at):
        gate_out[:, at] = dot(rows_ref[...], gate_ref[:half, at])
        up_out[:, at] = dot(rows_ref[...], up_ref[:half, at])

    for copy in copies:
        copy.wait()


def middle_kernel(*refs, experts):
    gate_in, up_in, down_in, gate_ref, up_ref, down_hbm = refs[experts : experts + 6]
    outs = refs[experts + 6 : -4]
    hidden_ref, down_out, rows_ref, sems = refs[-4:]
    half = rows_ref.shape[1]
    copies = strip_copies(down_hbm, half, down_out, sems)
    rows_ref[...] = stack(refs[:experts])
    units = gate_ref.shape[1]

    @tiles(units, min(TILE, units))
    def _(at):
        gate = gate_in[:, at] + dot(rows_ref[...], gate_ref[half:, at])
        up = up_in[:, at] + dot(rows_ref[...], up_ref[half:, at])
        hidden_ref[:, at] = (jax.nn.silu(gate) * up).astype(BF16)

    @tiles(half, min(TILE, half))
    def _(at):
        store_rows(outs, at, dot(hidden_ref[...], down_in[:, at]))

    for copy in copies:
        copy.wait()


def end_kernel(hidden_ref, down_ref, *outs):
    half = down_ref.shape[1]

    @tiles(half, min(TILE, half))
    def _(at):
        store_rows(outs, at, dot(hidden_ref[...], down_ref[:, at]))


def mix_kernel(high_ref, low_ref, *refs, layers, part):
    outs, stream_ref = refs[-layers:], refs[-layers - 1]
    blocks = refs[: -layers - 1]
    order = same_core_first(len(blocks))
    returned = stack([blocks[order.index(e)] for e in range(len(blocks))])
    mixed = dot(high_ref[...], returned) + dot(low_ref[...], returned)
    batch, half = outs[0].shape
    for j, ref in enumerate(outs):
        value = mixed[j * batch : (j + 1) * batch]
        if j == 0:
            value = value + stream_ref[:, part * half : (part + 1) * half]
        ref[...] = value.astype(ref.dtype)


def add_kernel(*refs):
    out_ref = refs[-1]
    span = refs[-2].shape[1]
    if out_ref.shape[1] > span:
        out_ref[:, :span] = refs[0][...]
        refs = refs[1:]
    total = refs[0][...]
    for ref in refs[1:-1]:
        total = total + ref[...].astype(F32)
    out_ref[:, out_ref.shape[1] - span :] = total.astype(BF16)


def in_hbm(value):
    return pltpu.with_memory_space_constraint(value, pltpu.HBM)


def swap(value, axis, step):
    if step == 0:
        return value
    count = lax.axis_size(axis)
    return lax.ppermute(value, axis, [(i, i ^ step) for i in range(count)])


def farthest_first(count):
    return [0, *range(count - 1, 0, -1)]


def same_core_first(count):
    return [*range(0, count, 2), *range(count - 1, 0, -2)]


def params(elements):
    return pltpu.CompilerParams(vmem_limit_bytes=min(48 * MIB, 2 * MIB + 10 * elements))


def shards(
    queries,
    cached_keys,
    cached_values,
    lengths,
    routes,
    residual,
    norm_gain,
    router,
    gate_proj,
    up_proj,
    down_proj,
):
    batch, width = queries.shape
    experts = router.shape[1]
    layers = lax.axis_size("attn")
    me = lax.axis_index("expert").astype(jnp.int32).reshape(1)
    router = router.T
    shape = jax.ShapeDtypeStruct
    operands = [
        in_hbm(a)
        for a in (
            lengths[None], queries, cached_keys, cached_values, routes.T, residual, norm_gain[None]
        )
    ]
    window, depth = cached_values.shape[1:]
    held = [a.shape for a in operands]
    held[3] = (batch, -(-window // LANES) * LANES, depth)
    half = width // 2
    stream, *payload = pl.pallas_call(
        attend_kernel,
        in_specs=[SCALAR] + [ANY] * len(operands),
        out_specs=[WHOLE] * 3,
        out_shape=[shape((batch, width), F32)]
        + [shape((batch, size), BF16) for size in (half + LANES, half)],
        scratch_shapes=[pltpu.VMEM(size, a.dtype) for size, a in zip(held, operands)]
        + [pltpu.SemaphoreType.DMA((5 + 2 * (batch // BLOCK),))],
        compiler_params=params(28 * batch * width),
        cost_estimate=LIGHT,
    )(me, *operands)

    payload = pass_on(payload, BUSY)

    order = same_core_first(experts)
    chunks, arrived = [], []
    for part in range(2):
        came = {j: swap(payload[part], "attn", j) for j in farthest_first(layers)}
        chunks += [came[j] for j in range(layers)]
        slots = pl.pallas_call(
            functools.partial(split_kernel, layers=layers, part=part),
            in_specs=[SCALAR] + [WHOLE] * len(chunks),
            out_specs=[WHOLE] * experts,
            out_shape=[shape((layers * CAP, half), BF16)] * experts,
            cost_estimate=MID if part else LIGHT,
            compiler_params=params(experts * layers * CAP * half),
        )(me, *chunks)
        arrived.append([swap(slots[e], "expert", e) for e in order])
    gates = pl.pallas_call(
        functools.partial(weigh_kernel, layers=layers),
        in_specs=[SCALAR] + [WHOLE] * (1 + len(chunks)),
        out_specs=[WHOLE] * 2,
        out_shape=[shape((layers * batch, experts * layers * CAP), BF16)] * 2,
        cost_estimate=LIGHT,
        compiler_params=params(layers * batch * width),
    )(me, router, *chunks)

    total_rows = experts * layers * CAP
    units = gate_proj.shape[2]
    gate, up, down = gate_proj[0], up_proj[0], in_hbm(down_proj[0])
    rows = pltpu.VMEM((total_rows, half), BF16)
    strips = pltpu.SemaphoreType.DMA((STRIPS,))
    halves = [shape((layers * CAP, half), BF16)] * experts
    *sums, down_first = pl.pallas_call(
        functools.partial(begin_kernel, experts=experts),
        in_specs=[WHOLE] * experts + [ANY] + [WHOLE] * 2 + [ANY],
        out_specs=[WHOLE] * 3,
        out_shape=[shape((total_rows, units), F32)] * 2 + [pltpu.VMEM((units, half), BF16)],
        scratch_shapes=[rows, strips],
        cost_estimate=pl.CostEstimate(
            flops=4 * total_rows * half * units, bytes_accessed=0, transcendentals=0
        ),
        compiler_params=params(total_rows * width),
    )(*arrived[0], gates[0], gate, up, down)
    *first, hidden, down_second = pl.pallas_call(
        functools.partial(middle_kernel, experts=experts),
        in_specs=[WHOLE] * (experts + 5) + [ANY],
        out_specs=[WHOLE] * (experts + 2),
        out_shape=halves + [shape((total_rows, units), BF16), pltpu.VMEM((units, half), BF16)],
        scratch_shapes=[rows, strips],
        compiler_params=params(total_rows * width),
    )(*arrived[1], *sums, down_first, gate, up, down)
    second = pl.pallas_call(
        end_kernel,
        in_specs=[WHOLE] * 2,
        out_specs=[WHOLE] * experts,
        out_shape=halves,
        cost_estimate=pl.CostEstimate(
            flops=2 * total_rows * half * units, bytes_accessed=0, transcendentals=0
        ),
        compiler_params=params(total_rows * width),
    )(hidden, down_second)

    done = []
    for part, blocks in enumerate((first, second)):
        returned = [swap(block, "expert", e) for e, block in zip(order, blocks)]
        mixed = pl.pallas_call(
            functools.partial(mix_kernel, layers=layers, part=part),
            in_specs=[WHOLE] * (3 + experts),
            out_specs=[WHOLE] * layers,
            out_shape=[shape((batch, half), BF16 if j else F32) for j in range(layers)],
            cost_estimate=LIGHT,
            compiler_params=params(experts * layers * CAP * half),
        )(*gates, *returned, stream)
        sums = [swap(mixed[j], "attn", j) for j in farthest_first(layers)]
        done = [
            pl.pallas_call(
                add_kernel,
                in_specs=[WHOLE] * (layers + len(done)),
                out_specs=WHOLE,
                out_shape=shape((batch, width if part else half), BF16),
                cost_estimate=LIGHT,
                compiler_params=params(layers * batch * width),
            )(*done, *sums)
        ]
    return done[0]


def solution(mesh):
    in_specs = (
        P(("groups", "attn", "expert"), None),
        P(("groups", "attn", "expert"), None, None),
        P(("groups", "attn", "expert"), None, None),
        P(("groups", "attn", "expert")),
        P(("groups", "attn", "expert"), None),
        P(("groups", "attn", "expert"), None),
        P(),
        P(),
        P("expert", None, "attn"),
        P("expert", None, "attn"),
        P("expert", "attn", None),
    )
    out_specs = P(("groups", "attn", "expert"), None)
    return jax.shard_map(shards, mesh=mesh, in_specs=in_specs, out_specs=out_specs, check_vma=False)
```

```python
import functools

import jax
import jax.numpy as jnp
from jax import lax
from jax.experimental import pallas as pl
from jax.experimental.pallas import tpu as pltpu
from jax.sharding import PartitionSpec as P

HS = 128
KVH = 4
GROUP = 6
CAP = 8
LANES = 128
PAIR = 2
BLOCK = 8
STRIPS = 3
TILE = 256
UNROLL = 2
MIB = 1 << 20
F32 = jnp.float32
BF16 = jnp.bfloat16
LIGHT = pl.CostEstimate(flops=0, bytes_accessed=0, transcendentals=0)
BUSY = pl.CostEstimate(flops=24 * 10**9, bytes_accessed=0, transcendentals=0)
MID = pl.CostEstimate(flops=2 * 10**9, bytes_accessed=0, transcendentals=0)
ANY = pl.BlockSpec(memory_space=pl.ANY)
WHOLE = pl.BlockSpec(memory_space=pltpu.VMEM)
SCALAR = pl.BlockSpec(memory_space=pltpu.SMEM)


def dot(a, b, dims=((1,), (0,))):
    return lax.dot_general(a, b, (dims, ((), ())), preferred_element_type=F32)


def iota(shape, dim):
    return lax.broadcasted_iota(jnp.int32, shape, dim)


def split(index, size):
    if size & (size - 1):
        return lax.div(index, size), lax.rem(index, size)
    return index >> (size.bit_length() - 1), index & (size - 1)


def slot_map(me, named, chunks, experts):
    named = named[:, 0:4].astype(F32).astype(jnp.int32)
    owners, places = named[:, 0:2] ^ me, named[:, 2:4]
    rows, slots = named.shape[0], experts * chunks * CAP
    group, place = split(iota((rows, slots), 1), CAP)
    expert, chunk = split(group, chunks)
    taken = [(owners[:, k : k + 1] == expert) & (places[:, k : k + 1] == place) for k in range(2)]
    here = split(iota((rows, slots), 0), rows // chunks)[0] == chunk
    return taken[0] & here, taken[1] & here


def dispatch(me, rows, named, chunks, experts):
    first, second = slot_map(me, named, chunks, experts)
    table = jnp.where(first | second, 1.0, 0.0).astype(BF16)
    return dot(table, rows, ((0,), (0,)))


def weigh_kernel(me_ref, router_ref, *refs, layers):
    high_ref, low_ref = refs[-2:]
    parts, named = gather(refs[:-2], layers)
    rows = jnp.concatenate(parts, axis=1)
    routes = named[:, 0:2].astype(F32).astype(jnp.int32)
    logits = dot(rows, router_ref[...], ((1,), (1,)))
    experts = logits.shape[1]
    lane = iota(logits.shape, 1)
    first = jnp.sum(jnp.where(lane == routes[:, 0:1], logits, 0.0), axis=1, keepdims=True)
    second = jnp.sum(jnp.where(lane == routes[:, 1:2], logits, 0.0), axis=1, keepdims=True)
    gate0 = 1.0 / (1.0 + jnp.exp(second - first))
    gate1 = 1.0 / (1.0 + jnp.exp(first - second))
    taken = slot_map(me_ref[0], named, layers, experts)
    gates = jnp.where(taken[0], gate0, jnp.where(taken[1], gate1, 0.0))
    high = gates.astype(BF16)
    high_ref[...] = high
    low_ref[...] = (gates - high.astype(F32)).astype(BF16)


def attend_kernel(
    _, lengths_hbm, queries_hbm, keys_hbm, values_hbm, routes_hbm, residual_hbm, gain_hbm,
    stream_ref, first_ref, second_ref,
    lengths_ref, queries_ref, keys_ref, values_ref, routes_ref, residual_ref, gain_ref, sems,
):
    batch, window, _ = keys_ref.shape
    width = queries_ref.shape[1]
    span = width // KVH
    parts = [pl.ds(begin, PAIR * HS) for begin in range(0, KVH * HS, PAIR * HS)]
    small = [
        (lengths_hbm, lengths_ref), (queries_hbm, queries_ref), (routes_hbm, routes_ref),
        (residual_hbm, residual_ref), (gain_hbm, gain_ref),
    ]
    blocks = [pl.ds(begin, BLOCK) for begin in range(0, batch, BLOCK)]
    groups = [
        small[:3],
        *[[(keys_hbm.at[block], keys_ref.at[block])] for block in blocks],
        *[[(values_hbm.at[block], values_ref.at[block, 0:window])] for block in blocks],
        small[3:],
    ]
    at, copies = 0, []
    for group in groups:
        copies.append([])
        for source, target in group:
            copies[-1].append(pltpu.make_async_copy(source, target, sems.at[at]))
            copies[-1][-1].start()
            at += 1

    def wait(group):
        for copy in copies[group]:
            copy.wait()

    padded = values_ref.shape[1]
    if padded > window:
        pad = (batch, padded - window, values_ref.shape[2])
        values_ref[:, window:, :] = jnp.zeros(pad, BF16)
    wait(0)
    same = iota((batch, batch), 0) == iota((batch, batch), 1)

    def upright(row):
        return jnp.sum(jnp.where(same, row, 0), axis=1, keepdims=True)

    named, lane = jnp.zeros((batch, LANES), jnp.int32), iota((batch, LANES), 1)
    before = iota((batch, batch), 1) < iota((batch, batch), 0)
    listed = [routes_ref[k : k + 1, :] for k in range(2)]
    for k in range(2):
        route = upright(listed[k])
        earlier = before & ((listed[0] == route) | (listed[1] == route))
        place = jnp.sum(jnp.where(earlier, 1, 0), axis=1, keepdims=True)
        named = jnp.where(lane == k, route, jnp.where(lane == 2 + k, place, named))
    named = named.astype(F32).astype(BF16)
    queries = queries_ref[...]
    lanes = PAIR * GROUP * batch
    full = -(-lanes // LANES) * LANES
    _, request = split(iota((window, full), 1), batch)
    length = jnp.zeros((1, full), jnp.int32)
    for r in range(batch):
        length = jnp.where(request[0:1] == r, lengths_ref[0:1, r : r + 1], length)
    visible = iota((window, full), 0) < length
    _, owner = split(iota((lanes, padded), 0), batch)
    spreads = []
    for i in range(len(parts)):
        spread = []
        for k in range(PAIR):
            at = [(i * PAIR + k) * span + g * HS for g in range(GROUP)]
            stacked = jnp.concatenate([queries[:, c : c + HS] for c in at], axis=0)
            blank = jnp.zeros_like(stacked)
            spread.append(
                jnp.concatenate([stacked if j == k else blank for j in range(PAIR)], axis=1)
            )
        if full > lanes:
            spread.append(jnp.zeros((full - lanes, PAIR * HS), BF16))
        spreads.append(jnp.concatenate(spread, axis=0))
    total = [jnp.zeros((window, full), F32) for _ in parts]
    for b, block in enumerate(blocks):
        wait(1 + b)
        for i, part in enumerate(parts):
            keys = keys_ref[block, :, part].reshape(BLOCK * window, PAIR * HS)
            products = dot(keys, spreads[i], ((1,), (1,)))
            for r in range(BLOCK):
                mine = request == b * BLOCK + r
                total[i] = jnp.where(mine, products[r * window : (r + 1) * window], total[i])
    weighted = []
    for scores in total:
        scores = jnp.where(visible, scores * HS ** (-0.5), -1e30)
        powers = jnp.exp(scores - jnp.max(scores, axis=0, keepdims=True))
        weights = powers / jnp.sum(powers, axis=0, keepdims=True)
        if padded > window:
            weights = jnp.concatenate([weights, jnp.zeros((padded - window, full), F32)], axis=0)
        weights = weights.T[:lanes]
        weighted.append(
            jnp.concatenate(
                [jnp.where(owner == r, weights, 0.0).astype(BF16) for r in range(batch)], axis=1
            )
        )
    mixed = [0.0] * len(parts)
    reach = BLOCK * padded
    for b, block in enumerate(blocks):
        wait(1 + len(blocks) + b)
        for i, part in enumerate(parts):
            values = values_ref[block, :, part].reshape(reach, PAIR * HS)
            mixed[i] = mixed[i] + dot(weighted[i][:, b * reach : (b + 1) * reach], values)
    attended = [
        block[h * batch : (h + 1) * batch, h // GROUP * HS : (h // GROUP + 1) * HS]
        for block in mixed
        for h in range(PAIR * GROUP)
    ]
    wait(-1)
    stream = residual_ref[...].astype(F32) + jnp.concatenate(attended, axis=1)
    scale = lax.rsqrt(jnp.mean(stream * stream, axis=1, keepdims=True) + 1e-05)
    stream_ref[...] = stream
    half = width // 2
    normed = (stream * scale * gain_ref[...]).astype(BF16)
    first_ref[:, :half] = normed[:, :half]
    first_ref[:, half:] = named
    second_ref[...] = normed[:, half:]


def pass_kernel(*_):
    pass


def pass_on(values, cost):
    return pl.pallas_call(
        pass_kernel,
        in_specs=[ANY] * len(values),
        out_specs=[ANY] * len(values),
        out_shape=[jax.ShapeDtypeStruct(value.shape, value.dtype) for value in values],
        input_output_aliases={i: i for i in range(len(values))},
        cost_estimate=cost,
        compiler_params=params(0),
    )(*values)


def stack(refs):
    return jnp.concatenate([ref[...] for ref in refs], axis=0)


def gather(refs, layers):
    first = stack(refs[:layers])
    half = first.shape[1] - LANES
    parts = [first[:, :half]] + [stack(refs[at : at + layers]) for at in range(layers, len(refs), layers)]
    return parts, first[:, half:]


def split_kernel(me_ref, *refs, layers, part):
    parts, named = gather(refs[: (1 + part) * layers], layers)
    outs = refs[(1 + part) * layers :]
    slots = dispatch(me_ref[0], parts[part], named, layers, len(outs))
    span = layers * CAP
    for e, ref in enumerate(outs):
        ref[...] = slots[e * span : (e + 1) * span].astype(BF16)


def strip_copies(source, begin, target, sems):
    strip = target.shape[1] // sems.shape[0]
    copies = [
        pltpu.make_async_copy(
            source.at[:, pl.ds(begin + c * strip, strip)],
            target.at[:, pl.ds(c * strip, strip)],
            sems.at[c],
        )
        for c in range(sems.shape[0])
    ]
    for copy in copies:
        copy.start()
    return copies


def tiles(count, tile):
    def run(body):
        @pl.loop(0, count // tile, unroll=UNROLL)
        def _(i):
            body(pl.ds(pl.multiple_of(i * tile, tile), tile))

    return run


def store_rows(outs, at, value):
    span = outs[0].shape[0]
    for e, ref in enumerate(outs):
        ref[:, at] = value[e * span : (e + 1) * span].astype(BF16)


def begin_kernel(*refs, experts):
    _, gate_ref, up_ref, down_hbm, gate_out, up_out, down_out, rows_ref, sems = refs[experts:]
    half = rows_ref.shape[1]
    copies = strip_copies(down_hbm, 0, down_out, sems)
    rows_ref[...] = stack(refs[:experts])
    units = gate_ref.shape[1]

    @tiles(units, min(TILE, units))
    def _(at):
        gate_out[:, at] = dot(rows_ref[...], gate_ref[:half, at])
        up_out[:, at] = dot(rows_ref[...], up_ref[:half, at])

    for copy in copies:
        copy.wait()


def middle_kernel(*refs, experts):
    gate_in, up_in, down_in, gate_ref, up_ref, down_hbm = refs[experts : experts + 6]
    outs = refs[experts + 6 : -4]
    hidden_ref, down_out, rows_ref, sems = refs[-4:]
    half = rows_ref.shape[1]
    copies = strip_copies(down_hbm, half, down_out, sems)
    rows_ref[...] = stack(refs[:experts])
    units = gate_ref.shape[1]

    @tiles(units, min(TILE, units))
    def _(at):
        gate = gate_in[:, at] + dot(rows_ref[...], gate_ref[half:, at])
        up = up_in[:, at] + dot(rows_ref[...], up_ref[half:, at])
        hidden_ref[:, at] = (jax.nn.silu(gate) * up).astype(BF16)

    @tiles(half, min(TILE, half))
    def _(at):
        store_rows(outs, at, dot(hidden_ref[...], down_in[:, at]))

    for copy in copies:
        copy.wait()


def end_kernel(hidden_ref, down_ref, *outs):
    half = down_ref.shape[1]

    @tiles(half, min(TILE, half))
    def _(at):
        store_rows(outs, at, dot(hidden_ref[...], down_ref[:, at]))


def mix_kernel(high_ref, low_ref, *refs, layers, part):
    outs, stream_ref = refs[-layers:], refs[-layers - 1]
    blocks = refs[: -layers - 1]
    order = even_first(len(blocks))
    returned = stack([blocks[order.index(e)] for e in range(len(blocks))])
    mixed = dot(high_ref[...], returned) + dot(low_ref[...], returned)
    batch, half = outs[0].shape
    for j, ref in enumerate(outs):
        value = mixed[j * batch : (j + 1) * batch]
        if j == 0:
            value = value + stream_ref[:, part * half : (part + 1) * half]
        ref[...] = value.astype(ref.dtype)


def add_kernel(*refs):
    out_ref = refs[-1]
    span = refs[-2].shape[1]
    if out_ref.shape[1] > span:
        out_ref[:, :span] = refs[0][...]
        refs = refs[1:]
    total = refs[0][...]
    for ref in refs[1:-1]:
        total = total + ref[...].astype(F32)
    out_ref[:, out_ref.shape[1] - span :] = total.astype(BF16)


def in_hbm(value):
    return pltpu.with_memory_space_constraint(value, pltpu.HBM)


def swap(value, axis, step):
    if step == 0:
        return value
    count = lax.axis_size(axis)
    return lax.ppermute(value, axis, [(i, i ^ step) for i in range(count)])


def even_first(count):
    return [*range(0, count, 2), *range(count - 1, 0, -2)]


def params(elements):
    return pltpu.CompilerParams(vmem_limit_bytes=min(48 * MIB, 2 * MIB + 10 * elements))


def shards(
    queries,
    cached_keys,
    cached_values,
    lengths,
    routes,
    residual,
    norm_gain,
    router,
    gate_proj,
    up_proj,
    down_proj,
):
    batch, width = queries.shape
    experts = router.shape[1]
    layers = lax.axis_size("attn")
    me = lax.axis_index("expert").astype(jnp.int32).reshape(1)
    router = router.T
    shape = jax.ShapeDtypeStruct
    operands = [
        in_hbm(a)
        for a in (
            lengths[None], queries, cached_keys, cached_values, routes.T, residual, norm_gain[None]
        )
    ]
    window, depth = cached_values.shape[1:]
    held = [a.shape for a in operands]
    held[3] = (batch, -(-window // LANES) * LANES, depth)
    half = width // 2
    stream, *payload = pl.pallas_call(
        attend_kernel,
        in_specs=[SCALAR] + [ANY] * len(operands),
        out_specs=[WHOLE] * 3,
        out_shape=[shape((batch, width), F32)]
        + [shape((batch, size), BF16) for size in (half + LANES, half)],
        scratch_shapes=[pltpu.VMEM(size, a.dtype) for size, a in zip(held, operands)]
        + [pltpu.SemaphoreType.DMA((5 + 2 * (batch // BLOCK),))],
        compiler_params=params(28 * batch * width),
        cost_estimate=LIGHT,
    )(me, *operands)

    payload = pass_on(payload, BUSY)

    order = even_first(experts)
    chunks, arrived = [], []
    for part in range(2):
        came = {j: swap(payload[part], "attn", j) for j in even_first(layers)}
        chunks += [came[j] for j in range(layers)]
        slots = pl.pallas_call(
            functools.partial(split_kernel, layers=layers, part=part),
            in_specs=[SCALAR] + [WHOLE] * len(chunks),
            out_specs=[WHOLE] * experts,
            out_shape=[shape((layers * CAP, half), BF16)] * experts,
            cost_estimate=MID if part else LIGHT,
            compiler_params=params(experts * layers * CAP * half),
        )(me, *chunks)
        arrived.append([swap(slots[e], "expert", e) for e in order])
    gates = pl.pallas_call(
        functools.partial(weigh_kernel, layers=layers),
        in_specs=[SCALAR] + [WHOLE] * (1 + len(chunks)),
        out_specs=[WHOLE] * 2,
        out_shape=[shape((layers * batch, experts * layers * CAP), BF16)] * 2,
        cost_estimate=LIGHT,
        compiler_params=params(layers * batch * width),
    )(me, router, *chunks)

    total_rows = experts * layers * CAP
    units = gate_proj.shape[2]
    gate, up, down = gate_proj[0], up_proj[0], in_hbm(down_proj[0])
    rows = pltpu.VMEM((total_rows, half), BF16)
    strips = pltpu.SemaphoreType.DMA((STRIPS,))
    halves = [shape((layers * CAP, half), BF16)] * experts
    *sums, down_first = pl.pallas_call(
        functools.partial(begin_kernel, experts=experts),
        in_specs=[WHOLE] * experts + [ANY] + [WHOLE] * 2 + [ANY],
        out_specs=[WHOLE] * 3,
        out_shape=[shape((total_rows, units), F32)] * 2 + [pltpu.VMEM((units, half), BF16)],
        scratch_shapes=[rows, strips],
        cost_estimate=pl.CostEstimate(
            flops=4 * total_rows * half * units, bytes_accessed=0, transcendentals=0
        ),
        compiler_params=params(total_rows * width),
    )(*arrived[0], gates[0], gate, up, down)
    *first, hidden, down_second = pl.pallas_call(
        functools.partial(middle_kernel, experts=experts),
        in_specs=[WHOLE] * (experts + 5) + [ANY],
        out_specs=[WHOLE] * (experts + 2),
        out_shape=halves + [shape((total_rows, units), BF16), pltpu.VMEM((units, half), BF16)],
        scratch_shapes=[rows, strips],
        compiler_params=params(total_rows * width),
    )(*arrived[1], *sums, down_first, gate, up, down)
    second = pl.pallas_call(
        end_kernel,
        in_specs=[WHOLE] * 2,
        out_specs=[WHOLE] * experts,
        out_shape=halves,
        cost_estimate=pl.CostEstimate(
            flops=2 * total_rows * half * units, bytes_accessed=0, transcendentals=0
        ),
        compiler_params=params(total_rows * width),
    )(hidden, down_second)

    done = []
    for part, blocks in enumerate((first, second)):
        returned = [swap(block, "expert", e) for e, block in zip(order, blocks)]
        mixed = pl.pallas_call(
            functools.partial(mix_kernel, layers=layers, part=part),
            in_specs=[WHOLE] * (3 + experts),
            out_specs=[WHOLE] * layers,
            out_shape=[shape((batch, half), BF16 if j else F32) for j in range(layers)],
            cost_estimate=LIGHT,
            compiler_params=params(experts * layers * CAP * half),
        )(*gates, *returned, stream)
        sums = [swap(mixed[j], "attn", j) for j in even_first(layers)]
        done = [
            pl.pallas_call(
                add_kernel,
                in_specs=[WHOLE] * (layers + len(done)),
                out_specs=WHOLE,
                out_shape=shape((batch, width if part else half), BF16),
                cost_estimate=LIGHT,
                compiler_params=params(layers * batch * width),
            )(*done, *sums)
        ]
    return done[0]


def solution(mesh):
    in_specs = (
        P(("groups", "attn", "expert"), None),
        P(("groups", "attn", "expert"), None, None),
        P(("groups", "attn", "expert"), None, None),
        P(("groups", "attn", "expert")),
        P(("groups", "attn", "expert"), None),
        P(("groups", "attn", "expert"), None),
        P(),
        P(),
        P("expert", None, "attn"),
        P("expert", None, "attn"),
        P("expert", "attn", None),
    )
    out_specs = P(("groups", "attn", "expert"), None)
    return jax.shard_map(shards, mesh=mesh, in_specs=in_specs, out_specs=out_specs, check_vma=False)
```

```python
import functools

import jax
import jax.numpy as jnp
from jax import lax
from jax.experimental import pallas as pl
from jax.experimental.pallas import tpu as pltpu
from jax.sharding import PartitionSpec as P

HS = 128
KVH = 4
GROUP = 6
CAP = 8
LANES = 128
PAIR = 2
BLOCK = 8
STRIPS = 3
TILE = 256
UNROLL = 2
MIB = 1 << 20
F32 = jnp.float32
BF16 = jnp.bfloat16
LIGHT = pl.CostEstimate(flops=0, bytes_accessed=0, transcendentals=0)
BUSY = pl.CostEstimate(flops=24 * 10**9, bytes_accessed=0, transcendentals=0)
MID = pl.CostEstimate(flops=2 * 10**9, bytes_accessed=0, transcendentals=0)
ANY = pl.BlockSpec(memory_space=pl.ANY)
WHOLE = pl.BlockSpec(memory_space=pltpu.VMEM)
SCALAR = pl.BlockSpec(memory_space=pltpu.SMEM)


def dot(a, b, dims=((1,), (0,))):
    return lax.dot_general(a, b, (dims, ((), ())), preferred_element_type=F32)


def iota(shape, dim):
    return lax.broadcasted_iota(jnp.int32, shape, dim)


def split(index, size):
    if size & (size - 1):
        return lax.div(index, size), lax.rem(index, size)
    return index >> (size.bit_length() - 1), index & (size - 1)


def slot_map(me, named, chunks, experts):
    named = named[:, 0:4].astype(F32).astype(jnp.int32)
    owners, places = named[:, 0:2] ^ me, named[:, 2:4]
    rows, slots = named.shape[0], experts * chunks * CAP
    group, place = split(iota((rows, slots), 1), CAP)
    expert, chunk = split(group, chunks)
    taken = [(owners[:, k : k + 1] == expert) & (places[:, k : k + 1] == place) for k in range(2)]
    here = split(iota((rows, slots), 0), rows // chunks)[0] == chunk
    return taken[0] & here, taken[1] & here


def dispatch(me, rows, named, chunks, experts):
    first, second = slot_map(me, named, chunks, experts)
    table = jnp.where(first | second, 1.0, 0.0).astype(BF16)
    return dot(table, rows, ((0,), (0,)))


def weigh_kernel(me_ref, router_ref, *refs, layers):
    high_ref, low_ref = refs[-2:]
    parts, named = gather(refs[:-2], layers)
    rows = jnp.concatenate(parts, axis=1)
    routes = named[:, 0:2].astype(F32).astype(jnp.int32)
    logits = dot(rows, router_ref[...], ((1,), (1,)))
    experts = logits.shape[1]
    lane = iota(logits.shape, 1)
    first = jnp.sum(jnp.where(lane == routes[:, 0:1], logits, 0.0), axis=1, keepdims=True)
    second = jnp.sum(jnp.where(lane == routes[:, 1:2], logits, 0.0), axis=1, keepdims=True)
    gate0 = 1.0 / (1.0 + jnp.exp(second - first))
    gate1 = 1.0 / (1.0 + jnp.exp(first - second))
    taken = slot_map(me_ref[0], named, layers, experts)
    gates = jnp.where(taken[0], gate0, jnp.where(taken[1], gate1, 0.0))
    high = gates.astype(BF16)
    high_ref[...] = high
    low_ref[...] = (gates - high.astype(F32)).astype(BF16)


def attend_kernel(
    _, lengths_hbm, queries_hbm, keys_hbm, values_hbm, routes_hbm, residual_hbm, gain_hbm,
    stream_ref, first_ref, second_ref,
    lengths_ref, queries_ref, keys_ref, values_ref, routes_ref, residual_ref, gain_ref, sems,
):
    batch, window, _ = keys_ref.shape
    width = queries_ref.shape[1]
    span = width // KVH
    parts = [pl.ds(begin, PAIR * HS) for begin in range(0, KVH * HS, PAIR * HS)]
    small = [
        (lengths_hbm, lengths_ref), (queries_hbm, queries_ref), (routes_hbm, routes_ref),
        (residual_hbm, residual_ref), (gain_hbm, gain_ref),
    ]
    blocks = [pl.ds(begin, BLOCK) for begin in range(0, batch, BLOCK)]
    groups = [
        small[:3],
        *[[(keys_hbm.at[block], keys_ref.at[block])] for block in blocks],
        *[[(values_hbm.at[block], values_ref.at[block, 0:window])] for block in blocks],
        small[3:],
    ]
    at, copies = 0, []
    for group in groups:
        copies.append([])
        for source, target in group:
            copies[-1].append(pltpu.make_async_copy(source, target, sems.at[at]))
            copies[-1][-1].start()
            at += 1

    def wait(group):
        for copy in copies[group]:
            copy.wait()

    padded = values_ref.shape[1]
    if padded > window:
        pad = (batch, padded - window, values_ref.shape[2])
        values_ref[:, window:, :] = jnp.zeros(pad, BF16)
    wait(0)
    same = iota((batch, batch), 0) == iota((batch, batch), 1)

    def upright(row):
        return jnp.sum(jnp.where(same, row, 0), axis=1, keepdims=True)

    named, lane = jnp.zeros((batch, LANES), jnp.int32), iota((batch, LANES), 1)
    before = iota((batch, batch), 1) < iota((batch, batch), 0)
    listed = [routes_ref[k : k + 1, :] for k in range(2)]
    for k in range(2):
        route = upright(listed[k])
        earlier = before & ((listed[0] == route) | (listed[1] == route))
        place = jnp.sum(jnp.where(earlier, 1, 0), axis=1, keepdims=True)
        named = jnp.where(lane == k, route, jnp.where(lane == 2 + k, place, named))
    named = named.astype(F32).astype(BF16)
    queries = queries_ref[...]
    lanes = PAIR * GROUP * batch
    full = -(-lanes // LANES) * LANES
    _, request = split(iota((window, full), 1), batch)
    length = jnp.zeros((1, full), jnp.int32)
    for r in range(batch):
        length = jnp.where(request[0:1] == r, lengths_ref[0:1, r : r + 1], length)
    visible = iota((window, full), 0) < length
    _, owner = split(iota((lanes, padded), 0), batch)
    spreads = []
    for i in range(len(parts)):
        spread = []
        for k in range(PAIR):
            at = [(i * PAIR + k) * span + g * HS for g in range(GROUP)]
            stacked = jnp.concatenate([queries[:, c : c + HS] for c in at], axis=0)
            blank = jnp.zeros_like(stacked)
            spread.append(
                jnp.concatenate([stacked if j == k else blank for j in range(PAIR)], axis=1)
            )
        if full > lanes:
            spread.append(jnp.zeros((full - lanes, PAIR * HS), BF16))
        spreads.append(jnp.concatenate(spread, axis=0))
    total = [jnp.zeros((window, full), F32) for _ in parts]
    for b, block in enumerate(blocks):
        wait(1 + b)
        for i, part in enumerate(parts):
            keys = keys_ref[block, :, part].reshape(BLOCK * window, PAIR * HS)
            products = dot(keys, spreads[i], ((1,), (1,)))
            for r in range(BLOCK):
                mine = request == b * BLOCK + r
                total[i] = jnp.where(mine, products[r * window : (r + 1) * window], total[i])
    weighted = []
    for scores in total:
        scores = jnp.where(visible, scores * HS ** (-0.5), -1e30)
        powers = jnp.exp(scores - jnp.max(scores, axis=0, keepdims=True))
        weights = powers / jnp.sum(powers, axis=0, keepdims=True)
        if padded > window:
            weights = jnp.concatenate([weights, jnp.zeros((padded - window, full), F32)], axis=0)
        weights = weights.T[:lanes]
        weighted.append(
            jnp.concatenate(
                [jnp.where(owner == r, weights, 0.0).astype(BF16) for r in range(batch)], axis=1
            )
        )
    mixed = [0.0] * len(parts)
    reach = BLOCK * padded
    for b, block in enumerate(blocks):
        wait(1 + len(blocks) + b)
        for i, part in enumerate(parts):
            values = values_ref[block, :, part].reshape(reach, PAIR * HS)
            mixed[i] = mixed[i] + dot(weighted[i][:, b * reach : (b + 1) * reach], values)
    attended = [
        block[h * batch : (h + 1) * batch, h // GROUP * HS : (h // GROUP + 1) * HS]
        for block in mixed
        for h in range(PAIR * GROUP)
    ]
    wait(-1)
    stream = residual_ref[...].astype(F32) + jnp.concatenate(attended, axis=1)
    scale = lax.rsqrt(jnp.mean(stream * stream, axis=1, keepdims=True) + 1e-05)
    stream_ref[...] = stream
    half = width // 2
    normed = (stream * scale * gain_ref[...]).astype(BF16)
    first_ref[:, :half] = normed[:, :half]
    first_ref[:, half:] = named
    second_ref[...] = normed[:, half:]


def pass_kernel(*_):
    pass


def pass_on(values, cost):
    return pl.pallas_call(
        pass_kernel,
        in_specs=[ANY] * len(values),
        out_specs=[ANY] * len(values),
        out_shape=[jax.ShapeDtypeStruct(value.shape, value.dtype) for value in values],
        input_output_aliases={i: i for i in range(len(values))},
        cost_estimate=cost,
        compiler_params=params(0),
    )(*values)


def stack(refs):
    return jnp.concatenate([ref[...] for ref in refs], axis=0)


def gather(refs, layers):
    first = stack(refs[:layers])
    half = first.shape[1] - LANES
    parts = [first[:, :half]] + [stack(refs[at : at + layers]) for at in range(layers, len(refs), layers)]
    return parts, first[:, half:]


def split_kernel(me_ref, *refs, layers, part):
    parts, named = gather(refs[: (1 + part) * layers], layers)
    outs = refs[(1 + part) * layers :]
    slots = dispatch(me_ref[0], parts[part], named, layers, len(outs))
    span = layers * CAP
    for e, ref in enumerate(outs):
        ref[...] = slots[e * span : (e + 1) * span].astype(BF16)


def strip_copies(source, begin, target, sems):
    strip = target.shape[1] // sems.shape[0]
    copies = [
        pltpu.make_async_copy(
            source.at[:, pl.ds(begin + c * strip, strip)],
            target.at[:, pl.ds(c * strip, strip)],
            sems.at[c],
        )
        for c in range(sems.shape[0])
    ]
    for copy in copies:
        copy.start()
    return copies


def tiles(count, tile):
    def run(body):
        @pl.loop(0, count // tile, unroll=UNROLL)
        def _(i):
            body(pl.ds(pl.multiple_of(i * tile, tile), tile))

    return run


def store_rows(outs, at, value):
    span = outs[0].shape[0]
    for e, ref in enumerate(outs):
        ref[:, at] = value[e * span : (e + 1) * span].astype(BF16)


def begin_kernel(*refs, experts):
    _, gate_ref, up_ref, down_hbm, gate_out, up_out, down_out, rows_ref, sems = refs[experts:]
    half = rows_ref.shape[1]
    copies = strip_copies(down_hbm, 0, down_out, sems)
    rows_ref[...] = stack(refs[:experts])
    units = gate_ref.shape[1]

    @tiles(units, min(TILE, units))
    def _(at):
        gate_out[:, at] = dot(rows_ref[...], gate_ref[:half, at])
        up_out[:, at] = dot(rows_ref[...], up_ref[:half, at])

    for copy in copies:
        copy.wait()


def middle_kernel(*refs, experts):
    gate_in, up_in, down_in, gate_ref, up_ref, down_hbm = refs[experts : experts + 6]
    outs = refs[experts + 6 : -4]
    hidden_ref, down_out, rows_ref, sems = refs[-4:]
    half = rows_ref.shape[1]
    copies = strip_copies(down_hbm, half, down_out, sems)
    rows_ref[...] = stack(refs[:experts])
    units = gate_ref.shape[1]

    @tiles(units, min(TILE, units))
    def _(at):
        gate = gate_in[:, at] + dot(rows_ref[...], gate_ref[half:, at])
        up = up_in[:, at] + dot(rows_ref[...], up_ref[half:, at])
        hidden_ref[:, at] = (jax.nn.silu(gate) * up).astype(BF16)

    @tiles(half, min(TILE, half))
    def _(at):
        store_rows(outs, at, dot(hidden_ref[...], down_in[:, at]))

    for copy in copies:
        copy.wait()


def end_kernel(hidden_ref, down_ref, *outs):
    half = down_ref.shape[1]

    @tiles(half, min(TILE, half))
    def _(at):
        store_rows(outs, at, dot(hidden_ref[...], down_ref[:, at]))


def mix_kernel(high_ref, low_ref, *refs, layers, part):
    outs, stream_ref = refs[-layers:], refs[-layers - 1]
    blocks = refs[: -layers - 1]
    order = even_first(len(blocks))
    returned = stack([blocks[order.index(e)] for e in range(len(blocks))])
    mixed = dot(high_ref[...], returned) + dot(low_ref[...], returned)
    batch, half = outs[0].shape
    for j, ref in enumerate(outs):
        value = mixed[j * batch : (j + 1) * batch]
        if j == 0:
            value = value + stream_ref[:, part * half : (part + 1) * half]
        ref[...] = value.astype(ref.dtype)


def add_kernel(*refs):
    out_ref = refs[-1]
    span = refs[-2].shape[1]
    if out_ref.shape[1] > span:
        out_ref[:, :span] = refs[0][...]
        refs = refs[1:]
    total = refs[0][...]
    for ref in refs[1:-1]:
        total = total + ref[...].astype(F32)
    out_ref[:, out_ref.shape[1] - span :] = total.astype(BF16)


def in_hbm(value):
    return pltpu.with_memory_space_constraint(value, pltpu.HBM)


def swap(value, axis, step):
    if step == 0:
        return value
    count = lax.axis_size(axis)
    return lax.ppermute(value, axis, [(i, i ^ step) for i in range(count)])


def even_first(count):
    return [*range(0, count, 2), *range(count - 1, 0, -2)]


def params(elements):
    return pltpu.CompilerParams(vmem_limit_bytes=min(48 * MIB, 2 * MIB + 10 * elements))


def shards(
    queries,
    cached_keys,
    cached_values,
    lengths,
    routes,
    residual,
    norm_gain,
    router,
    gate_proj,
    up_proj,
    down_proj,
):
    batch, width = queries.shape
    experts = router.shape[1]
    layers = lax.axis_size("attn")
    me = lax.axis_index("expert").astype(jnp.int32).reshape(1)
    router = router.T
    shape = jax.ShapeDtypeStruct
    operands = [
        in_hbm(a)
        for a in (
            lengths[None], queries, cached_keys, cached_values, routes.T, residual, norm_gain[None]
        )
    ]
    window, depth = cached_values.shape[1:]
    held = [a.shape for a in operands]
    held[3] = (batch, -(-window // LANES) * LANES, depth)
    half = width // 2
    stream, *payload = pl.pallas_call(
        attend_kernel,
        in_specs=[SCALAR] + [ANY] * len(operands),
        out_specs=[WHOLE] * 3,
        out_shape=[shape((batch, width), F32)]
        + [shape((batch, size), BF16) for size in (half + LANES, half)],
        scratch_shapes=[pltpu.VMEM(size, a.dtype) for size, a in zip(held, operands)]
        + [pltpu.SemaphoreType.DMA((5 + 2 * (batch // BLOCK),))],
        compiler_params=params(28 * batch * width),
        cost_estimate=LIGHT,
    )(me, *operands)

    payload = pass_on(payload, BUSY)

    order = even_first(experts)
    placed = [0, *even_first(layers)[:0:-1]]
    chunks, arrived = [], []
    for part in range(2):
        came = {j: swap(payload[part], "attn", j) for j in even_first(layers)}
        chunks += [came[j] for j in placed]
        slots = pl.pallas_call(
            functools.partial(split_kernel, layers=layers, part=part),
            in_specs=[SCALAR] + [WHOLE] * len(chunks),
            out_specs=[WHOLE] * experts,
            out_shape=[shape((layers * CAP, half), BF16)] * experts,
            cost_estimate=MID if part else LIGHT,
            compiler_params=params(experts * layers * CAP * half),
        )(me, *chunks)
        arrived.append([swap(slots[e], "expert", e) for e in order])
    gates = pl.pallas_call(
        functools.partial(weigh_kernel, layers=layers),
        in_specs=[SCALAR] + [WHOLE] * (1 + len(chunks)),
        out_specs=[WHOLE] * 2,
        out_shape=[shape((layers * batch, experts * layers * CAP), BF16)] * 2,
        cost_estimate=LIGHT,
        compiler_params=params(layers * batch * width),
    )(me, router, *chunks)

    total_rows = experts * layers * CAP
    units = gate_proj.shape[2]
    gate, up, down = gate_proj[0], up_proj[0], in_hbm(down_proj[0])
    rows = pltpu.VMEM((total_rows, half), BF16)
    strips = pltpu.SemaphoreType.DMA((STRIPS,))
    halves = [shape((layers * CAP, half), BF16)] * experts
    *sums, down_first = pl.pallas_call(
        functools.partial(begin_kernel, experts=experts),
        in_specs=[WHOLE] * experts + [ANY] + [WHOLE] * 2 + [ANY],
        out_specs=[WHOLE] * 3,
        out_shape=[shape((total_rows, units), F32)] * 2 + [pltpu.VMEM((units, half), BF16)],
        scratch_shapes=[rows, strips],
        cost_estimate=pl.CostEstimate(
            flops=4 * total_rows * half * units, bytes_accessed=0, transcendentals=0
        ),
        compiler_params=params(total_rows * width),
    )(*arrived[0], gates[0], gate, up, down)
    *first, hidden, down_second = pl.pallas_call(
        functools.partial(middle_kernel, experts=experts),
        in_specs=[WHOLE] * (experts + 5) + [ANY],
        out_specs=[WHOLE] * (experts + 2),
        out_shape=halves + [shape((total_rows, units), BF16), pltpu.VMEM((units, half), BF16)],
        scratch_shapes=[rows, strips],
        compiler_params=params(total_rows * width),
    )(*arrived[1], *sums, down_first, gate, up, down)
    second = pl.pallas_call(
        end_kernel,
        in_specs=[WHOLE] * 2,
        out_specs=[WHOLE] * experts,
        out_shape=halves,
        cost_estimate=pl.CostEstimate(
            flops=2 * total_rows * half * units, bytes_accessed=0, transcendentals=0
        ),
        compiler_params=params(total_rows * width),
    )(hidden, down_second)

    done = []
    for part, blocks in enumerate((first, second)):
        returned = [swap(block, "expert", e) for e, block in zip(order, blocks)]
        mixed = pl.pallas_call(
            functools.partial(mix_kernel, layers=layers, part=part),
            in_specs=[WHOLE] * (3 + experts),
            out_specs=[WHOLE] * layers,
            out_shape=[shape((batch, half), BF16 if j else F32) for j in range(layers)],
            cost_estimate=LIGHT,
            compiler_params=params(experts * layers * CAP * half),
        )(*gates, *returned, stream)
        sums = [swap(mixed[placed.index(j)], "attn", j) for j in even_first(layers)]
        done = [
            pl.pallas_call(
                add_kernel,
                in_specs=[WHOLE] * (layers + len(done)),
                out_specs=WHOLE,
                out_shape=shape((batch, width if part else half), BF16),
                cost_estimate=LIGHT,
                compiler_params=params(layers * batch * width),
            )(*done, *sums)
        ]
    return done[0]


def solution(mesh):
    in_specs = (
        P(("groups", "attn", "expert"), None),
        P(("groups", "attn", "expert"), None, None),
        P(("groups", "attn", "expert"), None, None),
        P(("groups", "attn", "expert")),
        P(("groups", "attn", "expert"), None),
        P(("groups", "attn", "expert"), None),
        P(),
        P(),
        P("expert", None, "attn"),
        P("expert", None, "attn"),
        P("expert", "attn", None),
    )
    out_specs = P(("groups", "attn", "expert"), None)
    return jax.shard_map(shards, mesh=mesh, in_specs=in_specs, out_specs=out_specs, check_vma=False)
```

```python
import functools

import jax
import jax.numpy as jnp
from jax import lax
from jax.experimental import pallas as pl
from jax.experimental.pallas import tpu as pltpu
from jax.sharding import PartitionSpec as P

HS = 128
KVH = 4
GROUP = 6
CAP = 8
LANES = 128
PAIR = 2
BLOCK = 8
STRIPS = 3
TILE = 256
UNROLL = 2
MIB = 1 << 20
F32 = jnp.float32
BF16 = jnp.bfloat16
LIGHT = pl.CostEstimate(flops=0, bytes_accessed=0, transcendentals=0)
BUSY = pl.CostEstimate(flops=24 * 10**9, bytes_accessed=0, transcendentals=0)
MID = pl.CostEstimate(flops=2 * 10**9, bytes_accessed=0, transcendentals=0)
ANY = pl.BlockSpec(memory_space=pl.ANY)
WHOLE = pl.BlockSpec(memory_space=pltpu.VMEM)
SCALAR = pl.BlockSpec(memory_space=pltpu.SMEM)


def dot(a, b, dims=((1,), (0,))):
    return lax.dot_general(a, b, (dims, ((), ())), preferred_element_type=F32)


def iota(shape, dim):
    return lax.broadcasted_iota(jnp.int32, shape, dim)


def split(index, size):
    if size & (size - 1):
        return lax.div(index, size), lax.rem(index, size)
    return index >> (size.bit_length() - 1), index & (size - 1)


def slot_map(me, named, chunks, experts):
    named = named[:, 0:4].astype(F32).astype(jnp.int32)
    owners, places = named[:, 0:2] ^ me, named[:, 2:4]
    rows, slots = named.shape[0], experts * chunks * CAP
    group, place = split(iota((rows, slots), 1), CAP)
    expert, chunk = split(group, chunks)
    taken = [(owners[:, k : k + 1] == expert) & (places[:, k : k + 1] == place) for k in range(2)]
    here = split(iota((rows, slots), 0), rows // chunks)[0] == chunk
    return taken[0] & here, taken[1] & here


def dispatch(me, rows, named, chunks, experts):
    first, second = slot_map(me, named, chunks, experts)
    table = jnp.where(first | second, 1.0, 0.0).astype(BF16)
    return dot(table, rows, ((0,), (0,)))


def weigh_kernel(me_ref, router_ref, *refs, layers):
    high_ref, low_ref = refs[-2:]
    parts, named = gather(refs[:-2], layers)
    rows = jnp.concatenate(parts, axis=1)
    routes = named[:, 0:2].astype(F32).astype(jnp.int32)
    logits = dot(rows, router_ref[...], ((1,), (1,)))
    experts = logits.shape[1]
    lane = iota(logits.shape, 1)
    first = jnp.sum(jnp.where(lane == routes[:, 0:1], logits, 0.0), axis=1, keepdims=True)
    second = jnp.sum(jnp.where(lane == routes[:, 1:2], logits, 0.0), axis=1, keepdims=True)
    gate0 = 1.0 / (1.0 + jnp.exp(second - first))
    gate1 = 1.0 / (1.0 + jnp.exp(first - second))
    taken = slot_map(me_ref[0], named, layers, experts)
    gates = jnp.where(taken[0], gate0, jnp.where(taken[1], gate1, 0.0))
    high = gates.astype(BF16)
    high_ref[...] = high
    low_ref[...] = (gates - high.astype(F32)).astype(BF16)


def attend_kernel(
    _, lengths_hbm, queries_hbm, keys_hbm, values_hbm, routes_hbm, residual_hbm, gain_hbm,
    stream_ref, first_ref, second_ref,
    lengths_ref, queries_ref, keys_ref, values_ref, routes_ref, residual_ref, gain_ref, sems,
):
    batch, window, _ = keys_ref.shape
    width = queries_ref.shape[1]
    span = width // KVH
    parts = [pl.ds(begin, PAIR * HS) for begin in range(0, KVH * HS, PAIR * HS)]
    small = [
        (lengths_hbm, lengths_ref), (queries_hbm, queries_ref), (routes_hbm, routes_ref),
        (residual_hbm, residual_ref), (gain_hbm, gain_ref),
    ]
    blocks = [pl.ds(begin, BLOCK) for begin in range(0, batch, BLOCK)]
    groups = [
        small[:3],
        *[[(keys_hbm.at[block], keys_ref.at[block])] for block in blocks],
        *[[(values_hbm.at[block], values_ref.at[block, 0:window])] for block in blocks],
        small[3:],
    ]
    at, copies = 0, []
    for group in groups:
        copies.append([])
        for source, target in group:
            copies[-1].append(pltpu.make_async_copy(source, target, sems.at[at]))
            copies[-1][-1].start()
            at += 1

    def wait(group):
        for copy in copies[group]:
            copy.wait()

    padded = values_ref.shape[1]
    if padded > window:
        pad = (batch, padded - window, values_ref.shape[2])
        values_ref[:, window:, :] = jnp.zeros(pad, BF16)
    wait(0)
    same = iota((batch, batch), 0) == iota((batch, batch), 1)

    def upright(row):
        return jnp.sum(jnp.where(same, row, 0), axis=1, keepdims=True)

    named, lane = jnp.zeros((batch, LANES), jnp.int32), iota((batch, LANES), 1)
    before = iota((batch, batch), 1) < iota((batch, batch), 0)
    listed = [routes_ref[k : k + 1, :] for k in range(2)]
    for k in range(2):
        route = upright(listed[k])
        earlier = before & ((listed[0] == route) | (listed[1] == route))
        place = jnp.sum(jnp.where(earlier, 1, 0), axis=1, keepdims=True)
        named = jnp.where(lane == k, route, jnp.where(lane == 2 + k, place, named))
    named = named.astype(F32).astype(BF16)
    queries = queries_ref[...]
    lanes = PAIR * GROUP * batch
    full = -(-lanes // LANES) * LANES
    _, request = split(iota((window, full), 1), batch)
    length = jnp.zeros((1, full), jnp.int32)
    for r in range(batch):
        length = jnp.where(request[0:1] == r, lengths_ref[0:1, r : r + 1], length)
    visible = iota((window, full), 0) < length
    _, owner = split(iota((lanes, padded), 0), batch)
    spreads = []
    for i in range(len(parts)):
        spread = []
        for k in range(PAIR):
            at = [(i * PAIR + k) * span + g * HS for g in range(GROUP)]
            stacked = jnp.concatenate([queries[:, c : c + HS] for c in at], axis=0)
            blank = jnp.zeros_like(stacked)
            spread.append(
                jnp.concatenate([stacked if j == k else blank for j in range(PAIR)], axis=1)
            )
        if full > lanes:
            spread.append(jnp.zeros((full - lanes, PAIR * HS), BF16))
        spreads.append(jnp.concatenate(spread, axis=0))
    total = [jnp.zeros((window, full), F32) for _ in parts]
    for b, block in enumerate(blocks):
        wait(1 + b)
        for i, part in enumerate(parts):
            keys = keys_ref[block, :, part].reshape(BLOCK * window, PAIR * HS)
            products = dot(keys, spreads[i], ((1,), (1,)))
            for r in range(BLOCK):
                mine = request == b * BLOCK + r
                total[i] = jnp.where(mine, products[r * window : (r + 1) * window], total[i])
    weighted = []
    for scores in total:
        scores = jnp.where(visible, scores * HS ** (-0.5), -1e30)
        powers = jnp.exp(scores - jnp.max(scores, axis=0, keepdims=True))
        weights = powers / jnp.sum(powers, axis=0, keepdims=True)
        if padded > window:
            weights = jnp.concatenate([weights, jnp.zeros((padded - window, full), F32)], axis=0)
        weights = weights.T[:lanes]
        weighted.append(
            jnp.concatenate(
                [jnp.where(owner == r, weights, 0.0).astype(BF16) for r in range(batch)], axis=1
            )
        )
    mixed = [0.0] * len(parts)
    reach = BLOCK * padded
    for b, block in enumerate(blocks):
        wait(1 + len(blocks) + b)
        for i, part in enumerate(parts):
            values = values_ref[block, :, part].reshape(reach, PAIR * HS)
            mixed[i] = mixed[i] + dot(weighted[i][:, b * reach : (b + 1) * reach], values)
    attended = [
        block[h * batch : (h + 1) * batch, h // GROUP * HS : (h // GROUP + 1) * HS]
        for block in mixed
        for h in range(PAIR * GROUP)
    ]
    wait(-1)
    stream = residual_ref[...].astype(F32) + jnp.concatenate(attended, axis=1)
    scale = lax.rsqrt(jnp.mean(stream * stream, axis=1, keepdims=True) + 1e-05)
    stream_ref[...] = stream
    half = width // 2
    normed = (stream * scale * gain_ref[...]).astype(BF16)
    first_ref[:, :half] = normed[:, :half]
    first_ref[:, half:] = named
    second_ref[...] = normed[:, half:]


def pass_kernel(*_):
    pass


def pass_on(values, cost):
    return pl.pallas_call(
        pass_kernel,
        in_specs=[ANY] * len(values),
        out_specs=[ANY] * len(values),
        out_shape=[jax.ShapeDtypeStruct(value.shape, value.dtype) for value in values],
        input_output_aliases={i: i for i in range(len(values))},
        cost_estimate=cost,
        compiler_params=params(0),
    )(*values)


def stack(refs):
    return jnp.concatenate([ref[...] for ref in refs], axis=0)


def gather(refs, layers):
    first = stack(refs[:layers])
    half = first.shape[1] - LANES
    parts = [first[:, :half]] + [stack(refs[at : at + layers]) for at in range(layers, len(refs), layers)]
    return parts, first[:, half:]


def split_kernel(me_ref, *refs, layers, part):
    parts, named = gather(refs[: (1 + part) * layers], layers)
    outs = refs[(1 + part) * layers :]
    slots = dispatch(me_ref[0], parts[part], named, layers, len(outs))
    span = layers * CAP
    for e, ref in enumerate(outs):
        ref[...] = slots[e * span : (e + 1) * span].astype(BF16)


def strip_copies(source, begin, target, sems):
    strip = target.shape[1] // sems.shape[0]
    copies = [
        pltpu.make_async_copy(
            source.at[:, pl.ds(begin + c * strip, strip)],
            target.at[:, pl.ds(c * strip, strip)],
            sems.at[c],
        )
        for c in range(sems.shape[0])
    ]
    for copy in copies:
        copy.start()
    return copies


def tiles(count, tile):
    def run(body):
        @pl.loop(0, count // tile, unroll=UNROLL)
        def _(i):
            body(pl.ds(pl.multiple_of(i * tile, tile), tile))

    return run


def store_rows(outs, at, value):
    span = outs[0].shape[0]
    for e, ref in enumerate(outs):
        ref[:, at] = value[e * span : (e + 1) * span].astype(BF16)


def begin_kernel(*refs, experts):
    _, gate_ref, up_ref, down_hbm, gate_out, up_out, down_out, rows_ref, sems = refs[experts:]
    half = rows_ref.shape[1]
    copies = strip_copies(down_hbm, 0, down_out, sems)
    rows_ref[...] = stack(refs[:experts])
    units = gate_ref.shape[1]

    @tiles(units, min(TILE, units))
    def _(at):
        gate_out[:, at] = dot(rows_ref[...], gate_ref[:half, at])
        up_out[:, at] = dot(rows_ref[...], up_ref[:half, at])

    for copy in copies:
        copy.wait()


def middle_kernel(*refs, experts):
    gate_in, up_in, down_in, gate_ref, up_ref, down_hbm = refs[experts : experts + 6]
    outs = refs[experts + 6 : -4]
    hidden_ref, down_out, rows_ref, sems = refs[-4:]
    half = rows_ref.shape[1]
    copies = strip_copies(down_hbm, half, down_out, sems)
    rows_ref[...] = stack(refs[:experts])
    units = gate_ref.shape[1]

    @tiles(units, min(TILE, units))
    def _(at):
        gate = gate_in[:, at] + dot(rows_ref[...], gate_ref[half:, at])
        up = up_in[:, at] + dot(rows_ref[...], up_ref[half:, at])
        hidden_ref[:, at] = (jax.nn.silu(gate) * up).astype(BF16)

    @tiles(half, min(TILE, half))
    def _(at):
        store_rows(outs, at, dot(hidden_ref[...], down_in[:, at]))

    for copy in copies:
        copy.wait()


def end_kernel(hidden_ref, down_ref, *outs):
    half = down_ref.shape[1]

    @tiles(half, min(TILE, half))
    def _(at):
        store_rows(outs, at, dot(hidden_ref[...], down_ref[:, at]))


def mix_kernel(high_ref, low_ref, *refs, layers, part):
    outs, stream_ref = refs[-layers:], refs[-layers - 1]
    blocks = refs[: -layers - 1]
    order = even_first(len(blocks))
    returned = stack([blocks[order.index(e)] for e in range(len(blocks))])
    mixed = dot(high_ref[...], returned) + dot(low_ref[...], returned)
    batch, half = outs[0].shape
    for j, ref in enumerate(outs):
        value = mixed[j * batch : (j + 1) * batch]
        if j == 0:
            value = value + stream_ref[:, part * half : (part + 1) * half]
        ref[...] = value.astype(ref.dtype)


def add_kernel(*refs):
    out_ref = refs[-1]
    span = refs[-2].shape[1]
    if out_ref.shape[1] > span:
        out_ref[:, :span] = refs[0][...]
        refs = refs[1:]
    total = refs[0][...]
    for ref in refs[1:-1]:
        total = total + ref[...].astype(F32)
    out_ref[:, out_ref.shape[1] - span :] = total.astype(BF16)


def in_hbm(value):
    return pltpu.with_memory_space_constraint(value, pltpu.HBM)


def swap(value, axis, step):
    if step == 0:
        return value
    count = lax.axis_size(axis)
    return lax.ppermute(value, axis, [(i, i ^ step) for i in range(count)])


def even_first(count):
    return [*range(0, count, 2), *range(count - 1, 0, -2)]


def params(elements):
    return pltpu.CompilerParams(vmem_limit_bytes=min(48 * MIB, 2 * MIB + 10 * elements))


def shards(
    queries,
    cached_keys,
    cached_values,
    lengths,
    routes,
    residual,
    norm_gain,
    router,
    gate_proj,
    up_proj,
    down_proj,
):
    batch, width = queries.shape
    experts = router.shape[1]
    layers = lax.axis_size("attn")
    me = lax.axis_index("expert").astype(jnp.int32).reshape(1)
    router = router.T
    shape = jax.ShapeDtypeStruct
    operands = [
        in_hbm(a)
        for a in (
            lengths[None], queries, cached_keys, cached_values, routes.T, residual, norm_gain[None]
        )
    ]
    window, depth = cached_values.shape[1:]
    held = [a.shape for a in operands]
    held[3] = (batch, -(-window // LANES) * LANES, depth)
    half = width // 2
    stream, *payload = pl.pallas_call(
        attend_kernel,
        in_specs=[SCALAR] + [ANY] * len(operands),
        out_specs=[WHOLE] * 3,
        out_shape=[shape((batch, width), F32)]
        + [shape((batch, size), BF16) for size in (half + LANES, half)],
        scratch_shapes=[pltpu.VMEM(size, a.dtype) for size, a in zip(held, operands)]
        + [pltpu.SemaphoreType.DMA((5 + 2 * (batch // BLOCK),))],
        compiler_params=params(28 * batch * width),
        cost_estimate=LIGHT,
    )(me, *operands)

    payload = pass_on(payload, BUSY)

    order = even_first(experts)
    placed = [0, *even_first(layers)[:0:-1]]
    chunks, arrived = [], []
    for part in range(2):
        came = {j: swap(payload[part], "attn", j) for j in even_first(layers)}
        chunks += [came[j] for j in placed]
        slots = pl.pallas_call(
            functools.partial(split_kernel, layers=layers, part=part),
            in_specs=[SCALAR] + [WHOLE] * len(chunks),
            out_specs=[WHOLE] * experts,
            out_shape=[shape((layers * CAP, half), BF16)] * experts,
            cost_estimate=MID if part else LIGHT,
            compiler_params=params(experts * layers * CAP * half),
        )(me, *chunks)
        arrived.append([swap(slots[e], "expert", e) for e in order])
    gates = pl.pallas_call(
        functools.partial(weigh_kernel, layers=layers),
        in_specs=[SCALAR] + [WHOLE] * (1 + len(chunks)),
        out_specs=[WHOLE] * 2,
        out_shape=[shape((layers * batch, experts * layers * CAP), BF16)] * 2,
        cost_estimate=LIGHT,
        compiler_params=params(layers * batch * width),
    )(me, router, *chunks)

    total_rows = experts * layers * CAP
    units = gate_proj.shape[2]
    gate, up, down = gate_proj[0], up_proj[0], in_hbm(down_proj[0])
    rows = pltpu.VMEM((total_rows, half), BF16)
    strips = pltpu.SemaphoreType.DMA((STRIPS,))
    halves = [shape((layers * CAP, half), BF16)] * experts
    *sums, down_first = pl.pallas_call(
        functools.partial(begin_kernel, experts=experts),
        in_specs=[WHOLE] * experts + [ANY] + [WHOLE] * 2 + [ANY],
        out_specs=[WHOLE] * 3,
        out_shape=[shape((total_rows, units), F32)] * 2 + [pltpu.VMEM((units, half), BF16)],
        scratch_shapes=[rows, strips],
        cost_estimate=pl.CostEstimate(
            flops=4 * total_rows * half * units, bytes_accessed=0, transcendentals=0
        ),
        compiler_params=params(total_rows * width),
    )(*arrived[0], gates[0], gate, up, down)
    *first, hidden, down_second = pl.pallas_call(
        functools.partial(middle_kernel, experts=experts),
        in_specs=[WHOLE] * (experts + 5) + [ANY],
        out_specs=[WHOLE] * (experts + 2),
        out_shape=halves + [shape((total_rows, units), BF16), pltpu.VMEM((units, half), BF16)],
        scratch_shapes=[rows, strips],
        compiler_params=params(total_rows * width),
    )(*arrived[1], *sums, down_first, gate, up, down)
    second = pl.pallas_call(
        end_kernel,
        in_specs=[WHOLE] * 2,
        out_specs=[WHOLE] * experts,
        out_shape=halves,
        cost_estimate=pl.CostEstimate(
            flops=2 * total_rows * half * units, bytes_accessed=0, transcendentals=0
        ),
        compiler_params=params(total_rows * width),
    )(hidden, down_second)

    done = []
    for part, blocks in enumerate((first, second)):
        returned = [swap(block, "expert", e) for e, block in zip(order, blocks)]
        mixed = pl.pallas_call(
            functools.partial(mix_kernel, layers=layers, part=part),
            in_specs=[WHOLE] * (3 + experts),
            out_specs=[WHOLE] * layers,
            out_shape=[shape((batch, half), BF16 if j else F32) for j in range(layers)],
            cost_estimate=LIGHT,
            compiler_params=params(experts * layers * CAP * half),
        )(*gates, *returned, stream)
        sums = [swap(mixed[placed.index(j)], "attn", j) for j in [0, *range(layers - 1, 0, -1)]]
        done = [
            pl.pallas_call(
                add_kernel,
                in_specs=[WHOLE] * (layers + len(done)),
                out_specs=WHOLE,
                out_shape=shape((batch, width if part else half), BF16),
                cost_estimate=LIGHT,
                compiler_params=params(layers * batch * width),
            )(*done, *sums)
        ]
    return done[0]


def solution(mesh):
    in_specs = (
        P(("groups", "attn", "expert"), None),
        P(("groups", "attn", "expert"), None, None),
        P(("groups", "attn", "expert"), None, None),
        P(("groups", "attn", "expert")),
        P(("groups", "attn", "expert"), None),
        P(("groups", "attn", "expert"), None),
        P(),
        P(),
        P("expert", None, "attn"),
        P("expert", None, "attn"),
        P("expert", "attn", None),
    )
    out_specs = P(("groups", "attn", "expert"), None)
    return jax.shard_map(shards, mesh=mesh, in_specs=in_specs, out_specs=out_specs, check_vma=False)
```

```python
import functools

import jax
import jax.numpy as jnp
from jax import lax
from jax.experimental import pallas as pl
from jax.experimental.pallas import tpu as pltpu
from jax.sharding import PartitionSpec as P

HS = 128
KVH = 4
GROUP = 6
CAP = 8
LANES = 128
PAIR = 2
BLOCK = 8
STRIPS = 3
TILE = 256
UNROLL = 2
MIB = 1 << 20
F32 = jnp.float32
BF16 = jnp.bfloat16
LIGHT = pl.CostEstimate(flops=0, bytes_accessed=0, transcendentals=0)
BUSY = pl.CostEstimate(flops=24 * 10**9, bytes_accessed=0, transcendentals=0)
MID = pl.CostEstimate(flops=2 * 10**9, bytes_accessed=0, transcendentals=0)
ANY = pl.BlockSpec(memory_space=pl.ANY)
WHOLE = pl.BlockSpec(memory_space=pltpu.VMEM)
SCALAR = pl.BlockSpec(memory_space=pltpu.SMEM)


def dot(a, b, dims=((1,), (0,))):
    return lax.dot_general(a, b, (dims, ((), ())), preferred_element_type=F32)


def iota(shape, dim):
    return lax.broadcasted_iota(jnp.int32, shape, dim)


def split(index, size):
    if size & (size - 1):
        return lax.div(index, size), lax.rem(index, size)
    return index >> (size.bit_length() - 1), index & (size - 1)


def slot_map(me, named, chunks, experts):
    named = named[:, 0:4].astype(F32).astype(jnp.int32)
    owners, places = named[:, 0:2] ^ me, named[:, 2:4]
    rows, slots = named.shape[0], experts * chunks * CAP
    group, place = split(iota((rows, slots), 1), CAP)
    expert, chunk = split(group, chunks)
    taken = [(owners[:, k : k + 1] == expert) & (places[:, k : k + 1] == place) for k in range(2)]
    here = split(iota((rows, slots), 0), rows // chunks)[0] == chunk
    return taken[0] & here, taken[1] & here


def dispatch(me, rows, named, chunks, experts):
    first, second = slot_map(me, named, chunks, experts)
    table = jnp.where(first | second, 1.0, 0.0).astype(BF16)
    return dot(table, rows, ((0,), (0,)))


def weigh_kernel(me_ref, router_ref, *refs, layers):
    high_ref, low_ref = refs[-2:]
    parts, named = gather(refs[:-2], layers)
    rows = jnp.concatenate(parts, axis=1)
    routes = named[:, 0:2].astype(F32).astype(jnp.int32)
    logits = dot(rows, router_ref[...], ((1,), (1,)))
    experts = logits.shape[1]
    lane = iota(logits.shape, 1)
    first = jnp.sum(jnp.where(lane == routes[:, 0:1], logits, 0.0), axis=1, keepdims=True)
    second = jnp.sum(jnp.where(lane == routes[:, 1:2], logits, 0.0), axis=1, keepdims=True)
    gate0 = 1.0 / (1.0 + jnp.exp(second - first))
    gate1 = 1.0 / (1.0 + jnp.exp(first - second))
    taken = slot_map(me_ref[0], named, layers, experts)
    gates = jnp.where(taken[0], gate0, jnp.where(taken[1], gate1, 0.0))
    high = gates.astype(BF16)
    high_ref[...] = high
    low_ref[...] = (gates - high.astype(F32)).astype(BF16)


def attend_kernel(
    _, lengths_hbm, queries_hbm, keys_hbm, values_hbm, routes_hbm, residual_hbm, gain_hbm,
    stream_ref, first_ref, second_ref,
    lengths_ref, queries_ref, keys_ref, values_ref, routes_ref, residual_ref, gain_ref, sems,
):
    batch, window, _ = keys_ref.shape
    width = queries_ref.shape[1]
    span = width // KVH
    parts = [pl.ds(begin, PAIR * HS) for begin in range(0, KVH * HS, PAIR * HS)]
    small = [
        (lengths_hbm, lengths_ref), (queries_hbm, queries_ref), (routes_hbm, routes_ref),
        (residual_hbm, residual_ref), (gain_hbm, gain_ref),
    ]
    blocks = [pl.ds(begin, BLOCK) for begin in range(0, batch, BLOCK)]
    groups = [
        small[:3],
        *[[(keys_hbm.at[block], keys_ref.at[block])] for block in blocks],
        *[[(values_hbm.at[block], values_ref.at[block, 0:window])] for block in blocks],
        small[3:],
    ]
    at, copies = 0, []
    for group in groups:
        copies.append([])
        for source, target in group:
            copies[-1].append(pltpu.make_async_copy(source, target, sems.at[at]))
            copies[-1][-1].start()
            at += 1

    def wait(group):
        for copy in copies[group]:
            copy.wait()

    padded = values_ref.shape[1]
    if padded > window:
        pad = (batch, padded - window, values_ref.shape[2])
        values_ref[:, window:, :] = jnp.zeros(pad, BF16)
    wait(0)
    same = iota((batch, batch), 0) == iota((batch, batch), 1)

    def upright(row):
        return jnp.sum(jnp.where(same, row, 0), axis=1, keepdims=True)

    named, lane = jnp.zeros((batch, LANES), jnp.int32), iota((batch, LANES), 1)
    before = iota((batch, batch), 1) < iota((batch, batch), 0)
    listed = [routes_ref[k : k + 1, :] for k in range(2)]
    for k in range(2):
        route = upright(listed[k])
        earlier = before & ((listed[0] == route) | (listed[1] == route))
        place = jnp.sum(jnp.where(earlier, 1, 0), axis=1, keepdims=True)
        named = jnp.where(lane == k, route, jnp.where(lane == 2 + k, place, named))
    named = named.astype(F32).astype(BF16)
    queries = queries_ref[...]
    lanes = PAIR * GROUP * batch
    full = -(-lanes // LANES) * LANES
    _, request = split(iota((window, full), 1), batch)
    length = jnp.zeros((1, full), jnp.int32)
    for r in range(batch):
        length = jnp.where(request[0:1] == r, lengths_ref[0:1, r : r + 1], length)
    visible = iota((window, full), 0) < length
    _, owner = split(iota((lanes, padded), 0), batch)
    spreads = []
    for i in range(len(parts)):
        spread = []
        for k in range(PAIR):
            at = [(i * PAIR + k) * span + g * HS for g in range(GROUP)]
            stacked = jnp.concatenate([queries[:, c : c + HS] for c in at], axis=0)
            blank = jnp.zeros_like(stacked)
            spread.append(
                jnp.concatenate([stacked if j == k else blank for j in range(PAIR)], axis=1)
            )
        if full > lanes:
            spread.append(jnp.zeros((full - lanes, PAIR * HS), BF16))
        spreads.append(jnp.concatenate(spread, axis=0))
    total = [jnp.zeros((window, full), F32) for _ in parts]
    for b, block in enumerate(blocks):
        wait(1 + b)
        for i, part in enumerate(parts):
            keys = keys_ref[block, :, part].reshape(BLOCK * window, PAIR * HS)
            products = dot(keys, spreads[i], ((1,), (1,)))
            for r in range(BLOCK):
                mine = request == b * BLOCK + r
                total[i] = jnp.where(mine, products[r * window : (r + 1) * window], total[i])
    weighted = []
    for scores in total:
        scores = jnp.where(visible, scores * HS ** (-0.5), -1e30)
        powers = jnp.exp(scores - jnp.max(scores, axis=0, keepdims=True))
        weights = powers / jnp.sum(powers, axis=0, keepdims=True)
        if padded > window:
            weights = jnp.concatenate([weights, jnp.zeros((padded - window, full), F32)], axis=0)
        weights = weights.T[:lanes]
        weighted.append(
            jnp.concatenate(
                [jnp.where(owner == r, weights, 0.0).astype(BF16) for r in range(batch)], axis=1
            )
        )
    mixed = [0.0] * len(parts)
    reach = BLOCK * padded
    for b, block in enumerate(blocks):
        wait(1 + len(blocks) + b)
        for i, part in enumerate(parts):
            values = values_ref[block, :, part].reshape(reach, PAIR * HS)
            mixed[i] = mixed[i] + dot(weighted[i][:, b * reach : (b + 1) * reach], values)
    attended = [
        block[h * batch : (h + 1) * batch, h // GROUP * HS : (h // GROUP + 1) * HS]
        for block in mixed
        for h in range(PAIR * GROUP)
    ]
    wait(-1)
    stream = residual_ref[...].astype(F32) + jnp.concatenate(attended, axis=1)
    scale = lax.rsqrt(jnp.mean(stream * stream, axis=1, keepdims=True) + 1e-05)
    stream_ref[...] = stream
    half = width // 2
    normed = (stream * scale * gain_ref[...]).astype(BF16)
    first_ref[:, :half] = normed[:, :half]
    first_ref[:, half:] = named
    second_ref[...] = normed[:, half:]


def pass_kernel(*_):
    pass


def pass_on(values, cost):
    return pl.pallas_call(
        pass_kernel,
        in_specs=[ANY] * len(values),
        out_specs=[ANY] * len(values),
        out_shape=[jax.ShapeDtypeStruct(value.shape, value.dtype) for value in values],
        input_output_aliases={i: i for i in range(len(values))},
        cost_estimate=cost,
        compiler_params=params(0),
    )(*values)


def stack(refs):
    return jnp.concatenate([ref[...] for ref in refs], axis=0)


def gather(refs, layers):
    first = stack(refs[:layers])
    half = first.shape[1] - LANES
    parts = [first[:, :half]] + [stack(refs[at : at + layers]) for at in range(layers, len(refs), layers)]
    return parts, first[:, half:]


def split_kernel(me_ref, *refs, layers, part):
    parts, named = gather(refs[: (1 + part) * layers], layers)
    outs = refs[(1 + part) * layers :]
    slots = dispatch(me_ref[0], parts[part], named, layers, len(outs))
    span = layers * CAP
    for e, ref in enumerate(outs):
        ref[...] = slots[e * span : (e + 1) * span].astype(BF16)


def strip_copies(source, begin, target, sems):
    strip = target.shape[1] // sems.shape[0]
    copies = [
        pltpu.make_async_copy(
            source.at[:, pl.ds(begin + c * strip, strip)],
            target.at[:, pl.ds(c * strip, strip)],
            sems.at[c],
        )
        for c in range(sems.shape[0])
    ]
    for copy in copies:
        copy.start()
    return copies


def tiles(count, tile):
    def run(body):
        @pl.loop(0, count // tile, unroll=UNROLL)
        def _(i):
            body(pl.ds(pl.multiple_of(i * tile, tile), tile))

    return run


def store_rows(outs, at, value):
    span = outs[0].shape[0]
    for e, ref in enumerate(outs):
        ref[:, at] = value[e * span : (e + 1) * span].astype(BF16)


def begin_kernel(*refs, experts):
    _, gate_ref, up_ref, down_hbm, gate_out, up_out, down_out, rows_ref, sems = refs[experts:]
    half = rows_ref.shape[1]
    copies = strip_copies(down_hbm, 0, down_out, sems)
    rows_ref[...] = stack(refs[:experts])
    units = gate_ref.shape[1]

    @tiles(units, min(TILE, units))
    def _(at):
        gate_out[:, at] = dot(rows_ref[...], gate_ref[:half, at])
        up_out[:, at] = dot(rows_ref[...], up_ref[:half, at])

    for copy in copies:
        copy.wait()


def middle_kernel(*refs, experts):
    gate_in, up_in, down_in, gate_ref, up_ref, down_hbm = refs[experts : experts + 6]
    outs = refs[experts + 6 : -4]
    hidden_ref, down_out, rows_ref, sems = refs[-4:]
    half = rows_ref.shape[1]
    copies = strip_copies(down_hbm, half, down_out, sems)
    rows_ref[...] = stack(refs[:experts])
    units = gate_ref.shape[1]

    @tiles(units, min(TILE, units))
    def _(at):
        gate = gate_in[:, at] + dot(rows_ref[...], gate_ref[half:, at])
        up = up_in[:, at] + dot(rows_ref[...], up_ref[half:, at])
        hidden_ref[:, at] = (jax.nn.silu(gate) * up).astype(BF16)

    @tiles(half, min(TILE, half))
    def _(at):
        store_rows(outs, at, dot(hidden_ref[...], down_in[:, at]))

    for copy in copies:
        copy.wait()


def end_kernel(hidden_ref, down_ref, *outs):
    half = down_ref.shape[1]

    @tiles(half, min(TILE, half))
    def _(at):
        store_rows(outs, at, dot(hidden_ref[...], down_ref[:, at]))


def mix_kernel(high_ref, low_ref, *refs, layers, part):
    refs = refs[part : len(refs) - part]
    outs, stream_ref = refs[-layers:], refs[-layers - 1]
    blocks = refs[: -layers - 1]
    order = even_first(len(blocks))
    returned = stack([blocks[order.index(e)] for e in range(len(blocks))])
    mixed = dot(high_ref[...], returned) + dot(low_ref[...], returned)
    batch, half = outs[0].shape
    for j, ref in enumerate(outs):
        value = mixed[j * batch : (j + 1) * batch]
        if j == 0:
            value = value + stream_ref[:, part * half : (part + 1) * half]
        ref[...] = value.astype(ref.dtype)


def add_kernel(*refs):
    out_ref, count = refs[-1], len(refs) // 2
    half = refs[0].shape[1]
    for begin, blocks in ((half, refs[:count]), (0, refs[count:-1])):
        total = blocks[0][...]
        for ref in blocks[1:]:
            total = total + ref[...].astype(F32)
        out_ref[:, begin : begin + half] = total.astype(BF16)


def in_hbm(value):
    return pltpu.with_memory_space_constraint(value, pltpu.HBM)


def swap(value, axis, step):
    if step == 0:
        return value
    count = lax.axis_size(axis)
    return lax.ppermute(value, axis, [(i, i ^ step) for i in range(count)])


def farthest_first(count):
    return [0, *range(count - 1, 0, -1)]


def even_first(count):
    return [*range(0, count, 2), *range(count - 1, 0, -2)]


def params(elements):
    return pltpu.CompilerParams(vmem_limit_bytes=min(48 * MIB, 2 * MIB + 10 * elements))


def shards(
    queries,
    cached_keys,
    cached_values,
    lengths,
    routes,
    residual,
    norm_gain,
    router,
    gate_proj,
    up_proj,
    down_proj,
):
    batch, width = queries.shape
    experts = router.shape[1]
    layers = lax.axis_size("attn")
    me = lax.axis_index("expert").astype(jnp.int32).reshape(1)
    router = router.T
    shape = jax.ShapeDtypeStruct
    operands = [
        in_hbm(a)
        for a in (
            lengths[None], queries, cached_keys, cached_values, routes.T, residual, norm_gain[None]
        )
    ]
    window, depth = cached_values.shape[1:]
    held = [a.shape for a in operands]
    held[3] = (batch, -(-window // LANES) * LANES, depth)
    half = width // 2
    stream, *payload = pl.pallas_call(
        attend_kernel,
        in_specs=[SCALAR] + [ANY] * len(operands),
        out_specs=[WHOLE] * 3,
        out_shape=[shape((batch, width), F32)]
        + [shape((batch, size), BF16) for size in (half + LANES, half)],
        scratch_shapes=[pltpu.VMEM(size, a.dtype) for size, a in zip(held, operands)]
        + [pltpu.SemaphoreType.DMA((5 + 2 * (batch // BLOCK),))],
        compiler_params=params(28 * batch * width),
        cost_estimate=LIGHT,
    )(me, *operands)

    payload = pass_on(payload, BUSY)

    order = even_first(experts)
    placed = [0, *even_first(layers)[:0:-1]]
    chunks, arrived = [], []
    for part in range(2):
        came = {j: swap(payload[part], "attn", j) for j in even_first(layers)}
        chunks += [came[j] for j in placed]
        slots = pl.pallas_call(
            functools.partial(split_kernel, layers=layers, part=part),
            in_specs=[SCALAR] + [WHOLE] * len(chunks),
            out_specs=[WHOLE] * experts,
            out_shape=[shape((layers * CAP, half), BF16)] * experts,
            cost_estimate=MID if part else LIGHT,
            compiler_params=params(experts * layers * CAP * half),
        )(me, *chunks)
        arrived.append([swap(slots[e], "expert", e) for e in order])
    gates = pl.pallas_call(
        functools.partial(weigh_kernel, layers=layers),
        in_specs=[SCALAR] + [WHOLE] * (1 + len(chunks)),
        out_specs=[WHOLE] * 2,
        out_shape=[shape((layers * batch, experts * layers * CAP), BF16)] * 2,
        cost_estimate=LIGHT,
        compiler_params=params(layers * batch * width),
    )(me, router, *chunks)

    total_rows = experts * layers * CAP
    units = gate_proj.shape[2]
    gate, up, down = gate_proj[0], up_proj[0], in_hbm(down_proj[0])
    rows = pltpu.VMEM((total_rows, half), BF16)
    strips = pltpu.SemaphoreType.DMA((STRIPS,))
    halves = [shape((layers * CAP, half), BF16)] * experts
    *sums, down_first = pl.pallas_call(
        functools.partial(begin_kernel, experts=experts),
        in_specs=[WHOLE] * experts + [ANY] + [WHOLE] * 2 + [ANY],
        out_specs=[WHOLE] * 3,
        out_shape=[shape((total_rows, units), F32)] * 2 + [pltpu.VMEM((units, half), BF16)],
        scratch_shapes=[rows, strips],
        cost_estimate=pl.CostEstimate(
            flops=4 * total_rows * half * units, bytes_accessed=0, transcendentals=0
        ),
        compiler_params=params(total_rows * width),
    )(*arrived[0], gates[0], gate, up, down)
    *first, hidden, down_second = pl.pallas_call(
        functools.partial(middle_kernel, experts=experts),
        in_specs=[WHOLE] * (experts + 5) + [ANY],
        out_specs=[WHOLE] * (experts + 2),
        out_shape=halves + [shape((total_rows, units), BF16), pltpu.VMEM((units, half), BF16)],
        scratch_shapes=[rows, strips],
        compiler_params=params(total_rows * width),
    )(*arrived[1], *sums, down_first, gate, up, down)
    second = pl.pallas_call(
        end_kernel,
        in_specs=[WHOLE] * 2,
        out_specs=[WHOLE] * experts,
        out_shape=halves,
        cost_estimate=pl.CostEstimate(
            flops=2 * total_rows * half * units, bytes_accessed=0, transcendentals=0
        ),
        compiler_params=params(total_rows * width),
    )(hidden, down_second)

    mixed, near = [], placed.index(1)
    for part, blocks in enumerate((first, second)):
        returned = [swap(block, "expert", e) for e, block in zip(order, blocks)]
        held = [mixed[0][near]] if part else []
        sizes = [shape((batch, half), BF16 if j else F32) for j in range(layers)]
        outs = pl.pallas_call(
            functools.partial(mix_kernel, layers=layers, part=part),
            in_specs=[WHOLE] * 2 + [ANY] * part + [WHOLE] * (1 + experts),
            out_specs=[WHOLE] * layers + [ANY] * part,
            out_shape=sizes + [shape((batch, half), BF16)] * part,
            input_output_aliases={2: layers} if part else {},
            cost_estimate=LIGHT,
            compiler_params=params(experts * layers * CAP * half),
        )(*gates, *held, *returned, stream)
        mixed.append(list(outs[:layers]))
        if part:
            mixed[0][near] = outs[layers]
    came = [
        swap(sums[placed.index(j)], "attn", j)
        for sums in mixed[::-1]
        for j in farthest_first(layers)
    ]
    return pl.pallas_call(
        add_kernel,
        in_specs=[WHOLE] * (2 * layers),
        out_specs=WHOLE,
        out_shape=shape((batch, width), BF16),
        cost_estimate=LIGHT,
        compiler_params=params(2 * layers * batch * width),
    )(*came)


def solution(mesh):
    in_specs = (
        P(("groups", "attn", "expert"), None),
        P(("groups", "attn", "expert"), None, None),
        P(("groups", "attn", "expert"), None, None),
        P(("groups", "attn", "expert")),
        P(("groups", "attn", "expert"), None),
        P(("groups", "attn", "expert"), None),
        P(),
        P(),
        P("expert", None, "attn"),
        P("expert", None, "attn"),
        P("expert", "attn", None),
    )
    out_specs = P(("groups", "attn", "expert"), None)
    return jax.shard_map(shards, mesh=mesh, in_specs=in_specs, out_specs=out_specs, check_vma=False)
```

```python
import functools

import jax
import jax.numpy as jnp
from jax import lax
from jax.experimental import pallas as pl
from jax.experimental.pallas import tpu as pltpu
from jax.sharding import PartitionSpec as P

HS = 128
KVH = 4
GROUP = 6
CAP = 8
LANES = 128
PAIR = 2
BLOCK = 8
STRIPS = 3
TILE = 256
UNROLL = 2
MIB = 1 << 20
F32 = jnp.float32
BF16 = jnp.bfloat16
LIGHT = pl.CostEstimate(flops=0, bytes_accessed=0, transcendentals=0)
BUSY = pl.CostEstimate(flops=24 * 10**9, bytes_accessed=0, transcendentals=0)
MID = pl.CostEstimate(flops=2 * 10**9, bytes_accessed=0, transcendentals=0)
ANY = pl.BlockSpec(memory_space=pl.ANY)
WHOLE = pl.BlockSpec(memory_space=pltpu.VMEM)
SCALAR = pl.BlockSpec(memory_space=pltpu.SMEM)


def dot(a, b, dims=((1,), (0,))):
    return lax.dot_general(a, b, (dims, ((), ())), preferred_element_type=F32)


def iota(shape, dim):
    return lax.broadcasted_iota(jnp.int32, shape, dim)


def split(index, size):
    if size & (size - 1):
        return lax.div(index, size), lax.rem(index, size)
    return index >> (size.bit_length() - 1), index & (size - 1)


def slot_map(me, named, chunks, experts):
    named = named[:, 0:4].astype(F32).astype(jnp.int32)
    owners, places = named[:, 0:2] ^ me, named[:, 2:4]
    rows, slots = named.shape[0], experts * chunks * CAP
    group, place = split(iota((rows, slots), 1), CAP)
    expert, chunk = split(group, chunks)
    taken = [(owners[:, k : k + 1] == expert) & (places[:, k : k + 1] == place) for k in range(2)]
    here = split(iota((rows, slots), 0), rows // chunks)[0] == chunk
    return taken[0] & here, taken[1] & here


def dispatch(me, rows, named, chunks, experts):
    first, second = slot_map(me, named, chunks, experts)
    table = jnp.where(first | second, 1.0, 0.0).astype(BF16)
    return dot(table, rows, ((0,), (0,)))


def weigh_kernel(me_ref, router_ref, *refs, layers):
    high_ref, low_ref = refs[-2:]
    parts, named = gather(refs[:-2], layers)
    rows = jnp.concatenate(parts, axis=1)
    routes = named[:, 0:2].astype(F32).astype(jnp.int32)
    logits = dot(rows, router_ref[...], ((1,), (1,)))
    experts = logits.shape[1]
    lane = iota(logits.shape, 1)
    first = jnp.sum(jnp.where(lane == routes[:, 0:1], logits, 0.0), axis=1, keepdims=True)
    second = jnp.sum(jnp.where(lane == routes[:, 1:2], logits, 0.0), axis=1, keepdims=True)
    gate0 = 1.0 / (1.0 + jnp.exp(second - first))
    gate1 = 1.0 / (1.0 + jnp.exp(first - second))
    taken = slot_map(me_ref[0], named, layers, experts)
    gates = jnp.where(taken[0], gate0, jnp.where(taken[1], gate1, 0.0))
    high = gates.astype(BF16)
    high_ref[...] = high
    low_ref[...] = (gates - high.astype(F32)).astype(BF16)


def attend_kernel(
    _, lengths_hbm, queries_hbm, keys_hbm, values_hbm, routes_hbm, residual_hbm, gain_hbm,
    stream_ref, first_ref, second_ref,
    lengths_ref, queries_ref, keys_ref, values_ref, routes_ref, residual_ref, gain_ref, sems,
):
    batch, window, _ = keys_ref.shape
    width = queries_ref.shape[1]
    span = width // KVH
    parts = [pl.ds(begin, PAIR * HS) for begin in range(0, KVH * HS, PAIR * HS)]
    small = [
        (lengths_hbm, lengths_ref), (queries_hbm, queries_ref), (routes_hbm, routes_ref),
        (residual_hbm, residual_ref), (gain_hbm, gain_ref),
    ]
    blocks = [pl.ds(begin, BLOCK) for begin in range(0, batch, BLOCK)]
    groups = [
        small[:3],
        *[[(keys_hbm.at[block], keys_ref.at[block])] for block in blocks],
        *[[(values_hbm.at[block], values_ref.at[block, 0:window])] for block in blocks],
        small[3:],
    ]
    at, copies = 0, []
    for group in groups:
        copies.append([])
        for source, target in group:
            copies[-1].append(pltpu.make_async_copy(source, target, sems.at[at]))
            copies[-1][-1].start()
            at += 1

    def wait(group):
        for copy in copies[group]:
            copy.wait()

    padded = values_ref.shape[1]
    if padded > window:
        pad = (batch, padded - window, values_ref.shape[2])
        values_ref[:, window:, :] = jnp.zeros(pad, BF16)
    wait(0)
    same = iota((batch, batch), 0) == iota((batch, batch), 1)

    def upright(row):
        return jnp.sum(jnp.where(same, row, 0), axis=1, keepdims=True)

    named, lane = jnp.zeros((batch, LANES), jnp.int32), iota((batch, LANES), 1)
    before = iota((batch, batch), 1) < iota((batch, batch), 0)
    listed = [routes_ref[k : k + 1, :] for k in range(2)]
    for k in range(2):
        route = upright(listed[k])
        earlier = before & ((listed[0] == route) | (listed[1] == route))
        place = jnp.sum(jnp.where(earlier, 1, 0), axis=1, keepdims=True)
        named = jnp.where(lane == k, route, jnp.where(lane == 2 + k, place, named))
    named = named.astype(F32).astype(BF16)
    queries = queries_ref[...]
    lanes = PAIR * GROUP * batch
    full = -(-lanes // LANES) * LANES
    _, request = split(iota((window, full), 1), batch)
    length = jnp.zeros((1, full), jnp.int32)
    for r in range(batch):
        length = jnp.where(request[0:1] == r, lengths_ref[0:1, r : r + 1], length)
    visible = iota((window, full), 0) < length
    _, owner = split(iota((lanes, padded), 0), batch)
    spreads = []
    for i in range(len(parts)):
        spread = []
        for k in range(PAIR):
            at = [(i * PAIR + k) * span + g * HS for g in range(GROUP)]
            stacked = jnp.concatenate([queries[:, c : c + HS] for c in at], axis=0)
            blank = jnp.zeros_like(stacked)
            spread.append(
                jnp.concatenate([stacked if j == k else blank for j in range(PAIR)], axis=1)
            )
        if full > lanes:
            spread.append(jnp.zeros((full - lanes, PAIR * HS), BF16))
        spreads.append(jnp.concatenate(spread, axis=0))
    total = [jnp.zeros((window, full), F32) for _ in parts]
    for b, block in enumerate(blocks):
        wait(1 + b)
        for i, part in enumerate(parts):
            keys = keys_ref[block, :, part].reshape(BLOCK * window, PAIR * HS)
            products = dot(keys, spreads[i], ((1,), (1,)))
            for r in range(BLOCK):
                mine = request == b * BLOCK + r
                total[i] = jnp.where(mine, products[r * window : (r + 1) * window], total[i])
    weighted = []
    for scores in total:
        scores = jnp.where(visible, scores * HS ** (-0.5), -1e30)
        powers = jnp.exp(scores - jnp.max(scores, axis=0, keepdims=True))
        weights = powers / jnp.sum(powers, axis=0, keepdims=True)
        if padded > window:
            weights = jnp.concatenate([weights, jnp.zeros((padded - window, full), F32)], axis=0)
        weights = weights.T[:lanes]
        weighted.append(
            jnp.concatenate(
                [jnp.where(owner == r, weights, 0.0).astype(BF16) for r in range(batch)], axis=1
            )
        )
    mixed = [0.0] * len(parts)
    reach = BLOCK * padded
    for b, block in enumerate(blocks):
        wait(1 + len(blocks) + b)
        for i, part in enumerate(parts):
            values = values_ref[block, :, part].reshape(reach, PAIR * HS)
            mixed[i] = mixed[i] + dot(weighted[i][:, b * reach : (b + 1) * reach], values)
    attended = [
        block[h * batch : (h + 1) * batch, h // GROUP * HS : (h // GROUP + 1) * HS]
        for block in mixed
        for h in range(PAIR * GROUP)
    ]
    wait(-1)
    stream = residual_ref[...].astype(F32) + jnp.concatenate(attended, axis=1)
    scale = lax.rsqrt(jnp.mean(stream * stream, axis=1, keepdims=True) + 1e-05)
    stream_ref[...] = stream
    half = width // 2
    normed = (stream * scale * gain_ref[...]).astype(BF16)
    first_ref[:, :half] = normed[:, :half]
    first_ref[:, half:] = named
    second_ref[...] = normed[:, half:]


def pass_kernel(*_):
    pass


def pass_on(values, cost):
    return pl.pallas_call(
        pass_kernel,
        in_specs=[ANY] * len(values),
        out_specs=[ANY] * len(values),
        out_shape=[jax.ShapeDtypeStruct(value.shape, value.dtype) for value in values],
        input_output_aliases={i: i for i in range(len(values))},
        cost_estimate=cost,
        compiler_params=params(0),
    )(*values)


def stack(refs):
    return jnp.concatenate([ref[...] for ref in refs], axis=0)


def gather(refs, layers):
    first = stack(refs[:layers])
    half = first.shape[1] - LANES
    parts = [first[:, :half]] + [stack(refs[at : at + layers]) for at in range(layers, len(refs), layers)]
    return parts, first[:, half:]


def split_kernel(me_ref, *refs, layers, part):
    parts, named = gather(refs[: (1 + part) * layers], layers)
    outs = refs[(1 + part) * layers :]
    slots = dispatch(me_ref[0], parts[part], named, layers, len(outs))
    span = layers * CAP
    for e, ref in enumerate(outs):
        ref[...] = slots[e * span : (e + 1) * span].astype(BF16)


def strip_copies(source, begin, target, sems):
    strip = target.shape[1] // sems.shape[0]
    copies = [
        pltpu.make_async_copy(
            source.at[:, pl.ds(begin + c * strip, strip)],
            target.at[:, pl.ds(c * strip, strip)],
            sems.at[c],
        )
        for c in range(sems.shape[0])
    ]
    for copy in copies:
        copy.start()
    return copies


def tiles(count, tile):
    def run(body):
        @pl.loop(0, count // tile, unroll=UNROLL)
        def _(i):
            body(pl.ds(pl.multiple_of(i * tile, tile), tile))

    return run


def store_rows(outs, at, value):
    span = outs[0].shape[0]
    for e, ref in enumerate(outs):
        ref[:, at] = value[e * span : (e + 1) * span].astype(BF16)


def begin_kernel(*refs, experts):
    _, gate_ref, up_ref, down_hbm, gate_out, up_out, down_out, rows_ref, sems = refs[experts:]
    half = rows_ref.shape[1]
    copies = strip_copies(down_hbm, 0, down_out, sems)
    rows_ref[...] = stack(refs[:experts])
    units = gate_ref.shape[1]

    @tiles(units, min(TILE, units))
    def _(at):
        gate_out[:, at] = dot(rows_ref[...], gate_ref[:half, at])
        up_out[:, at] = dot(rows_ref[...], up_ref[:half, at])

    for copy in copies:
        copy.wait()


def middle_kernel(*refs, experts):
    gate_in, up_in, down_in, gate_ref, up_ref, down_hbm = refs[experts : experts + 6]
    outs = refs[experts + 6 : -4]
    hidden_ref, down_out, rows_ref, sems = refs[-4:]
    half = rows_ref.shape[1]
    copies = strip_copies(down_hbm, half, down_out, sems)
    rows_ref[...] = stack(refs[:experts])
    units = gate_ref.shape[1]

    @tiles(units, min(TILE, units))
    def _(at):
        gate = gate_in[:, at] + dot(rows_ref[...], gate_ref[half:, at])
        up = up_in[:, at] + dot(rows_ref[...], up_ref[half:, at])
        hidden_ref[:, at] = (jax.nn.silu(gate) * up).astype(BF16)

    @tiles(half, min(TILE, half))
    def _(at):
        store_rows(outs, at, dot(hidden_ref[...], down_in[:, at]))

    for copy in copies:
        copy.wait()


def end_kernel(hidden_ref, down_ref, *outs):
    half = down_ref.shape[1]

    @tiles(half, min(TILE, half))
    def _(at):
        store_rows(outs, at, dot(hidden_ref[...], down_ref[:, at]))


def mix_kernel(high_ref, low_ref, *refs, layers, part):
    refs = refs[part : len(refs) - part]
    outs, stream_ref = refs[-layers:], refs[-layers - 1]
    blocks = refs[: -layers - 1]
    order = even_first(len(blocks))
    returned = stack([blocks[order.index(e)] for e in range(len(blocks))])
    mixed = dot(high_ref[...], returned) + dot(low_ref[...], returned)
    batch, half = outs[0].shape
    for j, ref in enumerate(outs):
        value = mixed[j * batch : (j + 1) * batch]
        if j == 0:
            value = value + stream_ref[:, part * half : (part + 1) * half]
        ref[...] = value.astype(ref.dtype)


def add_kernel(*refs):
    out_ref, count = refs[-1], len(refs) // 2
    half = refs[0].shape[1]
    for begin, blocks in ((half, refs[:count]), (0, refs[count:-1])):
        total = blocks[0][...]
        for ref in blocks[1:]:
            total = total + ref[...].astype(F32)
        out_ref[:, begin : begin + half] = total.astype(BF16)


def in_hbm(value):
    return pltpu.with_memory_space_constraint(value, pltpu.HBM)


def swap(value, axis, step):
    if step == 0:
        return value
    count = lax.axis_size(axis)
    return lax.ppermute(value, axis, [(i, i ^ step) for i in range(count)])


def farthest_first(count):
    return [0, *range(count - 1, 0, -1)]


def even_first(count):
    return [*range(0, count, 2), *range(count - 1, 0, -2)]


def params(elements):
    return pltpu.CompilerParams(vmem_limit_bytes=min(48 * MIB, 2 * MIB + 10 * elements))


def shards(
    queries,
    cached_keys,
    cached_values,
    lengths,
    routes,
    residual,
    norm_gain,
    router,
    gate_proj,
    up_proj,
    down_proj,
):
    batch, width = queries.shape
    experts = router.shape[1]
    layers = lax.axis_size("attn")
    me = lax.axis_index("expert").astype(jnp.int32).reshape(1)
    router = router.T
    shape = jax.ShapeDtypeStruct
    operands = [
        in_hbm(a)
        for a in (
            lengths[None], queries, cached_keys, cached_values, routes.T, residual, norm_gain[None]
        )
    ]
    window, depth = cached_values.shape[1:]
    held = [a.shape for a in operands]
    held[3] = (batch, -(-window // LANES) * LANES, depth)
    half = width // 2
    stream, *payload = pl.pallas_call(
        attend_kernel,
        in_specs=[SCALAR] + [ANY] * len(operands),
        out_specs=[WHOLE] * 3,
        out_shape=[shape((batch, width), F32)]
        + [shape((batch, size), BF16) for size in (half + LANES, half)],
        scratch_shapes=[pltpu.VMEM(size, a.dtype) for size, a in zip(held, operands)]
        + [pltpu.SemaphoreType.DMA((5 + 2 * (batch // BLOCK),))],
        compiler_params=params(28 * batch * width),
        cost_estimate=LIGHT,
    )(me, *operands)

    payload = pass_on(payload, BUSY)

    order = even_first(experts)
    placed = list(range(layers))
    chunks, arrived = [], []
    for part in range(2):
        came = {j: swap(payload[part], "attn", j) for j in even_first(layers)}
        chunks += [came[j] for j in placed]
        slots = pl.pallas_call(
            functools.partial(split_kernel, layers=layers, part=part),
            in_specs=[SCALAR] + [WHOLE] * len(chunks),
            out_specs=[WHOLE] * experts,
            out_shape=[shape((layers * CAP, half), BF16)] * experts,
            cost_estimate=MID if part else LIGHT,
            compiler_params=params(experts * layers * CAP * half),
        )(me, *chunks)
        arrived.append([swap(slots[e], "expert", e) for e in order])
    gates = pl.pallas_call(
        functools.partial(weigh_kernel, layers=layers),
        in_specs=[SCALAR] + [WHOLE] * (1 + len(chunks)),
        out_specs=[WHOLE] * 2,
        out_shape=[shape((layers * batch, experts * layers * CAP), BF16)] * 2,
        cost_estimate=LIGHT,
        compiler_params=params(layers * batch * width),
    )(me, router, *chunks)

    total_rows = experts * layers * CAP
    units = gate_proj.shape[2]
    gate, up, down = gate_proj[0], up_proj[0], in_hbm(down_proj[0])
    rows = pltpu.VMEM((total_rows, half), BF16)
    strips = pltpu.SemaphoreType.DMA((STRIPS,))
    halves = [shape((layers * CAP, half), BF16)] * experts
    *sums, down_first = pl.pallas_call(
        functools.partial(begin_kernel, experts=experts),
        in_specs=[WHOLE] * experts + [ANY] + [WHOLE] * 2 + [ANY],
        out_specs=[WHOLE] * 3,
        out_shape=[shape((total_rows, units), F32)] * 2 + [pltpu.VMEM((units, half), BF16)],
        scratch_shapes=[rows, strips],
        cost_estimate=pl.CostEstimate(
            flops=4 * total_rows * half * units, bytes_accessed=0, transcendentals=0
        ),
        compiler_params=params(total_rows * width),
    )(*arrived[0], gates[0], gate, up, down)
    *first, hidden, down_second = pl.pallas_call(
        functools.partial(middle_kernel, experts=experts),
        in_specs=[WHOLE] * (experts + 5) + [ANY],
        out_specs=[WHOLE] * (experts + 2),
        out_shape=halves + [shape((total_rows, units), BF16), pltpu.VMEM((units, half), BF16)],
        scratch_shapes=[rows, strips],
        compiler_params=params(total_rows * width),
    )(*arrived[1], *sums, down_first, gate, up, down)
    second = pl.pallas_call(
        end_kernel,
        in_specs=[WHOLE] * 2,
        out_specs=[WHOLE] * experts,
        out_shape=halves,
        cost_estimate=pl.CostEstimate(
            flops=2 * total_rows * half * units, bytes_accessed=0, transcendentals=0
        ),
        compiler_params=params(total_rows * width),
    )(hidden, down_second)

    mixed, near = [], placed.index(1)
    for part, blocks in enumerate((first, second)):
        returned = [swap(block, "expert", e) for e, block in zip(order, blocks)]
        held = [mixed[0][near]] if part else []
        sizes = [shape((batch, half), BF16 if j else F32) for j in range(layers)]
        outs = pl.pallas_call(
            functools.partial(mix_kernel, layers=layers, part=part),
            in_specs=[WHOLE] * 2 + [ANY] * part + [WHOLE] * (1 + experts),
            out_specs=[WHOLE] * layers + [ANY] * part,
            out_shape=sizes + [shape((batch, half), BF16)] * part,
            input_output_aliases={2: layers} if part else {},
            cost_estimate=LIGHT,
            compiler_params=params(experts * layers * CAP * half),
        )(*gates, *held, *returned, stream)
        mixed.append(list(outs[:layers]))
        if part:
            mixed[0][near] = outs[layers]
    came = [
        swap(sums[placed.index(j)], "attn", j)
        for sums in mixed[::-1]
        for j in farthest_first(layers)
    ]
    return pl.pallas_call(
        add_kernel,
        in_specs=[WHOLE] * (2 * layers),
        out_specs=WHOLE,
        out_shape=shape((batch, width), BF16),
        cost_estimate=LIGHT,
        compiler_params=params(2 * layers * batch * width),
    )(*came)


def solution(mesh):
    in_specs = (
        P(("groups", "attn", "expert"), None),
        P(("groups", "attn", "expert"), None, None),
        P(("groups", "attn", "expert"), None, None),
        P(("groups", "attn", "expert")),
        P(("groups", "attn", "expert"), None),
        P(("groups", "attn", "expert"), None),
        P(),
        P(),
        P("expert", None, "attn"),
        P("expert", None, "attn"),
        P("expert", "attn", None),
    )
    out_specs = P(("groups", "attn", "expert"), None)
    return jax.shard_map(shards, mesh=mesh, in_specs=in_specs, out_specs=out_specs, check_vma=False)
```

```python
import functools

import jax
import jax.numpy as jnp
from jax import lax
from jax.experimental import pallas as pl
from jax.experimental.pallas import tpu as pltpu
from jax.sharding import PartitionSpec as P

HS = 128
KVH = 4
GROUP = 6
CAP = 8
LANES = 128
PAIR = 2
BLOCK = 8
STRIPS = 3
TILE = 256
UNROLL = 4
MIB = 1 << 20
F32 = jnp.float32
BF16 = jnp.bfloat16
LIGHT = pl.CostEstimate(flops=0, bytes_accessed=0, transcendentals=0)
BUSY = pl.CostEstimate(flops=24 * 10**9, bytes_accessed=0, transcendentals=0)
MID = pl.CostEstimate(flops=2 * 10**9, bytes_accessed=0, transcendentals=0)
ANY = pl.BlockSpec(memory_space=pl.ANY)
WHOLE = pl.BlockSpec(memory_space=pltpu.VMEM)
SCALAR = pl.BlockSpec(memory_space=pltpu.SMEM)


def dot(a, b, dims=((1,), (0,))):
    return lax.dot_general(a, b, (dims, ((), ())), preferred_element_type=F32)


def iota(shape, dim):
    return lax.broadcasted_iota(jnp.int32, shape, dim)


def split(index, size):
    if size & (size - 1):
        return lax.div(index, size), lax.rem(index, size)
    return index >> (size.bit_length() - 1), index & (size - 1)


def slot_map(me, named, chunks, experts):
    named = named[:, 0:4].astype(F32).astype(jnp.int32)
    owners, places = named[:, 0:2] ^ me, named[:, 2:4]
    rows, slots = named.shape[0], experts * chunks * CAP
    group, place = split(iota((rows, slots), 1), CAP)
    expert, chunk = split(group, chunks)
    taken = [(owners[:, k : k + 1] == expert) & (places[:, k : k + 1] == place) for k in range(2)]
    here = split(iota((rows, slots), 0), rows // chunks)[0] == chunk
    return taken[0] & here, taken[1] & here


def dispatch(me, rows, named, chunks, experts):
    first, second = slot_map(me, named, chunks, experts)
    table = jnp.where(first | second, 1.0, 0.0).astype(BF16)
    return dot(table, rows, ((0,), (0,)))


def weigh_kernel(me_ref, router_ref, *refs, layers):
    high_ref, low_ref = refs[-2:]
    parts, named = gather(refs[:-2], layers)
    rows = jnp.concatenate(parts, axis=1)
    routes = named[:, 0:2].astype(F32).astype(jnp.int32)
    logits = dot(rows, router_ref[...], ((1,), (1,)))
    experts = logits.shape[1]
    lane = iota(logits.shape, 1)
    first = jnp.sum(jnp.where(lane == routes[:, 0:1], logits, 0.0), axis=1, keepdims=True)
    second = jnp.sum(jnp.where(lane == routes[:, 1:2], logits, 0.0), axis=1, keepdims=True)
    gate0 = 1.0 / (1.0 + jnp.exp(second - first))
    gate1 = 1.0 / (1.0 + jnp.exp(first - second))
    taken = slot_map(me_ref[0], named, layers, experts)
    gates = jnp.where(taken[0], gate0, jnp.where(taken[1], gate1, 0.0))
    high = gates.astype(BF16)
    high_ref[...] = high
    low_ref[...] = (gates - high.astype(F32)).astype(BF16)


def attend_kernel(
    _, lengths_hbm, queries_hbm, keys_hbm, values_hbm, routes_hbm, residual_hbm, gain_hbm,
    stream_ref, first_ref, second_ref,
    lengths_ref, queries_ref, keys_ref, values_ref, routes_ref, residual_ref, gain_ref, sems,
):
    batch, window, _ = keys_ref.shape
    width = queries_ref.shape[1]
    span = width // KVH
    parts = [pl.ds(begin, PAIR * HS) for begin in range(0, KVH * HS, PAIR * HS)]
    small = [
        (lengths_hbm, lengths_ref), (queries_hbm, queries_ref), (routes_hbm, routes_ref),
        (residual_hbm, residual_ref), (gain_hbm, gain_ref),
    ]
    blocks = [pl.ds(begin, BLOCK) for begin in range(0, batch, BLOCK)]
    groups = [
        small[:3],
        *[[(keys_hbm.at[block], keys_ref.at[block])] for block in blocks],
        [(values_hbm.at[block], values_ref.at[block, 0:window]) for block in blocks],
        small[3:],
    ]
    at, copies = 0, []
    for group in groups:
        copies.append([])
        for source, target in group:
            copies[-1].append(pltpu.make_async_copy(source, target, sems.at[at]))
            copies[-1][-1].start()
            at += 1

    def wait(group):
        for copy in copies[group]:
            copy.wait()

    padded = values_ref.shape[1]
    if padded > window:
        pad = (batch, padded - window, values_ref.shape[2])
        values_ref[:, window:, :] = jnp.zeros(pad, BF16)
    wait(0)
    same = iota((batch, batch), 0) == iota((batch, batch), 1)

    def upright(row):
        return jnp.sum(jnp.where(same, row, 0), axis=1, keepdims=True)

    named, lane = jnp.zeros((batch, LANES), jnp.int32), iota((batch, LANES), 1)
    before = iota((batch, batch), 1) < iota((batch, batch), 0)
    listed = [routes_ref[k : k + 1, :] for k in range(2)]
    for k in range(2):
        route = upright(listed[k])
        earlier = before & ((listed[0] == route) | (listed[1] == route))
        place = jnp.sum(jnp.where(earlier, 1, 0), axis=1, keepdims=True)
        named = jnp.where(lane == k, route, jnp.where(lane == 2 + k, place, named))
    named = named.astype(F32).astype(BF16)
    queries = queries_ref[...]
    lanes = PAIR * GROUP * batch
    full = -(-lanes // LANES) * LANES
    _, request = split(iota((window, full), 1), batch)
    length = jnp.zeros((1, full), jnp.int32)
    for r in range(batch):
        length = jnp.where(request[0:1] == r, lengths_ref[0:1, r : r + 1], length)
    visible = iota((window, full), 0) < length
    _, owner = split(iota((lanes, padded), 0), batch)
    spreads = []
    for i in range(len(parts)):
        spread = []
        for k in range(PAIR):
            at = [(i * PAIR + k) * span + g * HS for g in range(GROUP)]
            stacked = jnp.concatenate([queries[:, c : c + HS] for c in at], axis=0)
            blank = jnp.zeros_like(stacked)
            spread.append(
                jnp.concatenate([stacked if j == k else blank for j in range(PAIR)], axis=1)
            )
        if full > lanes:
            spread.append(jnp.zeros((full - lanes, PAIR * HS), BF16))
        spreads.append(jnp.concatenate(spread, axis=0))
    total = [jnp.zeros((window, full), F32) for _ in parts]
    for b, block in enumerate(blocks):
        wait(1 + b)
        for i, part in enumerate(parts):
            keys = keys_ref[block, :, part].reshape(BLOCK * window, PAIR * HS)
            products = dot(keys, spreads[i], ((1,), (1,)))
            for r in range(BLOCK):
                mine = request == b * BLOCK + r
                total[i] = jnp.where(mine, products[r * window : (r + 1) * window], total[i])
    weighted = []
    for scores in total:
        scores = jnp.where(visible, scores * HS ** (-0.5), -1e30)
        powers = jnp.exp(scores - jnp.max(scores, axis=0, keepdims=True))
        weights = powers / jnp.sum(powers, axis=0, keepdims=True)
        if padded > window:
            weights = jnp.concatenate([weights, jnp.zeros((padded - window, full), F32)], axis=0)
        weights = weights.T[:lanes]
        weighted.append(
            jnp.concatenate(
                [jnp.where(owner == r, weights, 0.0).astype(BF16) for r in range(batch)], axis=1
            )
        )
    wait(-2)
    attended = []
    for weights, part in zip(weighted, parts):
        values = values_ref[:, :, part].reshape(batch * padded, PAIR * HS)
        mixed = dot(weights, values)
        attended += [
            mixed[h * batch : (h + 1) * batch, h // GROUP * HS : (h // GROUP + 1) * HS]
            for h in range(PAIR * GROUP)
        ]
    wait(-1)
    stream = residual_ref[...].astype(F32) + jnp.concatenate(attended, axis=1)
    scale = lax.rsqrt(jnp.mean(stream * stream, axis=1, keepdims=True) + 1e-05)
    stream_ref[...] = stream
    half = width // 2
    normed = (stream * scale * gain_ref[...]).astype(BF16)
    first_ref[:, :half] = normed[:, :half]
    first_ref[:, half:] = named
    second_ref[...] = normed[:, half:]


def pass_kernel(*_):
    pass


def pass_on(values, cost):
    return pl.pallas_call(
        pass_kernel,
        in_specs=[ANY] * len(values),
        out_specs=[ANY] * len(values),
        out_shape=[jax.ShapeDtypeStruct(value.shape, value.dtype) for value in values],
        input_output_aliases={i: i for i in range(len(values))},
        cost_estimate=cost,
        compiler_params=params(0),
    )(*values)


def stack(refs):
    return jnp.concatenate([ref[...] for ref in refs], axis=0)


def gather(refs, layers):
    first = stack(refs[:layers])
    half = first.shape[1] - LANES
    parts = [first[:, :half]] + [stack(refs[at : at + layers]) for at in range(layers, len(refs), layers)]
    return parts, first[:, half:]


def split_kernel(me_ref, *refs, layers, part):
    parts, named = gather(refs[: (1 + part) * layers], layers)
    outs = refs[(1 + part) * layers :]
    slots = dispatch(me_ref[0], parts[part], named, layers, len(outs))
    span = layers * CAP
    for e, ref in enumerate(outs):
        ref[...] = slots[e * span : (e + 1) * span].astype(BF16)


def strip_copies(source, begin, target, sems):
    strip = target.shape[1] // sems.shape[0]
    copies = [
        pltpu.make_async_copy(
            source.at[:, pl.ds(begin + c * strip, strip)],
            target.at[:, pl.ds(c * strip, strip)],
            sems.at[c],
        )
        for c in range(sems.shape[0])
    ]
    for copy in copies:
        copy.start()
    return copies


def tiles(count, tile):
    steps = count // tile
    unroll = max(u for u in range(1, UNROLL + 1) if steps % u == 0)

    def run(body):
        @pl.loop(0, steps, unroll=unroll)
        def _(i):
            body(pl.ds(pl.multiple_of(i * tile, tile), tile))

    return run


def store_rows(outs, at, value):
    span = outs[0].shape[0]
    for e, ref in enumerate(outs):
        ref[:, at] = value[e * span : (e + 1) * span].astype(BF16)


def begin_kernel(*refs, experts):
    _, gate_ref, up_ref, down_hbm, gate_out, up_out, down_out, rows_ref, sems = refs[experts:]
    half = rows_ref.shape[1]
    copies = strip_copies(down_hbm, 0, down_out, sems)
    rows_ref[...] = stack(refs[:experts])
    units = gate_ref.shape[1]

    @tiles(units, min(TILE, units))
    def _(at):
        gate_out[:, at] = dot(rows_ref[...], gate_ref[:half, at])
        up_out[:, at] = dot(rows_ref[...], up_ref[:half, at])

    for copy in copies:
        copy.wait()


def middle_kernel(*refs, experts):
    gate_in, up_in, down_in, gate_ref, up_ref, down_hbm = refs[experts : experts + 6]
    outs = refs[experts + 6 : -4]
    hidden_ref, down_out, rows_ref, sems = refs[-4:]
    half = rows_ref.shape[1]
    copies = strip_copies(down_hbm, half, down_out, sems)
    rows_ref[...] = stack(refs[:experts])
    units = gate_ref.shape[1]

    @tiles(units, min(TILE, units))
    def _(at):
        gate = gate_in[:, at] + dot(rows_ref[...], gate_ref[half:, at])
        up = up_in[:, at] + dot(rows_ref[...], up_ref[half:, at])
        hidden_ref[:, at] = (jax.nn.silu(gate) * up).astype(BF16)

    @tiles(half, min(TILE, half))
    def _(at):
        store_rows(outs, at, dot(hidden_ref[...], down_in[:, at]))

    for copy in copies:
        copy.wait()


def end_kernel(hidden_ref, down_ref, *outs):
    half = down_ref.shape[1]

    @tiles(half, min(TILE, half))
    def _(at):
        store_rows(outs, at, dot(hidden_ref[...], down_ref[:, at]))


def mix_kernel(high_ref, low_ref, *refs, layers, part):
    outs, stream_ref = refs[-layers:], refs[-layers - 1]
    blocks = refs[: -layers - 1]
    order = same_core_first(len(blocks))
    returned = stack([blocks[order.index(e)] for e in range(len(blocks))])
    mixed = dot(high_ref[...], returned) + dot(low_ref[...], returned)
    batch, half = outs[0].shape
    for j, ref in enumerate(outs):
        value = mixed[j * batch : (j + 1) * batch]
        if j == 0:
            value = value + stream_ref[:, part * half : (part + 1) * half]
        ref[...] = value.astype(ref.dtype)


def add_kernel(*refs):
    out_ref = refs[-1]
    span = refs[-2].shape[1]
    if out_ref.shape[1] > span:
        out_ref[:, :span] = refs[0][...]
        refs = refs[1:]
    total = refs[0][...]
    for ref in refs[1:-1]:
        total = total + ref[...].astype(F32)
    out_ref[:, out_ref.shape[1] - span :] = total.astype(BF16)


def in_hbm(value):
    return pltpu.with_memory_space_constraint(value, pltpu.HBM)


def swap(value, axis, step):
    if step == 0:
        return value
    count = lax.axis_size(axis)
    return lax.ppermute(value, axis, [(i, i ^ step) for i in range(count)])


def farthest_first(count):
    return [0, *range(count - 1, 0, -1)]


def same_core_first(count):
    return [*range(0, count, 2), *range(count - 1, 0, -2)]


def params(elements):
    return pltpu.CompilerParams(vmem_limit_bytes=min(48 * MIB, 2 * MIB + 10 * elements))


def shards(
    queries,
    cached_keys,
    cached_values,
    lengths,
    routes,
    residual,
    norm_gain,
    router,
    gate_proj,
    up_proj,
    down_proj,
):
    batch, width = queries.shape
    experts = router.shape[1]
    layers = lax.axis_size("attn")
    me = lax.axis_index("expert").astype(jnp.int32).reshape(1)
    router = router.T
    shape = jax.ShapeDtypeStruct
    operands = [
        in_hbm(a)
        for a in (
            lengths[None], queries, cached_keys, cached_values, routes.T, residual, norm_gain[None]
        )
    ]
    window, depth = cached_values.shape[1:]
    held = [a.shape for a in operands]
    held[3] = (batch, -(-window // LANES) * LANES, depth)
    half = width // 2
    stream, *payload = pl.pallas_call(
        attend_kernel,
        in_specs=[SCALAR] + [ANY] * len(operands),
        out_specs=[WHOLE] * 3,
        out_shape=[shape((batch, width), F32)]
        + [shape((batch, size), BF16) for size in (half + LANES, half)],
        scratch_shapes=[pltpu.VMEM(size, a.dtype) for size, a in zip(held, operands)]
        + [pltpu.SemaphoreType.DMA((5 + 2 * (batch // BLOCK),))],
        compiler_params=params(28 * batch * width),
        cost_estimate=LIGHT,
    )(me, *operands)

    payload = pass_on(payload, BUSY)

    order = same_core_first(experts)
    chunks, arrived = [], []
    for part in range(2):
        came = {j: swap(payload[part], "attn", j) for j in farthest_first(layers)}
        chunks += [came[j] for j in range(layers)]
        slots = pl.pallas_call(
            functools.partial(split_kernel, layers=layers, part=part),
            in_specs=[SCALAR] + [WHOLE] * len(chunks),
            out_specs=[WHOLE] * experts,
            out_shape=[shape((layers * CAP, half), BF16)] * experts,
            cost_estimate=MID if part else LIGHT,
            compiler_params=params(experts * layers * CAP * half),
        )(me, *chunks)
        arrived.append([swap(slots[e], "expert", e) for e in order])
    gates = pl.pallas_call(
        functools.partial(weigh_kernel, layers=layers),
        in_specs=[SCALAR] + [WHOLE] * (1 + len(chunks)),
        out_specs=[WHOLE] * 2,
        out_shape=[shape((layers * batch, experts * layers * CAP), BF16)] * 2,
        cost_estimate=LIGHT,
        compiler_params=params(layers * batch * width),
    )(me, router, *chunks)

    total_rows = experts * layers * CAP
    units = gate_proj.shape[2]
    gate, up, down = gate_proj[0], up_proj[0], in_hbm(down_proj[0])
    rows = pltpu.VMEM((total_rows, half), BF16)
    strips = pltpu.SemaphoreType.DMA((STRIPS,))
    halves = [shape((layers * CAP, half), BF16)] * experts
    *sums, down_first = pl.pallas_call(
        functools.partial(begin_kernel, experts=experts),
        in_specs=[WHOLE] * experts + [ANY] + [WHOLE] * 2 + [ANY],
        out_specs=[WHOLE] * 3,
        out_shape=[shape((total_rows, units), F32)] * 2 + [pltpu.VMEM((units, half), BF16)],
        scratch_shapes=[rows, strips],
        cost_estimate=pl.CostEstimate(
            flops=4 * total_rows * half * units, bytes_accessed=0, transcendentals=0
        ),
        compiler_params=params(total_rows * width),
    )(*arrived[0], gates[0], gate, up, down)
    *first, hidden, down_second = pl.pallas_call(
        functools.partial(middle_kernel, experts=experts),
        in_specs=[WHOLE] * (experts + 5) + [ANY],
        out_specs=[WHOLE] * (experts + 2),
        out_shape=halves + [shape((total_rows, units), BF16), pltpu.VMEM((units, half), BF16)],
        scratch_shapes=[rows, strips],
        compiler_params=params(total_rows * width),
    )(*arrived[1], *sums, down_first, gate, up, down)
    second = pl.pallas_call(
        end_kernel,
        in_specs=[WHOLE] * 2,
        out_specs=[WHOLE] * experts,
        out_shape=halves,
        cost_estimate=pl.CostEstimate(
            flops=2 * total_rows * half * units, bytes_accessed=0, transcendentals=0
        ),
        compiler_params=params(total_rows * width),
    )(hidden, down_second)

    done = []
    for part, blocks in enumerate((first, second)):
        returned = [swap(block, "expert", e) for e, block in zip(order, blocks)]
        mixed = pl.pallas_call(
            functools.partial(mix_kernel, layers=layers, part=part),
            in_specs=[WHOLE] * (3 + experts),
            out_specs=[WHOLE] * layers,
            out_shape=[shape((batch, half), BF16 if j else F32) for j in range(layers)],
            cost_estimate=LIGHT,
            compiler_params=params(experts * layers * CAP * half),
        )(*gates, *returned, stream)
        sums = [swap(mixed[j], "attn", j) for j in farthest_first(layers)]
        done = [
            pl.pallas_call(
                add_kernel,
                in_specs=[WHOLE] * (layers + len(done)),
                out_specs=WHOLE,
                out_shape=shape((batch, width if part else half), BF16),
                cost_estimate=LIGHT,
                compiler_params=params(layers * batch * width),
            )(*done, *sums)
        ]
    return done[0]


def solution(mesh):
    in_specs = (
        P(("groups", "attn", "expert"), None),
        P(("groups", "attn", "expert"), None, None),
        P(("groups", "attn", "expert"), None, None),
        P(("groups", "attn", "expert")),
        P(("groups", "attn", "expert"), None),
        P(("groups", "attn", "expert"), None),
        P(),
        P(),
        P("expert", None, "attn"),
        P("expert", None, "attn"),
        P("expert", "attn", None),
    )
    out_specs = P(("groups", "attn", "expert"), None)
    return jax.shard_map(shards, mesh=mesh, in_specs=in_specs, out_specs=out_specs, check_vma=False)
```

```python
import functools

import jax
import jax.numpy as jnp
from jax import lax
from jax.experimental import pallas as pl
from jax.experimental.pallas import tpu as pltpu
from jax.sharding import PartitionSpec as P

HS = 128
KVH = 4
GROUP = 6
CAP = 8
LANES = 128
PAIR = 2
BLOCK = 8
STRIPS = 3
TILE = 256
UNROLL = 8
MIB = 1 << 20
F32 = jnp.float32
BF16 = jnp.bfloat16
LIGHT = pl.CostEstimate(flops=0, bytes_accessed=0, transcendentals=0)
BUSY = pl.CostEstimate(flops=24 * 10**9, bytes_accessed=0, transcendentals=0)
MID = pl.CostEstimate(flops=2 * 10**9, bytes_accessed=0, transcendentals=0)
ANY = pl.BlockSpec(memory_space=pl.ANY)
WHOLE = pl.BlockSpec(memory_space=pltpu.VMEM)
SCALAR = pl.BlockSpec(memory_space=pltpu.SMEM)


def dot(a, b, dims=((1,), (0,))):
    return lax.dot_general(a, b, (dims, ((), ())), preferred_element_type=F32)


def iota(shape, dim):
    return lax.broadcasted_iota(jnp.int32, shape, dim)


def split(index, size):
    if size & (size - 1):
        return lax.div(index, size), lax.rem(index, size)
    return index >> (size.bit_length() - 1), index & (size - 1)


def slot_map(me, named, chunks, experts):
    named = named[:, 0:4].astype(F32).astype(jnp.int32)
    owners, places = named[:, 0:2] ^ me, named[:, 2:4]
    rows, slots = named.shape[0], experts * chunks * CAP
    group, place = split(iota((rows, slots), 1), CAP)
    expert, chunk = split(group, chunks)
    taken = [(owners[:, k : k + 1] == expert) & (places[:, k : k + 1] == place) for k in range(2)]
    here = split(iota((rows, slots), 0), rows // chunks)[0] == chunk
    return taken[0] & here, taken[1] & here


def dispatch(me, rows, named, chunks, experts):
    first, second = slot_map(me, named, chunks, experts)
    table = jnp.where(first | second, 1.0, 0.0).astype(BF16)
    return dot(table, rows, ((0,), (0,)))


def weigh_kernel(me_ref, router_ref, *refs, layers):
    high_ref, low_ref = refs[-2:]
    parts, named = gather(refs[:-2], layers)
    rows = jnp.concatenate(parts, axis=1)
    routes = named[:, 0:2].astype(F32).astype(jnp.int32)
    logits = dot(rows, router_ref[...], ((1,), (1,)))
    experts = logits.shape[1]
    lane = iota(logits.shape, 1)
    first = jnp.sum(jnp.where(lane == routes[:, 0:1], logits, 0.0), axis=1, keepdims=True)
    second = jnp.sum(jnp.where(lane == routes[:, 1:2], logits, 0.0), axis=1, keepdims=True)
    gate0 = 1.0 / (1.0 + jnp.exp(second - first))
    gate1 = 1.0 / (1.0 + jnp.exp(first - second))
    taken = slot_map(me_ref[0], named, layers, experts)
    gates = jnp.where(taken[0], gate0, jnp.where(taken[1], gate1, 0.0))
    high = gates.astype(BF16)
    high_ref[...] = high
    low_ref[...] = (gates - high.astype(F32)).astype(BF16)


def attend_kernel(
    _, lengths_hbm, queries_hbm, keys_hbm, values_hbm, routes_hbm, residual_hbm, gain_hbm,
    stream_ref, first_ref, second_ref,
    lengths_ref, queries_ref, keys_ref, values_ref, routes_ref, residual_ref, gain_ref, sems,
):
    batch, window, _ = keys_ref.shape
    width = queries_ref.shape[1]
    span = width // KVH
    parts = [pl.ds(begin, PAIR * HS) for begin in range(0, KVH * HS, PAIR * HS)]
    small = [
        (lengths_hbm, lengths_ref), (queries_hbm, queries_ref), (routes_hbm, routes_ref),
        (residual_hbm, residual_ref), (gain_hbm, gain_ref),
    ]
    blocks = [pl.ds(begin, BLOCK) for begin in range(0, batch, BLOCK)]
    groups = [
        small[:3],
        *[[(keys_hbm.at[block], keys_ref.at[block])] for block in blocks],
        [(values_hbm.at[block], values_ref.at[block, 0:window]) for block in blocks],
        small[3:],
    ]
    at, copies = 0, []
    for group in groups:
        copies.append([])
        for source, target in group:
            copies[-1].append(pltpu.make_async_copy(source, target, sems.at[at]))
            copies[-1][-1].start()
            at += 1

    def wait(group):
        for copy in copies[group]:
            copy.wait()

    padded = values_ref.shape[1]
    if padded > window:
        pad = (batch, padded - window, values_ref.shape[2])
        values_ref[:, window:, :] = jnp.zeros(pad, BF16)
    wait(0)
    same = iota((batch, batch), 0) == iota((batch, batch), 1)

    def upright(row):
        return jnp.sum(jnp.where(same, row, 0), axis=1, keepdims=True)

    named, lane = jnp.zeros((batch, LANES), jnp.int32), iota((batch, LANES), 1)
    before = iota((batch, batch), 1) < iota((batch, batch), 0)
    listed = [routes_ref[k : k + 1, :] for k in range(2)]
    for k in range(2):
        route = upright(listed[k])
        earlier = before & ((listed[0] == route) | (listed[1] == route))
        place = jnp.sum(jnp.where(earlier, 1, 0), axis=1, keepdims=True)
        named = jnp.where(lane == k, route, jnp.where(lane == 2 + k, place, named))
    named = named.astype(F32).astype(BF16)
    queries = queries_ref[...]
    lanes = PAIR * GROUP * batch
    full = -(-lanes // LANES) * LANES
    _, request = split(iota((window, full), 1), batch)
    length = jnp.zeros((1, full), jnp.int32)
    for r in range(batch):
        length = jnp.where(request[0:1] == r, lengths_ref[0:1, r : r + 1], length)
    visible = iota((window, full), 0) < length
    _, owner = split(iota((lanes, padded), 0), batch)
    spreads = []
    for i in range(len(parts)):
        spread = []
        for k in range(PAIR):
            at = [(i * PAIR + k) * span + g * HS for g in range(GROUP)]
            stacked = jnp.concatenate([queries[:, c : c + HS] for c in at], axis=0)
            blank = jnp.zeros_like(stacked)
            spread.append(
                jnp.concatenate([stacked if j == k else blank for j in range(PAIR)], axis=1)
            )
        if full > lanes:
            spread.append(jnp.zeros((full - lanes, PAIR * HS), BF16))
        spreads.append(jnp.concatenate(spread, axis=0))
    total = [jnp.zeros((window, full), F32) for _ in parts]
    for b, block in enumerate(blocks):
        wait(1 + b)
        for i, part in enumerate(parts):
            keys = keys_ref[block, :, part].reshape(BLOCK * window, PAIR * HS)
            products = dot(keys, spreads[i], ((1,), (1,)))
            for r in range(BLOCK):
                mine = request == b * BLOCK + r
                total[i] = jnp.where(mine, products[r * window : (r + 1) * window], total[i])
    weighted = []
    for scores in total:
        scores = jnp.where(visible, scores * HS ** (-0.5), -1e30)
        powers = jnp.exp(scores - jnp.max(scores, axis=0, keepdims=True))
        weights = powers / jnp.sum(powers, axis=0, keepdims=True)
        if padded > window:
            weights = jnp.concatenate([weights, jnp.zeros((padded - window, full), F32)], axis=0)
        weights = weights.T[:lanes]
        weighted.append(
            jnp.concatenate(
                [jnp.where(owner == r, weights, 0.0).astype(BF16) for r in range(batch)], axis=1
            )
        )
    wait(-2)
    attended = []
    for weights, part in zip(weighted, parts):
        values = values_ref[:, :, part].reshape(batch * padded, PAIR * HS)
        mixed = dot(weights, values)
        attended += [
            mixed[h * batch : (h + 1) * batch, h // GROUP * HS : (h // GROUP + 1) * HS]
            for h in range(PAIR * GROUP)
        ]
    wait(-1)
    stream = residual_ref[...].astype(F32) + jnp.concatenate(attended, axis=1)
    scale = lax.rsqrt(jnp.mean(stream * stream, axis=1, keepdims=True) + 1e-05)
    stream_ref[...] = stream
    half = width // 2
    normed = (stream * scale * gain_ref[...]).astype(BF16)
    first_ref[:, :half] = normed[:, :half]
    first_ref[:, half:] = named
    second_ref[...] = normed[:, half:]


def pass_kernel(*_):
    pass


def pass_on(values, cost):
    return pl.pallas_call(
        pass_kernel,
        in_specs=[ANY] * len(values),
        out_specs=[ANY] * len(values),
        out_shape=[jax.ShapeDtypeStruct(value.shape, value.dtype) for value in values],
        input_output_aliases={i: i for i in range(len(values))},
        cost_estimate=cost,
        compiler_params=params(0),
    )(*values)


def stack(refs):
    return jnp.concatenate([ref[...] for ref in refs], axis=0)


def gather(refs, layers):
    first = stack(refs[:layers])
    half = first.shape[1] - LANES
    parts = [first[:, :half]] + [stack(refs[at : at + layers]) for at in range(layers, len(refs), layers)]
    return parts, first[:, half:]


def split_kernel(me_ref, *refs, layers, part):
    parts, named = gather(refs[: (1 + part) * layers], layers)
    outs = refs[(1 + part) * layers :]
    slots = dispatch(me_ref[0], parts[part], named, layers, len(outs))
    span = layers * CAP
    for e, ref in enumerate(outs):
        ref[...] = slots[e * span : (e + 1) * span].astype(BF16)


def strip_copies(source, begin, target, sems):
    strip = target.shape[1] // sems.shape[0]
    copies = [
        pltpu.make_async_copy(
            source.at[:, pl.ds(begin + c * strip, strip)],
            target.at[:, pl.ds(c * strip, strip)],
            sems.at[c],
        )
        for c in range(sems.shape[0])
    ]
    for copy in copies:
        copy.start()
    return copies


def tiles(count, tile):
    steps = count // tile
    unroll = max(u for u in range(1, UNROLL + 1) if steps % u == 0)

    def run(body):
        @pl.loop(0, steps, unroll=unroll)
        def _(i):
            body(pl.ds(pl.multiple_of(i * tile, tile), tile))

    return run


def store_rows(outs, at, value):
    span = outs[0].shape[0]
    for e, ref in enumerate(outs):
        ref[:, at] = value[e * span : (e + 1) * span].astype(BF16)


def begin_kernel(*refs, experts):
    _, gate_ref, up_ref, down_hbm, gate_out, up_out, down_out, rows_ref, sems = refs[experts:]
    half = rows_ref.shape[1]
    copies = strip_copies(down_hbm, 0, down_out, sems)
    rows_ref[...] = stack(refs[:experts])
    units = gate_ref.shape[1]

    @tiles(units, min(TILE, units))
    def _(at):
        gate_out[:, at] = dot(rows_ref[...], gate_ref[:half, at])
        up_out[:, at] = dot(rows_ref[...], up_ref[:half, at])

    for copy in copies:
        copy.wait()


def middle_kernel(*refs, experts):
    gate_in, up_in, down_in, gate_ref, up_ref, down_hbm = refs[experts : experts + 6]
    outs = refs[experts + 6 : -4]
    hidden_ref, down_out, rows_ref, sems = refs[-4:]
    half = rows_ref.shape[1]
    copies = strip_copies(down_hbm, half, down_out, sems)
    rows_ref[...] = stack(refs[:experts])
    units = gate_ref.shape[1]

    @tiles(units, min(TILE, units))
    def _(at):
        gate = gate_in[:, at] + dot(rows_ref[...], gate_ref[half:, at])
        up = up_in[:, at] + dot(rows_ref[...], up_ref[half:, at])
        hidden_ref[:, at] = (jax.nn.silu(gate) * up).astype(BF16)

    @tiles(half, min(TILE, half))
    def _(at):
        store_rows(outs, at, dot(hidden_ref[...], down_in[:, at]))

    for copy in copies:
        copy.wait()


def end_kernel(hidden_ref, down_ref, *outs):
    half = down_ref.shape[1]

    @tiles(half, min(TILE, half))
    def _(at):
        store_rows(outs, at, dot(hidden_ref[...], down_ref[:, at]))


def mix_kernel(high_ref, low_ref, *refs, layers, part):
    outs, stream_ref = refs[-layers:], refs[-layers - 1]
    blocks = refs[: -layers - 1]
    order = same_core_first(len(blocks))
    returned = stack([blocks[order.index(e)] for e in range(len(blocks))])
    mixed = dot(high_ref[...], returned) + dot(low_ref[...], returned)
    batch, half = outs[0].shape
    for j, ref in enumerate(outs):
        value = mixed[j * batch : (j + 1) * batch]
        if j == 0:
            value = value + stream_ref[:, part * half : (part + 1) * half]
        ref[...] = value.astype(ref.dtype)


def add_kernel(*refs):
    out_ref = refs[-1]
    span = refs[-2].shape[1]
    if out_ref.shape[1] > span:
        out_ref[:, :span] = refs[0][...]
        refs = refs[1:]
    total = refs[0][...]
    for ref in refs[1:-1]:
        total = total + ref[...].astype(F32)
    out_ref[:, out_ref.shape[1] - span :] = total.astype(BF16)


def in_hbm(value):
    return pltpu.with_memory_space_constraint(value, pltpu.HBM)


def swap(value, axis, step):
    if step == 0:
        return value
    count = lax.axis_size(axis)
    return lax.ppermute(value, axis, [(i, i ^ step) for i in range(count)])


def farthest_first(count):
    return [0, *range(count - 1, 0, -1)]


def same_core_first(count):
    return [*range(0, count, 2), *range(count - 1, 0, -2)]


def params(elements):
    return pltpu.CompilerParams(vmem_limit_bytes=min(48 * MIB, 2 * MIB + 10 * elements))


def shards(
    queries,
    cached_keys,
    cached_values,
    lengths,
    routes,
    residual,
    norm_gain,
    router,
    gate_proj,
    up_proj,
    down_proj,
):
    batch, width = queries.shape
    experts = router.shape[1]
    layers = lax.axis_size("attn")
    me = lax.axis_index("expert").astype(jnp.int32).reshape(1)
    router = router.T
    shape = jax.ShapeDtypeStruct
    operands = [
        in_hbm(a)
        for a in (
            lengths[None], queries, cached_keys, cached_values, routes.T, residual, norm_gain[None]
        )
    ]
    window, depth = cached_values.shape[1:]
    held = [a.shape for a in operands]
    held[3] = (batch, -(-window // LANES) * LANES, depth)
    half = width // 2
    stream, *payload = pl.pallas_call(
        attend_kernel,
        in_specs=[SCALAR] + [ANY] * len(operands),
        out_specs=[WHOLE] * 3,
        out_shape=[shape((batch, width), F32)]
        + [shape((batch, size), BF16) for size in (half + LANES, half)],
        scratch_shapes=[pltpu.VMEM(size, a.dtype) for size, a in zip(held, operands)]
        + [pltpu.SemaphoreType.DMA((5 + 2 * (batch // BLOCK),))],
        compiler_params=params(28 * batch * width),
        cost_estimate=LIGHT,
    )(me, *operands)

    payload = pass_on(payload, BUSY)

    order = same_core_first(experts)
    chunks, arrived = [], []
    for part in range(2):
        came = {j: swap(payload[part], "attn", j) for j in farthest_first(layers)}
        chunks += [came[j] for j in range(layers)]
        slots = pl.pallas_call(
            functools.partial(split_kernel, layers=layers, part=part),
            in_specs=[SCALAR] + [WHOLE] * len(chunks),
            out_specs=[WHOLE] * experts,
            out_shape=[shape((layers * CAP, half), BF16)] * experts,
            cost_estimate=MID if part else LIGHT,
            compiler_params=params(experts * layers * CAP * half),
        )(me, *chunks)
        arrived.append([swap(slots[e], "expert", e) for e in order])
    gates = pl.pallas_call(
        functools.partial(weigh_kernel, layers=layers),
        in_specs=[SCALAR] + [WHOLE] * (1 + len(chunks)),
        out_specs=[WHOLE] * 2,
        out_shape=[shape((layers * batch, experts * layers * CAP), BF16)] * 2,
        cost_estimate=LIGHT,
        compiler_params=params(layers * batch * width),
    )(me, router, *chunks)

    total_rows = experts * layers * CAP
    units = gate_proj.shape[2]
    gate, up, down = gate_proj[0], up_proj[0], in_hbm(down_proj[0])
    rows = pltpu.VMEM((total_rows, half), BF16)
    strips = pltpu.SemaphoreType.DMA((STRIPS,))
    halves = [shape((layers * CAP, half), BF16)] * experts
    *sums, down_first = pl.pallas_call(
        functools.partial(begin_kernel, experts=experts),
        in_specs=[WHOLE] * experts + [ANY] + [WHOLE] * 2 + [ANY],
        out_specs=[WHOLE] * 3,
        out_shape=[shape((total_rows, units), F32)] * 2 + [pltpu.VMEM((units, half), BF16)],
        scratch_shapes=[rows, strips],
        cost_estimate=pl.CostEstimate(
            flops=4 * total_rows * half * units, bytes_accessed=0, transcendentals=0
        ),
        compiler_params=params(total_rows * width),
    )(*arrived[0], gates[0], gate, up, down)
    *first, hidden, down_second = pl.pallas_call(
        functools.partial(middle_kernel, experts=experts),
        in_specs=[WHOLE] * (experts + 5) + [ANY],
        out_specs=[WHOLE] * (experts + 2),
        out_shape=halves + [shape((total_rows, units), BF16), pltpu.VMEM((units, half), BF16)],
        scratch_shapes=[rows, strips],
        compiler_params=params(total_rows * width),
    )(*arrived[1], *sums, down_first, gate, up, down)
    second = pl.pallas_call(
        end_kernel,
        in_specs=[WHOLE] * 2,
        out_specs=[WHOLE] * experts,
        out_shape=halves,
        cost_estimate=pl.CostEstimate(
            flops=2 * total_rows * half * units, bytes_accessed=0, transcendentals=0
        ),
        compiler_params=params(total_rows * width),
    )(hidden, down_second)

    done = []
    for part, blocks in enumerate((first, second)):
        returned = [swap(block, "expert", e) for e, block in zip(order, blocks)]
        mixed = pl.pallas_call(
            functools.partial(mix_kernel, layers=layers, part=part),
            in_specs=[WHOLE] * (3 + experts),
            out_specs=[WHOLE] * layers,
            out_shape=[shape((batch, half), BF16 if j else F32) for j in range(layers)],
            cost_estimate=LIGHT,
            compiler_params=params(experts * layers * CAP * half),
        )(*gates, *returned, stream)
        sums = [swap(mixed[j], "attn", j) for j in farthest_first(layers)]
        done = [
            pl.pallas_call(
                add_kernel,
                in_specs=[WHOLE] * (layers + len(done)),
                out_specs=WHOLE,
                out_shape=shape((batch, width if part else half), BF16),
                cost_estimate=LIGHT,
                compiler_params=params(layers * batch * width),
            )(*done, *sums)
        ]
    return done[0]


def solution(mesh):
    in_specs = (
        P(("groups", "attn", "expert"), None),
        P(("groups", "attn", "expert"), None, None),
        P(("groups", "attn", "expert"), None, None),
        P(("groups", "attn", "expert")),
        P(("groups", "attn", "expert"), None),
        P(("groups", "attn", "expert"), None),
        P(),
        P(),
        P("expert", None, "attn"),
        P("expert", None, "attn"),
        P("expert", "attn", None),
    )
    out_specs = P(("groups", "attn", "expert"), None)
    return jax.shard_map(shards, mesh=mesh, in_specs=in_specs, out_specs=out_specs, check_vma=False)
```

```python
import functools

import jax
import jax.numpy as jnp
from jax import lax
from jax.experimental import pallas as pl
from jax.experimental.pallas import tpu as pltpu
from jax.sharding import PartitionSpec as P

HS = 128
KVH = 4
GROUP = 6
CAP = 8
LANES = 128
PAIR = 2
BLOCK = 8
STRIPS = 3
TILE = 256
UNROLL = 6
MIB = 1 << 20
F32 = jnp.float32
BF16 = jnp.bfloat16
LIGHT = pl.CostEstimate(flops=0, bytes_accessed=0, transcendentals=0)
BUSY = pl.CostEstimate(flops=24 * 10**9, bytes_accessed=0, transcendentals=0)
MID = pl.CostEstimate(flops=2 * 10**9, bytes_accessed=0, transcendentals=0)
ANY = pl.BlockSpec(memory_space=pl.ANY)
WHOLE = pl.BlockSpec(memory_space=pltpu.VMEM)
SCALAR = pl.BlockSpec(memory_space=pltpu.SMEM)


def dot(a, b, dims=((1,), (0,))):
    return lax.dot_general(a, b, (dims, ((), ())), preferred_element_type=F32)


def iota(shape, dim):
    return lax.broadcasted_iota(jnp.int32, shape, dim)


def split(index, size):
    if size & (size - 1):
        return lax.div(index, size), lax.rem(index, size)
    return index >> (size.bit_length() - 1), index & (size - 1)


def slot_map(me, named, chunks, experts):
    named = named[:, 0:4].astype(F32).astype(jnp.int32)
    owners, places = named[:, 0:2] ^ me, named[:, 2:4]
    rows, slots = named.shape[0], experts * chunks * CAP
    group, place = split(iota((rows, slots), 1), CAP)
    expert, chunk = split(group, chunks)
    taken = [(owners[:, k : k + 1] == expert) & (places[:, k : k + 1] == place) for k in range(2)]
    here = split(iota((rows, slots), 0), rows // chunks)[0] == chunk
    return taken[0] & here, taken[1] & here


def dispatch(me, rows, named, chunks, experts):
    first, second = slot_map(me, named, chunks, experts)
    table = jnp.where(first | second, 1.0, 0.0).astype(BF16)
    return dot(table, rows, ((0,), (0,)))


def weigh_kernel(me_ref, router_ref, *refs, layers):
    high_ref, low_ref = refs[-2:]
    parts, named = gather(refs[:-2], layers)
    rows = jnp.concatenate(parts, axis=1)
    routes = named[:, 0:2].astype(F32).astype(jnp.int32)
    logits = dot(rows, router_ref[...], ((1,), (1,)))
    experts = logits.shape[1]
    lane = iota(logits.shape, 1)
    first = jnp.sum(jnp.where(lane == routes[:, 0:1], logits, 0.0), axis=1, keepdims=True)
    second = jnp.sum(jnp.where(lane == routes[:, 1:2], logits, 0.0), axis=1, keepdims=True)
    gate0 = 1.0 / (1.0 + jnp.exp(second - first))
    gate1 = 1.0 / (1.0 + jnp.exp(first - second))
    taken = slot_map(me_ref[0], named, layers, experts)
    gates = jnp.where(taken[0], gate0, jnp.where(taken[1], gate1, 0.0))
    high = gates.astype(BF16)
    high_ref[...] = high
    low_ref[...] = (gates - high.astype(F32)).astype(BF16)


def attend_kernel(
    _, lengths_hbm, queries_hbm, keys_hbm, values_hbm, routes_hbm, residual_hbm, gain_hbm,
    stream_ref, first_ref, second_ref,
    lengths_ref, queries_ref, keys_ref, values_ref, routes_ref, residual_ref, gain_ref, sems,
):
    batch, window, _ = keys_ref.shape
    width = queries_ref.shape[1]
    span = width // KVH
    parts = [pl.ds(begin, PAIR * HS) for begin in range(0, KVH * HS, PAIR * HS)]
    small = [
        (lengths_hbm, lengths_ref), (queries_hbm, queries_ref), (routes_hbm, routes_ref),
        (residual_hbm, residual_ref), (gain_hbm, gain_ref),
    ]
    blocks = [pl.ds(begin, BLOCK) for begin in range(0, batch, BLOCK)]
    groups = [
        small[:3],
        *[[(keys_hbm.at[block], keys_ref.at[block])] for block in blocks],
        [(values_hbm.at[block], values_ref.at[block, 0:window]) for block in blocks],
        small[3:],
    ]
    at, copies = 0, []
    for group in groups:
        copies.append([])
        for source, target in group:
            copies[-1].append(pltpu.make_async_copy(source, target, sems.at[at]))
            copies[-1][-1].start()
            at += 1

    def wait(group):
        for copy in copies[group]:
            copy.wait()

    padded = values_ref.shape[1]
    if padded > window:
        pad = (batch, padded - window, values_ref.shape[2])
        values_ref[:, window:, :] = jnp.zeros(pad, BF16)
    wait(0)
    same = iota((batch, batch), 0) == iota((batch, batch), 1)

    def upright(row):
        return jnp.sum(jnp.where(same, row, 0), axis=1, keepdims=True)

    named, lane = jnp.zeros((batch, LANES), jnp.int32), iota((batch, LANES), 1)
    before = iota((batch, batch), 1) < iota((batch, batch), 0)
    listed = [routes_ref[k : k + 1, :] for k in range(2)]
    for k in range(2):
        route = upright(listed[k])
        earlier = before & ((listed[0] == route) | (listed[1] == route))
        place = jnp.sum(jnp.where(earlier, 1, 0), axis=1, keepdims=True)
        named = jnp.where(lane == k, route, jnp.where(lane == 2 + k, place, named))
    named = named.astype(F32).astype(BF16)
    queries = queries_ref[...]
    lanes = PAIR * GROUP * batch
    full = -(-lanes // LANES) * LANES
    _, request = split(iota((window, full), 1), batch)
    length = jnp.zeros((1, full), jnp.int32)
    for r in range(batch):
        length = jnp.where(request[0:1] == r, lengths_ref[0:1, r : r + 1], length)
    visible = iota((window, full), 0) < length
    _, owner = split(iota((lanes, padded), 0), batch)
    spreads = []
    for i in range(len(parts)):
        spread = []
        for k in range(PAIR):
            at = [(i * PAIR + k) * span + g * HS for g in range(GROUP)]
            stacked = jnp.concatenate([queries[:, c : c + HS] for c in at], axis=0)
            blank = jnp.zeros_like(stacked)
            spread.append(
                jnp.concatenate([stacked if j == k else blank for j in range(PAIR)], axis=1)
            )
        if full > lanes:
            spread.append(jnp.zeros((full - lanes, PAIR * HS), BF16))
        spreads.append(jnp.concatenate(spread, axis=0))
    total = [jnp.zeros((window, full), F32) for _ in parts]
    for b, block in enumerate(blocks):
        wait(1 + b)
        for i, part in enumerate(parts):
            keys = keys_ref[block, :, part].reshape(BLOCK * window, PAIR * HS)
            products = dot(keys, spreads[i], ((1,), (1,)))
            for r in range(BLOCK):
                mine = request == b * BLOCK + r
                total[i] = jnp.where(mine, products[r * window : (r + 1) * window], total[i])
    weighted = []
    for scores in total:
        scores = jnp.where(visible, scores * HS ** (-0.5), -1e30)
        powers = jnp.exp(scores - jnp.max(scores, axis=0, keepdims=True))
        weights = powers / jnp.sum(powers, axis=0, keepdims=True)
        if padded > window:
            weights = jnp.concatenate([weights, jnp.zeros((padded - window, full), F32)], axis=0)
        weights = weights.T[:lanes]
        weighted.append(
            jnp.concatenate(
                [jnp.where(owner == r, weights, 0.0).astype(BF16) for r in range(batch)], axis=1
            )
        )
    wait(-2)
    attended = []
    for weights, part in zip(weighted, parts):
        values = values_ref[:, :, part].reshape(batch * padded, PAIR * HS)
        mixed = dot(weights, values)
        attended += [
            mixed[h * batch : (h + 1) * batch, h // GROUP * HS : (h // GROUP + 1) * HS]
            for h in range(PAIR * GROUP)
        ]
    wait(-1)
    stream = residual_ref[...].astype(F32) + jnp.concatenate(attended, axis=1)
    scale = lax.rsqrt(jnp.mean(stream * stream, axis=1, keepdims=True) + 1e-05)
    stream_ref[...] = stream
    half = width // 2
    normed = (stream * scale * gain_ref[...]).astype(BF16)
    first_ref[:, :half] = normed[:, :half]
    first_ref[:, half:] = named
    second_ref[...] = normed[:, half:]


def pass_kernel(*_):
    pass


def pass_on(values, cost):
    return pl.pallas_call(
        pass_kernel,
        in_specs=[ANY] * len(values),
        out_specs=[ANY] * len(values),
        out_shape=[jax.ShapeDtypeStruct(value.shape, value.dtype) for value in values],
        input_output_aliases={i: i for i in range(len(values))},
        cost_estimate=cost,
        compiler_params=params(0),
    )(*values)


def stack(refs):
    return jnp.concatenate([ref[...] for ref in refs], axis=0)


def gather(refs, layers):
    first = stack(refs[:layers])
    half = first.shape[1] - LANES
    parts = [first[:, :half]] + [stack(refs[at : at + layers]) for at in range(layers, len(refs), layers)]
    return parts, first[:, half:]


def split_kernel(me_ref, *refs, layers, part):
    parts, named = gather(refs[: (1 + part) * layers], layers)
    outs = refs[(1 + part) * layers :]
    slots = dispatch(me_ref[0], parts[part], named, layers, len(outs))
    span = layers * CAP
    for e, ref in enumerate(outs):
        ref[...] = slots[e * span : (e + 1) * span].astype(BF16)


def strip_copies(source, begin, target, sems):
    strip = target.shape[1] // sems.shape[0]
    copies = [
        pltpu.make_async_copy(
            source.at[:, pl.ds(begin + c * strip, strip)],
            target.at[:, pl.ds(c * strip, strip)],
            sems.at[c],
        )
        for c in range(sems.shape[0])
    ]
    for copy in copies:
        copy.start()
    return copies


def tiles(count, tile):
    steps = count // tile
    unroll = max(u for u in range(1, UNROLL + 1) if steps % u == 0)

    def run(body):
        @pl.loop(0, steps, unroll=unroll)
        def _(i):
            body(pl.ds(pl.multiple_of(i * tile, tile), tile))

    return run


def store_rows(outs, at, value):
    span = outs[0].shape[0]
    for e, ref in enumerate(outs):
        ref[:, at] = value[e * span : (e + 1) * span].astype(BF16)


def begin_kernel(*refs, experts):
    _, gate_ref, up_ref, down_hbm, gate_out, up_out, down_out, rows_ref, sems = refs[experts:]
    half = rows_ref.shape[1]
    copies = strip_copies(down_hbm, 0, down_out, sems)
    rows_ref[...] = stack(refs[:experts])
    units = gate_ref.shape[1]

    @tiles(units, min(TILE, units))
    def _(at):
        gate_out[:, at] = dot(rows_ref[...], gate_ref[:half, at])
        up_out[:, at] = dot(rows_ref[...], up_ref[:half, at])

    for copy in copies:
        copy.wait()


def middle_kernel(*refs, experts):
    gate_in, up_in, down_in, gate_ref, up_ref, down_hbm = refs[experts : experts + 6]
    outs = refs[experts + 6 : -4]
    hidden_ref, down_out, rows_ref, sems = refs[-4:]
    half = rows_ref.shape[1]
    copies = strip_copies(down_hbm, half, down_out, sems)
    rows_ref[...] = stack(refs[:experts])
    units = gate_ref.shape[1]

    @tiles(units, min(TILE, units))
    def _(at):
        gate = gate_in[:, at] + dot(rows_ref[...], gate_ref[half:, at])
        up = up_in[:, at] + dot(rows_ref[...], up_ref[half:, at])
        hidden_ref[:, at] = (jax.nn.silu(gate) * up).astype(BF16)

    @tiles(half, min(TILE, half))
    def _(at):
        store_rows(outs, at, dot(hidden_ref[...], down_in[:, at]))

    for copy in copies:
        copy.wait()


def end_kernel(hidden_ref, down_ref, *outs):
    half = down_ref.shape[1]

    @tiles(half, min(TILE, half))
    def _(at):
        store_rows(outs, at, dot(hidden_ref[...], down_ref[:, at]))


def mix_kernel(high_ref, low_ref, *refs, layers, part):
    outs, stream_ref = refs[-layers:], refs[-layers - 1]
    blocks = refs[: -layers - 1]
    order = same_core_first(len(blocks))
    returned = stack([blocks[order.index(e)] for e in range(len(blocks))])
    mixed = dot(high_ref[...], returned) + dot(low_ref[...], returned)
    batch, half = outs[0].shape
    for j, ref in enumerate(outs):
        value = mixed[j * batch : (j + 1) * batch]
        if j == 0:
            value = value + stream_ref[:, part * half : (part + 1) * half]
        ref[...] = value.astype(ref.dtype)


def add_kernel(*refs):
    out_ref = refs[-1]
    span = refs[-2].shape[1]
    if out_ref.shape[1] > span:
        out_ref[:, :span] = refs[0][...]
        refs = refs[1:]
    total = refs[0][...]
    for ref in refs[1:-1]:
        total = total + ref[...].astype(F32)
    out_ref[:, out_ref.shape[1] - span :] = total.astype(BF16)


def in_hbm(value):
    return pltpu.with_memory_space_constraint(value, pltpu.HBM)


def swap(value, axis, step):
    if step == 0:
        return value
    count = lax.axis_size(axis)
    return lax.ppermute(value, axis, [(i, i ^ step) for i in range(count)])


def farthest_first(count):
    return [0, *range(count - 1, 0, -1)]


def same_core_first(count):
    return [*range(0, count, 2), *range(count - 1, 0, -2)]


def params(elements):
    return pltpu.CompilerParams(vmem_limit_bytes=min(48 * MIB, 2 * MIB + 10 * elements))


def shards(
    queries,
    cached_keys,
    cached_values,
    lengths,
    routes,
    residual,
    norm_gain,
    router,
    gate_proj,
    up_proj,
    down_proj,
):
    batch, width = queries.shape
    experts = router.shape[1]
    layers = lax.axis_size("attn")
    me = lax.axis_index("expert").astype(jnp.int32).reshape(1)
    router = router.T
    shape = jax.ShapeDtypeStruct
    operands = [
        in_hbm(a)
        for a in (
            lengths[None], queries, cached_keys, cached_values, routes.T, residual, norm_gain[None]
        )
    ]
    window, depth = cached_values.shape[1:]
    held = [a.shape for a in operands]
    held[3] = (batch, -(-window // LANES) * LANES, depth)
    half = width // 2
    stream, *payload = pl.pallas_call(
        attend_kernel,
        in_specs=[SCALAR] + [ANY] * len(operands),
        out_specs=[WHOLE] * 3,
        out_shape=[shape((batch, width), F32)]
        + [shape((batch, size), BF16) for size in (half + LANES, half)],
        scratch_shapes=[pltpu.VMEM(size, a.dtype) for size, a in zip(held, operands)]
        + [pltpu.SemaphoreType.DMA((5 + 2 * (batch // BLOCK),))],
        compiler_params=params(28 * batch * width),
        cost_estimate=LIGHT,
    )(me, *operands)

    payload = pass_on(payload, BUSY)

    order = same_core_first(experts)
    chunks, arrived = [], []
    for part in range(2):
        came = {j: swap(payload[part], "attn", j) for j in farthest_first(layers)}
        chunks += [came[j] for j in range(layers)]
        slots = pl.pallas_call(
            functools.partial(split_kernel, layers=layers, part=part),
            in_specs=[SCALAR] + [WHOLE] * len(chunks),
            out_specs=[WHOLE] * experts,
            out_shape=[shape((layers * CAP, half), BF16)] * experts,
            cost_estimate=MID if part else LIGHT,
            compiler_params=params(experts * layers * CAP * half),
        )(me, *chunks)
        arrived.append([swap(slots[e], "expert", e) for e in order])
    gates = pl.pallas_call(
        functools.partial(weigh_kernel, layers=layers),
        in_specs=[SCALAR] + [WHOLE] * (1 + len(chunks)),
        out_specs=[WHOLE] * 2,
        out_shape=[shape((layers * batch, experts * layers * CAP), BF16)] * 2,
        cost_estimate=LIGHT,
        compiler_params=params(layers * batch * width),
    )(me, router, *chunks)

    total_rows = experts * layers * CAP
    units = gate_proj.shape[2]
    gate, up, down = gate_proj[0], up_proj[0], in_hbm(down_proj[0])
    rows = pltpu.VMEM((total_rows, half), BF16)
    strips = pltpu.SemaphoreType.DMA((STRIPS,))
    halves = [shape((layers * CAP, half), BF16)] * experts
    *sums, down_first = pl.pallas_call(
        functools.partial(begin_kernel, experts=experts),
        in_specs=[WHOLE] * experts + [ANY] + [WHOLE] * 2 + [ANY],
        out_specs=[WHOLE] * 3,
        out_shape=[shape((total_rows, units), F32)] * 2 + [pltpu.VMEM((units, half), BF16)],
        scratch_shapes=[rows, strips],
        cost_estimate=pl.CostEstimate(
            flops=4 * total_rows * half * units, bytes_accessed=0, transcendentals=0
        ),
        compiler_params=params(total_rows * width),
    )(*arrived[0], gates[0], gate, up, down)
    *first, hidden, down_second = pl.pallas_call(
        functools.partial(middle_kernel, experts=experts),
        in_specs=[WHOLE] * (experts + 5) + [ANY],
        out_specs=[WHOLE] * (experts + 2),
        out_shape=halves + [shape((total_rows, units), BF16), pltpu.VMEM((units, half), BF16)],
        scratch_shapes=[rows, strips],
        compiler_params=params(total_rows * width),
    )(*arrived[1], *sums, down_first, gate, up, down)
    second = pl.pallas_call(
        end_kernel,
        in_specs=[WHOLE] * 2,
        out_specs=[WHOLE] * experts,
        out_shape=halves,
        cost_estimate=pl.CostEstimate(
            flops=2 * total_rows * half * units, bytes_accessed=0, transcendentals=0
        ),
        compiler_params=params(total_rows * width),
    )(hidden, down_second)

    done = []
    for part, blocks in enumerate((first, second)):
        returned = [swap(block, "expert", e) for e, block in zip(order, blocks)]
        mixed = pl.pallas_call(
            functools.partial(mix_kernel, layers=layers, part=part),
            in_specs=[WHOLE] * (3 + experts),
            out_specs=[WHOLE] * layers,
            out_shape=[shape((batch, half), BF16 if j else F32) for j in range(layers)],
            cost_estimate=LIGHT,
            compiler_params=params(experts * layers * CAP * half),
        )(*gates, *returned, stream)
        sums = [swap(mixed[j], "attn", j) for j in farthest_first(layers)]
        done = [
            pl.pallas_call(
                add_kernel,
                in_specs=[WHOLE] * (layers + len(done)),
                out_specs=WHOLE,
                out_shape=shape((batch, width if part else half), BF16),
                cost_estimate=LIGHT,
                compiler_params=params(layers * batch * width),
            )(*done, *sums)
        ]
    return done[0]


def solution(mesh):
    in_specs = (
        P(("groups", "attn", "expert"), None),
        P(("groups", "attn", "expert"), None, None),
        P(("groups", "attn", "expert"), None, None),
        P(("groups", "attn", "expert")),
        P(("groups", "attn", "expert"), None),
        P(("groups", "attn", "expert"), None),
        P(),
        P(),
        P("expert", None, "attn"),
        P("expert", None, "attn"),
        P("expert", "attn", None),
    )
    out_specs = P(("groups", "attn", "expert"), None)
    return jax.shard_map(shards, mesh=mesh, in_specs=in_specs, out_specs=out_specs, check_vma=False)
```
